32 devices in a mesh: scene: 4 (over y, x), view: 4 (over z), row: 2 (over core).
Axes of the slice: x: 2, y: 2, z: 4, core: 2. Of those that a mesh axis runs over, the one named last changes fastest.
Arguments:
- latents: bfloat16 [4, 16, 2, 32, 1536], P('scene', 'view', 'row'), may hold values from -6 to 6
- norm_gain: float32 [1536], replicated, may hold values from 0.5 to 4
- w_query: bfloat16 [1536, 768], replicated, may hold values from -0.15625 to 0.15625
- w_key: bfloat16 [1536, 768], replicated, may hold values from -0.15625 to 0.15625
- w_value: bfloat16 [1536, 768], replicated, may hold values from -0.15625 to 0.15625
- w_out: bfloat16 [768, 1536], replicated, may hold values from -0.21875 to 0.21875
- kernel: bfloat16 [9, 1536], replicated, may hold values from -4 to 4
- partners: int32 [4, 16, 3], P('scene', 'view'), may hold values from -1 to 15, as said below
- counts: int32 [4, 16], P('scene', 'view'), may hold values from 2 to 3, as said below
- cotangent: bfloat16 [4, 16, 2, 32, 1536], P('scene', 'view', 'row'), may hold values from -1.5 to 1.5
Outputs:
- grad_query: float32 [1536, 768], P(('scene', 'view', 'row'))
- grad_key: float32 [1536, 768], P(('scene', 'view', 'row'))
- grad_value: float32 [1536, 768], P(('scene', 'view', 'row'))
- grad_out: float32 [768, 1536], P(('scene', 'view', 'row'))
The draws below stay inside these ranges and needn't reach their ends.
Inputs may be any that keep to these rules, and one draw needn't show every extreme that they name: Entries j < counts of a view are distinct views held by other groups of 4 views (views 4 * i to 4 * i + 3 form group i); all partners that the views of one group take from another group are one and the same view; entries from counts on are -1. `counts`: the first view of every group has 3 partners.
All inputs are finite; a program needn't handle non-finite values.
Results may differ from the reference program's by a relative error of at most 0.0049.
The reference program's roundings to bfloat16 on the way count: a program that leaves them out, or rounds other values in their place, can miss the bound.
Values may be sent and summed in bfloat16 or wider, within the bound.
No kernel may reach another device: no remote copies, remote signals or barrier semaphores. Data moves between devices by JAX's collectives and lax.ppermute only.
A program may use at most 192 MiB of HBM per device.

```python
import jax
import jax.numpy as jnp
from jax import lax

D = 1536
HEADS = 12
HEAD_DIM = 64
W = 32
VIEW_DEV = 4
ROWS_DEV = 1
SCENES = 4
VIEWS = 16
H = 2
MAXP = 3
INNER = 768
N_ROW = 2


def pair_tables(key):
    group_count = VIEWS // VIEW_DEV
    key_local, key_order, key_count = jax.random.split(key, 3)
    chosen = jax.random.randint(key_local, (SCENES, group_count, group_count), 0, VIEW_DEV)
    order_keys = jax.random.split(key_order, SCENES * VIEWS)
    orders = jax.vmap(lambda order_key: jax.random.permutation(order_key, group_count - 1))(order_keys)
    orders = orders.reshape(SCENES, VIEWS, group_count - 1)[:, :, :MAXP]
    home = jnp.arange(VIEWS, dtype=jnp.int32) // VIEW_DEV
    source = (home[None, :, None] + 1 + orders) % group_count
    chosen_rows = jnp.take(chosen, home, axis=1)
    local_view = jnp.take_along_axis(chosen_rows, source, axis=2)
    partner_ids = source * VIEW_DEV + local_view
    drawn = jax.random.randint(key_count, (SCENES, VIEWS), 2, MAXP + 1)
    count_rows = jnp.where((jnp.arange(VIEWS) % VIEW_DEV == 0)[None, :], MAXP, drawn)
    partner_ids = jnp.where(jnp.arange(MAXP)[None, None, :] < count_rows[:, :, None], partner_ids, -1)
    return (partner_ids.astype(jnp.int32), count_rows.astype(jnp.int32))


def draw_partners(key, part):
    return pair_tables(key)[0]


def draw_counts(key, part):
    return pair_tables(key)[1]


def draw_norm_gain(key, part):
    key = jax.random.fold_in(key, 5)
    return jax.random.uniform(key, (D,), jnp.float32, 0.5, 1.5)


def block_levels(own_key, dims, pieces, low, top_value):
    gain, own = 1.0, jax.random.fold_in(own_key, 6)
    for position, parts in pieces:
        steps = jnp.exp(jax.random.uniform(jax.random.fold_in(own, position), (parts,), jnp.float32, low / len(pieces), top_value / len(pieces)))
        gain = gain * jnp.repeat(steps, dims[position] // parts).reshape([-1 if axis == position else 1 for axis in range(len(dims))])
    return gain


def normal_values(rng, dims, scale, most, pieces=(), kind=jnp.bfloat16):
    gain = block_levels(rng, dims, pieces, -0.22, 0.18) if pieces else 1.0
    entries = jax.random.normal(rng, dims, jnp.float32) * scale * gain
    return jnp.minimum(jnp.maximum(entries, -most), most).astype(kind)


def setup_inputs(seed: int = 0) -> dict:
    seeds = jax.random.split(jax.random.key(seed), 11)
    return {
        "latents": normal_values(seeds[0], (SCENES, VIEWS, H, W, D), 1.0, 6.0, ((0, 4), (1, 4), (2, 2))),
        "norm_gain": draw_norm_gain(jax.random.fold_in(seeds[10], 71), 0),
        "w_query": normal_values(seeds[2], (D, INNER), D ** -0.5, 0.15625),
        "w_key": normal_values(seeds[3], (D, INNER), D ** -0.5, 0.15625),
        "w_value": normal_values(seeds[4], (D, INNER), D ** -0.5, 0.15625),
        "w_out": normal_values(seeds[5], (INNER, D), INNER ** -0.5, 0.21875),
        "kernel": normal_values(seeds[6], (9, D), 0.3, 4.0),
        "partners": draw_partners(jax.random.fold_in(seeds[10], 71), 0),
        "counts": draw_counts(jax.random.fold_in(seeds[10], 71), 0),
        "cotangent": normal_values(seeds[9], (SCENES, VIEWS, H, W, D), 0.1, 1.5, ((0, 4), (1, 4), (2, 2))),
    }


epsilon = 1e-06

def rim_conv(padded, kernel, rows, columns):
    result = padded[:, 1:1 + rows, 1:1 + columns].astype(jnp.float32)
    for row_step in range(3):
        for col_step in range(3):
            result = result + kernel[3 * row_step + col_step].astype(jnp.float32) * padded[:, 2 - row_step:2 - row_step + rows, 2 - col_step:2 - col_step + columns].astype(jnp.float32)
    return result.astype(jnp.bfloat16)

def rounded(values):
    return lax.optimization_barrier(values.astype(jnp.bfloat16)).astype(jnp.float32)

def reference(latents, norm_gain, w_query, w_key, w_value, w_out, kernel, partners, counts, cotangent):
    inner_width = HEADS * HEAD_DIM
    scale = HEAD_DIM ** (-0.5)
    view_tokens = H * W
    strip_tokens = ROWS_DEV * W
    block_count = 1 + MAXP
    group_count = VIEWS // VIEW_DEV
    pair_weight = jnp.concatenate((w_key, w_value), axis=1)

    def one_scene(carry, inputs):
        scene_lat, scene_partners, scene_counts, scene_grad = inputs
        lat_f = scene_lat.astype(jnp.float32)
        normed = (lat_f * lax.rsqrt(lax.optimization_barrier(jnp.mean(lat_f * lat_f, -1, keepdims=True)) + epsilon) * norm_gain).astype(jnp.bfloat16)
        flat_rows = normed.reshape(VIEWS * view_tokens, D)
        queries = jnp.dot(flat_rows, w_query, preferred_element_type=jnp.float32).astype(jnp.bfloat16)
        queries = queries.reshape(VIEWS, N_ROW, strip_tokens, HEADS, HEAD_DIM)
        key_value = jnp.dot(flat_rows, pair_weight, preferred_element_type=jnp.float32).astype(jnp.bfloat16)
        key_value = key_value.reshape(VIEWS, view_tokens, 2 * inner_width)
        padded = jnp.pad(scene_grad, ((0, 0), (1, 1), (1, 1), (0, 0)))
        upstream = rim_conv(padded, kernel, H, W)
        up_flat = upstream.reshape(VIEWS * view_tokens, D)
        out_grad = jnp.dot(up_flat, w_out.T, preferred_element_type=jnp.float32).astype(jnp.bfloat16)
        out_grad = out_grad.reshape(VIEWS, N_ROW, strip_tokens, HEADS, HEAD_DIM)

        def view_terms(view_index):
            partner_row = scene_partners[view_index]
            alive_slots = jnp.arange(MAXP, dtype=jnp.int32) < scene_counts[view_index]
            safe_ids = jnp.where(alive_slots, partner_row, 0).astype(jnp.int32)
            block_ids = jnp.concatenate((view_index[None].astype(jnp.int32), safe_ids))
            blocks = key_value[block_ids].reshape(block_count * view_tokens, 2, HEADS, HEAD_DIM).astype(jnp.float32)
            key_rows = blocks[:, 0]
            value_rows = blocks[:, 1]
            key_alive = jnp.repeat(jnp.concatenate((jnp.ones((1,), bool), alive_slots)), view_tokens)
            query_rows = queries[view_index].astype(jnp.float32)
            scores = jnp.einsum('rqhd,khd->rhqk', query_rows, key_rows) * scale
            scores = jnp.where(key_alive, scores, -1e+30)
            highest = lax.optimization_barrier(jnp.max(scores, -1, keepdims=True))
            expo = jnp.exp(scores - highest)
            attention = expo / lax.optimization_barrier(jnp.sum(expo, -1, keepdims=True))
            attention_b = rounded(attention)
            mixed = jnp.einsum('rhqk,khd->rqhd', attention_b, value_rows).astype(jnp.bfloat16).reshape(view_tokens, inner_width)
            grad_rows = out_grad[view_index].astype(jnp.float32)
            dprob = jnp.einsum('rqhd,khd->rhqk', grad_rows, value_rows)
            row_delta = lax.optimization_barrier(jnp.sum(attention * dprob, -1, keepdims=True))
            dscore = rounded(attention * (dprob - row_delta) * scale)
            dquery = jnp.einsum('rhqk,khd->rqhd', dscore, key_rows).astype(jnp.bfloat16).reshape(view_tokens, inner_width)
            dkey = jnp.einsum('rhqk,rqhd->rkhd', dscore, query_rows).reshape(N_ROW, block_count, view_tokens, inner_width)
            dvalue = jnp.einsum('rhqk,rqhd->rkhd', attention_b, grad_rows).reshape(N_ROW, block_count, view_tokens, inner_width)
            return (mixed, dquery, jnp.concatenate((dkey, dvalue), -1), block_ids)

        def group(totals, group_index):
            members = group_index * VIEW_DEV + jnp.arange(VIEW_DEV, dtype=jnp.int32)
            mixed, dquery, dpair, block_ids = jax.vmap(view_terms)(members)
            spread = jnp.moveaxis(dpair, 1, 0).reshape(N_ROW, VIEW_DEV * block_count, view_tokens, 2 * inner_width)
            partial_sum = jnp.zeros((N_ROW, VIEWS, view_tokens, 2 * inner_width), jnp.float32)
            partial_sum = partial_sum.at[:, block_ids.reshape(-1)].add(spread)
            totals = totals + lax.optimization_barrier(jnp.sum(rounded(partial_sum), axis=0))
            return (totals, (mixed, dquery))
        start = jnp.zeros((VIEWS, view_tokens, 2 * inner_width), jnp.float32)
        totals, (mixed, dquery) = lax.scan(group, start, jnp.arange(group_count, dtype=jnp.int32))
        mixed = mixed.reshape(VIEWS * view_tokens, inner_width)
        dquery = dquery.reshape(VIEWS * view_tokens, inner_width)
        dpair = totals.reshape(VIEWS * view_tokens, 2 * inner_width)
        rows_f = flat_rows.astype(jnp.float32)
        grad_query = jnp.dot(flat_rows.T, dquery, preferred_element_type=jnp.float32)
        grad_key = jnp.dot(rows_f.T, dpair[:, :inner_width], precision=lax.Precision.HIGHEST)
        grad_value = jnp.dot(rows_f.T, dpair[:, inner_width:], precision=lax.Precision.HIGHEST)
        grad_out = jnp.dot(mixed.T, up_flat, preferred_element_type=jnp.float32)
        return ((carry[0] + grad_query, carry[1] + grad_key, carry[2] + grad_value, carry[3] + grad_out), None)
    zero_in = jnp.zeros((D, inner_width), jnp.float32)
    zero_out = jnp.zeros((inner_width, D), jnp.float32)
    grads, _ = lax.scan(one_scene, (zero_in, zero_in, zero_in, zero_out), (latents, partners, counts, cotangent))
    return (grads[0], grads[1], grads[2], grads[3])
```

```python
import functools

import jax
import jax.numpy as jnp
from jax import lax
from jax.experimental import pallas as pl
from jax.experimental.pallas import tpu as pltpu
from jax.sharding import PartitionSpec as P

HEAD_DIM = 64
EPSILON = 1e-06
MASKED = -1e30
MIB = 1024 * 1024

VMEM = pl.BlockSpec(memory_space=pltpu.VMEM)
SMEM = pl.BlockSpec(memory_space=pltpu.SMEM)


def dot_nn(a, b):
    return lax.dot_general(a, b, (((1,), (0,)), ((), ())), preferred_element_type=jnp.float32)


def dot_nt(a, b):
    return lax.dot_general(a, b, (((1,), (1,)), ((), ())), preferred_element_type=jnp.float32)


def dot_tn(a, b):
    return lax.dot_general(a, b, (((0,), (0,)), ((), ())), preferred_element_type=jnp.float32)


def normalized(tokens, gain):
    x = tokens.astype(jnp.float32)
    mean = jnp.mean(x * x, -1, keepdims=True)
    return (x * lax.rsqrt(mean + EPSILON) * gain).astype(jnp.bfloat16)


def request_kernel(views, slots, groups, partners, counts, request, alive):
    for g in range(groups):
        request[g] = 0
        for u in range(views):
            alive[g * views + u] = 0
    for u in range(views):
        for j in range(slots):

            @pl.when(j < counts[u])
            def _():
                partner = partners[u, j]
                group = lax.div(partner, jnp.int32(views))
                request[group] = lax.rem(partner, jnp.int32(views))
                alive[group * views + u] = 1


def project_kernel(
    scalars, lat_own, lat_other, cot_own, cot_other, gain, taps, w_q, w_k, w_v, w_o,
    normed, queries, keys, values, upstream, out_grad,
):
    views, strip, width = lat_own.shape
    for u in range(views):
        for half, source in enumerate((lat_own, lat_other)):
            start = (2 * u + half) * strip
            normed[start : start + strip, :] = normalized(source[u], gain[...])
    rows = normed[...]
    queries[...] = dot_nn(rows, w_q[...]).astype(jnp.bfloat16)
    keys[...] = dot_nn(rows, w_k[...]).astype(jnp.bfloat16)
    values[...] = dot_nn(rows, w_v[...]).astype(jnp.bfloat16)

    first = scalars[0] == 0
    chunk = 512
    column = lax.broadcasted_iota(jnp.int32, (strip, 1), 0)
    not_first = (column > 0).astype(jnp.float32)
    not_last = (column < strip - 1).astype(jnp.float32)
    for c in range(0, width, chunk):
        lanes = slice(c, c + chunk)
        tap = taps[:, lanes].astype(jnp.float32)
        top, middle, bottom = tap[0:3], tap[3:6], tap[6:9]
        cross = (jnp.where(first, top, bottom), jnp.where(first, bottom, top))
        for u in range(views):
            strips = [ref[u, :, lanes].astype(jnp.float32) for ref in (cot_own, cot_other)]
            shifted = []
            for x in strips:
                after = pltpu.roll(x, strip - 1, 0) * not_last
                before = pltpu.roll(x, 1, 0) * not_first
                shifted.append((after, x, before))
            for half in range(2):
                total = strips[half]
                for b in range(3):
                    total = total + middle[b : b + 1] * shifted[half][b]
                    total = total + cross[half][b : b + 1] * shifted[1 - half][b]
                start = (2 * u + half) * strip
                upstream[start : start + strip, lanes] = total.astype(jnp.bfloat16)
    out_grad[...] = dot_nt(upstream[...], w_o[...]).astype(jnp.bfloat16)


def attention_kernel(
    views, scalars, alive, got_own, got_other, normed, queries, keys, values, out_grad, gain, w_k, w_v,
    normed_all, mixed, dquery, dkey, dvalue,
):
    groups, strip, _ = got_own.shape
    tokens = queries.shape[0]
    view_tokens = tokens // views
    scale = HEAD_DIM ** (-0.5)
    here = scalars[1]
    normed_all[:tokens, :] = normed[...]
    pair = 2 * HEAD_DIM
    span = 2 * view_tokens
    column_view = lax.broadcasted_iota(jnp.int32, (1, views * span), 1) // span
    slot_alive = []
    for j in range(groups - 1):
        group = j + (j >= here).astype(jnp.int32)
        start = tokens + 2 * j * strip
        normed_all[start : start + strip, :] = normalized(got_own[group], gain[...])
        normed_all[start + strip : start + 2 * strip, :] = normalized(got_other[group], gain[...])
        taken = jnp.zeros((1, views * span), jnp.int32)
        for u in range(views):
            taken = jnp.where(column_view == u, alive[group * views + u], taken)
        slot_alive.append(taken > 0)
    fetched = normed_all[tokens:, :]
    fetched_keys = dot_nn(fetched, w_k[...]).astype(jnp.bfloat16)
    fetched_values = dot_nn(fetched, w_v[...]).astype(jnp.bfloat16)
    low = lax.broadcasted_iota(jnp.int32, (1, 1, pair), 2) < HEAD_DIM
    low_b = low.astype(jnp.bfloat16)
    high_b = 1 - low_b

    def stacked(x):
        x = x.reshape(views, view_tokens, pair)
        return jnp.concatenate((x * low_b, x * high_b), axis=1).reshape(views * span, pair)

    def unstacked(x):
        x = x.reshape(views, 2, view_tokens, pair)
        return jnp.where(low, x[:, 0], x[:, 1]).reshape(tokens, pair).astype(jnp.bfloat16)

    def own_nt(a, b):
        return jnp.concatenate(
            [
                dot_nt(a[u * view_tokens : (u + 1) * view_tokens], b[u * span : (u + 1) * span])
                for u in range(views)
            ],
            axis=1,
        )

    def own_tn(a, b):
        return jnp.concatenate(
            [
                dot_tn(a[:, u * span : (u + 1) * span], b[u * view_tokens : (u + 1) * view_tokens])
                for u in range(views)
            ],
            axis=0,
        )

    def own_nn(a, b):
        return jnp.concatenate(
            [
                dot_nn(a[:, u * span : (u + 1) * span], b[u * span : (u + 1) * span])
                for u in range(views)
            ],
            axis=0,
        )

    for p in range(queries.shape[1] // pair):
        lanes = slice(p * pair, (p + 1) * pair)
        q = stacked(queries[:, lanes])
        g = stacked(out_grad[:, lanes])
        k_own, v_own = keys[:, lanes], values[:, lanes]
        k_far, v_far = fetched_keys[:, lanes], fetched_values[:, lanes]
        s_own = own_nt(k_own, q) * scale
        s_far = dot_nt(k_far, q) * scale
        s_far = jnp.concatenate(
            [
                jnp.where(slot_alive[j], s_far[j * view_tokens : (j + 1) * view_tokens], MASKED)
                for j in range(groups - 1)
            ],
            axis=0,
        )
        highest = jnp.maximum(
            jnp.max(s_own, 0, keepdims=True), jnp.max(s_far, 0, keepdims=True)
        )
        e_own = jnp.exp(s_own - highest)
        e_far = jnp.exp(s_far - highest)
        inverse = 1.0 / (jnp.sum(e_own, 0, keepdims=True) + jnp.sum(e_far, 0, keepdims=True))
        a_own = e_own * inverse
        a_far = e_far * inverse
        ab_own = a_own.astype(jnp.bfloat16)
        ab_far = a_far.astype(jnp.bfloat16)
        mixed[:, lanes] = unstacked(own_tn(ab_own, v_own) + dot_tn(ab_far, v_far))
        dvalue[:tokens, lanes] = own_nn(ab_own, g).astype(jnp.bfloat16)
        dvalue[tokens:, lanes] = dot_nn(ab_far, g).astype(jnp.bfloat16)
        dp_own = own_nt(v_own, g)
        dp_far = dot_nt(v_far, g)
        delta = jnp.sum(a_own * dp_own, 0, keepdims=True) + jnp.sum(a_far * dp_far, 0, keepdims=True)
        ds_own = (a_own * (dp_own - delta) * scale).astype(jnp.bfloat16)
        ds_far = (a_far * (dp_far - delta) * scale).astype(jnp.bfloat16)
        dquery[:, lanes] = unstacked(own_tn(ds_own, k_own) + dot_tn(ds_far, k_far))
        dkey[:tokens, lanes] = own_nn(ds_own, q).astype(jnp.bfloat16)
        dkey[tokens:, lanes] = dot_nn(ds_far, q).astype(jnp.bfloat16)


def outer_kernel(first, scalars, left, right, send, keep):
    size = send.shape[1]
    other = right[...]
    for i in range(2):
        start = pl.multiple_of(scalars[first + i] * size, size)
        send[i] = dot_tn(left[:, pl.ds(start, size)], other).astype(jnp.bfloat16)
    for i in range(2):
        start = pl.multiple_of(scalars[first + 2 + i] * size, size)
        keep[i] = dot_tn(left[:, pl.ds(start, size)], other)


def out_kernel(strip, scalars, mine, theirs, upstream, send, keep):
    tokens, inner = mine.shape
    width = upstream.shape[1] // 2
    start = pl.multiple_of(scalars[0] * width, width)
    right = upstream[:, pl.ds(start, width)]
    swapped = theirs[...].reshape(tokens // (2 * strip), 2, strip, inner)
    swapped = jnp.concatenate((swapped[:, 1:], swapped[:, :1]), axis=1).reshape(tokens, inner)
    from_mine = dot_tn(mine[...], right)
    from_theirs = dot_tn(swapped, right)
    keep_mine = scalars[0] == scalars[2]
    send[...] = jnp.where(keep_mine, from_theirs, from_mine).astype(jnp.bfloat16)
    keep[...] = jnp.where(keep_mine, from_mine, from_theirs)


def params(mebibytes):
    return pltpu.CompilerParams(vmem_limit_bytes=mebibytes * MIB)


def shape(dims, kind):
    return jax.ShapeDtypeStruct(dims, kind)


def shards(latents, norm_gain, w_query, w_key, w_value, w_out, kernel, partners, counts, cotangent):
    views, strip_rows, columns, width = latents.shape[1:]
    inner = w_query.shape[1]
    groups, rows = lax.axis_size("view"), lax.axis_size("row")
    scenes = lax.axis_size("scene")
    assert (strip_rows, rows, scenes) == (1, 2, 4)
    strip = strip_rows * columns
    slots = partners.shape[2]
    part = inner // rows
    tokens = views * 2 * strip
    key_tokens = tokens + (groups - 1) * 2 * strip
    bf16, f32, i32 = jnp.bfloat16, jnp.float32, jnp.int32

    row, view, scene = lax.axis_index("row"), lax.axis_index("view"), lax.axis_index("scene")
    x, y = scene % 2, scene // 2
    scalars = jnp.stack(
        (
            row, view, y, x,
            1 - x, 3 - x, x, 2 + x,
            2 - 2 * y, 3 - 2 * y, 2 * y, 2 * y + 1,
        )
    ).astype(i32)
    swap = [(0, 1), (1, 0)]
    along_x = [(i, i ^ 1) for i in range(scenes)]
    along_y = [(i, i ^ 2) for i in range(scenes)]

    request, alive = pl.pallas_call(
        functools.partial(request_kernel, views, slots, groups),
        in_specs=[SMEM, SMEM],
        out_specs=(SMEM, SMEM),
        out_shape=(shape((groups,), i32), shape((groups * views,), i32)),
        name="requests",
    )(partners[0], counts[0])
    granted = lax.all_to_all(request, "view", split_axis=0, concat_axis=0, tiled=True)

    lat = latents[0].reshape(views, strip, width)
    cot = cotangent[0].reshape(views, strip, width)
    lat_other = lax.ppermute(lat, "row", swap)
    cot_other = lax.ppermute(cot, "row", swap)

    outgoing = jnp.take(lat, granted, axis=0, mode="clip")
    got_own = lax.all_to_all(outgoing, "view", split_axis=0, concat_axis=0, tiled=True)
    got_other = lax.ppermute(got_own, "row", swap)

    gain = norm_gain.reshape(1, width)
    half_columns = pl.BlockSpec((width, part), lambda i, s: (0, s[0]))
    half_rows = pl.BlockSpec((part, width), lambda i, s: (s[0], 0))

    def whole(dims):
        return pl.BlockSpec(dims, lambda i, s: (0,) * len(dims))

    strip_spec = whole((views, strip, width))
    token_spec, part_spec = whole((tokens, width)), whole((tokens, part))
    normed, queries, keys, values, upstream, out_grad = pl.pallas_call(
        project_kernel,
        grid_spec=pltpu.PrefetchScalarGridSpec(
            num_scalar_prefetch=1,
            grid=(1,),
            in_specs=[
                strip_spec, strip_spec, strip_spec, strip_spec, whole((1, width)), whole((9, width)),
                half_columns, half_columns, half_columns, half_rows,
            ],
            out_specs=[token_spec, part_spec, part_spec, part_spec, token_spec, part_spec],
        ),
        out_shape=[
            shape((tokens, width), bf16),
            shape((tokens, part), bf16),
            shape((tokens, part), bf16),
            shape((tokens, part), bf16),
            shape((tokens, width), bf16),
            shape((tokens, part), bf16),
        ],
        compiler_params=params(40),
        cost_estimate=pl.CostEstimate(
            flops=8 * tokens * width * part + 40 * tokens * width,
            bytes_accessed=8 * width * part + 16 * tokens * width,
            transcendentals=tokens,
        ),
        name="project",
    )(scalars, lat, lat_other, cot, cot_other, gain, kernel, w_query, w_key, w_value, w_out)

    normed_all, mixed, dquery, dkey, dvalue = pl.pallas_call(
        functools.partial(attention_kernel, views),
        grid_spec=pltpu.PrefetchScalarGridSpec(
            num_scalar_prefetch=2,
            grid=(1,),
            in_specs=[
                pl.BlockSpec((groups, strip, width), lambda i, s, a: (0, 0, 0)),
                pl.BlockSpec((groups, strip, width), lambda i, s, a: (0, 0, 0)),
                pl.BlockSpec((tokens, width), lambda i, s, a: (0, 0)),
                pl.BlockSpec((tokens, part), lambda i, s, a: (0, 0)),
                pl.BlockSpec((tokens, part), lambda i, s, a: (0, 0)),
                pl.BlockSpec((tokens, part), lambda i, s, a: (0, 0)),
                pl.BlockSpec((tokens, part), lambda i, s, a: (0, 0)),
                pl.BlockSpec((1, width), lambda i, s, a: (0, 0)),
                pl.BlockSpec((width, part), lambda i, s, a: (0, s[0])),
                pl.BlockSpec((width, part), lambda i, s, a: (0, s[0])),
            ],
            out_specs=[
                pl.BlockSpec((key_tokens, width), lambda i, s, a: (0, 0)),
                pl.BlockSpec((tokens, part), lambda i, s, a: (0, 0)),
                pl.BlockSpec((tokens, part), lambda i, s, a: (0, 0)),
                pl.BlockSpec((key_tokens, part), lambda i, s, a: (0, 0)),
                pl.BlockSpec((key_tokens, part), lambda i, s, a: (0, 0)),
            ],
        ),
        out_shape=[
            shape((key_tokens, width), bf16),
            shape((tokens, part), bf16),
            shape((tokens, part), bf16),
            shape((key_tokens, part), bf16),
            shape((key_tokens, part), bf16),
        ],
        compiler_params=params(44),
        cost_estimate=pl.CostEstimate(
            flops=4 * (key_tokens - tokens) * width * part + 24 * groups * 2 * strip * tokens * part,
            bytes_accessed=4 * width * part + 8 * key_tokens * width,
            transcendentals=groups * 2 * strip * tokens * part // HEAD_DIM,
        ),
        name="attention",
    )(
        scalars, alive, got_own, got_other, normed, queries, keys, values, out_grad, gain, w_key, w_value
    )
    mixed_other = lax.ppermute(mixed, "row", swap)

    def outer(left, right, first, name):
        blocks = (2, width // 4, part)
        return pl.pallas_call(
            functools.partial(outer_kernel, first),
            in_specs=[SMEM, VMEM, VMEM],
            out_specs=(VMEM, VMEM),
            out_shape=(shape(blocks, bf16), shape(blocks, f32)),
            compiler_params=params(24),
            cost_estimate=pl.CostEstimate(
                flops=2 * left.shape[0] * width * part,
                bytes_accessed=6 * width * part // 2 + 2 * left.shape[0] * (width + part),
                transcendentals=0,
            ),
            name=name,
        )(scalars, left, right)

    q_send, q_keep = outer(normed_all[:tokens], dquery, 4, "grad_query")
    k_send, k_keep = outer(normed_all, dkey, 4, "grad_key")
    v_send, v_keep = outer(normed_all, dvalue, 8, "grad_value")
    o_send, o_keep = pl.pallas_call(
        functools.partial(out_kernel, strip),
        in_specs=[SMEM, VMEM, VMEM, VMEM],
        out_specs=(VMEM, VMEM),
        out_shape=(shape((inner // 2, width // 2), bf16), shape((inner // 2, width // 2), f32)),
        compiler_params=params(24),
        cost_estimate=pl.CostEstimate(
            flops=2 * tokens * width * part,
            bytes_accessed=6 * width * part // 2 + 2 * tokens * (width + inner),
            transcendentals=0,
        ),
        name="grad_out",
    )(scalars, mixed, mixed_other, upstream)
    o_send = o_send.reshape(2, inner // 4, width // 2)
    o_keep = o_keep.reshape(2, inner // 4, width // 2)

    def summed(send, keep, order, index):
        got = lax.ppermute(send, "scene", order[0])
        later = lax.dynamic_index_in_dim(keep, 1 - index, 0, False) + lax.dynamic_index_in_dim(
            got, 1 - index, 0, False
        ).astype(f32)
        got_later = lax.ppermute(later.astype(bf16), "scene", order[1])
        mine = lax.dynamic_index_in_dim(keep, index, 0, False) + lax.dynamic_index_in_dim(
            got, index, 0, False
        ).astype(f32)
        mine = (mine + got_later.astype(f32)).astype(bf16)
        spread = mine.reshape(groups * rows, mine.shape[0] // (groups * rows), mine.shape[1])
        got = lax.all_to_all(spread, ("view", "row"), split_axis=0, concat_axis=0, tiled=True)
        got = got.reshape(groups, rows, spread.shape[1], spread.shape[2]).astype(f32)
        total = jnp.sum(got, axis=0)
        return jnp.moveaxis(total, 0, 1).reshape(spread.shape[1], rows * spread.shape[2])

    return (
        summed(q_send, q_keep, (along_x, along_y), y),
        summed(k_send, k_keep, (along_x, along_y), y),
        summed(v_send, v_keep, (along_y, along_x), x),
        summed(o_send, o_keep, (along_y, along_x), x),
    )


def solution(mesh):
    tokens = P("scene", "view", "row", None, None)
    everywhere = P()
    grads = P(("scene", "view", "row"), None)
    return jax.shard_map(
        shards,
        mesh=mesh,
        in_specs=(
            tokens, everywhere, everywhere, everywhere, everywhere, everywhere, everywhere,
            P("scene", "view", None), P("scene", "view"), tokens,
        ),
        out_specs=(grads, grads, grads, grads),
        check_vma=False,
    )
```

```python
import functools

import jax
import jax.numpy as jnp
from jax import lax
from jax.experimental import pallas as pl
from jax.experimental.pallas import tpu as pltpu
from jax.sharding import PartitionSpec as P

HEAD_DIM = 64
EPSILON = 1e-06
MASKED = -1e30
MIB = 1024 * 1024

VMEM = pl.BlockSpec(memory_space=pltpu.VMEM)
HBM = pl.BlockSpec(memory_space=pltpu.HBM)
SMEM = pl.BlockSpec(memory_space=pltpu.SMEM)


def dot_nn(a, b):
    return lax.dot_general(a, b, (((1,), (0,)), ((), ())), preferred_element_type=jnp.float32)


def dot_nt(a, b):
    return lax.dot_general(a, b, (((1,), (1,)), ((), ())), preferred_element_type=jnp.float32)


def dot_tn(a, b):
    return lax.dot_general(a, b, (((0,), (0,)), ((), ())), preferred_element_type=jnp.float32)


def normalized(tokens, gain):
    x = tokens.astype(jnp.float32)
    mean = jnp.mean(x * x, -1, keepdims=True)
    return (x * lax.rsqrt(mean + EPSILON) * gain).astype(jnp.bfloat16)


def request_kernel(views, slots, groups, partners, counts, request, alive):
    for g in range(groups):
        request[g] = 0
        for u in range(views):
            alive[g * views + u] = 0
    for u in range(views):
        for j in range(slots):

            @pl.when(j < counts[0, u])
            def _():
                partner = partners[0, u, j]
                group = lax.div(partner, jnp.int32(views))
                request[group] = lax.rem(partner, jnp.int32(views))
                alive[group * views + u] = 1


def pick_kernel(groups, scalars, *refs):
    requests, lat, outgoing = refs[: groups - 1], refs[groups - 1], refs[groups:]
    for request, out in zip(requests, outgoing):
        out[...] = lat[request[scalars[1]]]


def weight_copy(scalars, source, target, arrived, index, axis):
    size = target.shape[axis]
    half = pl.ds(pl.multiple_of(scalars[0] * size, size), size)
    part = source.at[:, half] if axis == 1 else source.at[half, :]
    return pltpu.make_async_copy(part, target, arrived.at[index])


def project_kernel(
    scalars, lat_own, lat_other, cot_own, cot_other, gain, taps, w_query, w_key, w_value, w_out,
    normed, queries, keys, values, upstream, out_grad, up_half, *refs,
):
    quarters, (w_q, w_k, w_v, w_o, arrived) = refs[:4], refs[4:]
    views, strip, width = lat_own.shape
    copies = [
        weight_copy(scalars, w_query, w_q, arrived, 0, 1),
        weight_copy(scalars, w_key, w_k, arrived, 1, 1),
        weight_copy(scalars, w_value, w_v, arrived, 2, 1),
        weight_copy(scalars, w_out, w_o, arrived, 3, 0),
    ]
    for copy in copies:
        copy.start()
    row = scalars[0]

    def strip_of(u, half):
        index = 2 * u + (row if half == 0 else 1 - row)
        return pl.ds(pl.multiple_of(index * strip, strip), strip)

    for u in range(views):
        for half, source in enumerate((lat_own, lat_other)):
            normed[strip_of(u, half), :] = normalized(source[u], gain[...])
    first = row == 0
    chunk = 512
    column = lax.broadcasted_iota(jnp.int32, (strip, 1), 0)
    not_first = (column > 0).astype(jnp.float32)
    not_last = (column < strip - 1).astype(jnp.float32)
    for c in range(0, width, chunk):
        lanes = slice(c, c + chunk)
        tap = taps[:, lanes].astype(jnp.float32)
        top, middle, bottom = tap[0:3], tap[3:6], tap[6:9]
        cross = (jnp.where(first, top, bottom), jnp.where(first, bottom, top))
        for u in range(views):
            strips = [ref[u, :, lanes].astype(jnp.float32) for ref in (cot_own, cot_other)]
            shifted = []
            for x in strips:
                after = pltpu.roll(x, strip - 1, 0) * not_last
                before = pltpu.roll(x, 1, 0) * not_first
                shifted.append((after, x, before))
            for half in range(2):
                total = strips[half]
                for b in range(3):
                    total = total + middle[b : b + 1] * shifted[half][b]
                    total = total + cross[half][b : b + 1] * shifted[1 - half][b]
                upstream[strip_of(u, half), lanes] = total.astype(jnp.bfloat16)
    size = width // 4
    for m, quarter in enumerate(quarters):
        start = pl.multiple_of(lax.bitwise_xor(scalars[2], jnp.int32(m)) * size, size)
        quarter[...] = normed[:, pl.ds(start, size)]
    up_half[...] = upstream[:, pl.ds(pl.multiple_of(row * (width // 2), width // 2), width // 2)]
    rows = normed[...]
    for copy, weight, result in zip(copies, (w_q, w_k, w_v), (queries, keys, values)):
        copy.wait()
        result[...] = dot_nn(rows, weight[...]).astype(jnp.bfloat16)
    copies[3].wait()
    out_grad[...] = dot_nt(upstream[...], w_o[...]).astype(jnp.bfloat16)


def attention_kernel(views, groups, scalars, alive, *refs):
    got_own, got_other, refs = refs[: groups - 1], refs[groups - 1 : 2 * groups - 2], refs[2 * groups - 2 :]
    normed, queries, keys, values, out_grad, gain, w_key, w_value, *refs = refs
    normed_all, mixed_t, dquery, dkey, dvalue, w_k, w_v, arrived = refs
    copies = [
        weight_copy(scalars, w_key, w_k, arrived, 0, 1),
        weight_copy(scalars, w_value, w_v, arrived, 1, 1),
    ]
    for copy in copies:
        copy.start()
    strip = got_own[0].shape[0]
    tokens = queries.shape[0]
    view_tokens = tokens // views
    scale = HEAD_DIM ** (-0.5)
    here = scalars[1]
    normed_all[:tokens, :] = normed[...]
    pair = 2 * HEAD_DIM
    span = 2 * view_tokens
    column_view = lax.broadcasted_iota(jnp.int32, (1, views * span), 1) // span
    slot_alive = []
    for j in range(groups - 1):
        group = lax.bitwise_xor(here, jnp.int32(j + 1))
        start = tokens + 2 * j * strip
        normed_all[start : start + strip, :] = normalized(got_own[j][...], gain[...])
        normed_all[start + strip : start + 2 * strip, :] = normalized(got_other[j][...], gain[...])
        taken = jnp.zeros((1, views * span), jnp.int32)
        for u in range(views):
            taken = jnp.where(column_view == u, alive[group * views + u], taken)
        slot_alive.append(taken > 0)
    fetched = normed_all[tokens:, :]
    for copy in copies:
        copy.wait()
    fetched_keys = dot_nn(fetched, w_k[...]).astype(jnp.bfloat16)
    fetched_values = dot_nn(fetched, w_v[...]).astype(jnp.bfloat16)
    low = lax.broadcasted_iota(jnp.int32, (1, 1, pair), 2) < HEAD_DIM
    low_b = low.astype(jnp.bfloat16)
    high_b = 1 - low_b

    def stacked(x):
        x = x.reshape(views, view_tokens, pair)
        return jnp.concatenate((x * low_b, x * high_b), axis=1).reshape(views * span, pair)

    def unstacked(x):
        x = x.reshape(views, 2, view_tokens, pair)
        return jnp.where(low, x[:, 0], x[:, 1]).reshape(tokens, pair)

    def own_nt(a, b):
        return jnp.concatenate(
            [
                dot_nt(a[u * view_tokens : (u + 1) * view_tokens], b[u * span : (u + 1) * span])
                for u in range(views)
            ],
            axis=1,
        )

    def own_tn(a, b):
        return jnp.concatenate(
            [
                dot_tn(a[:, u * span : (u + 1) * span], b[u * view_tokens : (u + 1) * view_tokens])
                for u in range(views)
            ],
            axis=0,
        )

    def own_nn(a, b):
        return jnp.concatenate(
            [
                dot_nn(a[:, u * span : (u + 1) * span], b[u * span : (u + 1) * span])
                for u in range(views)
            ],
            axis=0,
        )

    for p in range(queries.shape[1] // pair):
        lanes = slice(p * pair, (p + 1) * pair)
        q = stacked(queries[:, lanes])
        g = stacked(out_grad[:, lanes])
        k_own, v_own = keys[:, lanes], values[:, lanes]
        k_far, v_far = fetched_keys[:, lanes], fetched_values[:, lanes]
        s_own = own_nt(k_own, q) * scale
        s_far = dot_nt(k_far, q) * scale
        s_far = jnp.concatenate(
            [
                jnp.where(slot_alive[j], s_far[j * view_tokens : (j + 1) * view_tokens], MASKED)
                for j in range(groups - 1)
            ],
            axis=0,
        )
        highest = jnp.maximum(
            jnp.max(s_own, 0, keepdims=True), jnp.max(s_far, 0, keepdims=True)
        )
        e_own = jnp.exp(s_own - highest)
        e_far = jnp.exp(s_far - highest)
        inverse = 1.0 / (jnp.sum(e_own, 0, keepdims=True) + jnp.sum(e_far, 0, keepdims=True))
        a_own = e_own * inverse
        a_far = e_far * inverse
        ab_own = a_own.astype(jnp.bfloat16)
        ab_far = a_far.astype(jnp.bfloat16)
        mix = unstacked(own_tn(ab_own, v_own) + dot_tn(ab_far, v_far))
        mixed_t[lanes, :] = mix.T.astype(jnp.bfloat16)
        dvalue[:tokens, lanes] = own_nn(ab_own, g).astype(jnp.bfloat16)
        dvalue[tokens:, lanes] = dot_nn(ab_far, g).astype(jnp.bfloat16)
        dp_own = own_nt(v_own, g)
        dp_far = dot_nt(v_far, g)
        delta = jnp.sum(a_own * dp_own, 0, keepdims=True) + jnp.sum(a_far * dp_far, 0, keepdims=True)
        ds_own = (a_own * (dp_own - delta) * scale).astype(jnp.bfloat16)
        ds_far = (a_far * (dp_far - delta) * scale).astype(jnp.bfloat16)
        dq = unstacked(own_tn(ds_own, k_own) + dot_tn(ds_far, k_far))
        dquery[:, lanes] = dq.astype(jnp.bfloat16)
        dkey[:tokens, lanes] = own_nn(ds_own, q).astype(jnp.bfloat16)
        dkey[tokens:, lanes] = dot_nn(ds_far, q).astype(jnp.bfloat16)


def key_value_kernel(scalars, left, dkey, dvalue, k_send, v_send, k_keep, v_keep):
    size = k_send.shape[1]
    x, y = scalars[3], scalars[4]
    for side, (k_out, v_out) in enumerate(((k_send, v_send), (k_keep, v_keep))):
        x_out = x if side else 1 - x
        y_out = y if side else 1 - y
        for right, result, blocks in (
            (dkey, k_out, (x_out, 2 + x_out)),
            (dvalue, v_out, (2 * y_out, 2 * y_out + 1)),
        ):
            for i, block in enumerate(blocks):
                columns = pl.ds(pl.multiple_of(block * size, size), size)
                result[i] = dot_tn(left[:, columns], right[...]).astype(result.dtype)


def half_sum_kernel(scalars, k_keep, k_got, v_keep, v_got, k_later, v_later, k_now, v_now):
    x, y = scalars[3], scalars[4]
    for index, keep, got, later, now in ((y, k_keep, k_got, k_later, k_now), (x, v_keep, v_got, v_later, v_now)):
        later[...] = (keep[1 - index] + got[1 - index].astype(jnp.float32)).astype(jnp.bfloat16)
        now[...] = keep[index] + got[index].astype(jnp.float32)


def pack_kernel(k_now, k_got, v_now, v_got, packed):
    size = k_now.shape[1]
    packed[:, :size] = (k_now[...] + k_got[...].astype(jnp.float32)).astype(jnp.bfloat16)
    packed[:, size:] = (v_now[...] + v_got[...].astype(jnp.float32)).astype(jnp.bfloat16)


def unpack_kernel(rows, packed, key, value):
    sources, _, both = packed.shape
    size = both // 2
    for r in range(rows):
        total = packed[r].astype(jnp.float32)
        for i in range(r + rows, sources, rows):
            total = total + packed[i].astype(jnp.float32)
        key[:, r * size : (r + 1) * size] = total[:, :size]
        value[:, r * size : (r + 1) * size] = total[:, size:]


def share_kernel(scalars, mine, theirs, *quarters):
    size = quarters[0].shape[0]
    for m, quarter in enumerate(quarters):
        scene = lax.bitwise_xor(scalars[2], jnp.int32(m))
        owner, place = lax.div(scene, jnp.int32(2)), lax.rem(scene, jnp.int32(2))
        rows = pl.ds(pl.multiple_of(place * size, size), size)
        is_mine = owner == scalars[0]

        @pl.when(is_mine)
        def _():
            quarter[...] = mine[rows, :]

        @pl.when(jnp.logical_not(is_mine))
        def _():
            quarter[...] = theirs[rows, :]


def query_out_kernel(*refs):
    normed, dquery, mixed_t, up_half, packed = refs[0:4], refs[4:8], refs[8:12], refs[12:16], refs[16]
    grad_q = dot_tn(normed[0][...], dquery[0][...])
    grad_o = dot_nn(mixed_t[0][...], up_half[0][...])
    for m in range(1, 4):
        grad_q = grad_q + dot_tn(normed[m][...], dquery[m][...])
        grad_o = grad_o + dot_nn(mixed_t[m][...], up_half[m][...])
    targets, size, _ = packed.shape
    for i in range(targets):
        packed[i] = jnp.concatenate(
            (
                grad_o[i * size : (i + 1) * size],
                grad_q[2 * i * size : (2 * i + 1) * size],
                grad_q[(2 * i + 1) * size : (2 * i + 2) * size],
            ),
            axis=1,
        ).astype(jnp.bfloat16)


def unpack_query_out_kernel(rows, packed, query, out):
    sources, size, width = packed.shape
    half, quarter = width // 2, width // 4
    for r in range(rows):
        total = packed[r].astype(jnp.float32)
        for i in range(r + rows, sources, rows):
            total = total + packed[i].astype(jnp.float32)
        out[:, r * half : (r + 1) * half] = total[:, :half]
        columns = slice(r * quarter, (r + 1) * quarter)
        query[:size, columns] = total[:, half : half + quarter]
        query[size:, columns] = total[:, half + quarter :]


def params(mebibytes):
    return pltpu.CompilerParams(vmem_limit_bytes=mebibytes * MIB)


def shape(dims, kind):
    return jax.ShapeDtypeStruct(dims, kind)


def shards(latents, norm_gain, w_query, w_key, w_value, w_out, kernel, partners, counts, cotangent):
    views, strip_rows, columns, width = latents.shape[1:]
    inner = w_query.shape[1]
    groups, rows = lax.axis_size("view"), lax.axis_size("row")
    scenes = lax.axis_size("scene")
    assert (strip_rows, rows, scenes) == (1, 2, 4)
    strip = strip_rows * columns
    slots = partners.shape[2]
    part = inner // rows
    tokens = views * 2 * strip
    key_tokens = tokens + (groups - 1) * 2 * strip
    bf16, f32, i32 = jnp.bfloat16, jnp.float32, jnp.int32

    row, view, scene = lax.axis_index("row"), lax.axis_index("view"), lax.axis_index("scene")
    scalars = jnp.stack((row, view, scene, scene % 2, scene // 2)).astype(i32)
    swap = [(0, 1), (1, 0)]
    across = [[(i, i ^ m) for i in range(scenes)] for m in range(scenes)]
    along_x, along_y = across[1], across[2]

    request, alive = pl.pallas_call(
        functools.partial(request_kernel, views, slots, groups),
        in_specs=[SMEM, SMEM],
        out_specs=(SMEM, SMEM),
        out_shape=(shape((groups,), i32), shape((groups * views,), i32)),
        name="requests",
    )(partners, counts)
    between = [[(i, i ^ d) for i in range(groups)] for d in range(1, groups)]
    granted = [lax.ppermute(request, "view", pairs) for pairs in between]

    lat = latents[0].reshape(views, strip, width)
    cot = cotangent[0].reshape(views, strip, width)
    lat_other = lax.ppermute(lat, "row", swap)
    cot_other = lax.ppermute(cot, "row", swap)

    outgoing = pl.pallas_call(
        functools.partial(pick_kernel, groups),
        in_specs=[SMEM] * groups + [VMEM],
        out_specs=[VMEM] * (groups - 1),
        out_shape=[shape((strip, width), bf16)] * (groups - 1),
        compiler_params=params(8),
        name="pick",
    )(scalars, *granted, lat)
    got_own = [lax.ppermute(part_out, "view", pairs) for part_out, pairs in zip(outgoing, between)]
    got_other = [lax.ppermute(got, "row", swap) for got in got_own]

    gain = norm_gain.reshape(1, width)
    normed, queries, keys, values, upstream, out_grad, up_half, *quarters = pl.pallas_call(
        project_kernel,
        in_specs=[SMEM] + [VMEM] * 6 + [HBM] * 4,
        out_specs=[VMEM] * 11,
        out_shape=[
            shape((tokens, width), bf16),
            shape((tokens, part), bf16),
            shape((tokens, part), bf16),
            shape((tokens, part), bf16),
            shape((tokens, width), bf16),
            shape((tokens, part), bf16),
            shape((tokens, width // 2), bf16),
        ]
        + [shape((tokens, width // 4), bf16)] * 4,
        scratch_shapes=[
            pltpu.VMEM((width, part), bf16),
            pltpu.VMEM((width, part), bf16),
            pltpu.VMEM((width, part), bf16),
            pltpu.VMEM((part, width), bf16),
            pltpu.SemaphoreType.DMA((4,)),
        ],
        compiler_params=params(28),
        cost_estimate=pl.CostEstimate(
            flops=8 * tokens * width * part + 40 * tokens * width,
            bytes_accessed=8 * width * part + 16 * tokens * width,
            transcendentals=tokens,
        ),
        name="project",
    )(scalars, lat, lat_other, cot, cot_other, gain, kernel, w_query, w_key, w_value, w_out)

    normed_far = [quarters[0]] + [lax.ppermute(quarters[m], "scene", across[m]) for m in range(1, 4)]
    up_far = [up_half] + [lax.ppermute(up_half, "scene", across[m]) for m in range(1, 4)]

    normed_all, mixed_t, dquery, dkey, dvalue = pl.pallas_call(
        functools.partial(attention_kernel, views, groups),
        in_specs=[SMEM] * 2 + [VMEM] * (2 * groups - 2 + 6) + [HBM] * 2,
        out_specs=[VMEM] * 5,
        out_shape=[
            shape((key_tokens, width), bf16),
            shape((part, tokens), bf16),
            shape((tokens, part), bf16),
            shape((key_tokens, part), bf16),
            shape((key_tokens, part), bf16),
        ],
        scratch_shapes=[
            pltpu.VMEM((width, part), bf16),
            pltpu.VMEM((width, part), bf16),
            pltpu.SemaphoreType.DMA((2,)),
        ],
        compiler_params=params(24 + groups),
        cost_estimate=pl.CostEstimate(
            flops=4 * (key_tokens - tokens) * width * part + 24 * groups * 2 * strip * tokens * part,
            bytes_accessed=4 * width * part + 8 * key_tokens * width,
            transcendentals=groups * 2 * strip * tokens * part // HEAD_DIM,
        ),
        name="attention",
    )(
        scalars, alive, *got_own, *got_other, normed, queries, keys, values, out_grad, gain, w_key, w_value
    )
    quarter = width // 4
    two, one = (2, quarter, part), (quarter, part)
    k_send, v_send, k_keep, v_keep = pl.pallas_call(
        key_value_kernel,
        in_specs=[SMEM] + [VMEM] * 3,
        out_specs=[VMEM] * 4,
        out_shape=[shape(two, bf16)] * 2 + [shape(two, f32)] * 2,
        compiler_params=params(24),
        cost_estimate=pl.CostEstimate(
            flops=4 * key_tokens * width * part, bytes_accessed=12 * width * part, transcendentals=0
        ),
        name="grad_key_value",
    )(scalars, normed_all, dkey, dvalue)
    k_got = lax.ppermute(k_send, "scene", along_x)
    v_got = lax.ppermute(v_send, "scene", along_y)

    mixed_other = lax.ppermute(mixed_t, "row", swap)
    dquery_far = [dquery] + [lax.ppermute(dquery, "scene", across[m]) for m in range(1, 4)]
    shares = pl.pallas_call(
        share_kernel,
        in_specs=[SMEM] + [VMEM] * 2,
        out_specs=[VMEM] * 4,
        out_shape=[shape((inner // 4, tokens), bf16)] * 4,
        compiler_params=params(8),
        name="share_mixed",
    )(scalars, mixed_t, mixed_other)
    mixed_far = [shares[0]] + [lax.ppermute(shares[m], "scene", across[m]) for m in range(1, 4)]
    targets = groups * rows
    q_rows, o_rows = width // (4 * targets), inner // (4 * targets)
    packed = pl.pallas_call(
        query_out_kernel,
        in_specs=[VMEM] * 16,
        out_specs=VMEM,
        out_shape=shape((targets, o_rows, width), bf16),
        compiler_params=params(16),
        cost_estimate=pl.CostEstimate(
            flops=4 * tokens * width * part, bytes_accessed=8 * tokens * width, transcendentals=0
        ),
        name="grad_query_out",
    )(*normed_far, *dquery_far, *mixed_far, *up_far)
    packed = lax.all_to_all(packed, ("view", "row"), split_axis=0, concat_axis=0, tiled=True)
    grad_query, grad_out = pl.pallas_call(
        functools.partial(unpack_query_out_kernel, rows),
        in_specs=[VMEM],
        out_specs=[VMEM] * 2,
        out_shape=[shape((q_rows, inner), f32), shape((o_rows, width), f32)],
        compiler_params=params(8),
        name="sum_query_out",
    )(packed)

    k_later, v_later, k_now, v_now = pl.pallas_call(
        half_sum_kernel,
        in_specs=[SMEM] + [VMEM] * 4,
        out_specs=[VMEM] * 4,
        out_shape=[shape(one, bf16)] * 2 + [shape(one, f32)] * 2,
        compiler_params=params(16),
        name="sum_first",
    )(scalars, k_keep, k_got, v_keep, v_got)
    k_got = lax.ppermute(k_later, "scene", along_y)
    v_got = lax.ppermute(v_later, "scene", along_x)
    packed = pl.pallas_call(
        pack_kernel,
        in_specs=[VMEM] * 4,
        out_specs=VMEM,
        out_shape=shape((quarter, 2 * part), bf16),
        compiler_params=params(16),
        name="sum_second",
    )(k_now, k_got, v_now, v_got)
    packed = packed.reshape(targets, q_rows, 2 * part)
    packed = lax.all_to_all(packed, ("view", "row"), split_axis=0, concat_axis=0, tiled=True)
    grad_key, grad_value = pl.pallas_call(
        functools.partial(unpack_kernel, rows),
        in_specs=[VMEM],
        out_specs=[VMEM] * 2,
        out_shape=[shape((q_rows, inner), f32)] * 2,
        compiler_params=params(8),
        name="sum_key_value",
    )(packed)
    return grad_query, grad_key, grad_value, grad_out


def solution(mesh):
    tokens = P("scene", "view", "row", None, None)
    everywhere = P()
    grads = P(("scene", "view", "row"), None)
    return jax.shard_map(
        shards,
        mesh=mesh,
        in_specs=(
            tokens, everywhere, everywhere, everywhere, everywhere, everywhere, everywhere,
            P("scene", "view", None), P("scene", "view"), tokens,
        ),
        out_specs=(grads, grads, grads, grads),
        check_vma=False,
    )
```

```python
import functools

import jax
import jax.numpy as jnp
from jax import lax
from jax.experimental import pallas as pl
from jax.experimental.pallas import tpu as pltpu
from jax.sharding import PartitionSpec as P

HEAD_DIM = 64
EPSILON = 1e-06
MASKED = -1e30
MIB = 1024 * 1024

VMEM = pl.BlockSpec(memory_space=pltpu.VMEM)
HBM = pl.BlockSpec(memory_space=pltpu.HBM)
SMEM = pl.BlockSpec(memory_space=pltpu.SMEM)


def dot_nn(a, b):
    return lax.dot_general(a, b, (((1,), (0,)), ((), ())), preferred_element_type=jnp.float32)


def dot_nt(a, b):
    return lax.dot_general(a, b, (((1,), (1,)), ((), ())), preferred_element_type=jnp.float32)


def dot_tt(a, b):
    return lax.dot_general(a, b, (((0,), (1,)), ((), ())), preferred_element_type=jnp.float32)


def dot_tn(a, b):
    return lax.dot_general(a, b, (((0,), (0,)), ((), ())), preferred_element_type=jnp.float32)


def normalized(tokens, gain):
    x = tokens.astype(jnp.float32)
    mean = jnp.mean(x * x, -1, keepdims=True)
    return (x * lax.rsqrt(mean + EPSILON) * gain).astype(jnp.bfloat16)


def request_kernel(views, slots, groups, partners, counts, request, alive):
    for g in range(groups):
        request[g] = 0
        for u in range(views):
            alive[g * views + u] = 0
    for u in range(views):
        for j in range(slots):

            @pl.when(j < counts[0, u])
            def _():
                partner = partners[0, u, j]
                group = lax.div(partner, jnp.int32(views))
                request[group] = lax.rem(partner, jnp.int32(views))
                alive[group * views + u] = 1


def pick_kernel(groups, scalars, *refs):
    requests, lat, outgoing = refs[: groups - 1], refs[groups - 1], refs[groups:]
    for request, out in zip(requests, outgoing):
        out[...] = lat[request[scalars[1]]]


def weight_copy(scalars, source, target, arrived, index, axis):
    size = target.shape[axis]
    half = pl.ds(pl.multiple_of(scalars[0] * size, size), size)
    part = source.at[:, half] if axis == 1 else source.at[half, :]
    return pltpu.make_async_copy(part, target, arrived.at[index])


def project_kernel(
    scalars, lat_own, lat_other, cot_own, cot_other, gain, taps, w_query, w_key, w_value, w_out,
    normed, queries, keys, values, out_grad, *refs,
):
    bundles, (upstream, w_q, w_k, w_v, w_o, arrived) = refs[:4], refs[4:]
    views, strip, width = lat_own.shape
    copies = [
        weight_copy(scalars, w_query, w_q, arrived, 0, 1),
        weight_copy(scalars, w_key, w_k, arrived, 1, 1),
        weight_copy(scalars, w_value, w_v, arrived, 2, 1),
        weight_copy(scalars, w_out, w_o, arrived, 3, 0),
    ]
    for copy in copies:
        copy.start()
    row = scalars[0]

    def strip_of(u, half):
        index = 2 * u + (row if half == 0 else 1 - row)
        return pl.ds(pl.multiple_of(index * strip, strip), strip)

    for u in range(views):
        for half, source in enumerate((lat_own, lat_other)):
            normed[strip_of(u, half), :] = normalized(source[u], gain[...])
    first = row == 0
    chunk = 512
    column = lax.broadcasted_iota(jnp.int32, (strip, 1), 0)
    not_first = (column > 0).astype(jnp.float32)
    not_last = (column < strip - 1).astype(jnp.float32)
    for c in range(0, width, chunk):
        lanes = slice(c, c + chunk)
        tap = taps[:, lanes].astype(jnp.float32)
        top, middle, bottom = tap[0:3], tap[3:6], tap[6:9]
        cross = (jnp.where(first, top, bottom), jnp.where(first, bottom, top))
        for u in range(views):
            strips = [ref[u, :, lanes].astype(jnp.float32) for ref in (cot_own, cot_other)]
            shifted = []
            for x in strips:
                after = pltpu.roll(x, strip - 1, 0) * not_last
                before = pltpu.roll(x, 1, 0) * not_first
                shifted.append((after, x, before))
            for half in range(2):
                total = strips[half]
                for b in range(3):
                    total = total + middle[b : b + 1] * shifted[half][b]
                    total = total + cross[half][b : b + 1] * shifted[1 - half][b]
                upstream[strip_of(u, half), lanes] = total.astype(jnp.bfloat16)
    size, half_size = width // 4, width // 2
    up_half = upstream[:, pl.ds(pl.multiple_of(row * half_size, half_size), half_size)]
    for m, bundle in enumerate(bundles):
        start = pl.multiple_of(lax.bitwise_xor(scalars[2], jnp.int32(m)) * size, size)
        bundle[:, :size] = normed[:, pl.ds(start, size)]
        bundle[:, size:] = up_half
    rows = normed[...]
    for copy, weight, result in zip(copies, (w_q, w_k, w_v), (queries, keys, values)):
        copy.wait()
        result[...] = dot_nn(rows, weight[...]).astype(jnp.bfloat16)
    copies[3].wait()
    out_grad[...] = dot_nt(upstream[...], w_o[...]).astype(jnp.bfloat16)


def attention_kernel(views, groups, scalars, alive, *refs):
    got_own, got_other, refs = refs[: groups - 1], refs[groups - 1 : 2 * groups - 2], refs[2 * groups - 2 :]
    normed, queries, keys, values, out_grad, gain, w_key, w_value, *refs = refs
    normed_all, mixed_t, dquery_t, dkey, dvalue, w_k, w_v, arrived = refs
    copies = [
        weight_copy(scalars, w_key, w_k, arrived, 0, 1),
        weight_copy(scalars, w_value, w_v, arrived, 1, 1),
    ]
    for copy in copies:
        copy.start()
    strip = got_own[0].shape[0]
    tokens = queries.shape[0]
    view_tokens = tokens // views
    scale = HEAD_DIM ** (-0.5)
    here = scalars[1]
    normed_all[:tokens, :] = normed[...]
    pair = 2 * HEAD_DIM
    span = 2 * view_tokens
    column_view = lax.broadcasted_iota(jnp.int32, (1, views * span), 1) // span
    slot_alive = []
    for j in range(groups - 1):
        group = lax.bitwise_xor(here, jnp.int32(j + 1))
        start = tokens + 2 * j * strip
        normed_all[start : start + strip, :] = normalized(got_own[j][...], gain[...])
        normed_all[start + strip : start + 2 * strip, :] = normalized(got_other[j][...], gain[...])
        taken = jnp.zeros((1, views * span), jnp.int32)
        for u in range(views):
            taken = jnp.where(column_view == u, alive[group * views + u], taken)
        slot_alive.append(taken > 0)
    fetched = normed_all[tokens:, :]
    for copy in copies:
        copy.wait()
    fetched_keys = dot_nn(fetched, w_k[...]).astype(jnp.bfloat16)
    fetched_values = dot_nn(fetched, w_v[...]).astype(jnp.bfloat16)
    low = lax.broadcasted_iota(jnp.int32, (1, 1, pair), 2) < HEAD_DIM
    low_b = low.astype(jnp.bfloat16)
    high_b = 1 - low_b

    def stacked(x):
        x = x.reshape(views, view_tokens, pair)
        return jnp.concatenate((x * low_b, x * high_b), axis=1).reshape(views * span, pair)

    def unstacked(x):
        x = x.reshape(views, 2, view_tokens, pair)
        return jnp.where(low, x[:, 0], x[:, 1]).reshape(tokens, pair)

    def own_nt(a, b):
        return jnp.concatenate(
            [
                dot_nt(a[u * view_tokens : (u + 1) * view_tokens], b[u * span : (u + 1) * span])
                for u in range(views)
            ],
            axis=1,
        )

    def own_tn(a, b):
        return jnp.concatenate(
            [
                dot_tn(a[:, u * span : (u + 1) * span], b[u * view_tokens : (u + 1) * view_tokens])
                for u in range(views)
            ],
            axis=0,
        )

    def own_nn(a, b):
        return jnp.concatenate(
            [
                dot_nn(a[:, u * span : (u + 1) * span], b[u * span : (u + 1) * span])
                for u in range(views)
            ],
            axis=0,
        )

    for p in range(queries.shape[1] // pair):
        lanes = slice(p * pair, (p + 1) * pair)
        q = stacked(queries[:, lanes])
        g = stacked(out_grad[:, lanes])
        k_own, v_own = keys[:, lanes], values[:, lanes]
        k_far, v_far = fetched_keys[:, lanes], fetched_values[:, lanes]
        s_own = own_nt(k_own, q) * scale
        s_far = dot_nt(k_far, q) * scale
        s_far = jnp.concatenate(
            [
                jnp.where(slot_alive[j], s_far[j * view_tokens : (j + 1) * view_tokens], MASKED)
                for j in range(groups - 1)
            ],
            axis=0,
        )
        highest = jnp.maximum(
            jnp.max(s_own, 0, keepdims=True), jnp.max(s_far, 0, keepdims=True)
        )
        e_own = jnp.exp(s_own - highest)
        e_far = jnp.exp(s_far - highest)
        inverse = 1.0 / (jnp.sum(e_own, 0, keepdims=True) + jnp.sum(e_far, 0, keepdims=True))
        a_own = e_own * inverse
        a_far = e_far * inverse
        ab_own = a_own.astype(jnp.bfloat16)
        ab_far = a_far.astype(jnp.bfloat16)
        mix = unstacked(own_tn(ab_own, v_own) + dot_tn(ab_far, v_far))
        mixed_t[lanes, :] = mix.T.astype(jnp.bfloat16)
        dvalue[:tokens, lanes] = own_nn(ab_own, g).astype(jnp.bfloat16)
        dvalue[tokens:, lanes] = dot_nn(ab_far, g).astype(jnp.bfloat16)
        dp_own = own_nt(v_own, g)
        dp_far = dot_nt(v_far, g)
        delta = jnp.sum(a_own * dp_own, 0, keepdims=True) + jnp.sum(a_far * dp_far, 0, keepdims=True)
        ds_own = (a_own * (dp_own - delta) * scale).astype(jnp.bfloat16)
        ds_far = (a_far * (dp_far - delta) * scale).astype(jnp.bfloat16)
        dq = unstacked(own_tn(ds_own, k_own) + dot_tn(ds_far, k_far))
        dquery_t[lanes, :] = dq.T.astype(jnp.bfloat16)
        dkey[:tokens, lanes] = own_nn(ds_own, q).astype(jnp.bfloat16)
        dkey[tokens:, lanes] = dot_nn(ds_far, q).astype(jnp.bfloat16)


def key_value_kernel(scalars, left, dkey, dvalue, k_send, v_send, k_keep, v_keep):
    size = k_send.shape[1]
    x, y = scalars[3], scalars[4]
    for side, (k_out, v_out) in enumerate(((k_send, v_send), (k_keep, v_keep))):
        x_out = x if side else 1 - x
        y_out = y if side else 1 - y
        for right, result, blocks in (
            (dkey, k_out, (x_out, 2 + x_out)),
            (dvalue, v_out, (2 * y_out, 2 * y_out + 1)),
        ):
            for i, block in enumerate(blocks):
                columns = pl.ds(pl.multiple_of(block * size, size), size)
                result[i] = dot_tn(left[:, columns], right[...]).astype(result.dtype)


def half_sum_kernel(scalars, k_keep, k_got, v_keep, v_got, k_later, v_later, k_now, v_now):
    x, y = scalars[3], scalars[4]
    for index, keep, got, later, now in ((y, k_keep, k_got, k_later, k_now), (x, v_keep, v_got, v_later, v_now)):
        later[...] = (keep[1 - index] + got[1 - index].astype(jnp.float32)).astype(jnp.bfloat16)
        now[...] = keep[index] + got[index].astype(jnp.float32)


def pack_kernel(k_now, k_got, v_now, v_got, packed):
    size = k_now.shape[1]
    packed[:, :size] = (k_now[...] + k_got[...].astype(jnp.float32)).astype(jnp.bfloat16)
    packed[:, size:] = (v_now[...] + v_got[...].astype(jnp.float32)).astype(jnp.bfloat16)


def unpack_kernel(rows, packed, key, value):
    sources, _, both = packed.shape
    size = both // 2
    for r in range(rows):
        total = packed[r].astype(jnp.float32)
        for i in range(r + rows, sources, rows):
            total = total + packed[i].astype(jnp.float32)
        key[:, r * size : (r + 1) * size] = total[:, :size]
        value[:, r * size : (r + 1) * size] = total[:, size:]


def share_kernel(scalars, dquery_t, mine, theirs, *bundles):
    inner = dquery_t.shape[0]
    size = bundles[0].shape[0] - inner
    for m, bundle in enumerate(bundles):
        scene = lax.bitwise_xor(scalars[2], jnp.int32(m))
        owner, place = lax.div(scene, jnp.int32(2)), lax.rem(scene, jnp.int32(2))
        rows = pl.ds(pl.multiple_of(place * size, size), size)
        is_mine = owner == scalars[0]
        bundle[:inner, :] = dquery_t[...]

        @pl.when(is_mine)
        def _():
            bundle[inner:, :] = mine[rows, :]

        @pl.when(jnp.logical_not(is_mine))
        def _():
            bundle[inner:, :] = theirs[rows, :]


def query_out_kernel(inner, *refs):
    early, late, packed = refs[0:4], refs[4:8], refs[8]
    quarter = packed.shape[2] // 4
    grad_q = grad_o = 0.0
    for left, right in zip(early, late):
        grad_q = grad_q + dot_tt(left[:, :quarter], right[:inner, :])
        grad_o = grad_o + dot_nn(right[inner:, :], left[:, quarter:])
    targets, size, _ = packed.shape
    for i in range(targets):
        packed[i] = jnp.concatenate(
            (
                grad_o[i * size : (i + 1) * size],
                grad_q[2 * i * size : (2 * i + 1) * size],
                grad_q[(2 * i + 1) * size : (2 * i + 2) * size],
            ),
            axis=1,
        ).astype(jnp.bfloat16)


def unpack_query_out_kernel(rows, packed, query, out):
    sources, size, width = packed.shape
    half, quarter = width // 2, width // 4
    for r in range(rows):
        total = packed[r].astype(jnp.float32)
        for i in range(r + rows, sources, rows):
            total = total + packed[i].astype(jnp.float32)
        out[:, r * half : (r + 1) * half] = total[:, :half]
        columns = slice(r * quarter, (r + 1) * quarter)
        query[:size, columns] = total[:, half : half + quarter]
        query[size:, columns] = total[:, half + quarter :]


def params(mebibytes):
    return pltpu.CompilerParams(vmem_limit_bytes=mebibytes * MIB)


def shape(dims, kind):
    return jax.ShapeDtypeStruct(dims, kind)


def shards(latents, norm_gain, w_query, w_key, w_value, w_out, kernel, partners, counts, cotangent):
    views, strip_rows, columns, width = latents.shape[1:]
    inner = w_query.shape[1]
    groups, rows = lax.axis_size("view"), lax.axis_size("row")
    scenes = lax.axis_size("scene")
    assert (strip_rows, rows, scenes) == (1, 2, 4)
    strip = strip_rows * columns
    slots = partners.shape[2]
    part = inner // rows
    tokens = views * 2 * strip
    key_tokens = tokens + (groups - 1) * 2 * strip
    bf16, f32, i32 = jnp.bfloat16, jnp.float32, jnp.int32

    row, view, scene = lax.axis_index("row"), lax.axis_index("view"), lax.axis_index("scene")
    scalars = jnp.stack((row, view, scene, scene % 2, scene // 2)).astype(i32)
    swap = [(0, 1), (1, 0)]
    across = [[(i, i ^ m) for i in range(scenes)] for m in range(scenes)]
    along_x, along_y = across[1], across[2]

    request, alive = pl.pallas_call(
        functools.partial(request_kernel, views, slots, groups),
        in_specs=[SMEM, SMEM],
        out_specs=(SMEM, SMEM),
        out_shape=(shape((groups,), i32), shape((groups * views,), i32)),
        name="requests",
    )(partners, counts)
    between = [[(i, i ^ d) for i in range(groups)] for d in range(1, groups)]
    granted = [lax.ppermute(request, "view", pairs) for pairs in between]

    lat = latents[0].reshape(views, strip, width)
    cot = cotangent[0].reshape(views, strip, width)
    lat_other = lax.ppermute(lat, "row", swap)
    cot_other = lax.ppermute(cot, "row", swap)

    gain = norm_gain.reshape(1, width)
    normed, queries, keys, values, out_grad, *early = pl.pallas_call(
        project_kernel,
        in_specs=[SMEM] + [VMEM] * 6 + [HBM] * 4,
        out_specs=[VMEM] * 9,
        out_shape=[
            shape((tokens, width), bf16),
            shape((tokens, part), bf16),
            shape((tokens, part), bf16),
            shape((tokens, part), bf16),
            shape((tokens, part), bf16),
        ]
        + [shape((tokens, 3 * width // 4), bf16)] * 4,
        scratch_shapes=[
            pltpu.VMEM((tokens, width), bf16),
            pltpu.VMEM((width, part), bf16),
            pltpu.VMEM((width, part), bf16),
            pltpu.VMEM((width, part), bf16),
            pltpu.VMEM((part, width), bf16),
            pltpu.SemaphoreType.DMA((4,)),
        ],
        compiler_params=params(52),
        cost_estimate=pl.CostEstimate(
            flops=8 * tokens * width * part + 40 * tokens * width,
            bytes_accessed=8 * width * part + 16 * tokens * width,
            transcendentals=tokens,
        ),
        name="project",
    )(scalars, lat, lat_other, cot, cot_other, gain, kernel, w_query, w_key, w_value, w_out)

    normed, granted = lax.optimization_barrier((normed, granted))
    outgoing = pl.pallas_call(
        functools.partial(pick_kernel, groups),
        in_specs=[SMEM] * groups + [VMEM],
        out_specs=[VMEM] * (groups - 1),
        out_shape=[shape((strip, width), bf16)] * (groups - 1),
        compiler_params=params(8),
        name="pick",
    )(scalars, *granted, lat)
    got_own = [lax.ppermute(part_out, "view", pairs) for part_out, pairs in zip(outgoing, between)]
    got_other = [lax.ppermute(got, "row", swap) for got in got_own]

    early, outgoing = lax.optimization_barrier((early, outgoing))
    early = [early[0]] + [lax.ppermute(early[m], "scene", across[m]) for m in range(1, 4)]

    normed_all, mixed_t, dquery_t, dkey, dvalue = pl.pallas_call(
        functools.partial(attention_kernel, views, groups),
        in_specs=[SMEM] * 2 + [VMEM] * (2 * groups - 2 + 6) + [HBM] * 2,
        out_specs=[VMEM] * 5,
        out_shape=[
            shape((key_tokens, width), bf16),
            shape((part, tokens), bf16),
            shape((part, tokens), bf16),
            shape((key_tokens, part), bf16),
            shape((key_tokens, part), bf16),
        ],
        scratch_shapes=[
            pltpu.VMEM((width, part), bf16),
            pltpu.VMEM((width, part), bf16),
            pltpu.SemaphoreType.DMA((2,)),
        ],
        compiler_params=params(50),
        cost_estimate=pl.CostEstimate(
            flops=4 * (key_tokens - tokens) * width * part + 24 * groups * 2 * strip * tokens * part,
            bytes_accessed=4 * width * part + 8 * key_tokens * width,
            transcendentals=groups * 2 * strip * tokens * part // HEAD_DIM,
        ),
        name="attention",
    )(
        scalars, alive, *got_own, *got_other, normed, queries, keys, values, out_grad, gain, w_key, w_value
    )
    quarter = width // 4
    two, one = (2, quarter, part), (quarter, part)
    k_send, v_send, k_keep, v_keep = pl.pallas_call(
        key_value_kernel,
        in_specs=[SMEM] + [VMEM] * 3,
        out_specs=[VMEM] * 4,
        out_shape=[shape(two, bf16)] * 2 + [shape(two, f32)] * 2,
        compiler_params=params(24),
        cost_estimate=pl.CostEstimate(
            flops=4 * key_tokens * width * part, bytes_accessed=12 * width * part, transcendentals=0
        ),
        name="grad_key_value",
    )(scalars, normed_all, dkey, dvalue)
    k_got = lax.ppermute(k_send, "scene", along_x)
    v_got = lax.ppermute(v_send, "scene", along_y)

    mixed_t, dquery_t, k_send, v_send = lax.optimization_barrier((mixed_t, dquery_t, k_send, v_send))
    mixed_other = lax.ppermute(mixed_t, "row", swap)
    late = pl.pallas_call(
        share_kernel,
        in_specs=[SMEM] + [VMEM] * 3,
        out_specs=[VMEM] * 4,
        out_shape=[shape((part + inner // 4, tokens), bf16)] * 4,
        compiler_params=params(8),
        name="share",
    )(scalars, dquery_t, mixed_t, mixed_other)
    late = [late[0]] + [lax.ppermute(late[m], "scene", across[m]) for m in range(1, 4)]
    targets = groups * rows
    q_rows, o_rows = width // (4 * targets), inner // (4 * targets)
    packed = pl.pallas_call(
        functools.partial(query_out_kernel, part),
        in_specs=[VMEM] * 8,
        out_specs=VMEM,
        out_shape=shape((targets, o_rows, width), bf16),
        compiler_params=params(16),
        cost_estimate=pl.CostEstimate(
            flops=4 * tokens * width * part, bytes_accessed=8 * tokens * width, transcendentals=0
        ),
        name="grad_query_out",
    )(*early, *late)
    packed = lax.all_to_all(packed, ("view", "row"), split_axis=0, concat_axis=0, tiled=True)
    grad_query, grad_out = pl.pallas_call(
        functools.partial(unpack_query_out_kernel, rows),
        in_specs=[VMEM],
        out_specs=[VMEM] * 2,
        out_shape=[shape((q_rows, inner), f32), shape((o_rows, width), f32)],
        compiler_params=params(8),
        name="sum_query_out",
    )(packed)

    k_later, v_later, k_now, v_now = pl.pallas_call(
        half_sum_kernel,
        in_specs=[SMEM] + [VMEM] * 4,
        out_specs=[VMEM] * 4,
        out_shape=[shape(one, bf16)] * 2 + [shape(one, f32)] * 2,
        compiler_params=params(16),
        name="sum_first",
    )(scalars, k_keep, k_got, v_keep, v_got)
    k_got = lax.ppermute(k_later, "scene", along_y)
    v_got = lax.ppermute(v_later, "scene", along_x)
    packed = pl.pallas_call(
        pack_kernel,
        in_specs=[VMEM] * 4,
        out_specs=VMEM,
        out_shape=shape((quarter, 2 * part), bf16),
        compiler_params=params(16),
        name="sum_second",
    )(k_now, k_got, v_now, v_got)
    packed = packed.reshape(targets, q_rows, 2 * part)
    packed = lax.all_to_all(packed, ("view", "row"), split_axis=0, concat_axis=0, tiled=True)
    grad_key, grad_value = pl.pallas_call(
        functools.partial(unpack_kernel, rows),
        in_specs=[VMEM],
        out_specs=[VMEM] * 2,
        out_shape=[shape((q_rows, inner), f32)] * 2,
        compiler_params=params(8),
        name="sum_key_value",
    )(packed)
    return grad_query, grad_key, grad_value, grad_out


def solution(mesh):
    tokens = P("scene", "view", "row", None, None)
    everywhere = P()
    grads = P(("scene", "view", "row"), None)
    return jax.shard_map(
        shards,
        mesh=mesh,
        in_specs=(
            tokens, everywhere, everywhere, everywhere, everywhere, everywhere, everywhere,
            P("scene", "view", None), P("scene", "view"), tokens,
        ),
        out_specs=(grads, grads, grads, grads),
        check_vma=False,
    )
```

```python
import functools

import jax
import jax.numpy as jnp
from jax import lax
from jax.experimental import pallas as pl
from jax.experimental.pallas import tpu as pltpu
from jax.sharding import PartitionSpec as P

HEAD_DIM = 64
EPSILON = 1e-06
MASKED = -1e30
MIB = 1024 * 1024
LITTLE = pl.CostEstimate(flops=1, bytes_accessed=1, transcendentals=0)

VMEM = pl.BlockSpec(memory_space=pltpu.VMEM)
HBM = pl.BlockSpec(memory_space=pltpu.HBM)
SMEM = pl.BlockSpec(memory_space=pltpu.SMEM)


def dot_nn(a, b):
    return lax.dot_general(a, b, (((1,), (0,)), ((), ())), preferred_element_type=jnp.float32)


def dot_nt(a, b):
    return lax.dot_general(a, b, (((1,), (1,)), ((), ())), preferred_element_type=jnp.float32)


def dot_tn(a, b):
    return lax.dot_general(a, b, (((0,), (0,)), ((), ())), preferred_element_type=jnp.float32)


def normalized(tokens, gain):
    x = tokens.astype(jnp.float32)
    mean = jnp.mean(x * x, -1, keepdims=True)
    return (x * lax.rsqrt(mean + EPSILON) * gain).astype(jnp.bfloat16)


def request_kernel(views, slots, groups, partners, counts, request, alive):
    for g in range(groups):
        request[g] = 0
        for u in range(views):
            alive[g * views + u] = 0
    for u in range(views):
        for j in range(slots):

            @pl.when(j < counts[0, u])
            def _():
                partner = partners[0, u, j]
                group = lax.div(partner, jnp.int32(views))
                request[group] = lax.rem(partner, jnp.int32(views))
                alive[group * views + u] = 1


def pick_kernel(groups, scalars, *refs):
    requests, lat, outgoing = refs[: groups - 1], refs[groups - 1], refs[groups:]
    for request, out in zip(requests, outgoing):
        out[...] = lat[request[scalars[1]]]


def weight_copy(scalars, source, target, arrived, index, axis):
    size = target.shape[axis]
    half = pl.ds(pl.multiple_of(scalars[0] * size, size), size)
    part = source.at[:, half] if axis == 1 else source.at[half, :]
    return pltpu.make_async_copy(part, target, arrived.at[index])


def project_kernel(
    scalars, lat_own_far, lat_other_far, cot_own_far, cot_other_far, gain, taps, w_query, w_key, w_value, w_out,
    normed, queries, keys, values, out_grad, up_half,
    lat_own, lat_other, cot_own, cot_other, upstream, w_q, w_k, w_v, w_o, arrived,
):
    views, strip, width = lat_own.shape
    inputs = [
        pltpu.make_async_copy(source, target, arrived.at[4 + i])
        for i, (source, target) in enumerate(
            (
                (lat_own_far, lat_own),
                (lat_other_far, lat_other),
                (cot_own_far, cot_own),
                (cot_other_far, cot_other),
            )
        )
    ]
    copies = [
        weight_copy(scalars, w_query, w_q, arrived, 0, 1),
        weight_copy(scalars, w_key, w_k, arrived, 1, 1),
        weight_copy(scalars, w_value, w_v, arrived, 2, 1),
        weight_copy(scalars, w_out, w_o, arrived, 3, 0),
    ]
    for copy in inputs + copies:
        copy.start()
    scale = gain[...].reshape(1, width)
    row = scalars[0]

    def strip_of(u, half):
        index = 2 * u + (row if half == 0 else 1 - row)
        return pl.ds(pl.multiple_of(index * strip, strip), strip)

    for half, source in enumerate((lat_own, lat_other)):
        inputs[half].wait()
        for u in range(views):
            normed[strip_of(u, half), :] = normalized(source[u], scale)
    first = row == 0
    for copy in inputs[2:]:
        copy.wait()
    chunk = 512
    column = lax.broadcasted_iota(jnp.int32, (strip, 1), 0)
    not_first = (column > 0).astype(jnp.float32)
    not_last = (column < strip - 1).astype(jnp.float32)
    for c in range(0, width, chunk):
        lanes = slice(c, c + chunk)
        tap = taps[:, lanes].astype(jnp.float32)
        top, middle, bottom = tap[0:3], tap[3:6], tap[6:9]
        cross = (jnp.where(first, top, bottom), jnp.where(first, bottom, top))
        for u in range(views):
            strips = [ref[u, :, lanes].astype(jnp.float32) for ref in (cot_own, cot_other)]
            shifted = []
            for x in strips:
                after = pltpu.roll(x, strip - 1, 0) * not_last
                before = pltpu.roll(x, 1, 0) * not_first
                shifted.append((after, x, before))
            for half in range(2):
                total = strips[half]
                for b in range(3):
                    total = total + middle[b : b + 1] * shifted[half][b]
                    total = total + cross[half][b : b + 1] * shifted[1 - half][b]
                upstream[strip_of(u, half), lanes] = total.astype(jnp.bfloat16)
    half_size = width // 2
    for scene in range(up_half.shape[0]):
        up_half[scene] = upstream[:, pl.ds(pl.multiple_of(row * half_size, half_size), half_size)]
    rows = normed[...]
    for copy, weight, result in zip(copies, (w_q, w_k, w_v), (queries, keys, values)):
        copy.wait()
        result[...] = dot_nn(rows, weight[...]).astype(jnp.bfloat16)
    copies[3].wait()
    out_grad[...] = dot_nt(upstream[...], w_o[...]).astype(jnp.bfloat16)


def attention_kernel(views, groups, scalars, alive, *refs):
    got_own, got_other, refs = refs[: groups - 1], refs[groups - 1 : 2 * groups - 2], refs[2 * groups - 2 :]
    normed, queries, keys, values, out_grad, gain, w_key, w_value, *refs = refs
    normed_all, mixed_t, dquery, dkey, dvalue, w_k, w_v, arrived = refs
    copies = [
        weight_copy(scalars, w_key, w_k, arrived, 0, 1),
        weight_copy(scalars, w_value, w_v, arrived, 1, 1),
    ]
    for copy in copies:
        copy.start()
    strip = got_own[0].shape[0]
    tokens = queries.shape[0]
    view_tokens = tokens // views
    scale = HEAD_DIM ** (-0.5)
    here = scalars[1]
    scale_row = gain[...].reshape(1, normed.shape[1])
    normed_all[:tokens, :] = normed[...]
    pair = 2 * HEAD_DIM
    span = 2 * view_tokens
    column_view = lax.broadcasted_iota(jnp.int32, (1, views * span), 1) // span
    slot_alive = []
    for j in range(groups - 1):
        group = lax.bitwise_xor(here, jnp.int32(j + 1))
        start = tokens + 2 * j * strip
        normed_all[start : start + strip, :] = normalized(got_own[j][...], scale_row)
        normed_all[start + strip : start + 2 * strip, :] = normalized(got_other[j][...], scale_row)
        taken = jnp.zeros((1, views * span), jnp.int32)
        for u in range(views):
            taken = jnp.where(column_view == u, alive[group * views + u], taken)
        slot_alive.append(taken > 0)
    low = lax.broadcasted_iota(jnp.int32, (1, 1, pair), 2) < HEAD_DIM
    low_b = low.astype(jnp.bfloat16)
    high_b = 1 - low_b

    def stacked(x):
        x = x.reshape(views, view_tokens, pair)
        return jnp.concatenate((x * low_b, x * high_b), axis=1).reshape(views * span, pair)

    def unstacked(x):
        x = x.reshape(views, 2, view_tokens, pair)
        return jnp.where(low, x[:, 0], x[:, 1]).reshape(tokens, pair)

    def own_nt(a, b):
        return jnp.concatenate(
            [
                dot_nt(a[u * view_tokens : (u + 1) * view_tokens], b[u * span : (u + 1) * span])
                for u in range(views)
            ],
            axis=1,
        )

    def own_tn(a, b):
        return jnp.concatenate(
            [
                dot_tn(a[:, u * span : (u + 1) * span], b[u * view_tokens : (u + 1) * view_tokens])
                for u in range(views)
            ],
            axis=0,
        )

    def own_nn(a, b):
        return jnp.concatenate(
            [
                dot_nn(a[:, u * span : (u + 1) * span], b[u * span : (u + 1) * span])
                for u in range(views)
            ],
            axis=0,
        )

    own = []
    for p in range(queries.shape[1] // pair):
        lanes = slice(p * pair, (p + 1) * pair)
        q, g = stacked(queries[:, lanes]), stacked(out_grad[:, lanes])
        k_own, v_own = keys[:, lanes], values[:, lanes]
        own.append((q, g, k_own, v_own, own_nt(k_own, q) * scale, own_nt(v_own, g)))
    fetched = normed_all[tokens:, :]
    for copy in copies:
        copy.wait()
    fetched_keys = dot_nn(fetched, w_k[...]).astype(jnp.bfloat16)
    fetched_values = dot_nn(fetched, w_v[...]).astype(jnp.bfloat16)
    for p, (q, g, k_own, v_own, s_own, dp_own) in enumerate(own):
        lanes = slice(p * pair, (p + 1) * pair)
        k_far, v_far = fetched_keys[:, lanes], fetched_values[:, lanes]
        s_far = dot_nt(k_far, q) * scale
        s_far = jnp.concatenate(
            [
                jnp.where(slot_alive[j], s_far[j * view_tokens : (j + 1) * view_tokens], MASKED)
                for j in range(groups - 1)
            ],
            axis=0,
        )
        highest = jnp.maximum(
            jnp.max(s_own, 0, keepdims=True), jnp.max(s_far, 0, keepdims=True)
        )
        e_own = jnp.exp(s_own - highest)
        e_far = jnp.exp(s_far - highest)
        inverse = 1.0 / (jnp.sum(e_own, 0, keepdims=True) + jnp.sum(e_far, 0, keepdims=True))
        a_own = e_own * inverse
        a_far = e_far * inverse
        ab_own = a_own.astype(jnp.bfloat16)
        ab_far = a_far.astype(jnp.bfloat16)
        mix = unstacked(own_tn(ab_own, v_own) + dot_tn(ab_far, v_far))
        mixed_t[lanes, :] = mix.T.astype(jnp.bfloat16)
        dvalue[:tokens, lanes] = own_nn(ab_own, g).astype(jnp.bfloat16)
        dvalue[tokens:, lanes] = dot_nn(ab_far, g).astype(jnp.bfloat16)
        dp_far = dot_nt(v_far, g)
        delta = jnp.sum(a_own * dp_own, 0, keepdims=True) + jnp.sum(a_far * dp_far, 0, keepdims=True)
        ds_own = (a_own * (dp_own - delta) * scale).astype(jnp.bfloat16)
        ds_far = (a_far * (dp_far - delta) * scale).astype(jnp.bfloat16)
        dq = unstacked(own_tn(ds_own, k_own) + dot_tn(ds_far, k_far))
        dquery[:, lanes] = dq.astype(jnp.bfloat16)
        dkey[:tokens, lanes] = own_nn(ds_own, q).astype(jnp.bfloat16)
        dkey[tokens:, lanes] = dot_nn(ds_far, q).astype(jnp.bfloat16)


def halves_kernel(scalars, left, right, x_send, y_send, x_keep, y_keep):
    size = x_send.shape[2]
    rows = x_send.shape[1]
    x, y = scalars[3], scalars[4]
    other = right[...]
    for dy, dx in ((1, 1), (0, 1), (1, 0), (0, 0)):
        block = 2 * lax.bitwise_xor(y, jnp.int32(dy)) + lax.bitwise_xor(x, jnp.int32(dx))
        columns = pl.ds(pl.multiple_of(block * 2 * rows, 2 * rows), 2 * rows)
        part = dot_tn(left[:, columns], other)
        x_out, y_out = (x_send if dx else x_keep), (y_send if dy else y_keep)
        x_out[dy] = part[:rows].astype(x_out.dtype)
        y_out[dx] = part[rows:].astype(y_out.dtype)


def first_sum_kernel(x_keep, x_got, y_keep, y_got, x_later, y_later, x_now, y_now):
    for keep, got, later, now in ((x_keep, x_got, x_later, x_now), (y_keep, y_got, y_later, y_now)):
        later[...] = (keep[1] + got[1].astype(jnp.float32)).astype(jnp.bfloat16)
        now[...] = keep[0] + got[0].astype(jnp.float32)


def second_sum_kernel(x_now, x_got, y_now, y_got, packed):
    rows = x_now.shape[0]
    packed[:rows, :] = (x_now[...] + x_got[...].astype(jnp.float32)).astype(jnp.bfloat16)
    packed[rows:, :] = (y_now[...] + y_got[...].astype(jnp.float32)).astype(jnp.bfloat16)


def last_sum_kernel(rows, packed, result):
    sources, _, size = packed.shape
    for r in range(rows):
        total = packed[r].astype(jnp.float32)
        for i in range(r + rows, sources, rows):
            total = total + packed[i].astype(jnp.float32)
        result[:, r * size : (r + 1) * size] = total


def share_kernel(scalars, mine, theirs, shares):
    size = shares.shape[1]
    for core, (here, there) in enumerate(((mine, theirs), (theirs, mine))):

        @pl.when(scalars[0] == core)
        def _():
            for i in range(2):
                shares[i] = here[i * size : (i + 1) * size, :]
                shares[2 + i] = there[i * size : (i + 1) * size, :]


def out_kernel(mixed_t, up_half, packed):
    total = dot_nn(mixed_t[0], up_half[0])
    for scene in range(1, mixed_t.shape[0]):
        total = total + dot_nn(mixed_t[scene], up_half[scene])
    packed[...] = total.astype(jnp.bfloat16)


def params(mebibytes):
    return pltpu.CompilerParams(vmem_limit_bytes=mebibytes * MIB)


def shape(dims, kind):
    return jax.ShapeDtypeStruct(dims, kind)


def shards(latents, norm_gain, w_query, w_key, w_value, w_out, kernel, partners, counts, cotangent):
    views, strip_rows, columns, width = latents.shape[1:]
    inner = w_query.shape[1]
    groups, rows = lax.axis_size("view"), lax.axis_size("row")
    scenes = lax.axis_size("scene")
    assert (strip_rows, rows, scenes) == (1, 2, 4)
    strip = strip_rows * columns
    slots = partners.shape[2]
    part = inner // rows
    tokens = views * 2 * strip
    key_tokens = tokens + (groups - 1) * 2 * strip
    bf16, f32, i32 = jnp.bfloat16, jnp.float32, jnp.int32

    row, view, scene = lax.axis_index("row"), lax.axis_index("view"), lax.axis_index("scene")
    scalars = jnp.stack((row, view, scene, scene % 2, scene // 2)).astype(i32)
    swap = [(0, 1), (1, 0)]
    along_x, along_y = [(i, i ^ 1) for i in range(scenes)], [(i, i ^ 2) for i in range(scenes)]

    request, alive = pl.pallas_call(
        functools.partial(request_kernel, views, slots, groups),
        in_specs=[SMEM, SMEM],
        out_specs=(SMEM, SMEM),
        out_shape=(shape((groups,), i32), shape((groups * views,), i32)),
        cost_estimate=LITTLE,
        name="requests",
    )(partners, counts)
    between = [[(i, i ^ d) for i in range(groups)] for d in range(1, groups)]
    granted = [lax.ppermute(request, "view", pairs) for pairs in between]

    lat = latents[0].reshape(views, strip, width)
    cot = cotangent[0].reshape(views, strip, width)
    lat_other = lax.ppermute(lat, "row", swap)
    cot_other = lax.ppermute(cot, "row", swap)

    normed, queries, keys, values, out_grad, up_half = pl.pallas_call(
        project_kernel,
        in_specs=[SMEM] + [HBM] * 4 + [VMEM] * 2 + [HBM] * 4,
        out_specs=[VMEM] * 6,
        out_shape=[
            shape((tokens, width), bf16),
            shape((tokens, part), bf16),
            shape((tokens, part), bf16),
            shape((tokens, part), bf16),
            shape((tokens, part), bf16),
            shape((scenes, tokens, width // 2), bf16),
        ],
        scratch_shapes=[pltpu.VMEM((views, strip, width), bf16)] * 4
        + [
            pltpu.VMEM((tokens, width), bf16),
            pltpu.VMEM((width, part), bf16),
            pltpu.VMEM((width, part), bf16),
            pltpu.VMEM((width, part), bf16),
            pltpu.VMEM((part, width), bf16),
            pltpu.SemaphoreType.DMA((8,)),
        ],
        compiler_params=params(51),
        cost_estimate=LITTLE,
        name="project",
    )(scalars, lat, lat_other, cot, cot_other, norm_gain, kernel, w_query, w_key, w_value, w_out)

    normed, granted = lax.optimization_barrier((normed, granted))
    outgoing = pl.pallas_call(
        functools.partial(pick_kernel, groups),
        in_specs=[SMEM] * groups + [VMEM],
        out_specs=[VMEM] * (groups - 1),
        out_shape=[shape((strip, width), bf16)] * (groups - 1),
        compiler_params=params(8),
        cost_estimate=LITTLE,
        name="pick",
    )(scalars, *granted, lat)
    got_own = [lax.ppermute(part_out, "view", pairs) for part_out, pairs in zip(outgoing, between)]
    got_other = [lax.ppermute(got, "row", swap) for got in got_own]

    up_far = lax.all_to_all(up_half, "scene", split_axis=0, concat_axis=0, tiled=True)

    normed_all, mixed_t, dquery, dkey, dvalue = pl.pallas_call(
        functools.partial(attention_kernel, views, groups),
        in_specs=[SMEM] * 2 + [VMEM] * (2 * groups - 2 + 6) + [HBM] * 2,
        out_specs=[VMEM] * 5,
        out_shape=[
            shape((key_tokens, width), bf16),
            shape((part, tokens), bf16),
            shape((tokens, part), bf16),
            shape((key_tokens, part), bf16),
            shape((key_tokens, part), bf16),
        ],
        scratch_shapes=[
            pltpu.VMEM((width, part), bf16),
            pltpu.VMEM((width, part), bf16),
            pltpu.SemaphoreType.DMA((2,)),
        ],
        compiler_params=params(48),
        cost_estimate=LITTLE,
        name="attention",
    )(
        scalars, alive, *got_own, *got_other, normed, queries, keys, values, out_grad, norm_gain, w_key, w_value
    )
    def call(kernel_body, results, operands, name, first=VMEM, mebibytes=16):
        outputs = pl.pallas_call(
            kernel_body,
            in_specs=[first] + [VMEM] * (len(operands) - 1),
            out_specs=[VMEM] * len(results),
            out_shape=results,
            compiler_params=params(mebibytes),
            cost_estimate=LITTLE,
            name=name,
        )(*operands)
        return list(outputs)

    def after(value, *earlier):
        return lax.optimization_barrier((value, *earlier))[0]

    half = width // 8
    blocks, block = (2, half, part), (half, part)

    def partial(left, right, name):
        results = [shape(blocks, bf16)] * 2 + [shape(blocks, f32)] * 2
        return call(halves_kernel, results, (scalars, left, right), name, SMEM, 24)

    def first_exchange(sends):
        return lax.ppermute(sends[0], "scene", along_x), lax.ppermute(sends[1], "scene", along_y)

    def first_sum(parts, got, name):
        results = [shape(block, bf16)] * 2 + [shape(block, f32)] * 2
        return call(first_sum_kernel, results, (parts[2], got[0], parts[3], got[1]), name)

    def second_exchange(sums):
        return lax.ppermute(sums[0], "scene", along_y), lax.ppermute(sums[1], "scene", along_x)

    def second_sum(sums, got, name):
        results = [shape((2 * half, part), bf16)]
        return call(second_sum_kernel, results, (sums[2], got[0], sums[3], got[1]), name)[0]

    targets = groups * rows

    def last_sum(packed, name):
        size = packed.shape[0] // targets
        packed = packed.reshape(targets, size, packed.shape[1])
        packed = lax.all_to_all(packed, ("view", "row"), split_axis=0, concat_axis=0, tiled=True)
        results = [shape((size, rows * packed.shape[2]), f32)]
        return call(functools.partial(last_sum_kernel, rows), results, (packed,), name)[0]

    q_parts = partial(normed, dquery, "grad_query")
    q_got = first_exchange(q_parts)
    k_parts = partial(normed_all, after(dkey, q_parts[0]), "grad_key")
    k_got = first_exchange(k_parts)
    v_parts = partial(normed_all, after(dvalue, k_parts[0]), "grad_value")
    v_got = first_exchange(v_parts)

    mixed_other = lax.ppermute(mixed_t, "row", swap)
    shares = call(
        share_kernel,
        [shape((scenes, inner // 4, tokens), bf16)],
        (scalars, mixed_t, mixed_other),
        "share",
        SMEM,
    )[0]
    mixed_far = lax.all_to_all(shares, "scene", split_axis=0, concat_axis=0, tiled=True)

    q_sums = first_sum(q_parts, q_got, "first_sum_query")
    q_got = second_exchange(q_sums)
    k_parts[2] = after(k_parts[2], q_sums[0])
    k_sums = first_sum(k_parts, k_got, "first_sum_key")
    k_got = second_exchange(k_sums)
    mixed_far = after(mixed_far, k_sums[0])
    o_packed = call(out_kernel, [shape((inner // 4, width // 2), bf16)], (mixed_far, up_far), "grad_out")[0]
    q_sums[2] = after(q_sums[2], o_packed)
    q_packed = second_sum(q_sums, q_got, "second_sum_query")
    v_parts[2] = after(v_parts[2], q_packed)
    v_sums = first_sum(v_parts, v_got, "first_sum_value")
    v_got = second_exchange(v_sums)
    k_sums[2] = after(k_sums[2], v_sums[0])
    k_packed = second_sum(k_sums, k_got, "second_sum_key")
    v_sums[2] = after(v_sums[2], k_packed)
    v_packed = second_sum(v_sums, v_got, "second_sum_value")
    return (
        last_sum(q_packed, "last_sum_query"),
        last_sum(k_packed, "last_sum_key"),
        last_sum(v_packed, "last_sum_value"),
        last_sum(o_packed, "last_sum_out"),
    )


def solution(mesh):
    tokens = P("scene", "view", "row", None, None)
    everywhere = P()
    grads = P(("scene", "view", "row"), None)
    return jax.shard_map(
        shards,
        mesh=mesh,
        in_specs=(
            tokens, everywhere, everywhere, everywhere, everywhere, everywhere, everywhere,
            P("scene", "view", None), P("scene", "view"), tokens,
        ),
        out_specs=(grads, grads, grads, grads),
        check_vma=False,
    )
```

```python
import functools

import jax
import jax.numpy as jnp
from jax import lax
from jax.experimental import pallas as pl
from jax.experimental.pallas import tpu as pltpu
from jax.sharding import PartitionSpec as P

HEAD_DIM = 64
EPSILON = 1e-06
MASKED = -1e30
MIB = 1024 * 1024
LITTLE = pl.CostEstimate(flops=1, bytes_accessed=1, transcendentals=0)

VMEM = pl.BlockSpec(memory_space=pltpu.VMEM)
HBM = pl.BlockSpec(memory_space=pltpu.HBM)
SMEM = pl.BlockSpec(memory_space=pltpu.SMEM)


def dot_nn(a, b):
    return lax.dot_general(a, b, (((1,), (0,)), ((), ())), preferred_element_type=jnp.float32)


def dot_nt(a, b):
    return lax.dot_general(a, b, (((1,), (1,)), ((), ())), preferred_element_type=jnp.float32)


def dot_tn(a, b):
    return lax.dot_general(a, b, (((0,), (0,)), ((), ())), preferred_element_type=jnp.float32)


def normalized(tokens, gain):
    x = tokens.astype(jnp.float32)
    mean = jnp.mean(x * x, -1, keepdims=True)
    return (x * lax.rsqrt(mean + EPSILON) * gain).astype(jnp.bfloat16)


def request_kernel(views, slots, groups, partners, counts, request, alive):
    for g in range(groups):
        request[g] = 0
        for u in range(views):
            alive[g * views + u] = 0
    for u in range(views):
        for j in range(slots):

            @pl.when(j < counts[0, u])
            def _():
                partner = partners[0, u, j]
                group = lax.div(partner, jnp.int32(views))
                request[group] = lax.rem(partner, jnp.int32(views))
                alive[group * views + u] = 1


def pick_kernel(groups, scalars, *refs):
    requests, lat, outgoing = refs[: groups - 1], refs[groups - 1], refs[groups:]
    for request, out in zip(requests, outgoing):
        out[...] = lat[request[scalars[1]]]


def weight_copy(scalars, source, target, arrived, index, axis):
    size = target.shape[axis]
    half = pl.ds(pl.multiple_of(scalars[0] * size, size), size)
    part = source.at[:, half] if axis == 1 else source.at[half, :]
    return pltpu.make_async_copy(part, target, arrived.at[index])


def project_kernel(
    scalars, lat_own_far, lat_other_far, cot_own_far, cot_other_far, gain, taps, w_query, w_key, w_value, w_out,
    normed, queries, keys, values, out_grad, upstream,
    lat_own, lat_other, cot_own, cot_other, w_q, w_k, w_v, w_o, arrived,
):
    views, strip, width = lat_own.shape
    inputs = [
        pltpu.make_async_copy(source, target, arrived.at[4 + i])
        for i, (source, target) in enumerate(
            (
                (lat_own_far, lat_own),
                (lat_other_far, lat_other),
                (cot_own_far, cot_own),
                (cot_other_far, cot_other),
            )
        )
    ]
    copies = [
        weight_copy(scalars, w_query, w_q, arrived, 0, 1),
        weight_copy(scalars, w_key, w_k, arrived, 1, 1),
        weight_copy(scalars, w_value, w_v, arrived, 2, 1),
        weight_copy(scalars, w_out, w_o, arrived, 3, 0),
    ]
    for copy in inputs + copies:
        copy.start()
    scale = gain[...].reshape(1, width)
    row = scalars[0]

    def strip_of(u, half):
        index = 2 * u + (row if half == 0 else 1 - row)
        return pl.ds(pl.multiple_of(index * strip, strip), strip)

    for half, source in enumerate((lat_own, lat_other)):
        inputs[half].wait()
        for u in range(views):
            normed[strip_of(u, half), :] = normalized(source[u], scale)
    first = row == 0
    for copy in inputs[2:]:
        copy.wait()
    chunk = 512
    column = lax.broadcasted_iota(jnp.int32, (strip, 1), 0)
    not_first = (column > 0).astype(jnp.float32)
    not_last = (column < strip - 1).astype(jnp.float32)
    for c in range(0, width, chunk):
        lanes = slice(c, c + chunk)
        tap = taps[:, lanes].astype(jnp.float32)
        top, middle, bottom = tap[0:3], tap[3:6], tap[6:9]
        cross = (jnp.where(first, top, bottom), jnp.where(first, bottom, top))
        for u in range(views):
            strips = [ref[u, :, lanes].astype(jnp.float32) for ref in (cot_own, cot_other)]
            shifted = []
            for x in strips:
                after = pltpu.roll(x, strip - 1, 0) * not_last
                before = pltpu.roll(x, 1, 0) * not_first
                shifted.append((after, x, before))
            for half in range(2):
                total = strips[half]
                for b in range(3):
                    total = total + middle[b : b + 1] * shifted[half][b]
                    total = total + cross[half][b : b + 1] * shifted[1 - half][b]
                upstream[strip_of(u, half), lanes] = total.astype(jnp.bfloat16)
    rows = normed[...]
    for copy, weight, result in zip(copies, (w_q, w_k, w_v), (queries, keys, values)):
        copy.wait()
        result[...] = dot_nn(rows, weight[...]).astype(jnp.bfloat16)
    copies[3].wait()
    out_grad[...] = dot_nt(upstream[...], w_o[...]).astype(jnp.bfloat16)


def attention_kernel(views, groups, scalars, alive, *refs):
    got_own, got_other, refs = refs[: groups - 1], refs[groups - 1 : 2 * groups - 2], refs[2 * groups - 2 :]
    normed, queries, keys, values, out_grad, gain, w_key, w_value, *refs = refs
    normed_all, mixed, dquery, dkey, dvalue, w_k, w_v, arrived = refs
    copies = [
        weight_copy(scalars, w_key, w_k, arrived, 0, 1),
        weight_copy(scalars, w_value, w_v, arrived, 1, 1),
    ]
    for copy in copies:
        copy.start()
    strip = got_own[0].shape[0]
    tokens = queries.shape[0]
    view_tokens = tokens // views
    scale = HEAD_DIM ** (-0.5)
    here = scalars[1]
    scale_row = gain[...].reshape(1, normed.shape[1])
    normed_all[:tokens, :] = normed[...]
    pair = 2 * HEAD_DIM
    span = 2 * view_tokens
    column_view = lax.broadcasted_iota(jnp.int32, (1, views * span), 1) // span
    slot_alive = []
    for j in range(groups - 1):
        group = lax.bitwise_xor(here, jnp.int32(j + 1))
        start = tokens + 2 * j * strip
        normed_all[start : start + strip, :] = normalized(got_own[j][...], scale_row)
        normed_all[start + strip : start + 2 * strip, :] = normalized(got_other[j][...], scale_row)
        taken = jnp.zeros((1, views * span), jnp.int32)
        for u in range(views):
            taken = jnp.where(column_view == u, alive[group * views + u], taken)
        slot_alive.append(taken > 0)
    low = lax.broadcasted_iota(jnp.int32, (1, 1, pair), 2) < HEAD_DIM
    low_b = low.astype(jnp.bfloat16)
    high_b = 1 - low_b

    def stacked(x):
        x = x.reshape(views, view_tokens, pair)
        return jnp.concatenate((x * low_b, x * high_b), axis=1).reshape(views * span, pair)

    def unstacked(x):
        x = x.reshape(views, 2, view_tokens, pair)
        return jnp.where(low, x[:, 0], x[:, 1]).reshape(tokens, pair)

    def own_nt(a, b):
        return jnp.concatenate(
            [
                dot_nt(a[u * view_tokens : (u + 1) * view_tokens], b[u * span : (u + 1) * span])
                for u in range(views)
            ],
            axis=1,
        )

    def own_tn(a, b):
        return jnp.concatenate(
            [
                dot_tn(a[:, u * span : (u + 1) * span], b[u * view_tokens : (u + 1) * view_tokens])
                for u in range(views)
            ],
            axis=0,
        )

    def own_nn(a, b):
        return jnp.concatenate(
            [
                dot_nn(a[:, u * span : (u + 1) * span], b[u * span : (u + 1) * span])
                for u in range(views)
            ],
            axis=0,
        )

    own = []
    for p in range(queries.shape[1] // pair):
        lanes = slice(p * pair, (p + 1) * pair)
        q, g = stacked(queries[:, lanes]), stacked(out_grad[:, lanes])
        k_own, v_own = keys[:, lanes], values[:, lanes]
        own.append((q, g, k_own, v_own, own_nt(k_own, q) * scale, own_nt(v_own, g)))
    fetched = normed_all[tokens:, :]
    for copy in copies:
        copy.wait()
    fetched_keys = dot_nn(fetched, w_k[...]).astype(jnp.bfloat16)
    fetched_values = dot_nn(fetched, w_v[...]).astype(jnp.bfloat16)
    for p, (q, g, k_own, v_own, s_own, dp_own) in enumerate(own):
        lanes = slice(p * pair, (p + 1) * pair)
        k_far, v_far = fetched_keys[:, lanes], fetched_values[:, lanes]
        s_far = dot_nt(k_far, q) * scale
        s_far = jnp.concatenate(
            [
                jnp.where(slot_alive[j], s_far[j * view_tokens : (j + 1) * view_tokens], MASKED)
                for j in range(groups - 1)
            ],
            axis=0,
        )
        highest = jnp.maximum(
            jnp.max(s_own, 0, keepdims=True), jnp.max(s_far, 0, keepdims=True)
        )
        e_own = jnp.exp(s_own - highest)
        e_far = jnp.exp(s_far - highest)
        inverse = 1.0 / (jnp.sum(e_own, 0, keepdims=True) + jnp.sum(e_far, 0, keepdims=True))
        a_own = e_own * inverse
        a_far = e_far * inverse
        ab_own = a_own.astype(jnp.bfloat16)
        ab_far = a_far.astype(jnp.bfloat16)
        mix = unstacked(own_tn(ab_own, v_own) + dot_tn(ab_far, v_far))
        mixed[:, lanes] = mix.astype(jnp.bfloat16)
        dvalue[:tokens, lanes] = own_nn(ab_own, g).astype(jnp.bfloat16)
        dvalue[tokens:, lanes] = dot_nn(ab_far, g).astype(jnp.bfloat16)
        dp_far = dot_nt(v_far, g)
        delta = jnp.sum(a_own * dp_own, 0, keepdims=True) + jnp.sum(a_far * dp_far, 0, keepdims=True)
        ds_own = (a_own * (dp_own - delta) * scale).astype(jnp.bfloat16)
        ds_far = (a_far * (dp_far - delta) * scale).astype(jnp.bfloat16)
        dq = unstacked(own_tn(ds_own, k_own) + dot_tn(ds_far, k_far))
        dquery[:, lanes] = dq.astype(jnp.bfloat16)
        dkey[:tokens, lanes] = own_nn(ds_own, q).astype(jnp.bfloat16)
        dkey[tokens:, lanes] = dot_nn(ds_far, q).astype(jnp.bfloat16)


def by_quarters(scalars, left, right, send, keep, x_first):
    size = send.shape[1]
    x, y = scalars[3], scalars[4]
    for target, first in ((send, 1), (keep, 0)):
        for second in (1, 0):
            dx, dy = (first, second) if x_first else (second, first)
            block = 2 * lax.bitwise_xor(y, jnp.int32(dy)) + lax.bitwise_xor(x, jnp.int32(dx))
            columns = pl.ds(pl.multiple_of(block * size, size), size)
            target[second] = dot_tn(left[:, columns], right[...]).astype(target.dtype)


def query_key_kernel(scalars, normed, dquery, normed_all, dkey, q_send, k_send, q_keep, k_keep):
    by_quarters(scalars, normed, dquery, q_send, q_keep, True)
    by_quarters(scalars, normed_all, dkey, k_send, k_keep, False)


def value_out_kernel(
    scalars, normed_all, dvalue, mine, theirs, upstream, v_send, o_send, v_keep, o_keep
):
    by_quarters(scalars, normed_all, dvalue, v_send, v_keep, True)
    row, x, y = scalars[0], scalars[3], scalars[4]
    size, width = o_send.shape[1:]
    right = upstream[:, pl.ds(pl.multiple_of(row * width, width), width)]
    from_mine, from_theirs = dot_tn(mine[...], right), dot_tn(theirs[...], right)
    keep_mine = row == y
    for block in range(2):
        place = pl.ds(lax.bitwise_xor(x, jnp.int32(block)), 1)
        rows = slice(block * size, (block + 1) * size)
        o_send[place] = jnp.where(keep_mine, from_theirs[rows], from_mine[rows])[None].astype(o_send.dtype)
        o_keep[place] = jnp.where(keep_mine, from_mine[rows], from_theirs[rows])[None]


def first_sum_kernel(x_keep, x_got, y_keep, y_got, x_later, y_later, x_now, y_now):
    for keep, got, later, now in ((x_keep, x_got, x_later, x_now), (y_keep, y_got, y_later, y_now)):
        later[...] = (keep[1] + got[1].astype(jnp.float32)).astype(jnp.bfloat16)
        now[...] = keep[0] + got[0].astype(jnp.float32)


def pack_query_key_kernel(q_now, q_got, k_now, k_got, packed):
    size = q_now.shape[1]
    packed[:, :size] = (q_now[...] + q_got[...].astype(jnp.float32)).astype(jnp.bfloat16)
    packed[:, size:] = (k_now[...] + k_got[...].astype(jnp.float32)).astype(jnp.bfloat16)


def pack_value_out_kernel(v_now, v_got, o_now, o_got, packed):
    grad_v = v_now[...] + v_got[...].astype(jnp.float32)
    grad_o = o_now[...] + o_got[...].astype(jnp.float32)
    targets, size, _ = packed.shape
    for i in range(targets):
        packed[i] = jnp.concatenate(
            (
                grad_o[i * size : (i + 1) * size],
                grad_v[2 * i * size : (2 * i + 1) * size],
                grad_v[(2 * i + 1) * size : (2 * i + 2) * size],
            ),
            axis=1,
        ).astype(jnp.bfloat16)


def summed_views(rows, packed):
    for r in range(rows):
        total = packed[r].astype(jnp.float32)
        for i in range(r + rows, packed.shape[0], rows):
            total = total + packed[i].astype(jnp.float32)
        yield r, total


def last_query_key_kernel(rows, packed, query, key):
    size = packed.shape[2] // 2
    for r, total in summed_views(rows, packed):
        columns = slice(r * size, (r + 1) * size)
        query[:, columns] = total[:, :size]
        key[:, columns] = total[:, size:]


def last_value_out_kernel(rows, packed, value, out):
    _, size, width = packed.shape
    half, quarter = width // 2, width // 4
    for r, total in summed_views(rows, packed):
        columns = slice(r * quarter, (r + 1) * quarter)
        out[:, r * half : (r + 1) * half] = total[:, :half]
        value[:size, columns] = total[:, half : half + quarter]
        value[size:, columns] = total[:, half + quarter :]


def params(mebibytes):
    return pltpu.CompilerParams(vmem_limit_bytes=mebibytes * MIB)


def shape(dims, kind):
    return jax.ShapeDtypeStruct(dims, kind)


def shards(latents, norm_gain, w_query, w_key, w_value, w_out, kernel, partners, counts, cotangent):
    views, strip_rows, columns, width = latents.shape[1:]
    inner = w_query.shape[1]
    groups, rows = lax.axis_size("view"), lax.axis_size("row")
    scenes = lax.axis_size("scene")
    assert (strip_rows, rows, scenes) == (1, 2, 4)
    strip = strip_rows * columns
    slots = partners.shape[2]
    part = inner // rows
    tokens = views * 2 * strip
    key_tokens = tokens + (groups - 1) * 2 * strip
    bf16, f32, i32 = jnp.bfloat16, jnp.float32, jnp.int32

    row, view, scene = lax.axis_index("row"), lax.axis_index("view"), lax.axis_index("scene")
    scalars = jnp.stack((row, view, scene, scene % 2, scene // 2)).astype(i32)
    swap = [(0, 1), (1, 0)]
    along_x, along_y = [(i, i ^ 1) for i in range(scenes)], [(i, i ^ 2) for i in range(scenes)]

    request, alive = pl.pallas_call(
        functools.partial(request_kernel, views, slots, groups),
        in_specs=[SMEM, SMEM],
        out_specs=(SMEM, SMEM),
        out_shape=(shape((groups,), i32), shape((groups * views,), i32)),
        cost_estimate=LITTLE,
        name="requests",
    )(partners, counts)
    between = [[(i, i ^ d) for i in range(groups)] for d in range(1, groups)]
    granted = [lax.ppermute(request, "view", pairs) for pairs in between]

    lat = latents[0].reshape(views, strip, width)
    cot = cotangent[0].reshape(views, strip, width)
    lat_other = lax.ppermute(lat, "row", swap)
    cot_other = lax.ppermute(cot, "row", swap)

    normed, queries, keys, values, out_grad, upstream = pl.pallas_call(
        project_kernel,
        in_specs=[SMEM] + [HBM] * 4 + [VMEM] * 2 + [HBM] * 4,
        out_specs=[VMEM] * 6,
        out_shape=[
            shape((tokens, width), bf16),
            shape((tokens, part), bf16),
            shape((tokens, part), bf16),
            shape((tokens, part), bf16),
            shape((tokens, part), bf16),
            shape((tokens, width), bf16),
        ],
        scratch_shapes=[pltpu.VMEM((views, strip, width), bf16)] * 4
        + [
            pltpu.VMEM((width, part), bf16),
            pltpu.VMEM((width, part), bf16),
            pltpu.VMEM((width, part), bf16),
            pltpu.VMEM((part, width), bf16),
            pltpu.SemaphoreType.DMA((8,)),
        ],
        compiler_params=params(51),
        cost_estimate=LITTLE,
        name="project",
    )(scalars, lat, lat_other, cot, cot_other, norm_gain, kernel, w_query, w_key, w_value, w_out)

    normed, granted = lax.optimization_barrier((normed, granted))
    outgoing = pl.pallas_call(
        functools.partial(pick_kernel, groups),
        in_specs=[SMEM] * groups + [VMEM],
        out_specs=[VMEM] * (groups - 1),
        out_shape=[shape((strip, width), bf16)] * (groups - 1),
        compiler_params=params(8),
        cost_estimate=LITTLE,
        name="pick",
    )(scalars, *granted, lat)
    got_own = [lax.ppermute(part_out, "view", pairs) for part_out, pairs in zip(outgoing, between)]
    got_other = [lax.ppermute(got, "row", swap) for got in got_own]

    normed_all, mixed, dquery, dkey, dvalue = pl.pallas_call(
        functools.partial(attention_kernel, views, groups),
        in_specs=[SMEM] * 2 + [VMEM] * (2 * groups - 2 + 6) + [HBM] * 2,
        out_specs=[VMEM] * 5,
        out_shape=[
            shape((key_tokens, width), bf16),
            shape((tokens, part), bf16),
            shape((tokens, part), bf16),
            shape((key_tokens, part), bf16),
            shape((key_tokens, part), bf16),
        ],
        scratch_shapes=[
            pltpu.VMEM((width, part), bf16),
            pltpu.VMEM((width, part), bf16),
            pltpu.SemaphoreType.DMA((2,)),
        ],
        compiler_params=params(48),
        cost_estimate=LITTLE,
        name="attention",
    )(
        scalars, alive, *got_own, *got_other, normed, queries, keys, values, out_grad, norm_gain, w_key, w_value
    )
    def call(kernel_body, results, operands, name, first=VMEM, mebibytes=16):
        outputs = pl.pallas_call(
            kernel_body,
            in_specs=[first] + [VMEM] * (len(operands) - 1),
            out_specs=[VMEM] * len(results),
            out_shape=results,
            compiler_params=params(mebibytes),
            cost_estimate=LITTLE,
            name=name,
        )(*operands)
        return list(outputs)

    def after(value, *earlier):
        return lax.optimization_barrier((value, *earlier))[0]

    targets = groups * rows
    q_size, o_size = width // 4, inner // 4
    q_rows, o_rows = q_size // targets, o_size // targets
    q_block, o_block = (q_size, part), (o_size, width // 2)

    def first_exchange(sends):
        return lax.ppermute(sends[0], "scene", along_x), lax.ppermute(sends[1], "scene", along_y)

    def first_sum(parts, got, name):
        blocks = [part_now.shape[1:] for part_now in parts[:2]]
        results = [shape(block, bf16) for block in blocks] + [shape(block, f32) for block in blocks]
        return call(first_sum_kernel, results, (parts[2], got[0], parts[3], got[1]), name)

    def second_exchange(sums):
        return lax.ppermute(sums[0], "scene", along_y), lax.ppermute(sums[1], "scene", along_x)

    def across_views(packed):
        return lax.all_to_all(packed, ("view", "row"), split_axis=0, concat_axis=0, tiled=True)

    mixed_other = lax.ppermute(mixed, "row", swap)

    results = [shape((2, *q_block), bf16)] * 2 + [shape((2, *q_block), f32)] * 2
    qk_parts = call(
        query_key_kernel, results, (scalars, normed, dquery, normed_all, dkey), "grad_query_key", SMEM, 24
    )
    qk_got = first_exchange(qk_parts)
    results = [shape((2, *block), kind) for kind in (bf16, f32) for block in (q_block, o_block)]
    vo_parts = call(
        value_out_kernel,
        results,
        (scalars, normed_all, after(dvalue, qk_parts[0]), mixed, mixed_other, upstream),
        "grad_value_out",
        SMEM,
        24,
    )
    vo_got = first_exchange(vo_parts)

    qk_sums = first_sum(qk_parts, qk_got, "first_sum_query_key")
    qk_got = second_exchange(qk_sums)
    packed = call(
        pack_query_key_kernel,
        [shape((q_size, 2 * part), bf16)],
        (qk_sums[2], qk_got[0], qk_sums[3], qk_got[1]),
        "second_sum_query_key",
    )[0]
    vo_parts[2] = after(vo_parts[2], packed)
    packed = across_views(packed.reshape(targets, q_rows, 2 * part))
    grad_query, grad_key = call(
        functools.partial(last_query_key_kernel, rows),
        [shape((q_rows, inner), f32)] * 2,
        (packed,),
        "last_sum_query_key",
    )

    vo_sums = first_sum(vo_parts, vo_got, "first_sum_value_out")
    vo_got = second_exchange(vo_sums)
    packed = call(
        pack_value_out_kernel,
        [shape((targets, o_rows, width), bf16)],
        (vo_sums[2], vo_got[0], vo_sums[3], vo_got[1]),
        "second_sum_value_out",
    )[0]
    packed = across_views(packed)
    grad_value, grad_out = call(
        functools.partial(last_value_out_kernel, rows),
        [shape((q_rows, inner), f32), shape((o_rows, width), f32)],
        (packed,),
        "last_sum_value_out",
    )
    return grad_query, grad_key, grad_value, grad_out


def solution(mesh):
    tokens = P("scene", "view", "row", None, None)
    everywhere = P()
    grads = P(("scene", "view", "row"), None)
    return jax.shard_map(
        shards,
        mesh=mesh,
        in_specs=(
            tokens, everywhere, everywhere, everywhere, everywhere, everywhere, everywhere,
            P("scene", "view", None), P("scene", "view"), tokens,
        ),
        out_specs=(grads, grads, grads, grads),
        check_vma=False,
    )
```

```python
import functools

import jax
import jax.numpy as jnp
from jax import lax
from jax.experimental import pallas as pl
from jax.experimental.pallas import tpu as pltpu
from jax.sharding import PartitionSpec as P

HEAD_DIM = 64
EPSILON = 1e-06
MASKED = -1e30
MIB = 1024 * 1024
LITTLE = pl.CostEstimate(flops=1, bytes_accessed=1, transcendentals=0)
MUCH = pl.CostEstimate(flops=40_000_000_000, bytes_accessed=1, transcendentals=0)

VMEM = pl.BlockSpec(memory_space=pltpu.VMEM)
HBM = pl.BlockSpec(memory_space=pltpu.HBM)
SMEM = pl.BlockSpec(memory_space=pltpu.SMEM)


def dot_nn(a, b):
    return lax.dot_general(a, b, (((1,), (0,)), ((), ())), preferred_element_type=jnp.float32)


def dot_nt(a, b):
    return lax.dot_general(a, b, (((1,), (1,)), ((), ())), preferred_element_type=jnp.float32)


def dot_tn(a, b):
    return lax.dot_general(a, b, (((0,), (0,)), ((), ())), preferred_element_type=jnp.float32)


def normalized(tokens, gain):
    x = tokens.astype(jnp.float32)
    mean = jnp.mean(x * x, -1, keepdims=True)
    return (x * lax.rsqrt(mean + EPSILON) * gain).astype(jnp.bfloat16)


def request_kernel(views, slots, groups, partners, counts, request, alive):
    for g in range(groups):
        request[g] = 0
        for u in range(views):
            alive[g * views + u] = 0
    for u in range(views):
        for j in range(slots):

            @pl.when(j < counts[0, u])
            def _():
                partner = partners[0, u, j]
                group = lax.div(partner, jnp.int32(views))
                request[group] = lax.rem(partner, jnp.int32(views))
                alive[group * views + u] = 1


def pick_kernel(groups, scalars, *refs):
    requests, lat, outgoing = refs[: groups - 1], refs[groups - 1], refs[groups:]
    for request, out in zip(requests, outgoing):
        out[...] = lat[request[scalars[1]]]


def weight_copy(scalars, source, target, arrived, index, axis):
    size = target.shape[axis]
    half = pl.ds(pl.multiple_of(scalars[0] * size, size), size)
    part = source.at[:, half] if axis == 1 else source.at[half, :]
    return pltpu.make_async_copy(part, target, arrived.at[index])


def project_kernel(
    scalars, lat_own_far, lat_other_far, cot_own_far, cot_other_far, gain, taps, w_query, w_key, w_value, w_out,
    normed, queries, keys, values, out_grad, upstream,
    lat_own, lat_other, cot_own, cot_other, w_q, w_k, w_v, w_o, arrived,
):
    views, strip, width = lat_own.shape
    inputs = [
        pltpu.make_async_copy(source, target, arrived.at[4 + i])
        for i, (source, target) in enumerate(
            (
                (lat_own_far, lat_own),
                (lat_other_far, lat_other),
                (cot_own_far, cot_own),
                (cot_other_far, cot_other),
            )
        )
    ]
    copies = [
        weight_copy(scalars, w_query, w_q, arrived, 0, 1),
        weight_copy(scalars, w_key, w_k, arrived, 1, 1),
        weight_copy(scalars, w_value, w_v, arrived, 2, 1),
        weight_copy(scalars, w_out, w_o, arrived, 3, 0),
    ]
    for copy in inputs + copies:
        copy.start()
    scale = gain[...].reshape(1, width)
    row = scalars[0]

    def strip_of(u, half):
        index = 2 * u + (row if half == 0 else 1 - row)
        return pl.ds(pl.multiple_of(index * strip, strip), strip)

    for half, source in enumerate((lat_own, lat_other)):
        inputs[half].wait()
        for u in range(views):
            normed[strip_of(u, half), :] = normalized(source[u], scale)
    first = row == 0
    for copy in inputs[2:]:
        copy.wait()
    chunk = 512
    column = lax.broadcasted_iota(jnp.int32, (strip, 1), 0)
    not_first = (column > 0).astype(jnp.float32)
    not_last = (column < strip - 1).astype(jnp.float32)
    for c in range(0, width, chunk):
        lanes = slice(c, c + chunk)
        tap = taps[:, lanes].astype(jnp.float32)
        top, middle, bottom = tap[0:3], tap[3:6], tap[6:9]
        cross = (jnp.where(first, top, bottom), jnp.where(first, bottom, top))
        for u in range(views):
            strips = [ref[u, :, lanes].astype(jnp.float32) for ref in (cot_own, cot_other)]
            shifted = []
            for x in strips:
                after = pltpu.roll(x, strip - 1, 0) * not_last
                before = pltpu.roll(x, 1, 0) * not_first
                shifted.append((after, x, before))
            for half in range(2):
                total = strips[half]
                for b in range(3):
                    total = total + middle[b : b + 1] * shifted[half][b]
                    total = total + cross[half][b : b + 1] * shifted[1 - half][b]
                upstream[strip_of(u, half), lanes] = total.astype(jnp.bfloat16)
    rows = normed[...]
    for copy, weight, result in zip(copies, (w_q, w_k, w_v), (queries, keys, values)):
        copy.wait()
        result[...] = dot_nn(rows, weight[...]).astype(jnp.bfloat16)
    copies[3].wait()
    out_grad[...] = dot_nt(upstream[...], w_o[...]).astype(jnp.bfloat16)


def attention_kernel(views, groups, scalars, alive, *refs):
    got_own, got_other, refs = refs[: groups - 1], refs[groups - 1 : 2 * groups - 2], refs[2 * groups - 2 :]
    queries, keys, values, out_grad, gain, w_key, w_value, *refs = refs
    normed_far, mixed, dquery, dkey, dvalue, w_k, w_v, arrived = refs
    copies = [
        weight_copy(scalars, w_key, w_k, arrived, 0, 1),
        weight_copy(scalars, w_value, w_v, arrived, 1, 1),
    ]
    for copy in copies:
        copy.start()
    strip = got_own[0].shape[0]
    tokens = queries.shape[0]
    view_tokens = tokens // views
    scale = HEAD_DIM ** (-0.5)
    here = scalars[1]
    scale_row = gain[...].reshape(1, normed_far.shape[1])
    pair = 2 * HEAD_DIM
    span = 2 * view_tokens
    column_view = lax.broadcasted_iota(jnp.int32, (1, views * span), 1) // span
    slot_alive = []
    for j in range(groups - 1):
        group = lax.bitwise_xor(here, jnp.int32(j + 1))
        start = 2 * j * strip
        normed_far[start : start + strip, :] = normalized(got_own[j][...], scale_row)
        normed_far[start + strip : start + 2 * strip, :] = normalized(got_other[j][...], scale_row)
        taken = jnp.zeros((1, views * span), jnp.int32)
        for u in range(views):
            taken = jnp.where(column_view == u, alive[group * views + u], taken)
        slot_alive.append(taken > 0)
    low = lax.broadcasted_iota(jnp.int32, (1, 1, pair), 2) < HEAD_DIM
    low_b = low.astype(jnp.bfloat16)
    high_b = 1 - low_b

    def stacked(x):
        x = x.reshape(views, view_tokens, pair)
        return jnp.concatenate((x * low_b, x * high_b), axis=1).reshape(views * span, pair)

    def unstacked(x):
        x = x.reshape(views, 2, view_tokens, pair)
        return jnp.where(low, x[:, 0], x[:, 1]).reshape(tokens, pair)

    def own_nt(a, b):
        return jnp.concatenate(
            [
                dot_nt(a[u * view_tokens : (u + 1) * view_tokens], b[u * span : (u + 1) * span])
                for u in range(views)
            ],
            axis=1,
        )

    def own_tn(a, b):
        return jnp.concatenate(
            [
                dot_tn(a[:, u * span : (u + 1) * span], b[u * view_tokens : (u + 1) * view_tokens])
                for u in range(views)
            ],
            axis=0,
        )

    def own_nn(a, b):
        return jnp.concatenate(
            [
                dot_nn(a[:, u * span : (u + 1) * span], b[u * span : (u + 1) * span])
                for u in range(views)
            ],
            axis=0,
        )

    own = []
    for p in range(queries.shape[1] // pair):
        lanes = slice(p * pair, (p + 1) * pair)
        q, g = stacked(queries[:, lanes]), stacked(out_grad[:, lanes])
        k_own, v_own = keys[:, lanes], values[:, lanes]
        own.append((q, g, k_own, v_own, own_nt(k_own, q) * scale, own_nt(v_own, g)))
    fetched = normed_far[...]
    for copy in copies:
        copy.wait()
    fetched_keys = dot_nn(fetched, w_k[...]).astype(jnp.bfloat16)
    fetched_values = dot_nn(fetched, w_v[...]).astype(jnp.bfloat16)
    for p, (q, g, k_own, v_own, s_own, dp_own) in enumerate(own):
        lanes = slice(p * pair, (p + 1) * pair)
        k_far, v_far = fetched_keys[:, lanes], fetched_values[:, lanes]
        s_far = dot_nt(k_far, q) * scale
        s_far = jnp.concatenate(
            [
                jnp.where(slot_alive[j], s_far[j * view_tokens : (j + 1) * view_tokens], MASKED)
                for j in range(groups - 1)
            ],
            axis=0,
        )
        highest = jnp.maximum(
            jnp.max(s_own, 0, keepdims=True), jnp.max(s_far, 0, keepdims=True)
        )
        e_own = jnp.exp(s_own - highest)
        e_far = jnp.exp(s_far - highest)
        inverse = 1.0 / (jnp.sum(e_own, 0, keepdims=True) + jnp.sum(e_far, 0, keepdims=True))
        a_own = e_own * inverse
        a_far = e_far * inverse
        ab_own = a_own.astype(jnp.bfloat16)
        ab_far = a_far.astype(jnp.bfloat16)
        mix = unstacked(own_tn(ab_own, v_own) + dot_tn(ab_far, v_far))
        mixed[:, lanes] = mix.astype(jnp.bfloat16)
        dvalue[:tokens, lanes] = own_nn(ab_own, g).astype(jnp.bfloat16)
        dvalue[tokens:, lanes] = dot_nn(ab_far, g).astype(jnp.bfloat16)
        dp_far = dot_nt(v_far, g)
        delta = jnp.sum(a_own * dp_own, 0, keepdims=True) + jnp.sum(a_far * dp_far, 0, keepdims=True)
        ds_own = (a_own * (dp_own - delta) * scale).astype(jnp.bfloat16)
        ds_far = (a_far * (dp_far - delta) * scale).astype(jnp.bfloat16)
        dq = unstacked(own_tn(ds_own, k_own) + dot_tn(ds_far, k_far))
        dquery[:, lanes] = dq.astype(jnp.bfloat16)
        dkey[:tokens, lanes] = own_nn(ds_own, q).astype(jnp.bfloat16)
        dkey[tokens:, lanes] = dot_nn(ds_far, q).astype(jnp.bfloat16)


def by_quarters(scalars, lefts, right, send, keep, x_first):
    size = send.shape[1]
    x, y = scalars[3], scalars[4]
    for target, first in ((send, 1), (keep, 0)):
        for second in (1, 0):
            dx, dy = (first, second) if x_first else (second, first)
            block = 2 * lax.bitwise_xor(y, jnp.int32(dy)) + lax.bitwise_xor(x, jnp.int32(dx))
            columns = pl.ds(pl.multiple_of(block * size, size), size)
            total, start = 0.0, 0
            for left in lefts:
                total = total + dot_tn(left[:, columns], right[start : start + left.shape[0], :])
                start += left.shape[0]
            target[second] = total.astype(target.dtype)


def query_key_kernel(scalars, normed, normed_far, dquery, dkey, q_send, k_send, q_keep, k_keep):
    by_quarters(scalars, (normed,), dquery, q_send, q_keep, True)
    by_quarters(scalars, (normed, normed_far), dkey, k_send, k_keep, False)


def value_out_kernel(
    scalars, normed, normed_far, dvalue, mine, theirs, upstream, v_send, o_send, v_keep, o_keep
):
    by_quarters(scalars, (normed, normed_far), dvalue, v_send, v_keep, True)
    row, x, y = scalars[0], scalars[3], scalars[4]
    size, width = o_send.shape[1:]
    right = upstream[:, pl.ds(pl.multiple_of(row * width, width), width)]
    from_mine, from_theirs = dot_tn(mine[...], right), dot_tn(theirs[...], right)
    keep_mine = row == y
    for block in range(2):
        place = pl.ds(lax.bitwise_xor(x, jnp.int32(block)), 1)
        rows = slice(block * size, (block + 1) * size)
        o_send[place] = jnp.where(keep_mine, from_theirs[rows], from_mine[rows])[None].astype(o_send.dtype)
        o_keep[place] = jnp.where(keep_mine, from_mine[rows], from_theirs[rows])[None]


def first_sum_kernel(x_keep, x_got, y_keep, y_got, x_later, y_later, x_now, y_now):
    for keep, got, later, now in ((x_keep, x_got, x_later, x_now), (y_keep, y_got, y_later, y_now)):
        later[...] = (keep[1] + got[1].astype(jnp.float32)).astype(jnp.bfloat16)
        now[...] = keep[0] + got[0].astype(jnp.float32)


def pack_query_key_kernel(q_now, q_got, k_now, k_got, packed):
    size = q_now.shape[1]
    packed[:, :size] = (q_now[...] + q_got[...].astype(jnp.float32)).astype(jnp.bfloat16)
    packed[:, size:] = (k_now[...] + k_got[...].astype(jnp.float32)).astype(jnp.bfloat16)


def pack_value_out_kernel(v_now, v_got, o_now, o_got, packed):
    grad_v = v_now[...] + v_got[...].astype(jnp.float32)
    grad_o = o_now[...] + o_got[...].astype(jnp.float32)
    targets, size, _ = packed.shape
    for i in range(targets):
        packed[i] = jnp.concatenate(
            (
                grad_o[i * size : (i + 1) * size],
                grad_v[2 * i * size : (2 * i + 1) * size],
                grad_v[(2 * i + 1) * size : (2 * i + 2) * size],
            ),
            axis=1,
        ).astype(jnp.bfloat16)


def summed_views(rows, packed):
    for r in range(rows):
        total = packed[r].astype(jnp.float32)
        for i in range(r + rows, packed.shape[0], rows):
            total = total + packed[i].astype(jnp.float32)
        yield r, total


def last_query_key_kernel(rows, packed, query, key):
    size = packed.shape[2] // 2
    for r, total in summed_views(rows, packed):
        columns = slice(r * size, (r + 1) * size)
        query[:, columns] = total[:, :size]
        key[:, columns] = total[:, size:]


def last_value_out_kernel(rows, packed, value, out):
    _, size, width = packed.shape
    half, quarter = width // 2, width // 4
    for r, total in summed_views(rows, packed):
        columns = slice(r * quarter, (r + 1) * quarter)
        out[:, r * half : (r + 1) * half] = total[:, :half]
        value[:size, columns] = total[:, half : half + quarter]
        value[size:, columns] = total[:, half + quarter :]


def params(mebibytes):
    return pltpu.CompilerParams(vmem_limit_bytes=mebibytes * MIB)


def shape(dims, kind):
    return jax.ShapeDtypeStruct(dims, kind)


def shards(latents, norm_gain, w_query, w_key, w_value, w_out, kernel, partners, counts, cotangent):
    views, strip_rows, columns, width = latents.shape[1:]
    inner = w_query.shape[1]
    groups, rows = lax.axis_size("view"), lax.axis_size("row")
    scenes = lax.axis_size("scene")
    assert (strip_rows, rows, scenes) == (1, 2, 4)
    strip = strip_rows * columns
    slots = partners.shape[2]
    part = inner // rows
    tokens = views * 2 * strip
    key_tokens = tokens + (groups - 1) * 2 * strip
    bf16, f32, i32 = jnp.bfloat16, jnp.float32, jnp.int32

    row, view, scene = lax.axis_index("row"), lax.axis_index("view"), lax.axis_index("scene")
    scalars = jnp.stack((row, view, scene, scene % 2, scene // 2)).astype(i32)
    swap = [(0, 1), (1, 0)]
    along_x, along_y = [(i, i ^ 1) for i in range(scenes)], [(i, i ^ 2) for i in range(scenes)]

    request, alive = pl.pallas_call(
        functools.partial(request_kernel, views, slots, groups),
        in_specs=[SMEM, SMEM],
        out_specs=(SMEM, SMEM),
        out_shape=(shape((groups,), i32), shape((groups * views,), i32)),
        cost_estimate=LITTLE,
        name="requests",
    )(partners, counts)
    between = [[(i, i ^ d) for i in range(groups)] for d in range(1, groups)]
    granted = [lax.ppermute(request, "view", pairs) for pairs in between]

    lat = latents[0].reshape(views, strip, width)
    cot = cotangent[0].reshape(views, strip, width)
    lat_other = lax.ppermute(lat, "row", swap)
    cot_other = lax.ppermute(cot, "row", swap)

    outgoing = pl.pallas_call(
        functools.partial(pick_kernel, groups),
        in_specs=[SMEM] * groups + [VMEM],
        out_specs=[VMEM] * (groups - 1),
        out_shape=[shape((strip, width), bf16)] * (groups - 1),
        compiler_params=params(8),
        cost_estimate=LITTLE,
        name="pick",
    )(scalars, *granted, lat)
    got_own = [lax.ppermute(part_out, "view", pairs) for part_out, pairs in zip(outgoing, between)]
    normed, queries, keys, values, out_grad, upstream = pl.pallas_call(
        project_kernel,
        in_specs=[SMEM] + [HBM] * 4 + [VMEM] * 2 + [HBM] * 4,
        out_specs=[VMEM] * 6,
        out_shape=[
            shape((tokens, width), bf16),
            shape((tokens, part), bf16),
            shape((tokens, part), bf16),
            shape((tokens, part), bf16),
            shape((tokens, part), bf16),
            shape((tokens, width), bf16),
        ],
        scratch_shapes=[pltpu.VMEM((views, strip, width), bf16)] * 4
        + [
            pltpu.VMEM((width, part), bf16),
            pltpu.VMEM((width, part), bf16),
            pltpu.VMEM((width, part), bf16),
            pltpu.VMEM((part, width), bf16),
            pltpu.SemaphoreType.DMA((8,)),
        ],
        compiler_params=params(51),
        cost_estimate=LITTLE,
        name="project",
    )(scalars, lat, lat_other, cot, cot_other, norm_gain, kernel, w_query, w_key, w_value, w_out)

    got_own, normed = lax.optimization_barrier((got_own, normed))
    got_other = [lax.ppermute(got, "row", swap) for got in got_own]

    normed_far, mixed, dquery, dkey, dvalue = pl.pallas_call(
        functools.partial(attention_kernel, views, groups),
        in_specs=[SMEM] * 2 + [VMEM] * (2 * groups - 2 + 5) + [HBM] * 2,
        out_specs=[VMEM] * 5,
        out_shape=[
            shape((key_tokens - tokens, width), bf16),
            shape((tokens, part), bf16),
            shape((tokens, part), bf16),
            shape((key_tokens, part), bf16),
            shape((key_tokens, part), bf16),
        ],
        scratch_shapes=[
            pltpu.VMEM((width, part), bf16),
            pltpu.VMEM((width, part), bf16),
            pltpu.SemaphoreType.DMA((2,)),
        ],
        compiler_params=params(48),
        cost_estimate=LITTLE,
        name="attention",
    )(
        scalars, alive, *got_own, *got_other, queries, keys, values, out_grad, norm_gain, w_key, w_value
    )
    def call(kernel_body, results, operands, name, first=VMEM, mebibytes=16, cost=LITTLE):
        outputs = pl.pallas_call(
            kernel_body,
            in_specs=[first] + [VMEM] * (len(operands) - 1),
            out_specs=[VMEM] * len(results),
            out_shape=results,
            compiler_params=params(mebibytes),
            cost_estimate=cost,
            name=name,
        )(*operands)
        return list(outputs)

    def after(value, *earlier):
        return lax.optimization_barrier((value, *earlier))[0]

    targets = groups * rows
    q_size, o_size = width // 4, inner // 4
    q_rows, o_rows = q_size // targets, o_size // targets
    q_block, o_block = (q_size, part), (o_size, width // 2)

    def first_exchange(sends):
        return lax.ppermute(sends[0], "scene", along_x), lax.ppermute(sends[1], "scene", along_y)

    def first_sum(parts, got, name, cost=LITTLE):
        blocks = [part_now.shape[1:] for part_now in parts[:2]]
        results = [shape(block, bf16) for block in blocks] + [shape(block, f32) for block in blocks]
        return call(first_sum_kernel, results, (parts[2], got[0], parts[3], got[1]), name, cost=cost)

    def second_exchange(sums):
        return lax.ppermute(sums[0], "scene", along_y), lax.ppermute(sums[1], "scene", along_x)

    def across_views(packed):
        return lax.all_to_all(packed, ("view", "row"), split_axis=0, concat_axis=0, tiled=True)

    mixed_other = lax.ppermute(mixed, "row", swap)

    results = [shape((2, *q_block), bf16)] * 2 + [shape((2, *q_block), f32)] * 2
    qk_parts = call(
        query_key_kernel, results, (scalars, normed, normed_far, dquery, dkey), "grad_query_key", SMEM, 24
    )
    qk_got = first_exchange(qk_parts)
    results = [shape((2, *block), kind) for kind in (bf16, f32) for block in (q_block, o_block)]
    vo_parts = call(
        value_out_kernel,
        results,
        (scalars, normed, normed_far, after(dvalue, qk_parts[0]), mixed, mixed_other, upstream),
        "grad_value_out",
        SMEM,
        24,
    )
    qk_parts[2] = after(qk_parts[2], vo_parts[0])
    qk_sums = first_sum(qk_parts, qk_got, "first_sum_query_key")
    vo_got = first_exchange([after(send, qk_sums[0]) for send in vo_parts[:2]])
    qk_got = second_exchange(qk_sums)
    packed = call(
        pack_query_key_kernel,
        [shape((q_size, 2 * part), bf16)],
        (qk_sums[2], qk_got[0], qk_sums[3], qk_got[1]),
        "second_sum_query_key",
    )[0]
    vo_parts[2] = after(vo_parts[2], packed)
    packed = across_views(packed.reshape(targets, q_rows, 2 * part))
    grad_query, grad_key = call(
        functools.partial(last_query_key_kernel, rows),
        [shape((q_rows, inner), f32)] * 2,
        (packed,),
        "last_sum_query_key",
    )

    vo_sums = first_sum(vo_parts, vo_got, "first_sum_value_out", MUCH)
    vo_got = second_exchange(vo_sums)
    packed = call(
        pack_value_out_kernel,
        [shape((targets, o_rows, width), bf16)],
        (vo_sums[2], vo_got[0], vo_sums[3], vo_got[1]),
        "second_sum_value_out",
        cost=MUCH,
    )[0]
    packed = across_views(packed)
    grad_value, grad_out = call(
        functools.partial(last_value_out_kernel, rows),
        [shape((q_rows, inner), f32), shape((o_rows, width), f32)],
        (packed,),
        "last_sum_value_out",
    )
    return grad_query, grad_key, grad_value, grad_out


def solution(mesh):
    tokens = P("scene", "view", "row", None, None)
    everywhere = P()
    grads = P(("scene", "view", "row"), None)
    return jax.shard_map(
        shards,
        mesh=mesh,
        in_specs=(
            tokens, everywhere, everywhere, everywhere, everywhere, everywhere, everywhere,
            P("scene", "view", None), P("scene", "view"), tokens,
        ),
        out_specs=(grads, grads, grads, grads),
        check_vma=False,
    )
```

```python
import functools

import jax
import jax.numpy as jnp
from jax import lax
from jax.experimental import pallas as pl
from jax.experimental.pallas import tpu as pltpu
from jax.sharding import PartitionSpec as P

HEAD_DIM = 64
EPSILON = 1e-06
MASKED = -1e30
MIB = 1024 * 1024
LITTLE = pl.CostEstimate(flops=1, bytes_accessed=1, transcendentals=0)
MUCH = pl.CostEstimate(flops=40_000_000_000, bytes_accessed=1, transcendentals=0)

VMEM = pl.BlockSpec(memory_space=pltpu.VMEM)
SMEM = pl.BlockSpec(memory_space=pltpu.SMEM)


def dot_nn(a, b):
    return lax.dot_general(a, b, (((1,), (0,)), ((), ())), preferred_element_type=jnp.float32)


def dot_nt(a, b):
    return lax.dot_general(a, b, (((1,), (1,)), ((), ())), preferred_element_type=jnp.float32)


def dot_tn(a, b):
    return lax.dot_general(a, b, (((0,), (0,)), ((), ())), preferred_element_type=jnp.float32)


def normalized(tokens, gain):
    x = tokens.astype(jnp.float32)
    mean = jnp.mean(x * x, -1, keepdims=True)
    return (x * lax.rsqrt(mean + EPSILON) * gain).astype(jnp.bfloat16)


def request_kernel(views, slots, groups, partners, counts, request, alive):
    for g in range(groups):
        request[g] = 0
        for u in range(views):
            alive[g * views + u] = 0
    for u in range(views):
        for j in range(slots):

            @pl.when(j < counts[0, u])
            def _():
                partner = partners[0, u, j]
                group = lax.div(partner, jnp.int32(views))
                request[group] = lax.rem(partner, jnp.int32(views))
                alive[group * views + u] = 1


def pick_kernel(groups, scalars, *refs):
    requests, lat, outgoing = refs[: groups - 1], refs[groups - 1], refs[groups:]
    for request, out in zip(requests, outgoing):
        out[...] = lat[request[scalars[1]]]


def core_half(scalars, size):
    return pl.ds(pl.multiple_of(scalars[0] * size, size), size)


def project_kernel(
    scalars, lat_own, lat_other, cot_own, cot_other, gain, taps, w_query, w_key, w_value, w_out,
    normed, queries, keys, values, out_grad, upstream,
):
    views, strip, width = lat_own.shape
    scale = gain[...].reshape(1, width)
    row = scalars[0]

    def strip_of(u, half):
        index = 2 * u + (row if half == 0 else 1 - row)
        return pl.ds(pl.multiple_of(index * strip, strip), strip)

    for half, source in enumerate((lat_own, lat_other)):
        for u in range(views):
            normed[strip_of(u, half), :] = normalized(source[u], scale)
    first = row == 0
    chunk = 512
    column = lax.broadcasted_iota(jnp.int32, (strip, 1), 0)
    not_first = (column > 0).astype(jnp.float32)
    not_last = (column < strip - 1).astype(jnp.float32)
    for c in range(0, width, chunk):
        lanes = slice(c, c + chunk)
        tap = taps[:, lanes].astype(jnp.float32)
        top, middle, bottom = tap[0:3], tap[3:6], tap[6:9]
        cross = (jnp.where(first, top, bottom), jnp.where(first, bottom, top))
        for u in range(views):
            strips = [ref[u, :, lanes].astype(jnp.float32) for ref in (cot_own, cot_other)]
            shifted = []
            for x in strips:
                after = pltpu.roll(x, strip - 1, 0) * not_last
                before = pltpu.roll(x, 1, 0) * not_first
                shifted.append((after, x, before))
            for half in range(2):
                total = strips[half]
                for b in range(3):
                    total = total + middle[b : b + 1] * shifted[half][b]
                    total = total + cross[half][b : b + 1] * shifted[1 - half][b]
                upstream[strip_of(u, half), lanes] = total.astype(jnp.bfloat16)
    rows = normed[...]
    half = core_half(scalars, queries.shape[1])
    for weight, result in ((w_query, queries), (w_key, keys), (w_value, values)):
        result[...] = dot_nn(rows, weight[:, half]).astype(jnp.bfloat16)
    out_grad[...] = dot_nt(upstream[...], w_out[half, :]).astype(jnp.bfloat16)


def attention_kernel(views, groups, scalars, alive, *refs):
    got_own, got_other, refs = refs[: groups - 1], refs[groups - 1 : 2 * groups - 2], refs[2 * groups - 2 :]
    queries, keys, values, out_grad, gain, w_key, w_value, *refs = refs
    normed_far, mixed, dquery, dkey, dvalue = refs
    strip = got_own[0].shape[0]
    tokens = queries.shape[0]
    view_tokens = tokens // views
    scale = HEAD_DIM ** (-0.5)
    here = scalars[1]
    scale_row = gain[...].reshape(1, normed_far.shape[1])
    pair = 2 * HEAD_DIM
    span = 2 * view_tokens
    column_view = lax.broadcasted_iota(jnp.int32, (1, views * span), 1) // span
    slot_alive = []
    for j in range(groups - 1):
        group = lax.bitwise_xor(here, jnp.int32(j + 1))
        start = 2 * j * strip
        normed_far[start : start + strip, :] = normalized(got_own[j][...], scale_row)
        normed_far[start + strip : start + 2 * strip, :] = normalized(got_other[j][...], scale_row)
        taken = jnp.zeros((1, views * span), jnp.int32)
        for u in range(views):
            taken = jnp.where(column_view == u, alive[group * views + u], taken)
        slot_alive.append(taken > 0)
    low = lax.broadcasted_iota(jnp.int32, (1, 1, pair), 2) < HEAD_DIM
    low_b = low.astype(jnp.bfloat16)
    high_b = 1 - low_b

    def stacked(x):
        x = x.reshape(views, view_tokens, pair)
        return jnp.concatenate((x * low_b, x * high_b), axis=1).reshape(views * span, pair)

    def unstacked(x):
        x = x.reshape(views, 2, view_tokens, pair)
        return jnp.where(low, x[:, 0], x[:, 1]).reshape(tokens, pair)

    def own_nt(a, b):
        return jnp.concatenate(
            [
                dot_nt(a[u * view_tokens : (u + 1) * view_tokens], b[u * span : (u + 1) * span])
                for u in range(views)
            ],
            axis=1,
        )

    def own_tn(a, b):
        return jnp.concatenate(
            [
                dot_tn(a[:, u * span : (u + 1) * span], b[u * view_tokens : (u + 1) * view_tokens])
                for u in range(views)
            ],
            axis=0,
        )

    def own_nn(a, b):
        return jnp.concatenate(
            [
                dot_nn(a[:, u * span : (u + 1) * span], b[u * span : (u + 1) * span])
                for u in range(views)
            ],
            axis=0,
        )

    own = []
    for p in range(queries.shape[1] // pair):
        lanes = slice(p * pair, (p + 1) * pair)
        q, g = stacked(queries[:, lanes]), stacked(out_grad[:, lanes])
        k_own, v_own = keys[:, lanes], values[:, lanes]
        own.append((q, g, k_own, v_own, own_nt(k_own, q) * scale, own_nt(v_own, g)))
    fetched = normed_far[...]
    half = core_half(scalars, queries.shape[1])
    fetched_keys = dot_nn(fetched, w_key[:, half]).astype(jnp.bfloat16)
    fetched_values = dot_nn(fetched, w_value[:, half]).astype(jnp.bfloat16)
    for p, (q, g, k_own, v_own, s_own, dp_own) in enumerate(own):
        lanes = slice(p * pair, (p + 1) * pair)
        k_far, v_far = fetched_keys[:, lanes], fetched_values[:, lanes]
        s_far = dot_nt(k_far, q) * scale
        s_far = jnp.concatenate(
            [
                jnp.where(slot_alive[j], s_far[j * view_tokens : (j + 1) * view_tokens], MASKED)
                for j in range(groups - 1)
            ],
            axis=0,
        )
        highest = jnp.maximum(
            jnp.max(s_own, 0, keepdims=True), jnp.max(s_far, 0, keepdims=True)
        )
        e_own = jnp.exp(s_own - highest)
        e_far = jnp.exp(s_far - highest)
        inverse = 1.0 / (jnp.sum(e_own, 0, keepdims=True) + jnp.sum(e_far, 0, keepdims=True))
        a_own = e_own * inverse
        a_far = e_far * inverse
        ab_own = a_own.astype(jnp.bfloat16)
        ab_far = a_far.astype(jnp.bfloat16)
        mix = unstacked(own_tn(ab_own, v_own) + dot_tn(ab_far, v_far))
        mixed[:, lanes] = mix.astype(jnp.bfloat16)
        dvalue[:tokens, lanes] = own_nn(ab_own, g).astype(jnp.bfloat16)
        dvalue[tokens:, lanes] = dot_nn(ab_far, g).astype(jnp.bfloat16)
        dp_far = dot_nt(v_far, g)
        delta = jnp.sum(a_own * dp_own, 0, keepdims=True) + jnp.sum(a_far * dp_far, 0, keepdims=True)
        ds_own = (a_own * (dp_own - delta) * scale).astype(jnp.bfloat16)
        ds_far = (a_far * (dp_far - delta) * scale).astype(jnp.bfloat16)
        dq = unstacked(own_tn(ds_own, k_own) + dot_tn(ds_far, k_far))
        dquery[:, lanes] = dq.astype(jnp.bfloat16)
        dkey[:tokens, lanes] = own_nn(ds_own, q).astype(jnp.bfloat16)
        dkey[tokens:, lanes] = dot_nn(ds_far, q).astype(jnp.bfloat16)


def by_quarters(scalars, lefts, right, send, keep, x_first):
    size = send.shape[1]
    x, y = scalars[3], scalars[4]
    for target, first in ((send, 1), (keep, 0)):
        for second in (1, 0):
            dx, dy = (first, second) if x_first else (second, first)
            block = 2 * lax.bitwise_xor(y, jnp.int32(dy)) + lax.bitwise_xor(x, jnp.int32(dx))
            columns = pl.ds(pl.multiple_of(block * size, size), size)
            total, start = 0.0, 0
            for left in lefts:
                total = total + dot_tn(left[:, columns], right[start : start + left.shape[0], :])
                start += left.shape[0]
            target[second] = total.astype(target.dtype)


def query_key_kernel(scalars, normed, normed_far, dquery, dkey, q_send, k_send, q_keep, k_keep):
    by_quarters(scalars, (normed,), dquery, q_send, q_keep, True)
    by_quarters(scalars, (normed, normed_far), dkey, k_send, k_keep, False)


def value_out_kernel(scalars, normed, normed_far, dvalue, mine, theirs, upstream, send, keep):
    row, x, y = scalars[0], scalars[3], scalars[4]
    odd = lax.rem(scalars[1], jnp.int32(2)) == 1
    _, _, pairs, size, width = send.shape
    half, quarter = width // 2, width // 4
    right = upstream[:, core_half(scalars, half)]
    from_mine, from_theirs = dot_tn(mine[...], right), dot_tn(theirs[...], right)
    for dy in range(2):
        grad_o = jnp.where(row == lax.bitwise_xor(y, jnp.int32(dy)), from_mine, from_theirs)
        low, high = grad_o[: 2 * pairs * size], grad_o[2 * pairs * size :]
        for dx in range(2):
            to_x = lax.bitwise_xor(x, jnp.int32(dx))
            o_part = jnp.where(to_x == 0, low, high)
            block = 2 * lax.bitwise_xor(y, jnp.int32(dy)) + to_x
            columns = pl.ds(pl.multiple_of(block * quarter, quarter), quarter)
            tokens = normed.shape[0]
            v_part = dot_tn(normed[:, columns], dvalue[:tokens, :])
            v_part = v_part + dot_tn(normed_far[:, columns], dvalue[tokens:, :])
            for pair in range(pairs):
                tiles = []
                for view in (2 * pair, 2 * pair + 1):
                    v_view = v_part[2 * view * size : 2 * (view + 1) * size]
                    tiles.append((o_part[view * size : (view + 1) * size], v_view[:size], v_view[size:]))
                for target, take_odd in ((send, jnp.logical_not(odd)), (keep, odd)):
                    tile = [jnp.where(take_odd, second, first) for first, second in zip(*tiles)]
                    target[dy, dx, pair] = jnp.concatenate(tile, axis=1).astype(target.dtype)


def view_sum_kernel(keep, got, x_send, y_send, x_keep, y_keep):
    half = keep.shape[4] // 2
    for second in range(2):
        for target, first in ((x_send, 1), (x_keep, 0)):
            total = keep[second, first, :, :, half:] + got[second, first, :, :, half:].astype(jnp.float32)
            target[second] = total.astype(target.dtype)
        for target, first in ((y_send, 1), (y_keep, 0)):
            total = keep[first, second, :, :, :half] + got[first, second, :, :, :half].astype(jnp.float32)
            target[second] = total.astype(target.dtype)


def first_sum_kernel(x_keep, x_got, y_keep, y_got, x_later, y_later, x_now, y_now):
    for keep, got, later, now in ((x_keep, x_got, x_later, x_now), (y_keep, y_got, y_later, y_now)):
        later[...] = (keep[1] + got[1].astype(jnp.float32)).astype(jnp.bfloat16)
        now[...] = keep[0] + got[0].astype(jnp.float32)


def pack_query_key_kernel(q_now, q_got, k_now, k_got, packed):
    size = q_now.shape[1]
    packed[:, :size] = (q_now[...] + q_got[...].astype(jnp.float32)).astype(jnp.bfloat16)
    packed[:, size:] = (k_now[...] + k_got[...].astype(jnp.float32)).astype(jnp.bfloat16)


def tile_halves_kernel(bit, out_and_value, scalars, *refs):
    addends, (send, keep) = refs[:-2], refs[-2:]
    count = keep.shape[0]
    mine = lax.rem(lax.div(scalars[1], jnp.int32(2 << bit)), jnp.int32(2))
    for target, part in ((send, 1 - mine), (keep, mine)):
        for i in range(count):
            place = pl.ds(part * count + i, 1)
            total = [now[place] + got[place].astype(jnp.float32) for now, got in zip(addends[::2], addends[1::2])]
            total = jnp.concatenate(total, axis=2) if out_and_value else total[0]
            target[i] = total[0].astype(target.dtype)


def tile_cores_kernel(scalars, keep, got, send, mine):
    total = keep[0] + got[0].astype(jnp.float32)
    size, width = mine.shape
    half, quarter = width // 2, width // 4
    parts = []
    for core in range(2):
        value = total[:, half + core * quarter : half + (core + 1) * quarter]
        out = total[core * size : (core + 1) * size, :half]
        parts.append(jnp.concatenate((out, value[:size], value[size:]), axis=1))
    send[...] = jnp.where(scalars[0] == 0, parts[1], parts[0])
    mine[...] = jnp.where(scalars[0] == 0, parts[0], parts[1])


def place_kernel(scalars, mine, theirs, value, out):
    size, width = mine.shape
    half, quarter = width // 2, width // 4
    for source, core in ((mine, scalars[0]), (theirs, 1 - scalars[0])):
        out[:, pl.ds(pl.multiple_of(core * half, half), half)] = source[:, :half]
        columns = pl.ds(pl.multiple_of(core * quarter, quarter), quarter)
        value[:size, columns] = source[:, half : half + quarter]
        value[size:, columns] = source[:, half + quarter :]


def summed_views(rows, packed):
    for r in range(rows):
        total = packed[r].astype(jnp.float32)
        for i in range(r + rows, packed.shape[0], rows):
            total = total + packed[i].astype(jnp.float32)
        yield r, total


def last_query_key_kernel(rows, packed, query, key):
    size = packed.shape[2] // 2
    for r, total in summed_views(rows, packed):
        columns = slice(r * size, (r + 1) * size)
        query[:, columns] = total[:, :size]
        key[:, columns] = total[:, size:]


def params(mebibytes):
    return pltpu.CompilerParams(vmem_limit_bytes=mebibytes * MIB)


def shape(dims, kind):
    return jax.ShapeDtypeStruct(dims, kind)


def shards(latents, norm_gain, w_query, w_key, w_value, w_out, kernel, partners, counts, cotangent):
    views, strip_rows, columns, width = latents.shape[1:]
    inner = w_query.shape[1]
    groups, rows = lax.axis_size("view"), lax.axis_size("row")
    scenes = lax.axis_size("scene")
    assert (strip_rows, rows, scenes) == (1, 2, 4)
    strip = strip_rows * columns
    slots = partners.shape[2]
    part = inner // rows
    tokens = views * 2 * strip
    key_tokens = tokens + (groups - 1) * 2 * strip
    bf16, f32, i32 = jnp.bfloat16, jnp.float32, jnp.int32

    row, view, scene = lax.axis_index("row"), lax.axis_index("view"), lax.axis_index("scene")
    scalars = jnp.stack((row, view, scene, scene % 2, scene // 2)).astype(i32)
    swap = [(0, 1), (1, 0)]
    along_x, along_y = [(i, i ^ 1) for i in range(scenes)], [(i, i ^ 2) for i in range(scenes)]

    request, alive = pl.pallas_call(
        functools.partial(request_kernel, views, slots, groups),
        in_specs=[SMEM, SMEM],
        out_specs=(SMEM, SMEM),
        out_shape=(shape((groups,), i32), shape((groups * views,), i32)),
        cost_estimate=MUCH,
        compiler_params=params(4),
        name="requests",
    )(partners, counts)
    between = [[(i, i ^ d) for i in range(groups)] for d in range(1, groups)]
    granted = [lax.ppermute(request, "view", pairs) for pairs in between]

    lat = latents[0].reshape(views, strip, width)
    cot = cotangent[0].reshape(views, strip, width)
    lat_other = lax.ppermute(lat, "row", swap)
    cot_other = lax.ppermute(cot, "row", swap)

    outgoing = pl.pallas_call(
        functools.partial(pick_kernel, groups),
        in_specs=[SMEM] * groups + [VMEM],
        out_specs=[VMEM] * (groups - 1),
        out_shape=[shape((strip, width), bf16)] * (groups - 1),
        compiler_params=params(8),
        cost_estimate=MUCH,
        name="pick",
    )(scalars, *granted, lat)
    got_own = [lax.ppermute(part_out, "view", pairs) for part_out, pairs in zip(outgoing, between)]
    normed, queries, keys, values, out_grad, upstream = pl.pallas_call(
        project_kernel,
        in_specs=[SMEM] + [VMEM] * 10,
        out_specs=[VMEM] * 6,
        out_shape=[
            shape((tokens, width), bf16),
            shape((tokens, part), bf16),
            shape((tokens, part), bf16),
            shape((tokens, part), bf16),
            shape((tokens, part), bf16),
            shape((tokens, width), bf16),
        ],
        compiler_params=params(28),
        cost_estimate=LITTLE,
        name="project",
    )(scalars, lat, lat_other, cot, cot_other, norm_gain, kernel, w_query, w_key, w_value, w_out)

    got_own, normed = lax.optimization_barrier((got_own, normed))
    got_other = [lax.ppermute(got, "row", swap) for got in got_own]

    normed_far, mixed, dquery, dkey, dvalue = pl.pallas_call(
        functools.partial(attention_kernel, views, groups),
        in_specs=[SMEM] * 2 + [VMEM] * (2 * groups - 2 + 7),
        out_specs=[VMEM] * 5,
        out_shape=[
            shape((key_tokens - tokens, width), bf16),
            shape((tokens, part), bf16),
            shape((tokens, part), bf16),
            shape((key_tokens, part), bf16),
            shape((key_tokens, part), bf16),
        ],
        compiler_params=params(28 + groups),
        cost_estimate=LITTLE,
        name="attention",
    )(
        scalars, alive, *got_own, *got_other, queries, keys, values, out_grad, norm_gain, w_key, w_value
    )
    def call(kernel_body, results, operands, name, first=VMEM, mebibytes=16, cost=LITTLE):
        outputs = pl.pallas_call(
            kernel_body,
            in_specs=[first] + [VMEM] * (len(operands) - 1),
            out_specs=[VMEM] * len(results),
            out_shape=results,
            compiler_params=params(mebibytes),
            cost_estimate=cost,
            name=name,
        )(*operands)
        return list(outputs)

    def after(value, *earlier):
        return lax.optimization_barrier((value, *earlier))[0]

    targets = groups * rows
    q_size = width // 4
    q_rows, o_rows = q_size // targets, inner // (4 * targets)
    q_block = (q_size, part)

    def first_exchange(sends):
        return lax.ppermute(sends[0], "scene", along_x), lax.ppermute(sends[1], "scene", along_y)

    def first_sum(parts, got, name, cost=LITTLE):
        blocks = [part_now.shape[1:] for part_now in parts[:2]]
        results = [shape(block, bf16) for block in blocks] + [shape(block, f32) for block in blocks]
        return call(first_sum_kernel, results, (parts[2], got[0], parts[3], got[1]), name, cost=cost)

    def second_exchange(sums):
        return lax.ppermute(sums[0], "scene", along_y), lax.ppermute(sums[1], "scene", along_x)

    def across_views(packed):
        return lax.all_to_all(packed, ("view", "row"), split_axis=0, concat_axis=0, tiled=True)

    mixed_other = lax.ppermute(mixed, "row", swap)

    results = [shape((2, *q_block), bf16)] * 2 + [shape((2, *q_block), f32)] * 2
    qk_parts = call(
        query_key_kernel, results, (scalars, normed, normed_far, dquery, dkey), "grad_query_key", SMEM, 24
    )
    qk_got = first_exchange(qk_parts)
    pairs = groups // 2
    tile = (2 * o_rows, width)
    send, keep = call(
        value_out_kernel,
        [shape((2, 2, pairs, *tile), kind) for kind in (bf16, f32)],
        (scalars, normed, normed_far, after(dvalue, qk_parts[0]), mixed, mixed_other, upstream),
        "grad_value_out",
        SMEM,
        24,
    )
    got = lax.ppermute(send, "view", [(i, i ^ 1) for i in range(groups)])
    qk_parts[2] = after(qk_parts[2], send)
    qk_sums = first_sum(qk_parts, qk_got, "first_sum_query_key")
    qk_got = second_exchange(qk_sums)
    packed = call(
        pack_query_key_kernel,
        [shape((q_size, 2 * part), bf16)],
        (qk_sums[2], qk_got[0], qk_sums[3], qk_got[1]),
        "second_sum_query_key",
    )[0]
    keep = after(keep, packed)
    packed = across_views(packed.reshape(targets, q_rows, 2 * part))
    grad_query, grad_key = call(
        functools.partial(last_query_key_kernel, rows),
        [shape((q_rows, inner), f32)] * 2,
        (packed,),
        "last_sum_query_key",
    )

    part_shape = (2, pairs, 2 * o_rows, width // 2)
    vo_parts = call(
        view_sum_kernel,
        [shape(part_shape, bf16)] * 2 + [shape(part_shape, f32)] * 2,
        (keep, got),
        "view_sum_value_out",
        cost=MUCH,
    )
    vo_got = first_exchange(vo_parts)
    vo_sums = first_sum(vo_parts, vo_got, "first_sum_value_out", MUCH)
    v_got, o_got = second_exchange(vo_sums)
    addends = (vo_sums[3], o_got, vo_sums[2], v_got)
    bit = pairs.bit_length() - 1
    while bit > 0:
        bit -= 1
        send, keep = call(
            functools.partial(tile_halves_kernel, bit, len(addends) == 4),
            [shape((1 << bit, *tile), kind) for kind in (bf16, f32)],
            (scalars, *addends),
            "view_bit_value_out",
            SMEM,
            cost=MUCH,
        )
        got = lax.ppermute(send, "view", [(i, i ^ (2 << bit)) for i in range(groups)])
        addends = (keep, got)
    send, mine = call(
        tile_cores_kernel,
        [shape((o_rows, width), f32)] * 2,
        (scalars, *addends),
        "last_sum_value_out",
        SMEM,
        cost=MUCH,
    )
    theirs = lax.ppermute(send, "row", swap)
    grad_value, grad_out = call(
        place_kernel,
        [shape((q_rows, inner), f32), shape((o_rows, width), f32)],
        (scalars, mine, theirs),
        "place_value_out",
        SMEM,
    )
    return grad_query, grad_key, grad_value, grad_out


def solution(mesh):
    tokens = P("scene", "view", "row", None, None)
    everywhere = P()
    grads = P(("scene", "view", "row"), None)
    return jax.shard_map(
        shards,
        mesh=mesh,
        in_specs=(
            tokens, everywhere, everywhere, everywhere, everywhere, everywhere, everywhere,
            P("scene", "view", None), P("scene", "view"), tokens,
        ),
        out_specs=(grads, grads, grads, grads),
        check_vma=False,
    )
```

```python
import functools

import jax
import jax.numpy as jnp
from jax import lax
from jax.experimental import pallas as pl
from jax.experimental.pallas import tpu as pltpu
from jax.sharding import PartitionSpec as P

HEAD_DIM = 64
EPSILON = 1e-06
MASKED = -1e30
MIB = 1024 * 1024
LITTLE = pl.CostEstimate(flops=1, bytes_accessed=1, transcendentals=0)
MUCH = pl.CostEstimate(flops=40_000_000_000, bytes_accessed=1, transcendentals=0)

VMEM = pl.BlockSpec(memory_space=pltpu.VMEM)
SMEM = pl.BlockSpec(memory_space=pltpu.SMEM)


def dot_nn(a, b):
    return lax.dot_general(a, b, (((1,), (0,)), ((), ())), preferred_element_type=jnp.float32)


def dot_nt(a, b):
    return lax.dot_general(a, b, (((1,), (1,)), ((), ())), preferred_element_type=jnp.float32)


def dot_tn(a, b):
    return lax.dot_general(a, b, (((0,), (0,)), ((), ())), preferred_element_type=jnp.float32)


def normalized(tokens, gain):
    x = tokens.astype(jnp.float32)
    mean = jnp.mean(x * x, -1, keepdims=True)
    return (x * lax.rsqrt(mean + EPSILON) * gain).astype(jnp.bfloat16)


def request_kernel(views, slots, groups, partners, counts, request, alive):
    for g in range(groups):
        request[g] = 0
        for u in range(views):
            alive[g * views + u] = 0
    for u in range(views):
        for j in range(slots):

            @pl.when(j < counts[0, u])
            def _():
                partner = partners[0, u, j]
                group = lax.div(partner, jnp.int32(views))
                request[group] = lax.rem(partner, jnp.int32(views))
                alive[group * views + u] = 1


def pick_kernel(groups, scalars, *refs):
    requests, lat, outgoing = refs[: groups - 1], refs[groups - 1], refs[groups:]
    for request, out in zip(requests, outgoing):
        out[...] = lat[request[scalars[1]]]


def core_half(scalars, size):
    return pl.ds(pl.multiple_of(scalars[0] * size, size), size)


def project_kernel(
    scalars, lat_own, lat_other, cot_own, cot_other, gain, taps, w_query, w_key, w_value, w_out,
    normed, queries, keys, values, out_grad, upstream,
):
    views, strip, width = lat_own.shape
    scale = gain[...].reshape(1, width)
    row = scalars[0]

    def strip_of(u, half):
        index = 2 * u + (row if half == 0 else 1 - row)
        return pl.ds(pl.multiple_of(index * strip, strip), strip)

    for half, source in enumerate((lat_own, lat_other)):
        for u in range(views):
            normed[strip_of(u, half), :] = normalized(source[u], scale)
    first = row == 0
    chunk = 512
    column = lax.broadcasted_iota(jnp.int32, (strip, 1), 0)
    not_first = (column > 0).astype(jnp.float32)
    not_last = (column < strip - 1).astype(jnp.float32)
    for c in range(0, width, chunk):
        lanes = slice(c, c + chunk)
        tap = taps[:, lanes].astype(jnp.float32)
        top, middle, bottom = tap[0:3], tap[3:6], tap[6:9]
        cross = (jnp.where(first, top, bottom), jnp.where(first, bottom, top))
        for u in range(views):
            strips = [ref[u, :, lanes].astype(jnp.float32) for ref in (cot_own, cot_other)]
            shifted = []
            for x in strips:
                after = pltpu.roll(x, strip - 1, 0) * not_last
                before = pltpu.roll(x, 1, 0) * not_first
                shifted.append((after, x, before))
            for half in range(2):
                total = strips[half]
                for b in range(3):
                    total = total + middle[b : b + 1] * shifted[half][b]
                    total = total + cross[half][b : b + 1] * shifted[1 - half][b]
                upstream[strip_of(u, half), lanes] = total.astype(jnp.bfloat16)
    rows = normed[...]
    half = core_half(scalars, queries.shape[1])
    for weight, result in ((w_query, queries), (w_key, keys), (w_value, values)):
        result[...] = dot_nn(rows, weight[:, half]).astype(jnp.bfloat16)
    out_grad[...] = dot_nt(upstream[...], w_out[half, :]).astype(jnp.bfloat16)


def attention_kernel(views, groups, scalars, alive, *refs):
    got_own, got_other, refs = refs[: groups - 1], refs[groups - 1 : 2 * groups - 2], refs[2 * groups - 2 :]
    queries, keys, values, out_grad, gain, w_key, w_value, *refs = refs
    normed_far, mixed, dquery, dkey, dvalue = refs
    strip = got_own[0].shape[0]
    tokens = queries.shape[0]
    view_tokens = tokens // views
    scale = HEAD_DIM ** (-0.5)
    here = scalars[1]
    scale_row = gain[...].reshape(1, normed_far.shape[1])
    pair = 2 * HEAD_DIM
    span = 2 * view_tokens
    column_view = lax.broadcasted_iota(jnp.int32, (1, views * span), 1) // span
    slot_alive = []
    for j in range(groups - 1):
        group = lax.bitwise_xor(here, jnp.int32(j + 1))
        start = 2 * j * strip
        normed_far[start : start + strip, :] = normalized(got_own[j][...], scale_row)
        normed_far[start + strip : start + 2 * strip, :] = normalized(got_other[j][...], scale_row)
        taken = jnp.zeros((1, views * span), jnp.int32)
        for u in range(views):
            taken = jnp.where(column_view == u, alive[group * views + u], taken)
        slot_alive.append(taken > 0)
    low = lax.broadcasted_iota(jnp.int32, (1, 1, pair), 2) < HEAD_DIM
    low_b = low.astype(jnp.bfloat16)
    high_b = 1 - low_b

    def stacked(x):
        x = x.reshape(views, view_tokens, pair)
        return jnp.concatenate((x * low_b, x * high_b), axis=1).reshape(views * span, pair)

    def unstacked(x):
        x = x.reshape(views, 2, view_tokens, pair)
        return jnp.where(low, x[:, 0], x[:, 1]).reshape(tokens, pair)

    def own_nt(a, b):
        return jnp.concatenate(
            [
                dot_nt(a[u * view_tokens : (u + 1) * view_tokens], b[u * span : (u + 1) * span])
                for u in range(views)
            ],
            axis=1,
        )

    def own_tn(a, b):
        return jnp.concatenate(
            [
                dot_tn(a[:, u * span : (u + 1) * span], b[u * view_tokens : (u + 1) * view_tokens])
                for u in range(views)
            ],
            axis=0,
        )

    def own_nn(a, b):
        return jnp.concatenate(
            [
                dot_nn(a[:, u * span : (u + 1) * span], b[u * span : (u + 1) * span])
                for u in range(views)
            ],
            axis=0,
        )

    own = []
    for p in range(queries.shape[1] // pair):
        lanes = slice(p * pair, (p + 1) * pair)
        q, g = stacked(queries[:, lanes]), stacked(out_grad[:, lanes])
        k_own, v_own = keys[:, lanes], values[:, lanes]
        own.append((q, g, k_own, v_own, own_nt(k_own, q) * scale, own_nt(v_own, g)))
    fetched = normed_far[...]
    half = core_half(scalars, queries.shape[1])
    fetched_keys = dot_nn(fetched, w_key[:, half]).astype(jnp.bfloat16)
    fetched_values = dot_nn(fetched, w_value[:, half]).astype(jnp.bfloat16)
    for p, (q, g, k_own, v_own, s_own, dp_own) in enumerate(own):
        lanes = slice(p * pair, (p + 1) * pair)
        k_far, v_far = fetched_keys[:, lanes], fetched_values[:, lanes]
        s_far = dot_nt(k_far, q) * scale
        s_far = jnp.concatenate(
            [
                jnp.where(slot_alive[j], s_far[j * view_tokens : (j + 1) * view_tokens], MASKED)
                for j in range(groups - 1)
            ],
            axis=0,
        )
        highest = jnp.maximum(
            jnp.max(s_own, 0, keepdims=True), jnp.max(s_far, 0, keepdims=True)
        )
        e_own = jnp.exp(s_own - highest)
        e_far = jnp.exp(s_far - highest)
        inverse = 1.0 / (jnp.sum(e_own, 0, keepdims=True) + jnp.sum(e_far, 0, keepdims=True))
        a_own = e_own * inverse
        a_far = e_far * inverse
        ab_own = a_own.astype(jnp.bfloat16)
        ab_far = a_far.astype(jnp.bfloat16)
        mix = unstacked(own_tn(ab_own, v_own) + dot_tn(ab_far, v_far))
        mixed[:, lanes] = mix.astype(jnp.bfloat16)
        dvalue[:tokens, lanes] = own_nn(ab_own, g).astype(jnp.bfloat16)
        dvalue[tokens:, lanes] = dot_nn(ab_far, g).astype(jnp.bfloat16)
        dp_far = dot_nt(v_far, g)
        delta = jnp.sum(a_own * dp_own, 0, keepdims=True) + jnp.sum(a_far * dp_far, 0, keepdims=True)
        ds_own = (a_own * (dp_own - delta) * scale).astype(jnp.bfloat16)
        ds_far = (a_far * (dp_far - delta) * scale).astype(jnp.bfloat16)
        dq = unstacked(own_tn(ds_own, k_own) + dot_tn(ds_far, k_far))
        dquery[:, lanes] = dq.astype(jnp.bfloat16)
        dkey[:tokens, lanes] = own_nn(ds_own, q).astype(jnp.bfloat16)
        dkey[tokens:, lanes] = dot_nn(ds_far, q).astype(jnp.bfloat16)


def by_quarters(scalars, lefts, right, send, keep, x_first):
    size = send.shape[1]
    x, y = scalars[3], scalars[4]
    for target, first in ((send, 1), (keep, 0)):
        for second in (1, 0):
            dx, dy = (first, second) if x_first else (second, first)
            block = 2 * lax.bitwise_xor(y, jnp.int32(dy)) + lax.bitwise_xor(x, jnp.int32(dx))
            columns = pl.ds(pl.multiple_of(block * size, size), size)
            total, start = 0.0, 0
            for left in lefts:
                total = total + dot_tn(left[:, columns], right[start : start + left.shape[0], :])
                start += left.shape[0]
            target[second] = total.astype(target.dtype)


def query_key_kernel(scalars, normed, normed_far, dquery, dkey, q_send, k_send, q_keep, k_keep):
    by_quarters(scalars, (normed,), dquery, q_send, q_keep, True)
    by_quarters(scalars, (normed, normed_far), dkey, k_send, k_keep, False)


def value_out_kernel(scalars, normed, normed_far, dvalue, mine, theirs, upstream, send, keep):
    row, x, y = scalars[0], scalars[3], scalars[4]
    odd = lax.rem(scalars[1], jnp.int32(2)) == 1
    _, _, pairs, size, width = send.shape
    half, quarter = width // 2, width // 4
    right = upstream[:, core_half(scalars, half)]
    from_mine, from_theirs = dot_tn(mine[...], right), dot_tn(theirs[...], right)
    for dy in range(2):
        grad_o = jnp.where(row == lax.bitwise_xor(y, jnp.int32(dy)), from_mine, from_theirs)
        low, high = grad_o[: 2 * pairs * size], grad_o[2 * pairs * size :]
        for dx in range(2):
            to_x = lax.bitwise_xor(x, jnp.int32(dx))
            o_part = jnp.where(to_x == 0, low, high)
            block = 2 * lax.bitwise_xor(y, jnp.int32(dy)) + to_x
            columns = pl.ds(pl.multiple_of(block * quarter, quarter), quarter)
            tokens = normed.shape[0]
            v_part = dot_tn(normed[:, columns], dvalue[:tokens, :])
            v_part = v_part + dot_tn(normed_far[:, columns], dvalue[tokens:, :])
            for pair in range(pairs):
                tiles = []
                for view in (2 * pair, 2 * pair + 1):
                    v_view = v_part[2 * view * size : 2 * (view + 1) * size]
                    tiles.append((o_part[view * size : (view + 1) * size], v_view[:size], v_view[size:]))
                for target, take_odd in ((send, jnp.logical_not(odd)), (keep, odd)):
                    tile = [jnp.where(take_odd, second, first) for first, second in zip(*tiles)]
                    target[dy, dx, pair] = jnp.concatenate(tile, axis=1).astype(target.dtype)


def view_sum_kernel(keep, got, x_send, y_send, x_keep, y_keep):
    half = keep.shape[4] // 2
    for second in range(2):
        for target, first in ((x_send, 1), (x_keep, 0)):
            total = keep[second, first, :, :, half:] + got[second, first, :, :, half:].astype(jnp.float32)
            target[second] = total.astype(target.dtype)
        for target, first in ((y_send, 1), (y_keep, 0)):
            total = keep[first, second, :, :, :half] + got[first, second, :, :, :half].astype(jnp.float32)
            target[second] = total.astype(target.dtype)


def first_sum_kernel(x_keep, x_got, y_keep, y_got, x_later, y_later, x_now, y_now):
    for keep, got, later, now in ((x_keep, x_got, x_later, x_now), (y_keep, y_got, y_later, y_now)):
        later[...] = (keep[1] + got[1].astype(jnp.float32)).astype(jnp.bfloat16)
        now[...] = keep[0] + got[0].astype(jnp.float32)


def pack_query_key_kernel(q_now, q_got, k_now, k_got, packed):
    size = q_now.shape[1]
    packed[:, :size] = (q_now[...] + q_got[...].astype(jnp.float32)).astype(jnp.bfloat16)
    packed[:, size:] = (k_now[...] + k_got[...].astype(jnp.float32)).astype(jnp.bfloat16)


def summed_tile(addends, place):
    place = pl.ds(place, 1)
    total = [now[place] + got[place].astype(jnp.float32) for now, got in zip(addends[::2], addends[1::2])]
    return (jnp.concatenate(total, axis=2) if len(total) == 2 else total[0])[0]


def view_bit(scalars, bit):
    return lax.rem(lax.div(scalars[1], jnp.int32(2 << bit)), jnp.int32(2))


def tile_halves_kernel(bit, scalars, *refs):
    addends, (send, keep) = refs[:-2], refs[-2:]
    count = keep.shape[0]
    mine = view_bit(scalars, bit)
    for target, part in ((send, 1 - mine), (keep, mine)):
        for i in range(count):
            target[i] = summed_tile(addends, part * count + i).astype(target.dtype)


def tile_cores_kernel(scalars, *refs):
    addends, (far_same, far_cross, near_cross, mine) = refs[:-4], refs[-4:]
    size, width = mine.shape
    half, quarter = width // 2, width // 4
    bit = view_bit(scalars, 0)
    for place, same, cross in ((1 - bit, far_same, far_cross), (bit, mine, near_cross)):
        total = summed_tile(addends, place)
        parts = []
        for core in range(2):
            value = total[:, half + core * quarter : half + (core + 1) * quarter]
            out = total[core * size : (core + 1) * size, :half]
            parts.append(jnp.concatenate((out, value[:size], value[size:]), axis=1))
        same[...] = jnp.where(scalars[0] == 0, parts[0], parts[1]).astype(same.dtype)
        cross[...] = jnp.where(scalars[0] == 0, parts[1], parts[0]).astype(cross.dtype)


def place_kernel(scalars, mine, far_same, near_cross, far_cross, value, out):
    size, width = mine.shape
    half, quarter = width // 2, width // 4
    for near, far, core in ((mine, far_same, scalars[0]), (near_cross, far_cross, 1 - scalars[0])):
        total = near[...] + far[...].astype(jnp.float32)
        out[:, pl.ds(pl.multiple_of(core * half, half), half)] = total[:, :half]
        columns = pl.ds(pl.multiple_of(core * quarter, quarter), quarter)
        value[:size, columns] = total[:, half : half + quarter]
        value[size:, columns] = total[:, half + quarter :]


def summed_views(rows, packed):
    for r in range(rows):
        total = packed[r].astype(jnp.float32)
        for i in range(r + rows, packed.shape[0], rows):
            total = total + packed[i].astype(jnp.float32)
        yield r, total


def last_query_key_kernel(rows, packed, query, key):
    size = packed.shape[2] // 2
    for r, total in summed_views(rows, packed):
        columns = slice(r * size, (r + 1) * size)
        query[:, columns] = total[:, :size]
        key[:, columns] = total[:, size:]


def params(mebibytes):
    return pltpu.CompilerParams(vmem_limit_bytes=mebibytes * MIB)


def shape(dims, kind):
    return jax.ShapeDtypeStruct(dims, kind)


def shards(latents, norm_gain, w_query, w_key, w_value, w_out, kernel, partners, counts, cotangent):
    views, strip_rows, columns, width = latents.shape[1:]
    inner = w_query.shape[1]
    groups, rows = lax.axis_size("view"), lax.axis_size("row")
    scenes = lax.axis_size("scene")
    assert (strip_rows, rows, scenes) == (1, 2, 4)
    strip = strip_rows * columns
    slots = partners.shape[2]
    part = inner // rows
    tokens = views * 2 * strip
    key_tokens = tokens + (groups - 1) * 2 * strip
    bf16, f32, i32 = jnp.bfloat16, jnp.float32, jnp.int32

    row, view, scene = lax.axis_index("row"), lax.axis_index("view"), lax.axis_index("scene")
    scalars = jnp.stack((row, view, scene, scene % 2, scene // 2)).astype(i32)
    swap = [(0, 1), (1, 0)]
    along_x, along_y = [(i, i ^ 1) for i in range(scenes)], [(i, i ^ 2) for i in range(scenes)]

    request, alive = pl.pallas_call(
        functools.partial(request_kernel, views, slots, groups),
        in_specs=[SMEM, SMEM],
        out_specs=(SMEM, SMEM),
        out_shape=(shape((groups,), i32), shape((groups * views,), i32)),
        cost_estimate=MUCH,
        compiler_params=params(4),
        name="requests",
    )(partners, counts)
    between = [[(i, i ^ d) for i in range(groups)] for d in range(1, groups)]
    granted = [lax.ppermute(request, "view", pairs) for pairs in between]

    lat = latents[0].reshape(views, strip, width)
    cot = cotangent[0].reshape(views, strip, width)
    lat_other = lax.ppermute(lat, "row", swap)
    cot_other = lax.ppermute(cot, "row", swap)

    outgoing = pl.pallas_call(
        functools.partial(pick_kernel, groups),
        in_specs=[SMEM] * groups + [VMEM],
        out_specs=[VMEM] * (groups - 1),
        out_shape=[shape((strip, width), bf16)] * (groups - 1),
        compiler_params=params(8),
        cost_estimate=MUCH,
        name="pick",
    )(scalars, *granted, lat)
    got_own = [lax.ppermute(part_out, "view", pairs) for part_out, pairs in zip(outgoing, between)]
    normed, queries, keys, values, out_grad, upstream = pl.pallas_call(
        project_kernel,
        in_specs=[SMEM] + [VMEM] * 10,
        out_specs=[VMEM] * 6,
        out_shape=[
            shape((tokens, width), bf16),
            shape((tokens, part), bf16),
            shape((tokens, part), bf16),
            shape((tokens, part), bf16),
            shape((tokens, part), bf16),
            shape((tokens, width), bf16),
        ],
        compiler_params=params(28),
        cost_estimate=LITTLE,
        name="project",
    )(scalars, lat, lat_other, cot, cot_other, norm_gain, kernel, w_query, w_key, w_value, w_out)

    got_own, normed = lax.optimization_barrier((got_own, normed))
    got_other = [lax.ppermute(got, "row", swap) for got in got_own]

    normed_far, mixed, dquery, dkey, dvalue = pl.pallas_call(
        functools.partial(attention_kernel, views, groups),
        in_specs=[SMEM] * 2 + [VMEM] * (2 * groups - 2 + 7),
        out_specs=[VMEM] * 5,
        out_shape=[
            shape((key_tokens - tokens, width), bf16),
            shape((tokens, part), bf16),
            shape((tokens, part), bf16),
            shape((key_tokens, part), bf16),
            shape((key_tokens, part), bf16),
        ],
        compiler_params=params(28 + groups),
        cost_estimate=LITTLE,
        name="attention",
    )(
        scalars, alive, *got_own, *got_other, queries, keys, values, out_grad, norm_gain, w_key, w_value
    )
    def call(kernel_body, results, operands, name, first=VMEM, mebibytes=16, cost=LITTLE):
        outputs = pl.pallas_call(
            kernel_body,
            in_specs=[first] + [VMEM] * (len(operands) - 1),
            out_specs=[VMEM] * len(results),
            out_shape=results,
            compiler_params=params(mebibytes),
            cost_estimate=cost,
            name=name,
        )(*operands)
        return list(outputs)

    def after(value, *earlier):
        return lax.optimization_barrier((value, *earlier))[0]

    targets = groups * rows
    q_size = width // 4
    q_rows, o_rows = q_size // targets, inner // (4 * targets)
    q_block = (q_size, part)

    def first_exchange(sends):
        return lax.ppermute(sends[0], "scene", along_x), lax.ppermute(sends[1], "scene", along_y)

    def first_sum(parts, got, name, cost=LITTLE):
        blocks = [part_now.shape[1:] for part_now in parts[:2]]
        results = [shape(block, bf16) for block in blocks] + [shape(block, f32) for block in blocks]
        return call(first_sum_kernel, results, (parts[2], got[0], parts[3], got[1]), name, cost=cost)

    def second_exchange(sums):
        return lax.ppermute(sums[0], "scene", along_y), lax.ppermute(sums[1], "scene", along_x)

    def across_views(packed):
        return lax.all_to_all(packed, ("view", "row"), split_axis=0, concat_axis=0, tiled=True)

    mixed_other = lax.ppermute(mixed, "row", swap)

    results = [shape((2, *q_block), bf16)] * 2 + [shape((2, *q_block), f32)] * 2
    qk_parts = call(
        query_key_kernel, results, (scalars, normed, normed_far, dquery, dkey), "grad_query_key", SMEM, 24
    )
    qk_got = first_exchange(qk_parts)
    pairs = groups // 2
    tile = (2 * o_rows, width)
    send, keep = call(
        value_out_kernel,
        [shape((2, 2, pairs, *tile), kind) for kind in (bf16, f32)],
        (scalars, normed, normed_far, after(dvalue, qk_parts[0]), mixed, mixed_other, upstream),
        "grad_value_out",
        SMEM,
        24,
    )
    got = lax.ppermute(send, "view", [(i, i ^ 1) for i in range(groups)])
    qk_parts[2] = after(qk_parts[2], send)
    qk_sums = first_sum(qk_parts, qk_got, "first_sum_query_key")
    qk_got = second_exchange(qk_sums)
    packed = call(
        pack_query_key_kernel,
        [shape((q_size, 2 * part), bf16)],
        (qk_sums[2], qk_got[0], qk_sums[3], qk_got[1]),
        "second_sum_query_key",
    )[0]
    keep = after(keep, packed)
    packed = across_views(packed.reshape(targets, q_rows, 2 * part))
    grad_query, grad_key = call(
        functools.partial(last_query_key_kernel, rows),
        [shape((q_rows, inner), f32)] * 2,
        (packed,),
        "last_sum_query_key",
    )

    part_shape = (2, pairs, 2 * o_rows, width // 2)
    vo_parts = call(
        view_sum_kernel,
        [shape(part_shape, bf16)] * 2 + [shape(part_shape, f32)] * 2,
        (keep, got),
        "view_sum_value_out",
        cost=MUCH,
    )
    vo_got = first_exchange(vo_parts)
    vo_sums = first_sum(vo_parts, vo_got, "first_sum_value_out")
    v_got, o_got = second_exchange(vo_sums)
    addends = (vo_sums[3], o_got, vo_sums[2], v_got)
    for bit in reversed(range(1, pairs.bit_length() - 1)):
        send, keep = call(
            functools.partial(tile_halves_kernel, bit),
            [shape((1 << bit, *tile), kind) for kind in (bf16, f32)],
            (scalars, *addends),
            "view_bit_value_out",
            SMEM,
        )
        addends = (keep, lax.ppermute(send, "view", [(i, i ^ (2 << bit)) for i in range(groups)]))
    far_same, far_cross, near_cross, mine = call(
        tile_cores_kernel,
        [shape((o_rows, width), kind) for kind in (bf16, bf16, f32, f32)],
        (scalars, *addends),
        "last_parts_value_out",
        SMEM,
    )
    far_same = lax.ppermute(far_same, "view", [(i, i ^ 2) for i in range(groups)])
    far_cross = lax.ppermute(far_cross, ("view", "row"), [(i, i ^ 5) for i in range(targets)])
    near_cross = lax.ppermute(near_cross, "row", swap)
    grad_value, grad_out = call(
        place_kernel,
        [shape((q_rows, inner), f32), shape((o_rows, width), f32)],
        (scalars, after(mine, grad_key), far_same, near_cross, far_cross),
        "last_sum_value_out",
        SMEM,
    )
    return grad_query, grad_key, grad_value, grad_out


def solution(mesh):
    tokens = P("scene", "view", "row", None, None)
    everywhere = P()
    grads = P(("scene", "view", "row"), None)
    return jax.shard_map(
        shards,
        mesh=mesh,
        in_specs=(
            tokens, everywhere, everywhere, everywhere, everywhere, everywhere, everywhere,
            P("scene", "view", None), P("scene", "view"), tokens,
        ),
        out_specs=(grads, grads, grads, grads),
        check_vma=False,
    )
```

```python
import functools

import jax
import jax.numpy as jnp
from jax import lax
from jax.experimental import pallas as pl
from jax.experimental.pallas import tpu as pltpu
from jax.sharding import PartitionSpec as P

HEAD_DIM = 64
EPSILON = 1e-06
SCALE = HEAD_DIM ** (-0.5)
MASKED = -1e30
MIB = 1024 * 1024
LITTLE = pl.CostEstimate(flops=1, bytes_accessed=1, transcendentals=0)
MUCH = pl.CostEstimate(flops=40_000_000_000, bytes_accessed=1, transcendentals=0)

VMEM = pl.BlockSpec(memory_space=pltpu.VMEM)
SMEM = pl.BlockSpec(memory_space=pltpu.SMEM)


def dot_nn(a, b):
    return lax.dot_general(a, b, (((1,), (0,)), ((), ())), preferred_element_type=jnp.float32)


def dot_nt(a, b):
    return lax.dot_general(a, b, (((1,), (1,)), ((), ())), preferred_element_type=jnp.float32)


def dot_tn(a, b):
    return lax.dot_general(a, b, (((0,), (0,)), ((), ())), preferred_element_type=jnp.float32)


def normalized(tokens, gain):
    x = tokens.astype(jnp.float32)
    mean = jnp.mean(x * x, -1, keepdims=True)
    return (x * lax.rsqrt(mean + EPSILON) * gain).astype(jnp.bfloat16)


def request_kernel(views, slots, groups, partners, request, alive):
    for g in range(groups):
        request[g] = 0
        for u in range(views):
            alive[g * views + u] = 0
    for u in range(views):
        for j in range(slots):
            partner = partners[0, u, j]

            @pl.when(partner >= 0)
            def _():
                group = lax.div(partner, jnp.int32(views))
                request[group] = lax.rem(partner, jnp.int32(views))
                alive[group * views + u] = 1


def pick_kernel(groups, scalars, *refs):
    requests, lat, outgoing = refs[: groups - 1], refs[groups - 1], refs[groups:]
    for request, out in zip(requests, outgoing):
        out[...] = lat[request[scalars[1]]]


def core_half(scalars, size):
    return pl.ds(pl.multiple_of(scalars[0] * size, size), size)


def project_kernel(
    scalars, lat_own, lat_other, cot_own, cot_other, gain, taps, w_query, w_key, w_value, w_out,
    normed, queries, keys, values, out_grad, upstream,
):
    views, strip, width = lat_own.shape
    scale = gain[...].reshape(1, width)
    row = scalars[0]

    def strip_of(u, half):
        index = 2 * u + (row if half == 0 else 1 - row)
        return pl.ds(pl.multiple_of(index * strip, strip), strip)

    for half, source in enumerate((lat_own, lat_other)):
        for u in range(views):
            normed[strip_of(u, half), :] = normalized(source[u], scale)
    first = row == 0
    chunk = 512
    column = lax.broadcasted_iota(jnp.int32, (strip, 1), 0)
    not_first = (column > 0).astype(jnp.float32)
    not_last = (column < strip - 1).astype(jnp.float32)
    for c in range(0, width, chunk):
        lanes = slice(c, c + chunk)
        tap = taps[:, lanes].astype(jnp.float32)
        top, middle, bottom = tap[0:3], tap[3:6], tap[6:9]
        cross = (jnp.where(first, top, bottom), jnp.where(first, bottom, top))
        for u in range(views):
            strips = [ref[u, :, lanes].astype(jnp.float32) for ref in (cot_own, cot_other)]
            shifted = []
            for x in strips:
                after = pltpu.roll(x, strip - 1, 0) * not_last
                before = pltpu.roll(x, 1, 0) * not_first
                shifted.append((after, x, before))
            for half in range(2):
                total = strips[half]
                for b in range(3):
                    total = total + middle[b : b + 1] * shifted[half][b]
                    total = total + cross[half][b : b + 1] * shifted[1 - half][b]
                upstream[strip_of(u, half), lanes] = total.astype(jnp.bfloat16)
    rows = normed[...]
    half = core_half(scalars, queries.shape[1])
    for weight, result in ((w_query, queries), (w_key, keys), (w_value, values)):
        result[...] = dot_nn(rows, weight[:, half]).astype(jnp.bfloat16)
    out_grad[...] = dot_nt(upstream[...], w_out[half, :]).astype(jnp.bfloat16)


def stacked(x, views):
    tokens, pair = x.shape
    low = (lax.broadcasted_iota(jnp.int32, (1, 1, pair), 2) < pair // 2).astype(x.dtype)
    x = x.reshape(views, tokens // views, pair)
    return jnp.concatenate((x * low, x * (1 - low)), axis=1).reshape(2 * tokens, pair)


def unstacked(x, views):
    rows, pair = x.shape
    low = lax.broadcasted_iota(jnp.int32, (1, 1, pair), 2) < pair // 2
    x = x.reshape(views, 2, rows // (2 * views), pair)
    return jnp.where(low, x[:, 0], x[:, 1]).reshape(rows // 2, pair)


def view_parts(x, views, axis):
    size = x.shape[axis] // views
    return [lax.slice_in_dim(x, u * size, (u + 1) * size, axis=axis) for u in range(views)]


def own_nt(a, b, views):
    pairs = zip(view_parts(a, views, 0), view_parts(b, views, 0))
    return jnp.concatenate([dot_nt(x, y) for x, y in pairs], axis=1)


def own_tn(a, b, views):
    pairs = zip(view_parts(a, views, 1), view_parts(b, views, 0))
    return jnp.concatenate([dot_tn(x, y) for x, y in pairs], axis=0)


def own_nn(a, b, views):
    pairs = zip(view_parts(a, views, 1), view_parts(b, views, 0))
    return jnp.concatenate([dot_nn(x, y) for x, y in pairs], axis=0)


def forward_kernel(views, groups, scalars, alive, *refs):
    got_own, got_other, refs = refs[: groups - 1], refs[groups - 1 : 2 * groups - 2], refs[2 * groups - 2 :]
    queries, keys, values, out_grad, gain, w_key, w_value, *refs = refs
    normed_far, keys_far, values_far, attention_own, attention_far, mixed, dvalue = refs
    strip = got_own[0].shape[0]
    tokens, part = queries.shape
    view_tokens = tokens // views
    here = scalars[1]
    scale_row = gain[...].reshape(1, normed_far.shape[1])
    pair = 2 * HEAD_DIM
    span = 2 * view_tokens
    column_view = lax.broadcasted_iota(jnp.int32, (1, views * span), 1) // span
    slot_alive = []
    for j in range(groups - 1):
        group = lax.bitwise_xor(here, jnp.int32(j + 1))
        start = 2 * j * strip
        normed_far[start : start + strip, :] = normalized(got_own[j][...], scale_row)
        normed_far[start + strip : start + 2 * strip, :] = normalized(got_other[j][...], scale_row)
        taken = jnp.zeros((1, views * span), jnp.int32)
        for u in range(views):
            taken = jnp.where(column_view == u, alive[group * views + u], taken)
        slot_alive.append(taken > 0)
    fetched = normed_far[...]
    half = core_half(scalars, part)
    keys_far[...] = dot_nn(fetched, w_key[:, half]).astype(jnp.bfloat16)
    values_far[...] = dot_nn(fetched, w_value[:, half]).astype(jnp.bfloat16)
    for p in range(part // pair):
        lanes = slice(p * pair, (p + 1) * pair)
        q, g = stacked(queries[:, lanes], views), stacked(out_grad[:, lanes], views)
        s_own = own_nt(keys[:, lanes], q, views) * SCALE
        s_far = dot_nt(keys_far[:, lanes], q) * SCALE
        s_far = jnp.concatenate(
            [
                jnp.where(slot_alive[j], s_far[j * view_tokens : (j + 1) * view_tokens], MASKED)
                for j in range(groups - 1)
            ],
            axis=0,
        )
        highest = jnp.maximum(jnp.max(s_own, 0, keepdims=True), jnp.max(s_far, 0, keepdims=True))
        e_own = jnp.exp(s_own - highest)
        e_far = jnp.exp(s_far - highest)
        inverse = 1.0 / (jnp.sum(e_own, 0, keepdims=True) + jnp.sum(e_far, 0, keepdims=True))
        a_own, a_far = e_own * inverse, e_far * inverse
        attention_own[p], attention_far[p] = a_own, a_far
        a_own, a_far = a_own.astype(jnp.bfloat16), a_far.astype(jnp.bfloat16)
        mix = own_tn(a_own, values[:, lanes], views) + dot_tn(a_far, values_far[:, lanes])
        mixed[:, lanes] = unstacked(mix, views).astype(jnp.bfloat16)
        dvalue[:tokens, lanes] = own_nn(a_own, g, views).astype(jnp.bfloat16)
        dvalue[tokens:, lanes] = dot_nn(a_far, g).astype(jnp.bfloat16)


def backward_kernel(
    views, queries, keys, values, out_grad, keys_far, values_far, attention_own, attention_far, dquery, dkey
):
    tokens, part = queries.shape
    pair = 2 * HEAD_DIM
    for p in range(part // pair):
        lanes = slice(p * pair, (p + 1) * pair)
        q, g = stacked(queries[:, lanes], views), stacked(out_grad[:, lanes], views)
        a_own, a_far = attention_own[p], attention_far[p]
        dp_own = own_nt(values[:, lanes], g, views)
        dp_far = dot_nt(values_far[:, lanes], g)
        delta = jnp.sum(a_own * dp_own, 0, keepdims=True) + jnp.sum(a_far * dp_far, 0, keepdims=True)
        ds_own = (a_own * (dp_own - delta) * SCALE).astype(jnp.bfloat16)
        ds_far = (a_far * (dp_far - delta) * SCALE).astype(jnp.bfloat16)
        dq = own_tn(ds_own, keys[:, lanes], views) + dot_tn(ds_far, keys_far[:, lanes])
        dquery[:, lanes] = unstacked(dq, views).astype(jnp.bfloat16)
        dkey[:tokens, lanes] = own_nn(ds_own, q, views).astype(jnp.bfloat16)
        dkey[tokens:, lanes] = dot_nn(ds_far, q).astype(jnp.bfloat16)


def by_quarters(scalars, lefts, right, send, keep, x_first):
    size = send.shape[1]
    x, y = scalars[3], scalars[4]
    for target, first in ((send, 1), (keep, 0)):
        for second in (1, 0):
            dx, dy = (first, second) if x_first else (second, first)
            block = 2 * lax.bitwise_xor(y, jnp.int32(dy)) + lax.bitwise_xor(x, jnp.int32(dx))
            columns = pl.ds(pl.multiple_of(block * size, size), size)
            total, start = 0.0, 0
            for left in lefts:
                total = total + dot_tn(left[:, columns], right[start : start + left.shape[0], :])
                start += left.shape[0]
            target[second] = total.astype(target.dtype)


def query_key_kernel(scalars, normed, normed_far, dquery, dkey, q_send, k_send, q_keep, k_keep):
    by_quarters(scalars, (normed,), dquery, q_send, q_keep, True)
    by_quarters(scalars, (normed, normed_far), dkey, k_send, k_keep, False)


def value_out_kernel(scalars, normed, normed_far, dvalue, mine, theirs, upstream, send, keep):
    row, x, y = scalars[0], scalars[3], scalars[4]
    odd = lax.rem(scalars[1], jnp.int32(2)) == 1
    _, _, pairs, size, width = send.shape
    half, quarter = width // 2, width // 4
    right = upstream[:, core_half(scalars, half)]
    from_mine, from_theirs = dot_tn(mine[...], right), dot_tn(theirs[...], right)
    for dy in range(2):
        grad_o = jnp.where(row == lax.bitwise_xor(y, jnp.int32(dy)), from_mine, from_theirs)
        low, high = grad_o[: 2 * pairs * size], grad_o[2 * pairs * size :]
        for dx in range(2):
            to_x = lax.bitwise_xor(x, jnp.int32(dx))
            o_part = jnp.where(to_x == 0, low, high)
            block = 2 * lax.bitwise_xor(y, jnp.int32(dy)) + to_x
            columns = pl.ds(pl.multiple_of(block * quarter, quarter), quarter)
            tokens = normed.shape[0]
            v_part = dot_tn(normed[:, columns], dvalue[:tokens, :])
            v_part = v_part + dot_tn(normed_far[:, columns], dvalue[tokens:, :])
            for pair in range(pairs):
                tiles = []
                for view in (2 * pair, 2 * pair + 1):
                    v_view = v_part[2 * view * size : 2 * (view + 1) * size]
                    tiles.append((o_part[view * size : (view + 1) * size], v_view[:size], v_view[size:]))
                for target, take_odd in ((send, jnp.logical_not(odd)), (keep, odd)):
                    tile = [jnp.where(take_odd, second, first) for first, second in zip(*tiles)]
                    target[dy, dx, pair] = jnp.concatenate(tile, axis=1).astype(target.dtype)


def view_sum_kernel(keep, got, x_send, y_send, x_keep, y_keep):
    half = keep.shape[4] // 2
    for second in range(2):
        for target, first in ((x_send, 1), (x_keep, 0)):
            total = keep[second, first, :, :, half:] + got[second, first, :, :, half:].astype(jnp.float32)
            target[second] = total.astype(target.dtype)
        for target, first in ((y_send, 1), (y_keep, 0)):
            total = keep[first, second, :, :, :half] + got[first, second, :, :, :half].astype(jnp.float32)
            target[second] = total.astype(target.dtype)


def first_sum_kernel(x_keep, x_got, y_keep, y_got, x_later, y_later, x_now, y_now):
    for keep, got, later, now in ((x_keep, x_got, x_later, x_now), (y_keep, y_got, y_later, y_now)):
        later[...] = (keep[1] + got[1].astype(jnp.float32)).astype(jnp.bfloat16)
        now[...] = keep[0] + got[0].astype(jnp.float32)


def pack_query_key_kernel(q_now, q_got, k_now, k_got, packed):
    size = q_now.shape[1]
    packed[:, :size] = (q_now[...] + q_got[...].astype(jnp.float32)).astype(jnp.bfloat16)
    packed[:, size:] = (k_now[...] + k_got[...].astype(jnp.float32)).astype(jnp.bfloat16)


def summed_tile(addends, place):
    place = pl.ds(place, 1)
    total = [now[place] + got[place].astype(jnp.float32) for now, got in zip(addends[::2], addends[1::2])]
    return (jnp.concatenate(total, axis=2) if len(total) == 2 else total[0])[0]


def view_bit(scalars, bit):
    return lax.rem(lax.div(scalars[1], jnp.int32(2 << bit)), jnp.int32(2))


def tile_halves_kernel(bit, scalars, *refs):
    addends, (send, keep) = refs[:-2], refs[-2:]
    count = keep.shape[0]
    mine = view_bit(scalars, bit)
    for target, part in ((send, 1 - mine), (keep, mine)):
        for i in range(count):
            target[i] = summed_tile(addends, part * count + i).astype(target.dtype)


def tile_cores_kernel(scalars, *refs):
    addends, (far_same, far_cross, near_cross, mine) = refs[:-4], refs[-4:]
    size, width = mine.shape
    half, quarter = width // 2, width // 4
    bit = view_bit(scalars, 0)
    for place, same, cross in ((1 - bit, far_same, far_cross), (bit, mine, near_cross)):
        total = summed_tile(addends, place)
        parts = []
        for core in range(2):
            value = total[:, half + core * quarter : half + (core + 1) * quarter]
            out = total[core * size : (core + 1) * size, :half]
            parts.append(jnp.concatenate((out, value[:size], value[size:]), axis=1))
        same[...] = jnp.where(scalars[0] == 0, parts[0], parts[1]).astype(same.dtype)
        cross[...] = jnp.where(scalars[0] == 0, parts[1], parts[0]).astype(cross.dtype)


def place_kernel(scalars, mine, far_same, near_cross, far_cross, value, out):
    size, width = mine.shape
    half, quarter = width // 2, width // 4
    for near, far, core in ((mine, far_same, scalars[0]), (near_cross, far_cross, 1 - scalars[0])):
        total = near[...] + far[...].astype(jnp.float32)
        out[:, pl.ds(pl.multiple_of(core * half, half), half)] = total[:, :half]
        columns = pl.ds(pl.multiple_of(core * quarter, quarter), quarter)
        value[:size, columns] = total[:, half : half + quarter]
        value[size:, columns] = total[:, half + quarter :]


def summed_views(rows, packed):
    for r in range(rows):
        total = packed[r].astype(jnp.float32)
        for i in range(r + rows, packed.shape[0], rows):
            total = total + packed[i].astype(jnp.float32)
        yield r, total


def last_query_key_kernel(rows, packed, query, key):
    size = packed.shape[2] // 2
    for r, total in summed_views(rows, packed):
        columns = slice(r * size, (r + 1) * size)
        query[:, columns] = total[:, :size]
        key[:, columns] = total[:, size:]


def params(mebibytes):
    return pltpu.CompilerParams(vmem_limit_bytes=mebibytes * MIB)


def shape(dims, kind):
    return jax.ShapeDtypeStruct(dims, kind)


def shards(latents, norm_gain, w_query, w_key, w_value, w_out, kernel, partners, counts, cotangent):
    views, strip_rows, columns, width = latents.shape[1:]
    inner = w_query.shape[1]
    groups, rows = lax.axis_size("view"), lax.axis_size("row")
    scenes = lax.axis_size("scene")
    assert (strip_rows, rows, scenes) == (1, 2, 4)
    strip = strip_rows * columns
    slots = partners.shape[2]
    part = inner // rows
    tokens = views * 2 * strip
    key_tokens = tokens + (groups - 1) * 2 * strip
    bf16, f32, i32 = jnp.bfloat16, jnp.float32, jnp.int32

    row, view, scene = lax.axis_index("row"), lax.axis_index("view"), lax.axis_index("scene")
    scalars = jnp.stack((row, view, scene, scene % 2, scene // 2)).astype(i32)
    swap = [(0, 1), (1, 0)]
    along_x, along_y = [(i, i ^ 1) for i in range(scenes)], [(i, i ^ 2) for i in range(scenes)]

    request, alive = pl.pallas_call(
        functools.partial(request_kernel, views, slots, groups),
        in_specs=[SMEM],
        out_specs=(SMEM, SMEM),
        out_shape=(shape((groups,), i32), shape((groups * views,), i32)),
        cost_estimate=MUCH,
        compiler_params=params(4),
        name="requests",
    )(partners)
    between = [[(i, i ^ d) for i in range(groups)] for d in range(1, groups)]
    granted = [lax.ppermute(request, "view", pairs) for pairs in between]

    lat = latents[0].reshape(views, strip, width)
    cot = cotangent[0].reshape(views, strip, width)
    lat_other = lax.ppermute(lat, "row", swap)
    cot_other = lax.ppermute(cot, "row", swap)

    outgoing = pl.pallas_call(
        functools.partial(pick_kernel, groups),
        in_specs=[SMEM] * groups + [VMEM],
        out_specs=[VMEM] * (groups - 1),
        out_shape=[shape((strip, width), bf16)] * (groups - 1),
        compiler_params=params(8),
        cost_estimate=MUCH,
        name="pick",
    )(scalars, *granted, lat)
    got_own = [lax.ppermute(part_out, "view", pairs) for part_out, pairs in zip(outgoing, between)]
    normed, queries, keys, values, out_grad, upstream = pl.pallas_call(
        project_kernel,
        in_specs=[SMEM] + [VMEM] * 10,
        out_specs=[VMEM] * 6,
        out_shape=[
            shape((tokens, width), bf16),
            shape((tokens, part), bf16),
            shape((tokens, part), bf16),
            shape((tokens, part), bf16),
            shape((tokens, part), bf16),
            shape((tokens, width), bf16),
        ],
        compiler_params=params(28),
        cost_estimate=LITTLE,
        name="project",
    )(scalars, lat, lat_other, cot, cot_other, norm_gain, kernel, w_query, w_key, w_value, w_out)

    got_own, normed = lax.optimization_barrier((got_own, normed))
    got_other = [lax.ppermute(got, "row", swap) for got in got_own]

    def call(kernel_body, results, operands, name, first=VMEM, mebibytes=16, cost=LITTLE):
        outputs = pl.pallas_call(
            kernel_body,
            in_specs=[first] + [VMEM] * (len(operands) - 1),
            out_specs=[VMEM] * len(results),
            out_shape=results,
            compiler_params=params(mebibytes),
            cost_estimate=cost,
            name=name,
        )(*operands)
        return list(outputs)

    far_tokens, head_pairs = key_tokens - tokens, part // (2 * HEAD_DIM)
    normed_far, keys_far, values_far, attention_own, attention_far, mixed, dvalue = pl.pallas_call(
        functools.partial(forward_kernel, views, groups),
        in_specs=[SMEM] * 2 + [VMEM] * (2 * groups - 2 + 7),
        out_specs=[VMEM] * 7,
        out_shape=[
            shape((far_tokens, width), bf16),
            shape((far_tokens, part), bf16),
            shape((far_tokens, part), bf16),
            shape((head_pairs, 2 * strip, 2 * tokens), f32),
            shape((head_pairs, far_tokens, 2 * tokens), f32),
            shape((tokens, part), bf16),
            shape((key_tokens, part), bf16),
        ],
        compiler_params=params(28 + groups // 2),
        cost_estimate=LITTLE,
        name="attention_forward",
    )(
        scalars, alive, *got_own, *got_other, queries, keys, values, out_grad, norm_gain, w_key, w_value
    )
    mixed_other = lax.ppermute(mixed, "row", swap)
    dquery, dkey = call(
        functools.partial(backward_kernel, views),
        [shape((tokens, part), bf16), shape((key_tokens, part), bf16)],
        (queries, keys, values, out_grad, keys_far, values_far, attention_own, attention_far),
        "attention_backward",
        mebibytes=28 + groups // 2,
    )

    def after(value, *earlier):
        return lax.optimization_barrier((value, *earlier))[0]

    targets = groups * rows
    q_size = width // 4
    q_rows, o_rows = q_size // targets, inner // (4 * targets)
    q_block = (q_size, part)

    def first_exchange(sends):
        return lax.ppermute(sends[0], "scene", along_x), lax.ppermute(sends[1], "scene", along_y)

    def first_sum(parts, got, name, cost=LITTLE):
        blocks = [part_now.shape[1:] for part_now in parts[:2]]
        results = [shape(block, bf16) for block in blocks] + [shape(block, f32) for block in blocks]
        return call(first_sum_kernel, results, (parts[2], got[0], parts[3], got[1]), name, cost=cost)

    def second_exchange(sums):
        return lax.ppermute(sums[0], "scene", along_y), lax.ppermute(sums[1], "scene", along_x)

    def across_views(packed):
        return lax.all_to_all(packed, ("view", "row"), split_axis=0, concat_axis=0, tiled=True)

    pairs = groups // 2
    tile = (2 * o_rows, width)
    send, keep = call(
        value_out_kernel,
        [shape((2, 2, pairs, *tile), kind) for kind in (bf16, f32)],
        (scalars, normed, normed_far, after(dvalue, dkey), mixed, mixed_other, upstream),
        "grad_value_out",
        SMEM,
        24,
    )
    got = lax.ppermute(send, "view", [(i, i ^ 1) for i in range(groups)])
    results = [shape((2, *q_block), bf16)] * 2 + [shape((2, *q_block), f32)] * 2
    qk_parts = call(
        query_key_kernel, results, (scalars, normed, normed_far, after(dquery, send), dkey), "grad_query_key", SMEM, 24
    )
    qk_got = first_exchange(qk_parts)
    qk_sums = first_sum(qk_parts, qk_got, "first_sum_query_key")
    qk_got = second_exchange(qk_sums)
    packed = call(
        pack_query_key_kernel,
        [shape((q_size, 2 * part), bf16)],
        (qk_sums[2], qk_got[0], qk_sums[3], qk_got[1]),
        "second_sum_query_key",
    )[0]
    part_shape = (2, pairs, 2 * o_rows, width // 2)
    vo_parts = call(
        view_sum_kernel,
        [shape(part_shape, bf16)] * 2 + [shape(part_shape, f32)] * 2,
        (keep, after(got, packed)),
        "view_sum_value_out",
    )
    vo_got = first_exchange(vo_parts)
    packed = across_views(after(packed, vo_parts[0]).reshape(targets, q_rows, 2 * part))
    grad_query, grad_key = call(
        functools.partial(last_query_key_kernel, rows),
        [shape((q_rows, inner), f32)] * 2,
        (packed,),
        "last_sum_query_key",
    )

    vo_sums = first_sum(vo_parts, vo_got, "first_sum_value_out", MUCH)
    v_got, o_got = second_exchange(vo_sums)
    addends = (vo_sums[3], o_got, vo_sums[2], v_got)
    for bit in reversed(range(1, pairs.bit_length() - 1)):
        send, keep = call(
            functools.partial(tile_halves_kernel, bit),
            [shape((1 << bit, *tile), kind) for kind in (bf16, f32)],
            (scalars, *addends),
            "view_bit_value_out",
            SMEM,
        )
        addends = (keep, lax.ppermute(send, "view", [(i, i ^ (2 << bit)) for i in range(groups)]))
    far_same, far_cross, near_cross, mine = call(
        tile_cores_kernel,
        [shape((o_rows, width), kind) for kind in (bf16, bf16, f32, f32)],
        (scalars, *addends),
        "last_parts_value_out",
        SMEM,
    )
    far_same = lax.ppermute(far_same, "view", [(i, i ^ 2) for i in range(groups)])
    far_cross = lax.ppermute(far_cross, ("view", "row"), [(i, i ^ 5) for i in range(targets)])
    near_cross = lax.ppermute(near_cross, "row", swap)
    grad_value, grad_out = call(
        place_kernel,
        [shape((q_rows, inner), f32), shape((o_rows, width), f32)],
        (scalars, after(mine, grad_key), far_same, near_cross, far_cross),
        "last_sum_value_out",
        SMEM,
    )
    return grad_query, grad_key, grad_value, grad_out


def solution(mesh):
    tokens = P("scene", "view", "row", None, None)
    everywhere = P()
    grads = P(("scene", "view", "row"), None)
    return jax.shard_map(
        shards,
        mesh=mesh,
        in_specs=(
            tokens, everywhere, everywhere, everywhere, everywhere, everywhere, everywhere,
            P("scene", "view", None), P("scene", "view"), tokens,
        ),
        out_specs=(grads, grads, grads, grads),
        check_vma=False,
    )
```

```python
import functools

import jax
import jax.numpy as jnp
from jax import lax
from jax.experimental import pallas as pl
from jax.experimental.pallas import tpu as pltpu
from jax.sharding import PartitionSpec as P

HEAD_DIM = 64
EPSILON = 1e-06
SCALE = HEAD_DIM ** (-0.5)
MASKED = -1e30
MIB = 1024 * 1024
LITTLE = pl.CostEstimate(flops=1, bytes_accessed=1, transcendentals=0)
MUCH = pl.CostEstimate(flops=40_000_000_000, bytes_accessed=1, transcendentals=0)

VMEM = pl.BlockSpec(memory_space=pltpu.VMEM)
SMEM = pl.BlockSpec(memory_space=pltpu.SMEM)


def dot_nn(a, b):
    return lax.dot_general(a, b, (((1,), (0,)), ((), ())), preferred_element_type=jnp.float32)


def dot_nt(a, b):
    return lax.dot_general(a, b, (((1,), (1,)), ((), ())), preferred_element_type=jnp.float32)


def dot_tn(a, b):
    return lax.dot_general(a, b, (((0,), (0,)), ((), ())), preferred_element_type=jnp.float32)


def normalized(tokens, gain):
    x = tokens.astype(jnp.float32)
    mean = jnp.mean(x * x, -1, keepdims=True)
    return (x * lax.rsqrt(mean + EPSILON) * gain).astype(jnp.bfloat16)


def pick_kernel(groups, scalars, *refs):
    tables, lat, outgoing = refs[: groups - 1], refs[groups - 1], refs[groups:]
    views = lat.shape[0]
    for table, out in zip(tables, outgoing):
        wanted = jnp.int32(0)
        for u in range(table.shape[1]):
            for j in range(table.shape[2]):
                partner = table[0, u, j]
                here = (partner >= 0) & (lax.div(partner, jnp.int32(views)) == scalars[1])
                wanted = jnp.where(here, lax.rem(partner, jnp.int32(views)), wanted)
        out[...] = lat[wanted]


def core_half(scalars, size):
    return pl.ds(pl.multiple_of(scalars[0] * size, size), size)


def project_kernel(
    scalars, lat_own, lat_other, cot_own, cot_other, gain, taps, w_query, w_key, w_value, w_out,
    normed, queries, keys, values, out_grad, upstream,
):
    views, strip, width = lat_own.shape
    scale = gain[...].reshape(1, width)
    row = scalars[0]

    def strip_of(u, half):
        index = 2 * u + (row if half == 0 else 1 - row)
        return pl.ds(pl.multiple_of(index * strip, strip), strip)

    for half, source in enumerate((lat_own, lat_other)):
        for u in range(views):
            normed[strip_of(u, half), :] = normalized(source[u], scale)
    first = row == 0
    chunk = 512
    column = lax.broadcasted_iota(jnp.int32, (strip, 1), 0)
    not_first = (column > 0).astype(jnp.float32)
    not_last = (column < strip - 1).astype(jnp.float32)
    for c in range(0, width, chunk):
        lanes = slice(c, c + chunk)
        tap = taps[:, lanes].astype(jnp.float32)
        top, middle, bottom = tap[0:3], tap[3:6], tap[6:9]
        cross = (jnp.where(first, top, bottom), jnp.where(first, bottom, top))
        for u in range(views):
            strips = [ref[u, :, lanes].astype(jnp.float32) for ref in (cot_own, cot_other)]
            shifted = []
            for x in strips:
                after = pltpu.roll(x, strip - 1, 0) * not_last
                before = pltpu.roll(x, 1, 0) * not_first
                shifted.append((after, x, before))
            for half in range(2):
                total = strips[half]
                for b in range(3):
                    total = total + middle[b : b + 1] * shifted[half][b]
                    total = total + cross[half][b : b + 1] * shifted[1 - half][b]
                upstream[strip_of(u, half), lanes] = total.astype(jnp.bfloat16)
    rows = normed[...]
    half = core_half(scalars, queries.shape[1])
    for weight, result in ((w_query, queries), (w_key, keys), (w_value, values)):
        result[...] = dot_nn(rows, weight[:, half]).astype(jnp.bfloat16)
    out_grad[...] = dot_nt(upstream[...], w_out[half, :]).astype(jnp.bfloat16)


def stacked(x, views):
    tokens, pair = x.shape
    low = (lax.broadcasted_iota(jnp.int32, (1, 1, pair), 2) < pair // 2).astype(x.dtype)
    x = x.reshape(views, tokens // views, pair)
    return jnp.concatenate((x * low, x * (1 - low)), axis=1).reshape(2 * tokens, pair)


def unstacked(x, views):
    rows, pair = x.shape
    low = lax.broadcasted_iota(jnp.int32, (1, 1, pair), 2) < pair // 2
    x = x.reshape(views, 2, rows // (2 * views), pair)
    return jnp.where(low, x[:, 0], x[:, 1]).reshape(rows // 2, pair)


def view_parts(x, views, axis):
    size = x.shape[axis] // views
    return [lax.slice_in_dim(x, u * size, (u + 1) * size, axis=axis) for u in range(views)]


def own_nt(a, b, views):
    pairs = zip(view_parts(a, views, 0), view_parts(b, views, 0))
    return jnp.concatenate([dot_nt(x, y) for x, y in pairs], axis=1)


def own_tn(a, b, views):
    pairs = zip(view_parts(a, views, 1), view_parts(b, views, 0))
    return jnp.concatenate([dot_tn(x, y) for x, y in pairs], axis=0)


def own_nn(a, b, views):
    pairs = zip(view_parts(a, views, 1), view_parts(b, views, 0))
    return jnp.concatenate([dot_nn(x, y) for x, y in pairs], axis=0)


def forward_kernel(views, groups, scalars, partners, *refs):
    got_own, got_other, refs = refs[: groups - 1], refs[groups - 1 : 2 * groups - 2], refs[2 * groups - 2 :]
    queries, keys, values, out_grad, gain, w_key, w_value, *refs = refs
    normed_far, keys_far, values_far, attention_own, attention_far, mixed, dvalue = refs
    strip = got_own[0].shape[0]
    tokens, part = queries.shape
    view_tokens = tokens // views
    here = scalars[1]
    scale_row = gain[...].reshape(1, normed_far.shape[1])
    pair = 2 * HEAD_DIM
    span = 2 * view_tokens
    column_view = lax.broadcasted_iota(jnp.int32, (1, views * span), 1) // span
    slot_alive = []
    for j in range(groups - 1):
        group = lax.bitwise_xor(here, jnp.int32(j + 1))
        start = 2 * j * strip
        normed_far[start : start + strip, :] = normalized(got_own[j][...], scale_row)
        normed_far[start + strip : start + 2 * strip, :] = normalized(got_other[j][...], scale_row)
        taken = jnp.zeros((1, views * span), jnp.int32)
        for u in range(views):
            found = jnp.int32(0)
            for slot in range(partners.shape[2]):
                partner = partners[0, u, slot]
                same = (partner >= 0) & (lax.div(partner, jnp.int32(views)) == group)
                found = jnp.where(same, 1, found)
            taken = jnp.where(column_view == u, found, taken)
        slot_alive.append(taken > 0)
    fetched = normed_far[...]
    half = core_half(scalars, part)
    keys_far[...] = dot_nn(fetched, w_key[:, half]).astype(jnp.bfloat16)
    values_far[...] = dot_nn(fetched, w_value[:, half]).astype(jnp.bfloat16)
    for p in range(part // pair):
        lanes = slice(p * pair, (p + 1) * pair)
        q, g = stacked(queries[:, lanes], views), stacked(out_grad[:, lanes], views)
        s_own = own_nt(keys[:, lanes], q, views) * SCALE
        s_far = dot_nt(keys_far[:, lanes], q) * SCALE
        s_far = jnp.concatenate(
            [
                jnp.where(slot_alive[j], s_far[j * view_tokens : (j + 1) * view_tokens], MASKED)
                for j in range(groups - 1)
            ],
            axis=0,
        )
        highest = jnp.maximum(jnp.max(s_own, 0, keepdims=True), jnp.max(s_far, 0, keepdims=True))
        e_own = jnp.exp(s_own - highest)
        e_far = jnp.exp(s_far - highest)
        inverse = 1.0 / (jnp.sum(e_own, 0, keepdims=True) + jnp.sum(e_far, 0, keepdims=True))
        a_own, a_far = e_own * inverse, e_far * inverse
        attention_own[p], attention_far[p] = a_own, a_far
        a_own, a_far = a_own.astype(jnp.bfloat16), a_far.astype(jnp.bfloat16)
        mix = own_tn(a_own, values[:, lanes], views) + dot_tn(a_far, values_far[:, lanes])
        mixed[:, lanes] = unstacked(mix, views).astype(jnp.bfloat16)
        dvalue[:tokens, lanes] = own_nn(a_own, g, views).astype(jnp.bfloat16)
        dvalue[tokens:, lanes] = dot_nn(a_far, g).astype(jnp.bfloat16)


def backward_kernel(
    views, queries, keys, values, out_grad, keys_far, values_far, attention_own, attention_far, dquery, dkey
):
    tokens, part = queries.shape
    pair = 2 * HEAD_DIM
    for p in range(part // pair):
        lanes = slice(p * pair, (p + 1) * pair)
        q, g = stacked(queries[:, lanes], views), stacked(out_grad[:, lanes], views)
        a_own, a_far = attention_own[p], attention_far[p]
        dp_own = own_nt(values[:, lanes], g, views)
        dp_far = dot_nt(values_far[:, lanes], g)
        delta = jnp.sum(a_own * dp_own, 0, keepdims=True) + jnp.sum(a_far * dp_far, 0, keepdims=True)
        ds_own = (a_own * (dp_own - delta) * SCALE).astype(jnp.bfloat16)
        ds_far = (a_far * (dp_far - delta) * SCALE).astype(jnp.bfloat16)
        dq = own_tn(ds_own, keys[:, lanes], views) + dot_tn(ds_far, keys_far[:, lanes])
        dquery[:, lanes] = unstacked(dq, views).astype(jnp.bfloat16)
        dkey[:tokens, lanes] = own_nn(ds_own, q, views).astype(jnp.bfloat16)
        dkey[tokens:, lanes] = dot_nn(ds_far, q).astype(jnp.bfloat16)


def by_quarters(scalars, lefts, right, send, keep, x_first):
    size = send.shape[1]
    x, y = scalars[3], scalars[4]
    for target, first in ((send, 1), (keep, 0)):
        for second in (1, 0):
            dx, dy = (first, second) if x_first else (second, first)
            block = 2 * lax.bitwise_xor(y, jnp.int32(dy)) + lax.bitwise_xor(x, jnp.int32(dx))
            columns = pl.ds(pl.multiple_of(block * size, size), size)
            total, start = 0.0, 0
            for left in lefts:
                total = total + dot_tn(left[:, columns], right[start : start + left.shape[0], :])
                start += left.shape[0]
            target[second] = total.astype(target.dtype)


def query_key_kernel(scalars, normed, normed_far, dquery, dkey, q_send, k_send, q_keep, k_keep):
    by_quarters(scalars, (normed,), dquery, q_send, q_keep, True)
    by_quarters(scalars, (normed, normed_far), dkey, k_send, k_keep, False)


def value_out_kernel(scalars, normed, normed_far, dvalue, mine, theirs, upstream, send, keep):
    row, x, y = scalars[0], scalars[3], scalars[4]
    odd = lax.rem(scalars[1], jnp.int32(2)) == 1
    _, _, pairs, size, width = send.shape
    half, quarter = width // 2, width // 4
    right = upstream[:, core_half(scalars, half)]
    from_mine, from_theirs = dot_tn(mine[...], right), dot_tn(theirs[...], right)
    for dy in range(2):
        grad_o = jnp.where(row == lax.bitwise_xor(y, jnp.int32(dy)), from_mine, from_theirs)
        low, high = grad_o[: 2 * pairs * size], grad_o[2 * pairs * size :]
        for dx in range(2):
            to_x = lax.bitwise_xor(x, jnp.int32(dx))
            o_part = jnp.where(to_x == 0, low, high)
            block = 2 * lax.bitwise_xor(y, jnp.int32(dy)) + to_x
            columns = pl.ds(pl.multiple_of(block * quarter, quarter), quarter)
            tokens = normed.shape[0]
            v_part = dot_tn(normed[:, columns], dvalue[:tokens, :])
            v_part = v_part + dot_tn(normed_far[:, columns], dvalue[tokens:, :])
            for pair in range(pairs):
                tiles = []
                for view in (2 * pair, 2 * pair + 1):
                    v_view = v_part[2 * view * size : 2 * (view + 1) * size]
                    tiles.append((o_part[view * size : (view + 1) * size], v_view[:size], v_view[size:]))
                for target, take_odd in ((send, jnp.logical_not(odd)), (keep, odd)):
                    tile = [jnp.where(take_odd, second, first) for first, second in zip(*tiles)]
                    target[dy, dx, pair] = jnp.concatenate(tile, axis=1).astype(target.dtype)


def view_sum_kernel(keep, got, x_send, y_send, x_keep, y_keep):
    half = keep.shape[4] // 2
    for second in range(2):
        for target, first in ((x_send, 1), (x_keep, 0)):
            total = keep[second, first, :, :, half:] + got[second, first, :, :, half:].astype(jnp.float32)
            target[second] = total.astype(target.dtype)
        for target, first in ((y_send, 1), (y_keep, 0)):
            total = keep[first, second, :, :, :half] + got[first, second, :, :, :half].astype(jnp.float32)
            target[second] = total.astype(target.dtype)


def first_sum_kernel(x_keep, x_got, y_keep, y_got, x_later, y_later, x_now, y_now):
    for keep, got, later, now in ((x_keep, x_got, x_later, x_now), (y_keep, y_got, y_later, y_now)):
        later[...] = (keep[1] + got[1].astype(jnp.float32)).astype(jnp.bfloat16)
        now[...] = keep[0] + got[0].astype(jnp.float32)


def query_key_tiles_kernel(scalars, q_now, q_got, k_now, k_got, send, keep):
    odd = lax.rem(scalars[1], jnp.int32(2)) == 1
    total = [now[...] + got[...].astype(jnp.float32) for now, got in ((q_now, q_got), (k_now, k_got))]
    total = jnp.concatenate(total, axis=1)
    pairs, size, _ = send.shape
    for pair in range(pairs):
        first = total[2 * pair * size : (2 * pair + 1) * size]
        second = total[(2 * pair + 1) * size : (2 * pair + 2) * size]
        send[pair] = jnp.where(odd, first, second).astype(send.dtype)
        keep[pair] = jnp.where(odd, second, first)


def summed_tile(addends, place):
    place = pl.ds(place, 1)
    total = [now[place] + got[place].astype(jnp.float32) for now, got in zip(addends[::2], addends[1::2])]
    return (jnp.concatenate(total, axis=2) if len(total) == 2 else total[0])[0]


def view_bit(scalars, bit):
    return lax.rem(lax.div(scalars[1], jnp.int32(2 << bit)), jnp.int32(2))


def tile_halves_kernel(bit, scalars, *refs):
    addends, (send, keep) = refs[:-2], refs[-2:]
    count = keep.shape[0]
    mine = view_bit(scalars, bit)
    for target, part in ((send, 1 - mine), (keep, mine)):
        for i in range(count):
            target[i] = summed_tile(addends, part * count + i).astype(target.dtype)


def query_key_cores(tile):
    size = tile.shape[0] // 2
    return tile[:size], tile[size:]


def value_out_cores(tile):
    size, width = tile.shape[0] // 2, tile.shape[1]
    half, quarter = width // 2, width // 4
    parts = []
    for core in range(2):
        value = tile[:, half + core * quarter : half + (core + 1) * quarter]
        out = tile[core * size : (core + 1) * size, :half]
        parts.append(jnp.concatenate((out, value[:size], value[size:]), axis=1))
    return parts


def tile_cores_kernel(split, scalars, *refs):
    addends, (far_same, far_cross, near_cross, mine) = refs[:-4], refs[-4:]
    bit = view_bit(scalars, 0)
    for place, same, cross in ((1 - bit, far_same, far_cross), (bit, mine, near_cross)):
        parts = split(summed_tile(addends, place))
        same[...] = jnp.where(scalars[0] == 0, parts[0], parts[1]).astype(same.dtype)
        cross[...] = jnp.where(scalars[0] == 0, parts[1], parts[0]).astype(cross.dtype)


def last_sums(scalars, mine, far_same, near_cross, far_cross):
    for near, far, core in ((mine, far_same, scalars[0]), (near_cross, far_cross, 1 - scalars[0])):
        yield near[...] + far[...].astype(jnp.float32), core


def place_query_key_kernel(scalars, mine, far_same, near_cross, far_cross, query, key):
    size = mine.shape[1] // 2
    for total, core in last_sums(scalars, mine, far_same, near_cross, far_cross):
        columns = pl.ds(pl.multiple_of(core * size, size), size)
        query[:, columns] = total[:, :size]
        key[:, columns] = total[:, size:]


def place_value_out_kernel(scalars, mine, far_same, near_cross, far_cross, value, out):
    size, width = mine.shape
    half, quarter = width // 2, width // 4
    for total, core in last_sums(scalars, mine, far_same, near_cross, far_cross):
        out[:, pl.ds(pl.multiple_of(core * half, half), half)] = total[:, :half]
        columns = pl.ds(pl.multiple_of(core * quarter, quarter), quarter)
        value[:size, columns] = total[:, half : half + quarter]
        value[size:, columns] = total[:, half + quarter :]


def params(mebibytes):
    return pltpu.CompilerParams(vmem_limit_bytes=mebibytes * MIB)


def shape(dims, kind):
    return jax.ShapeDtypeStruct(dims, kind)


def shards(latents, norm_gain, w_query, w_key, w_value, w_out, kernel, partners, counts, cotangent):
    views, strip_rows, columns, width = latents.shape[1:]
    inner = w_query.shape[1]
    groups, rows = lax.axis_size("view"), lax.axis_size("row")
    scenes = lax.axis_size("scene")
    assert (strip_rows, rows, scenes) == (1, 2, 4)
    strip = strip_rows * columns
    part = inner // rows
    tokens = views * 2 * strip
    key_tokens = tokens + (groups - 1) * 2 * strip
    bf16, f32, i32 = jnp.bfloat16, jnp.float32, jnp.int32

    row, view, scene = lax.axis_index("row"), lax.axis_index("view"), lax.axis_index("scene")
    scalars = jnp.stack((row, view, scene, scene % 2, scene // 2)).astype(i32)
    swap = [(0, 1), (1, 0)]
    along_x, along_y = [(i, i ^ 1) for i in range(scenes)], [(i, i ^ 2) for i in range(scenes)]

    between = [[(i, i ^ d) for i in range(groups)] for d in range(1, groups)]
    granted = [lax.ppermute(partners, "view", pairs) for pairs in between]

    lat = latents[0].reshape(views, strip, width)
    cot = cotangent[0].reshape(views, strip, width)
    lat_other = lax.ppermute(lat, "row", swap)
    cot_other = lax.ppermute(cot, "row", swap)

    outgoing = pl.pallas_call(
        functools.partial(pick_kernel, groups),
        in_specs=[SMEM] * groups + [VMEM],
        out_specs=[VMEM] * (groups - 1),
        out_shape=[shape((strip, width), bf16)] * (groups - 1),
        compiler_params=params(8),
        cost_estimate=MUCH,
        name="pick",
    )(scalars, *granted, lat)
    got_own = [lax.ppermute(part_out, "view", pairs) for part_out, pairs in zip(outgoing, between)]
    normed, queries, keys, values, out_grad, upstream = pl.pallas_call(
        project_kernel,
        in_specs=[SMEM] + [VMEM] * 10,
        out_specs=[VMEM] * 6,
        out_shape=[
            shape((tokens, width), bf16),
            shape((tokens, part), bf16),
            shape((tokens, part), bf16),
            shape((tokens, part), bf16),
            shape((tokens, part), bf16),
            shape((tokens, width), bf16),
        ],
        compiler_params=params(28),
        cost_estimate=LITTLE,
        name="project",
    )(scalars, lat, lat_other, cot, cot_other, norm_gain, kernel, w_query, w_key, w_value, w_out)

    got_own, normed = lax.optimization_barrier((got_own, normed))
    got_other = [lax.ppermute(got, "row", swap) for got in got_own]

    def call(kernel_body, results, operands, name, first=VMEM, mebibytes=16, cost=LITTLE):
        outputs = pl.pallas_call(
            kernel_body,
            in_specs=[first] + [VMEM] * (len(operands) - 1),
            out_specs=[VMEM] * len(results),
            out_shape=results,
            compiler_params=params(mebibytes),
            cost_estimate=cost,
            name=name,
        )(*operands)
        return list(outputs)

    far_tokens, head_pairs = key_tokens - tokens, part // (2 * HEAD_DIM)
    normed_far, keys_far, values_far, attention_own, attention_far, mixed, dvalue = pl.pallas_call(
        functools.partial(forward_kernel, views, groups),
        in_specs=[SMEM] * 2 + [VMEM] * (2 * groups - 2 + 7),
        out_specs=[VMEM] * 7,
        out_shape=[
            shape((far_tokens, width), bf16),
            shape((far_tokens, part), bf16),
            shape((far_tokens, part), bf16),
            shape((head_pairs, 2 * strip, 2 * tokens), f32),
            shape((head_pairs, far_tokens, 2 * tokens), f32),
            shape((tokens, part), bf16),
            shape((key_tokens, part), bf16),
        ],
        compiler_params=params(28 + groups // 2),
        cost_estimate=LITTLE,
        name="attention_forward",
    )(
        scalars, partners, *got_own, *got_other, queries, keys, values, out_grad, norm_gain, w_key, w_value
    )
    mixed_other = lax.ppermute(mixed, "row", swap)
    dquery, dkey = call(
        functools.partial(backward_kernel, views),
        [shape((tokens, part), bf16), shape((key_tokens, part), bf16)],
        (queries, keys, values, out_grad, keys_far, values_far, attention_own, attention_far),
        "attention_backward",
        mebibytes=28 + groups // 2,
    )

    def after(value, *earlier):
        return lax.optimization_barrier((value, *earlier))[0]

    targets = groups * rows
    q_size = width // 4
    q_rows, o_rows = q_size // targets, inner // (4 * targets)
    q_block = (q_size, part)

    def first_exchange(sends):
        return lax.ppermute(sends[0], "scene", along_x), lax.ppermute(sends[1], "scene", along_y)

    def first_sum(parts, got, name, cost=LITTLE):
        blocks = [part_now.shape[1:] for part_now in parts[:2]]
        results = [shape(block, bf16) for block in blocks] + [shape(block, f32) for block in blocks]
        return call(first_sum_kernel, results, (parts[2], got[0], parts[3], got[1]), name, cost=cost)

    def second_exchange(sums):
        return lax.ppermute(sums[0], "scene", along_y), lax.ppermute(sums[1], "scene", along_x)

    pairs = groups // 2
    neighbours = [(i, i ^ 1) for i in range(groups)]
    split_rows = {"query_key": q_rows, "value_out": o_rows}

    def last_parts(addends, split, name):
        tile = (addends[0].shape[1], sum(now.shape[2] for now in addends[::2]))
        for bit in reversed(range(1, pairs.bit_length() - 1)):
            send, keep = call(
                functools.partial(tile_halves_kernel, bit),
                [shape((1 << bit, *tile), kind) for kind in (bf16, f32)],
                (scalars, *addends),
                "view_bit_" + name,
                SMEM,
            )
            addends = (keep, lax.ppermute(send, "view", [(i, i ^ (2 << bit)) for i in range(groups)]))
        lanes = tile[0] * tile[1] // (2 * split_rows[name])
        far_same, far_cross, near_cross, mine = call(
            functools.partial(tile_cores_kernel, split),
            [shape((split_rows[name], lanes), kind) for kind in (bf16, bf16, f32, f32)],
            (scalars, *addends),
            "last_parts_" + name,
            SMEM,
        )
        far_same = lax.ppermute(far_same, "view", [(i, i ^ 2) for i in range(groups)])
        far_cross = lax.ppermute(far_cross, ("view", "row"), [(i, i ^ 5) for i in range(targets)])
        near_cross = lax.ppermute(near_cross, "row", swap)
        return mine, far_same, near_cross, far_cross

    tile = (2 * o_rows, width)
    send, keep = call(
        value_out_kernel,
        [shape((2, 2, pairs, *tile), kind) for kind in (bf16, f32)],
        (scalars, normed, normed_far, after(dvalue, dkey), mixed, mixed_other, upstream),
        "grad_value_out",
        SMEM,
        24,
    )
    got = lax.ppermute(send, "view", neighbours)
    results = [shape((2, *q_block), bf16)] * 2 + [shape((2, *q_block), f32)] * 2
    qk_parts = call(
        query_key_kernel, results, (scalars, normed, normed_far, after(dquery, send), dkey), "grad_query_key", SMEM, 24
    )
    qk_got = first_exchange(qk_parts)
    qk_sums = first_sum(qk_parts, qk_got, "first_sum_query_key")
    qk_got = second_exchange(qk_sums)
    qk_tile = (2 * q_rows, 2 * part)
    qk_send, qk_keep = call(
        query_key_tiles_kernel,
        [shape((pairs, *qk_tile), kind) for kind in (bf16, f32)],
        (scalars, qk_sums[2], qk_got[0], qk_sums[3], qk_got[1]),
        "second_sum_query_key",
        SMEM,
    )
    qk_addends = (qk_keep, lax.ppermute(qk_send, "view", neighbours))
    part_shape = (2, pairs, 2 * o_rows, width // 2)
    vo_parts = call(
        view_sum_kernel,
        [shape(part_shape, bf16)] * 2 + [shape(part_shape, f32)] * 2,
        (keep, after(got, qk_send)),
        "view_sum_value_out",
    )
    vo_got = first_exchange(vo_parts)
    vo_sums = first_sum(vo_parts, vo_got, "first_sum_value_out")
    v_got, o_got = second_exchange(vo_sums)
    addends = (vo_sums[3], o_got, vo_sums[2], v_got)
    qk_parts = last_parts((after(qk_addends[0], vo_sums[0]), qk_addends[1]), query_key_cores, "query_key")
    vo_parts = last_parts((after(addends[0], qk_parts[0]), *addends[1:]), value_out_cores, "value_out")
    grad_query, grad_key = call(
        place_query_key_kernel,
        [shape((q_rows, inner), f32)] * 2,
        (scalars, *qk_parts),
        "last_sum_query_key",
        SMEM,
    )
    grad_value, grad_out = call(
        place_value_out_kernel,
        [shape((q_rows, inner), f32), shape((o_rows, width), f32)],
        (scalars, after(vo_parts[0], grad_query), *vo_parts[1:]),
        "last_sum_value_out",
        SMEM,
    )
    return grad_query, grad_key, grad_value, grad_out


def solution(mesh):
    tokens = P("scene", "view", "row", None, None)
    everywhere = P()
    grads = P(("scene", "view", "row"), None)
    return jax.shard_map(
        shards,
        mesh=mesh,
        in_specs=(
            tokens, everywhere, everywhere, everywhere, everywhere, everywhere, everywhere,
            P("scene", "view", None), P("scene", "view"), tokens,
        ),
        out_specs=(grads, grads, grads, grads),
        check_vma=False,
    )
```

```python
import functools

import jax
import jax.numpy as jnp
from jax import lax
from jax.experimental import pallas as pl
from jax.experimental.pallas import tpu as pltpu
from jax.sharding import PartitionSpec as P

HEAD_DIM = 64
EPSILON = 1e-06
SCALE = HEAD_DIM ** (-0.5)
MASKED = -1e30
MIB = 1024 * 1024
LITTLE = pl.CostEstimate(flops=1, bytes_accessed=1, transcendentals=0)
MUCH = pl.CostEstimate(flops=40_000_000_000, bytes_accessed=1, transcendentals=0)

VMEM = pl.BlockSpec(memory_space=pltpu.VMEM)
SMEM = pl.BlockSpec(memory_space=pltpu.SMEM)


def dot_nn(a, b):
    return lax.dot_general(a, b, (((1,), (0,)), ((), ())), preferred_element_type=jnp.float32)


def dot_nt(a, b):
    return lax.dot_general(a, b, (((1,), (1,)), ((), ())), preferred_element_type=jnp.float32)


def dot_tn(a, b):
    return lax.dot_general(a, b, (((0,), (0,)), ((), ())), preferred_element_type=jnp.float32)


def normalized(tokens, gain):
    x = tokens.astype(jnp.float32)
    mean = jnp.mean(x * x, -1, keepdims=True)
    return (x * lax.rsqrt(mean + EPSILON) * gain).astype(jnp.bfloat16)


def request_kernel(views, slots, groups, partners, request, alive):
    for g in range(groups):
        request[g] = 0
        for u in range(views):
            alive[g * views + u] = 0
    for u in range(views):
        for j in range(slots):
            partner = partners[0, u, j]

            @pl.when(partner >= 0)
            def _():
                group = lax.div(partner, jnp.int32(views))
                request[group] = lax.rem(partner, jnp.int32(views))
                alive[group * views + u] = 1


def pick_kernel(groups, scalars, *refs):
    requests, lat, outgoing = refs[: groups - 1], refs[groups - 1], refs[groups:]
    for request, out in zip(requests, outgoing):
        out[...] = lat[request[scalars[1]]]


def core_half(scalars, size):
    return pl.ds(pl.multiple_of(scalars[0] * size, size), size)


def project_kernel(
    scalars, lat_own, lat_other, cot_own, cot_other, gain, taps, w_query, w_key, w_value, w_out,
    normed, queries, keys, values, out_grad, upstream,
):
    views, strip, width = lat_own.shape
    scale = gain[...].reshape(1, width)
    row = scalars[0]

    def strip_of(u, half):
        index = 2 * u + (row if half == 0 else 1 - row)
        return pl.ds(pl.multiple_of(index * strip, strip), strip)

    for half, source in enumerate((lat_own, lat_other)):
        for u in range(views):
            normed[strip_of(u, half), :] = normalized(source[u], scale)
    first = row == 0
    chunk = 512
    column = lax.broadcasted_iota(jnp.int32, (strip, 1), 0)
    not_first = (column > 0).astype(jnp.float32)
    not_last = (column < strip - 1).astype(jnp.float32)
    for c in range(0, width, chunk):
        lanes = slice(c, c + chunk)
        tap = taps[:, lanes].astype(jnp.float32)
        top, middle, bottom = tap[0:3], tap[3:6], tap[6:9]
        cross = (jnp.where(first, top, bottom), jnp.where(first, bottom, top))
        for u in range(views):
            strips = [ref[u, :, lanes].astype(jnp.float32) for ref in (cot_own, cot_other)]
            shifted = []
            for x in strips:
                after = pltpu.roll(x, strip - 1, 0) * not_last
                before = pltpu.roll(x, 1, 0) * not_first
                shifted.append((after, x, before))
            for half in range(2):
                total = strips[half]
                for b in range(3):
                    total = total + middle[b : b + 1] * shifted[half][b]
                    total = total + cross[half][b : b + 1] * shifted[1 - half][b]
                upstream[strip_of(u, half), lanes] = total.astype(jnp.bfloat16)
    rows = normed[...]
    half = core_half(scalars, queries.shape[1])
    for weight, result in ((w_query, queries), (w_key, keys), (w_value, values)):
        result[...] = dot_nn(rows, weight[:, half]).astype(jnp.bfloat16)
    out_grad[...] = dot_nt(upstream[...], w_out[half, :]).astype(jnp.bfloat16)


def stacked(x, views):
    tokens, pair = x.shape
    low = (lax.broadcasted_iota(jnp.int32, (1, 1, pair), 2) < pair // 2).astype(x.dtype)
    x = x.reshape(views, tokens // views, pair)
    return jnp.concatenate((x * low, x * (1 - low)), axis=1).reshape(2 * tokens, pair)


def unstacked(x, views):
    rows, pair = x.shape
    low = lax.broadcasted_iota(jnp.int32, (1, 1, pair), 2) < pair // 2
    x = x.reshape(views, 2, rows // (2 * views), pair)
    return jnp.where(low, x[:, 0], x[:, 1]).reshape(rows // 2, pair)


def view_parts(x, views, axis):
    size = x.shape[axis] // views
    return [lax.slice_in_dim(x, u * size, (u + 1) * size, axis=axis) for u in range(views)]


def own_nt(a, b, views):
    pairs = zip(view_parts(a, views, 0), view_parts(b, views, 0))
    return jnp.concatenate([dot_nt(x, y) for x, y in pairs], axis=1)


def own_tn(a, b, views):
    pairs = zip(view_parts(a, views, 1), view_parts(b, views, 0))
    return jnp.concatenate([dot_tn(x, y) for x, y in pairs], axis=0)


def own_nn(a, b, views):
    pairs = zip(view_parts(a, views, 1), view_parts(b, views, 0))
    return jnp.concatenate([dot_nn(x, y) for x, y in pairs], axis=0)


def forward_kernel(views, groups, scalars, alive, *refs):
    got_own, got_other, refs = refs[: groups - 1], refs[groups - 1 : 2 * groups - 2], refs[2 * groups - 2 :]
    queries, keys, values, out_grad, gain, w_key, w_value, *refs = refs
    normed_far, keys_far, values_far, attention_own, attention_far, mixed, dvalue = refs
    strip = got_own[0].shape[0]
    tokens, part = queries.shape
    view_tokens = tokens // views
    here = scalars[1]
    scale_row = gain[...].reshape(1, normed_far.shape[1])
    pair = 2 * HEAD_DIM
    span = 2 * view_tokens
    column_view = lax.broadcasted_iota(jnp.int32, (1, views * span), 1) // span
    slot_alive = []
    for j in range(groups - 1):
        group = lax.bitwise_xor(here, jnp.int32(j + 1))
        start = 2 * j * strip
        normed_far[start : start + strip, :] = normalized(got_own[j][...], scale_row)
        normed_far[start + strip : start + 2 * strip, :] = normalized(got_other[j][...], scale_row)
        taken = jnp.zeros((1, views * span), jnp.int32)
        for u in range(views):
            taken = jnp.where(column_view == u, alive[group * views + u], taken)
        slot_alive.append(taken > 0)
    fetched = normed_far[...]
    half = core_half(scalars, part)
    keys_far[...] = dot_nn(fetched, w_key[:, half]).astype(jnp.bfloat16)
    values_far[...] = dot_nn(fetched, w_value[:, half]).astype(jnp.bfloat16)
    for p in range(part // pair):
        lanes = slice(p * pair, (p + 1) * pair)
        q, g = stacked(queries[:, lanes], views), stacked(out_grad[:, lanes], views)
        s_own = own_nt(keys[:, lanes], q, views) * SCALE
        s_far = dot_nt(keys_far[:, lanes], q) * SCALE
        s_far = jnp.concatenate(
            [
                jnp.where(slot_alive[j], s_far[j * view_tokens : (j + 1) * view_tokens], MASKED)
                for j in range(groups - 1)
            ],
            axis=0,
        )
        highest = jnp.maximum(jnp.max(s_own, 0, keepdims=True), jnp.max(s_far, 0, keepdims=True))
        e_own = jnp.exp(s_own - highest)
        e_far = jnp.exp(s_far - highest)
        inverse = 1.0 / (jnp.sum(e_own, 0, keepdims=True) + jnp.sum(e_far, 0, keepdims=True))
        a_own, a_far = e_own * inverse, e_far * inverse
        attention_own[p], attention_far[p] = a_own, a_far
        a_own, a_far = a_own.astype(jnp.bfloat16), a_far.astype(jnp.bfloat16)
        mix = own_tn(a_own, values[:, lanes], views) + dot_tn(a_far, values_far[:, lanes])
        mixed[:, lanes] = unstacked(mix, views).astype(jnp.bfloat16)
        dvalue[:tokens, lanes] = own_nn(a_own, g, views).astype(jnp.bfloat16)
        dvalue[tokens:, lanes] = dot_nn(a_far, g).astype(jnp.bfloat16)


def backward_kernel(
    views, queries, keys, values, out_grad, keys_far, values_far, attention_own, attention_far, dquery, dkey
):
    tokens, part = queries.shape
    pair = 2 * HEAD_DIM
    for p in range(part // pair):
        lanes = slice(p * pair, (p + 1) * pair)
        q, g = stacked(queries[:, lanes], views), stacked(out_grad[:, lanes], views)
        a_own, a_far = attention_own[p], attention_far[p]
        dp_own = own_nt(values[:, lanes], g, views)
        dp_far = dot_nt(values_far[:, lanes], g)
        delta = jnp.sum(a_own * dp_own, 0, keepdims=True) + jnp.sum(a_far * dp_far, 0, keepdims=True)
        ds_own = (a_own * (dp_own - delta) * SCALE).astype(jnp.bfloat16)
        ds_far = (a_far * (dp_far - delta) * SCALE).astype(jnp.bfloat16)
        dq = own_tn(ds_own, keys[:, lanes], views) + dot_tn(ds_far, keys_far[:, lanes])
        dquery[:, lanes] = unstacked(dq, views).astype(jnp.bfloat16)
        dkey[:tokens, lanes] = own_nn(ds_own, q, views).astype(jnp.bfloat16)
        dkey[tokens:, lanes] = dot_nn(ds_far, q).astype(jnp.bfloat16)


def halves_kernel(scalars, *refs):
    lefts, (right, x_send, y_send, x_keep, y_keep) = refs[:-5], refs[-5:]
    rows = x_send.shape[1]
    x, y = scalars[3], scalars[4]
    for dy, dx in ((1, 1), (0, 1), (1, 0), (0, 0)):
        block = 2 * lax.bitwise_xor(y, jnp.int32(dy)) + lax.bitwise_xor(x, jnp.int32(dx))
        columns = pl.ds(pl.multiple_of(block * 2 * rows, 2 * rows), 2 * rows)
        total, start = 0.0, 0
        for left in lefts:
            total = total + dot_tn(left[:, columns], right[start : start + left.shape[0], :])
            start += left.shape[0]
        x_out, y_out = (x_send if dx else x_keep), (y_send if dy else y_keep)
        x_out[dy] = total[:rows].astype(x_out.dtype)
        y_out[dx] = total[rows:].astype(y_out.dtype)


def value_out_kernel(scalars, normed, normed_far, dvalue, mine, theirs, upstream, send, keep):
    row, x, y = scalars[0], scalars[3], scalars[4]
    odd = lax.rem(scalars[1], jnp.int32(2)) == 1
    _, _, pairs, size, width = send.shape
    half, quarter = width // 2, width // 4
    right = upstream[:, core_half(scalars, half)]
    from_mine, from_theirs = dot_tn(mine[...], right), dot_tn(theirs[...], right)
    for dy in range(2):
        grad_o = jnp.where(row == lax.bitwise_xor(y, jnp.int32(dy)), from_mine, from_theirs)
        low, high = grad_o[: 2 * pairs * size], grad_o[2 * pairs * size :]
        for dx in range(2):
            to_x = lax.bitwise_xor(x, jnp.int32(dx))
            o_part = jnp.where(to_x == 0, low, high)
            block = 2 * lax.bitwise_xor(y, jnp.int32(dy)) + to_x
            columns = pl.ds(pl.multiple_of(block * quarter, quarter), quarter)
            tokens = normed.shape[0]
            v_part = dot_tn(normed[:, columns], dvalue[:tokens, :])
            v_part = v_part + dot_tn(normed_far[:, columns], dvalue[tokens:, :])
            for pair in range(pairs):
                tiles = []
                for view in (2 * pair, 2 * pair + 1):
                    v_view = v_part[2 * view * size : 2 * (view + 1) * size]
                    tiles.append((o_part[view * size : (view + 1) * size], v_view[:size], v_view[size:]))
                for target, take_odd in ((send, jnp.logical_not(odd)), (keep, odd)):
                    tile = [jnp.where(take_odd, second, first) for first, second in zip(*tiles)]
                    target[dy, dx, pair] = jnp.concatenate(tile, axis=1).astype(target.dtype)


def view_sum_kernel(keep, got, x_send, y_send, x_keep, y_keep):
    half = keep.shape[4] // 2
    for second in range(2):
        for target, first in ((x_send, 1), (x_keep, 0)):
            total = keep[second, first, :, :, half:] + got[second, first, :, :, half:].astype(jnp.float32)
            target[second] = total.astype(target.dtype)
        for target, first in ((y_send, 1), (y_keep, 0)):
            total = keep[first, second, :, :, :half] + got[first, second, :, :, :half].astype(jnp.float32)
            target[second] = total.astype(target.dtype)


def first_sum_kernel(x_keep, x_got, y_keep, y_got, x_later, y_later, x_now, y_now):
    for keep, got, later, now in ((x_keep, x_got, x_later, x_now), (y_keep, y_got, y_later, y_now)):
        later[...] = (keep[1] + got[1].astype(jnp.float32)).astype(jnp.bfloat16)
        now[...] = keep[0] + got[0].astype(jnp.float32)


def view_tiles_kernel(scalars, x_now, x_got, y_now, y_got, send, keep):
    odd = lax.rem(scalars[1], jnp.int32(2)) == 1
    pairs, size, _ = send.shape
    for half, (now, got) in enumerate(((x_now, x_got), (y_now, y_got))):
        total = now[...] + got[...].astype(jnp.float32)
        for i in range(pairs // 2):
            first, second = total[2 * i * size : (2 * i + 1) * size], total[(2 * i + 1) * size : (2 * i + 2) * size]
            pair = half * (pairs // 2) + i
            send[pair] = jnp.where(odd, first, second).astype(send.dtype)
            keep[pair] = jnp.where(odd, second, first)


def summed_tile(addends, place):
    place = pl.ds(place, 1)
    total = [now[place] + got[place].astype(jnp.float32) for now, got in zip(addends[::2], addends[1::2])]
    return (jnp.concatenate(total, axis=2) if len(total) == 2 else total[0])[0]


def view_bit(scalars, bit):
    return lax.rem(lax.div(scalars[1], jnp.int32(2 << bit)), jnp.int32(2))


def tile_halves_kernel(bit, scalars, *refs):
    addends, (send, keep) = refs[:-2], refs[-2:]
    count = keep.shape[0]
    mine = view_bit(scalars, bit)
    for target, part in ((send, 1 - mine), (keep, mine)):
        for i in range(count):
            target[i] = summed_tile(addends, part * count + i).astype(target.dtype)


def row_cores(tile):
    size = tile.shape[0] // 2
    return tile[:size], tile[size:]


def value_out_cores(tile):
    size, width = tile.shape[0] // 2, tile.shape[1]
    half, quarter = width // 2, width // 4
    parts = []
    for core in range(2):
        value = tile[:, half + core * quarter : half + (core + 1) * quarter]
        out = tile[core * size : (core + 1) * size, :half]
        parts.append(jnp.concatenate((out, value[:size], value[size:]), axis=1))
    return parts


def tile_cores_kernel(split, scalars, *refs):
    addends, (far_same, far_cross, near_cross, mine) = refs[:-4], refs[-4:]
    bit = view_bit(scalars, 0)
    for place, same, cross in ((1 - bit, far_same, far_cross), (bit, mine, near_cross)):
        parts = split(summed_tile(addends, place))
        same[...] = jnp.where(scalars[0] == 0, parts[0], parts[1]).astype(same.dtype)
        cross[...] = jnp.where(scalars[0] == 0, parts[1], parts[0]).astype(cross.dtype)


def last_sums(scalars, mine, far_same, near_cross, far_cross):
    for near, far, core in ((mine, far_same, scalars[0]), (near_cross, far_cross, 1 - scalars[0])):
        yield near[...] + far[...].astype(jnp.float32), core


def place_kernel(scalars, mine, far_same, near_cross, far_cross, result):
    size = mine.shape[1]
    for total, core in last_sums(scalars, mine, far_same, near_cross, far_cross):
        result[:, pl.ds(pl.multiple_of(core * size, size), size)] = total


def place_value_out_kernel(scalars, mine, far_same, near_cross, far_cross, value, out):
    size, width = mine.shape
    half, quarter = width // 2, width // 4
    for total, core in last_sums(scalars, mine, far_same, near_cross, far_cross):
        out[:, pl.ds(pl.multiple_of(core * half, half), half)] = total[:, :half]
        columns = pl.ds(pl.multiple_of(core * quarter, quarter), quarter)
        value[:size, columns] = total[:, half : half + quarter]
        value[size:, columns] = total[:, half + quarter :]


def params(mebibytes):
    return pltpu.CompilerParams(vmem_limit_bytes=mebibytes * MIB)


def shape(dims, kind):
    return jax.ShapeDtypeStruct(dims, kind)


def shards(latents, norm_gain, w_query, w_key, w_value, w_out, kernel, partners, counts, cotangent):
    views, strip_rows, columns, width = latents.shape[1:]
    inner = w_query.shape[1]
    slots = partners.shape[2]
    groups, rows = lax.axis_size("view"), lax.axis_size("row")
    scenes = lax.axis_size("scene")
    assert (strip_rows, rows, scenes) == (1, 2, 4)
    strip = strip_rows * columns
    part = inner // rows
    tokens = views * 2 * strip
    key_tokens = tokens + (groups - 1) * 2 * strip
    bf16, f32, i32 = jnp.bfloat16, jnp.float32, jnp.int32

    row, view, scene = lax.axis_index("row"), lax.axis_index("view"), lax.axis_index("scene")
    scalars = jnp.stack((row, view, scene, scene % 2, scene // 2)).astype(i32)
    swap = [(0, 1), (1, 0)]
    along_x, along_y = [(i, i ^ 1) for i in range(scenes)], [(i, i ^ 2) for i in range(scenes)]

    request, alive = pl.pallas_call(
        functools.partial(request_kernel, views, slots, groups),
        in_specs=[SMEM],
        out_specs=(SMEM, SMEM),
        out_shape=(shape((groups,), i32), shape((groups * views,), i32)),
        cost_estimate=MUCH,
        compiler_params=params(4),
        name="requests",
    )(partners)
    between = [[(i, i ^ d) for i in range(groups)] for d in range(1, groups)]
    granted = [lax.ppermute(request, "view", pairs) for pairs in between]

    lat = latents[0].reshape(views, strip, width)
    cot = cotangent[0].reshape(views, strip, width)
    lat_other = lax.ppermute(lat, "row", swap)
    cot_other = lax.ppermute(cot, "row", swap)

    outgoing = pl.pallas_call(
        functools.partial(pick_kernel, groups),
        in_specs=[SMEM] * groups + [VMEM],
        out_specs=[VMEM] * (groups - 1),
        out_shape=[shape((strip, width), bf16)] * (groups - 1),
        compiler_params=params(8),
        cost_estimate=MUCH,
        name="pick",
    )(scalars, *granted, lat)
    got_own = [lax.ppermute(part_out, "view", pairs) for part_out, pairs in zip(outgoing, between)]
    normed, queries, keys, values, out_grad, upstream = pl.pallas_call(
        project_kernel,
        in_specs=[SMEM] + [VMEM] * 10,
        out_specs=[VMEM] * 6,
        out_shape=[
            shape((tokens, width), bf16),
            shape((tokens, part), bf16),
            shape((tokens, part), bf16),
            shape((tokens, part), bf16),
            shape((tokens, part), bf16),
            shape((tokens, width), bf16),
        ],
        compiler_params=params(28),
        cost_estimate=LITTLE,
        name="project",
    )(scalars, lat, lat_other, cot, cot_other, norm_gain, kernel, w_query, w_key, w_value, w_out)

    got_own, normed = lax.optimization_barrier((got_own, normed))
    got_other = [lax.ppermute(got, "row", swap) for got in got_own]

    def call(kernel_body, results, operands, name, first=VMEM, mebibytes=16, cost=LITTLE):
        outputs = pl.pallas_call(
            kernel_body,
            in_specs=[first] + [VMEM] * (len(operands) - 1),
            out_specs=[VMEM] * len(results),
            out_shape=results,
            compiler_params=params(mebibytes),
            cost_estimate=cost,
            name=name,
        )(*operands)
        return list(outputs)

    far_tokens, head_pairs = key_tokens - tokens, part // (2 * HEAD_DIM)
    normed_far, keys_far, values_far, attention_own, attention_far, mixed, dvalue = pl.pallas_call(
        functools.partial(forward_kernel, views, groups),
        in_specs=[SMEM] * 2 + [VMEM] * (2 * groups - 2 + 7),
        out_specs=[VMEM] * 7,
        out_shape=[
            shape((far_tokens, width), bf16),
            shape((far_tokens, part), bf16),
            shape((far_tokens, part), bf16),
            shape((head_pairs, 2 * strip, 2 * tokens), f32),
            shape((head_pairs, far_tokens, 2 * tokens), f32),
            shape((tokens, part), bf16),
            shape((key_tokens, part), bf16),
        ],
        compiler_params=params(28 + groups // 2),
        cost_estimate=LITTLE,
        name="attention_forward",
    )(
        scalars, alive, *got_own, *got_other, queries, keys, values, out_grad, norm_gain, w_key, w_value
    )
    mixed_other = lax.ppermute(mixed, "row", swap)
    dquery, dkey = call(
        functools.partial(backward_kernel, views),
        [shape((tokens, part), bf16), shape((key_tokens, part), bf16)],
        (queries, keys, values, out_grad, keys_far, values_far, attention_own, attention_far),
        "attention_backward",
        mebibytes=28 + groups // 2,
    )

    def after(value, *earlier):
        return lax.optimization_barrier((value, *earlier))[0]

    targets = groups * rows
    q_size = width // 4
    q_rows, o_rows = q_size // targets, inner // (4 * targets)

    def first_exchange(sends):
        return lax.ppermute(sends[0], "scene", along_x), lax.ppermute(sends[1], "scene", along_y)

    def first_sum(parts, got, name, cost=LITTLE):
        blocks = [part_now.shape[1:] for part_now in parts[:2]]
        results = [shape(block, bf16) for block in blocks] + [shape(block, f32) for block in blocks]
        return call(first_sum_kernel, results, (parts[2], got[0], parts[3], got[1]), name, cost=cost)

    def second_exchange(sums):
        return lax.ppermute(sums[0], "scene", along_y), lax.ppermute(sums[1], "scene", along_x)

    pairs = groups // 2
    neighbours = [(i, i ^ 1) for i in range(groups)]
    split_rows = {"query": q_rows, "key": q_rows, "value_out": o_rows}

    def last_parts(addends, split, name):
        tile = (addends[0].shape[1], sum(now.shape[2] for now in addends[::2]))
        for bit in reversed(range(1, pairs.bit_length() - 1)):
            send, keep = call(
                functools.partial(tile_halves_kernel, bit),
                [shape((1 << bit, *tile), kind) for kind in (bf16, f32)],
                (scalars, *addends),
                "view_bit_" + name,
                SMEM,
            )
            addends = (keep, lax.ppermute(send, "view", [(i, i ^ (2 << bit)) for i in range(groups)]))
        lanes = tile[0] * tile[1] // (2 * split_rows[name])
        far_same, far_cross, near_cross, mine = call(
            functools.partial(tile_cores_kernel, split),
            [shape((split_rows[name], lanes), kind) for kind in (bf16, bf16, f32, f32)],
            (scalars, *addends),
            "last_parts_" + name,
            SMEM,
        )
        far_same = lax.ppermute(far_same, "view", [(i, i ^ 2) for i in range(groups)])
        far_cross = lax.ppermute(far_cross, ("view", "row"), [(i, i ^ 5) for i in range(targets)])
        near_cross = lax.ppermute(near_cross, "row", swap)
        return mine, far_same, near_cross, far_cross

    tile = (2 * o_rows, width)
    send, keep = call(
        value_out_kernel,
        [shape((2, 2, pairs, *tile), kind) for kind in (bf16, f32)],
        (scalars, normed, normed_far, after(dvalue, dkey), mixed, mixed_other, upstream),
        "grad_value_out",
        SMEM,
        24,
    )
    got = lax.ppermute(send, "view", neighbours)
    def partial(lefts, right, name):
        block = (2, q_size // 2, part)
        results = [shape(block, bf16)] * 2 + [shape(block, f32)] * 2
        parts = call(halves_kernel, results, (scalars, *lefts, right), name, SMEM, 24)
        return parts, first_exchange(parts)

    def view_tiles(sums, got, name):
        send, keep = call(
            view_tiles_kernel,
            [shape((pairs, 2 * q_rows, part), kind) for kind in (bf16, f32)],
            (scalars, sums[2], got[0], sums[3], got[1]),
            name,
            SMEM,
        )
        return keep, lax.ppermute(send, "view", neighbours)

    q_parts, q_got = partial((normed,), after(dquery, send), "grad_query")
    k_parts, k_got = partial((normed, normed_far), after(dkey, q_parts[0]), "grad_key")
    q_sums = first_sum(q_parts, q_got, "first_sum_query")
    q_got = second_exchange(q_sums)
    k_parts[2] = after(k_parts[2], q_sums[0])
    k_sums = first_sum(k_parts, k_got, "first_sum_key")
    k_got = second_exchange(k_sums)
    q_sums[2] = after(q_sums[2], k_sums[0])
    q_addends = view_tiles(q_sums, q_got, "view_tiles_query")
    k_sums[2] = after(k_sums[2], q_addends[0])
    k_addends = view_tiles(k_sums, k_got, "view_tiles_key")
    q_last = last_parts((after(q_addends[0], k_addends[0]), q_addends[1]), row_cores, "query")
    part_shape = (2, pairs, 2 * o_rows, width // 2)
    vo_parts = call(
        view_sum_kernel,
        [shape(part_shape, bf16)] * 2 + [shape(part_shape, f32)] * 2,
        (keep, after(got, q_last[0])),
        "view_sum_value_out",
    )
    vo_got = first_exchange(vo_parts)
    k_last = last_parts((after(k_addends[0], vo_parts[0]), k_addends[1]), row_cores, "key")
    grad_query = call(place_kernel, [shape((q_rows, inner), f32)], (scalars, *q_last), "last_sum_query", SMEM)[0]
    vo_parts[2] = after(vo_parts[2], k_last[0], grad_query)
    vo_sums = first_sum(vo_parts, vo_got, "first_sum_value_out")
    v_got, o_got = second_exchange(vo_sums)
    vo_addends = (after(vo_sums[3], k_last[1], k_last[3]), o_got, vo_sums[2], v_got)
    vo_last = last_parts(vo_addends, value_out_cores, "value_out")
    grad_key = call(place_kernel, [shape((q_rows, inner), f32)], (scalars, *k_last), "last_sum_key", SMEM)[0]
    grad_value, grad_out = call(
        place_value_out_kernel,
        [shape((q_rows, inner), f32), shape((o_rows, width), f32)],
        (scalars, after(vo_last[0], grad_key), *vo_last[1:]),
        "last_sum_value_out",
        SMEM,
    )
    return grad_query, grad_key, grad_value, grad_out


def solution(mesh):
    tokens = P("scene", "view", "row", None, None)
    everywhere = P()
    grads = P(("scene", "view", "row"), None)
    return jax.shard_map(
        shards,
        mesh=mesh,
        in_specs=(
            tokens, everywhere, everywhere, everywhere, everywhere, everywhere, everywhere,
            P("scene", "view", None), P("scene", "view"), tokens,
        ),
        out_specs=(grads, grads, grads, grads),
        check_vma=False,
    )
```

```python
import functools

import jax
import jax.numpy as jnp
from jax import lax
from jax.experimental import pallas as pl
from jax.experimental.pallas import tpu as pltpu
from jax.sharding import PartitionSpec as P

HEAD_DIM = 64
EPSILON = 1e-06
SCALE = HEAD_DIM ** (-0.5)
MASKED = -1e30
MIB = 1024 * 1024
LITTLE = pl.CostEstimate(flops=1, bytes_accessed=1, transcendentals=0)
MUCH = pl.CostEstimate(flops=40_000_000_000, bytes_accessed=1, transcendentals=0)

VMEM = pl.BlockSpec(memory_space=pltpu.VMEM)
SMEM = pl.BlockSpec(memory_space=pltpu.SMEM)


def dot_nn(a, b):
    return lax.dot_general(a, b, (((1,), (0,)), ((), ())), preferred_element_type=jnp.float32)


def dot_nt(a, b):
    return lax.dot_general(a, b, (((1,), (1,)), ((), ())), preferred_element_type=jnp.float32)


def dot_tn(a, b):
    return lax.dot_general(a, b, (((0,), (0,)), ((), ())), preferred_element_type=jnp.float32)


def normalized(tokens, gain):
    x = tokens.astype(jnp.float32)
    mean = jnp.mean(x * x, -1, keepdims=True)
    return (x * lax.rsqrt(mean + EPSILON) * gain).astype(jnp.bfloat16)


def request_kernel(views, slots, groups, partners, request, alive):
    for g in range(groups):
        request[g] = 0
        for u in range(views):
            alive[g * views + u] = 0
    for u in range(views):
        for j in range(slots):
            partner = partners[0, u, j]

            @pl.when(partner >= 0)
            def _():
                group = lax.div(partner, jnp.int32(views))
                request[group] = lax.rem(partner, jnp.int32(views))
                alive[group * views + u] = 1


def pick_kernel(groups, scalars, *refs):
    requests, lat, outgoing = refs[: groups - 1], refs[groups - 1], refs[groups:]
    for request, out in zip(requests, outgoing):
        out[...] = lat[request[scalars[1]]]


def core_half(scalars, size):
    return pl.ds(pl.multiple_of(scalars[0] * size, size), size)


def stacked(x, views):
    tokens, pair = x.shape
    low = (lax.broadcasted_iota(jnp.int32, (1, 1, pair), 2) < pair // 2).astype(x.dtype)
    x = x.reshape(views, tokens // views, pair)
    return jnp.concatenate((x * low, x * (1 - low)), axis=1).reshape(2 * tokens, pair)


def unstacked(x, views):
    rows, pair = x.shape
    low = lax.broadcasted_iota(jnp.int32, (1, 1, pair), 2) < pair // 2
    x = x.reshape(views, 2, rows // (2 * views), pair)
    return jnp.where(low, x[:, 0], x[:, 1]).reshape(rows // 2, pair)


def view_parts(x, views, axis):
    size = x.shape[axis] // views
    return [lax.slice_in_dim(x, u * size, (u + 1) * size, axis=axis) for u in range(views)]


def own_nt(a, b, views):
    pairs = zip(view_parts(a, views, 0), view_parts(b, views, 0))
    return jnp.concatenate([dot_nt(x, y) for x, y in pairs], axis=1)


def own_tn(a, b, views):
    pairs = zip(view_parts(a, views, 1), view_parts(b, views, 0))
    return jnp.concatenate([dot_tn(x, y) for x, y in pairs], axis=0)


def own_nn(a, b, views):
    pairs = zip(view_parts(a, views, 1), view_parts(b, views, 0))
    return jnp.concatenate([dot_nn(x, y) for x, y in pairs], axis=0)


def project_kernel(
    scalars, lat_own, lat_other, cot_own, cot_other, gain, taps, w_query, w_key, w_value, w_out,
    normed_t, keys, values, upstream, query_stack, grad_stack, scores_own, dprob_own, normed,
):
    views, strip, width = lat_own.shape
    scale = gain[...].reshape(1, width)
    row = scalars[0]

    def strip_of(u, half):
        index = 2 * u + (row if half == 0 else 1 - row)
        return pl.ds(pl.multiple_of(index * strip, strip), strip)

    for half, source in enumerate((lat_own, lat_other)):
        for u in range(views):
            normed[strip_of(u, half), :] = normalized(source[u], scale)
    first = row == 0
    chunk = 512
    column = lax.broadcasted_iota(jnp.int32, (strip, 1), 0)
    not_first = (column > 0).astype(jnp.float32)
    not_last = (column < strip - 1).astype(jnp.float32)
    for c in range(0, width, chunk):
        lanes = slice(c, c + chunk)
        tap = taps[:, lanes].astype(jnp.float32)
        top, middle, bottom = tap[0:3], tap[3:6], tap[6:9]
        cross = (jnp.where(first, top, bottom), jnp.where(first, bottom, top))
        for u in range(views):
            strips = [ref[u, :, lanes].astype(jnp.float32) for ref in (cot_own, cot_other)]
            shifted = []
            for x in strips:
                after = pltpu.roll(x, strip - 1, 0) * not_last
                before = pltpu.roll(x, 1, 0) * not_first
                shifted.append((after, x, before))
            for half in range(2):
                total = strips[half]
                for b in range(3):
                    total = total + middle[b : b + 1] * shifted[half][b]
                    total = total + cross[half][b : b + 1] * shifted[1 - half][b]
                upstream[strip_of(u, half), lanes] = total.astype(jnp.bfloat16)
    rows = normed[...]
    normed_t[...] = rows.T
    part = keys.shape[1]
    half = core_half(scalars, part)
    queries = dot_nn(rows, w_query[:, half]).astype(jnp.bfloat16)
    keys[...] = dot_nn(rows, w_key[:, half]).astype(jnp.bfloat16)
    values[...] = dot_nn(rows, w_value[:, half]).astype(jnp.bfloat16)
    out_grad = dot_nt(upstream[...], w_out[half, :]).astype(jnp.bfloat16)
    pair = 2 * HEAD_DIM
    for p in range(part // pair):
        lanes = slice(p * pair, (p + 1) * pair)
        q, g = stacked(queries[:, lanes], views), stacked(out_grad[:, lanes], views)
        query_stack[p], grad_stack[p] = q, g
        scores_own[p] = own_nt(keys[:, lanes], q, views) * SCALE
        dprob_own[p] = own_nt(values[:, lanes], g, views)


def forward_kernel(views, groups, scalars, alive, *refs):
    got_own, got_other, refs = refs[: groups - 1], refs[groups - 1 : 2 * groups - 2], refs[2 * groups - 2 :]
    query_stack, grad_stack, scores_own, values, gain, w_key, w_value, *refs = refs
    normed_far_t, keys_far, values_far, attention_own, attention_far, mixed_t, dvalue, normed_far = refs
    strip = got_own[0].shape[0]
    tokens, part = values.shape
    view_tokens = tokens // views
    here = scalars[1]
    scale_row = gain[...].reshape(1, normed_far.shape[1])
    pair = 2 * HEAD_DIM
    span = 2 * view_tokens
    column_view = lax.broadcasted_iota(jnp.int32, (1, views * span), 1) // span
    slot_alive = []
    for j in range(groups - 1):
        group = lax.bitwise_xor(here, jnp.int32(j + 1))
        start = 2 * j * strip
        normed_far[start : start + strip, :] = normalized(got_own[j][...], scale_row)
        normed_far[start + strip : start + 2 * strip, :] = normalized(got_other[j][...], scale_row)
        taken = jnp.zeros((1, views * span), jnp.int32)
        for u in range(views):
            taken = jnp.where(column_view == u, alive[group * views + u], taken)
        slot_alive.append(taken > 0)
    fetched = normed_far[...]
    normed_far_t[...] = fetched.T
    half = core_half(scalars, part)
    keys_far[...] = dot_nn(fetched, w_key[:, half]).astype(jnp.bfloat16)
    values_far[...] = dot_nn(fetched, w_value[:, half]).astype(jnp.bfloat16)
    for p in range(part // pair):
        lanes = slice(p * pair, (p + 1) * pair)
        q, g, s_own = query_stack[p], grad_stack[p], scores_own[p]
        s_far = dot_nt(keys_far[:, lanes], q) * SCALE
        s_far = jnp.concatenate(
            [
                jnp.where(slot_alive[j], s_far[j * view_tokens : (j + 1) * view_tokens], MASKED)
                for j in range(groups - 1)
            ],
            axis=0,
        )
        highest = jnp.maximum(jnp.max(s_own, 0, keepdims=True), jnp.max(s_far, 0, keepdims=True))
        e_own = jnp.exp(s_own - highest)
        e_far = jnp.exp(s_far - highest)
        inverse = 1.0 / (jnp.sum(e_own, 0, keepdims=True) + jnp.sum(e_far, 0, keepdims=True))
        a_own, a_far = e_own * inverse, e_far * inverse
        attention_own[p], attention_far[p] = a_own, a_far
        a_own, a_far = a_own.astype(jnp.bfloat16), a_far.astype(jnp.bfloat16)
        mix = own_tn(a_own, values[:, lanes], views) + dot_tn(a_far, values_far[:, lanes])
        mixed_t[lanes, :] = unstacked(mix, views).T.astype(jnp.bfloat16)
        dvalue[:tokens, lanes] = own_nn(a_own, g, views).astype(jnp.bfloat16)
        dvalue[tokens:, lanes] = dot_nn(a_far, g).astype(jnp.bfloat16)


def backward_kernel(
    views, query_stack, grad_stack, dprob_own, keys, keys_far, values_far, attention_own, attention_far, dquery, dkey
):
    tokens, part = keys.shape
    pair = 2 * HEAD_DIM
    for p in range(part // pair):
        lanes = slice(p * pair, (p + 1) * pair)
        q, g, dp_own = query_stack[p], grad_stack[p], dprob_own[p]
        a_own, a_far = attention_own[p], attention_far[p]
        dp_far = dot_nt(values_far[:, lanes], g)
        delta = jnp.sum(a_own * dp_own, 0, keepdims=True) + jnp.sum(a_far * dp_far, 0, keepdims=True)
        ds_own = (a_own * (dp_own - delta) * SCALE).astype(jnp.bfloat16)
        ds_far = (a_far * (dp_far - delta) * SCALE).astype(jnp.bfloat16)
        dq = own_tn(ds_own, keys[:, lanes], views) + dot_tn(ds_far, keys_far[:, lanes])
        dquery[:, lanes] = unstacked(dq, views).astype(jnp.bfloat16)
        dkey[:tokens, lanes] = own_nn(ds_own, q, views).astype(jnp.bfloat16)
        dkey[tokens:, lanes] = dot_nn(ds_far, q).astype(jnp.bfloat16)


def times(lefts, right):
    total, start = 0.0, 0
    for left in lefts:
        total = total + dot_nn(left, right[start : start + left.shape[1], :])
        start += left.shape[1]
    return total


def by_quarters(scalars, lefts, right, send, keep, x_first):
    size = send.shape[1]
    x, y = scalars[3], scalars[4]
    for target, first in ((send, 1), (keep, 0)):
        for second in (1, 0):
            dx, dy = (first, second) if x_first else (second, first)
            block = 2 * lax.bitwise_xor(y, jnp.int32(dy)) + lax.bitwise_xor(x, jnp.int32(dx))
            rows = pl.ds(pl.multiple_of(block * size, size), size)
            target[second] = times([left[rows, :] for left in lefts], right).astype(target.dtype)


def query_key_kernel(scalars, normed_t, normed_far_t, dquery, dkey, q_send, k_send, q_keep, k_keep):
    by_quarters(scalars, (normed_t,), dquery, q_send, q_keep, True)
    by_quarters(scalars, (normed_t, normed_far_t), dkey, k_send, k_keep, False)


def value_out_kernel(scalars, normed_t, normed_far_t, dvalue, mine, theirs, upstream, send, keep):
    row, x, y = scalars[0], scalars[3], scalars[4]
    odd = lax.rem(scalars[1], jnp.int32(2)) == 1
    _, _, pairs, size, width = send.shape
    half, quarter = width // 2, width // 4
    places = [(dy, dx, pair) for dy in range(2) for dx in range(2) for pair in range(pairs)]
    rows = {"send": ([], [], []), "keep": ([], [], [])}
    for dy in range(2):
        to_y = lax.bitwise_xor(y, jnp.int32(dy))
        for dx in range(2):
            to_x = lax.bitwise_xor(x, jnp.int32(dx))
            out_rows = pl.ds(pl.multiple_of(to_x * (half // 4), half // 4), half // 4)
            out_block = jnp.where(row == to_y, mine[out_rows, :], theirs[out_rows, :])
            value_rows = pl.ds(pl.multiple_of((2 * to_y + to_x) * quarter, quarter), quarter)
            blocks = (normed_t[value_rows, :], normed_far_t[value_rows, :], out_block)
            for pair in range(pairs):
                for i, block in enumerate(blocks):
                    count = size if i == 2 else 2 * size
                    first = block[2 * pair * count : (2 * pair + 1) * count]
                    second = block[(2 * pair + 1) * count : (2 * pair + 2) * count]
                    rows["send"][i].append(jnp.where(odd, first, second))
                    rows["keep"][i].append(jnp.where(odd, second, first))
    right = upstream[:, core_half(scalars, half)]
    for target, name in ((send, "send"), (keep, "keep")):
        own, far, out = [jnp.concatenate(parts, axis=0) for parts in rows[name]]
        grad_v = times((own, far), dvalue).astype(target.dtype)
        grad_o = dot_nn(out, right).astype(target.dtype)
        for i, place in enumerate(places):
            target[(*place, slice(None), slice(0, half))] = grad_o[i * size : (i + 1) * size]
            for core in range(2):
                columns = slice(half + core * quarter, half + (core + 1) * quarter)
                part = grad_v[(2 * i + core) * size : (2 * i + core + 1) * size]
                target[(*place, slice(None), columns)] = part


def view_sum_kernel(keep, got, x_send, y_send, x_keep, y_keep):
    half = keep.shape[4] // 2
    for second in range(2):
        for target, first in ((x_send, 1), (x_keep, 0)):
            total = keep[second, first, :, :, half:] + got[second, first, :, :, half:].astype(jnp.float32)
            target[second] = total.astype(target.dtype)
        for target, first in ((y_send, 1), (y_keep, 0)):
            total = keep[first, second, :, :, :half] + got[first, second, :, :, :half].astype(jnp.float32)
            target[second] = total.astype(target.dtype)


def first_sum_kernel(x_keep, x_got, y_keep, y_got, x_later, y_later, x_now, y_now):
    for keep, got, later, now in ((x_keep, x_got, x_later, x_now), (y_keep, y_got, y_later, y_now)):
        later[...] = (keep[1] + got[1].astype(jnp.float32)).astype(jnp.bfloat16)
        now[...] = keep[0] + got[0].astype(jnp.float32)


def pack_query_key_kernel(q_now, q_got, k_now, k_got, packed):
    size = q_now.shape[1]
    packed[:, :size] = (q_now[...] + q_got[...].astype(jnp.float32)).astype(jnp.bfloat16)
    packed[:, size:] = (k_now[...] + k_got[...].astype(jnp.float32)).astype(jnp.bfloat16)


def summed_tile(addends, place):
    place = pl.ds(place, 1)
    total = [now[place] + got[place].astype(jnp.float32) for now, got in zip(addends[::2], addends[1::2])]
    return (jnp.concatenate(total, axis=2) if len(total) == 2 else total[0])[0]


def view_bit(scalars, bit):
    return lax.rem(lax.div(scalars[1], jnp.int32(2 << bit)), jnp.int32(2))


def tile_halves_kernel(bit, scalars, *refs):
    addends, (send, keep) = refs[:-2], refs[-2:]
    count = keep.shape[0]
    mine = view_bit(scalars, bit)
    for target, part in ((send, 1 - mine), (keep, mine)):
        for i in range(count):
            target[i] = summed_tile(addends, part * count + i).astype(target.dtype)


def tile_cores_kernel(scalars, *refs):
    addends, (far_same, far_cross, near_cross, mine) = refs[:-4], refs[-4:]
    size, width = mine.shape
    half, quarter = width // 2, width // 4
    bit = view_bit(scalars, 0)
    for place, same, cross in ((1 - bit, far_same, far_cross), (bit, mine, near_cross)):
        total = summed_tile(addends, place)
        parts = []
        for core in range(2):
            value = total[:, half + core * quarter : half + (core + 1) * quarter]
            out = total[core * size : (core + 1) * size, :half]
            parts.append(jnp.concatenate((out, value[:size], value[size:]), axis=1))
        same[...] = jnp.where(scalars[0] == 0, parts[0], parts[1]).astype(same.dtype)
        cross[...] = jnp.where(scalars[0] == 0, parts[1], parts[0]).astype(cross.dtype)


def place_kernel(scalars, mine, far_same, near_cross, far_cross, value, out):
    size, width = mine.shape
    half, quarter = width // 2, width // 4
    for near, far, core in ((mine, far_same, scalars[0]), (near_cross, far_cross, 1 - scalars[0])):
        total = near[...] + far[...].astype(jnp.float32)
        out[:, pl.ds(pl.multiple_of(core * half, half), half)] = total[:, :half]
        columns = pl.ds(pl.multiple_of(core * quarter, quarter), quarter)
        value[:size, columns] = total[:, half : half + quarter]
        value[size:, columns] = total[:, half + quarter :]


def summed_views(rows, packed):
    for r in range(rows):
        total = packed[r].astype(jnp.float32)
        for i in range(r + rows, packed.shape[0], rows):
            total = total + packed[i].astype(jnp.float32)
        yield r, total


def last_query_key_kernel(rows, packed, query, key):
    size = packed.shape[2] // 2
    for r, total in summed_views(rows, packed):
        columns = slice(r * size, (r + 1) * size)
        query[:, columns] = total[:, :size]
        key[:, columns] = total[:, size:]


def params(mebibytes):
    return pltpu.CompilerParams(vmem_limit_bytes=mebibytes * MIB)


def shape(dims, kind):
    return jax.ShapeDtypeStruct(dims, kind)


def shards(latents, norm_gain, w_query, w_key, w_value, w_out, kernel, partners, counts, cotangent):
    views, strip_rows, columns, width = latents.shape[1:]
    inner = w_query.shape[1]
    groups, rows = lax.axis_size("view"), lax.axis_size("row")
    scenes = lax.axis_size("scene")
    assert (strip_rows, rows, scenes) == (1, 2, 4)
    strip = strip_rows * columns
    slots = partners.shape[2]
    part = inner // rows
    tokens = views * 2 * strip
    key_tokens = tokens + (groups - 1) * 2 * strip
    bf16, f32, i32 = jnp.bfloat16, jnp.float32, jnp.int32

    row, view, scene = lax.axis_index("row"), lax.axis_index("view"), lax.axis_index("scene")
    scalars = jnp.stack((row, view, scene, scene % 2, scene // 2)).astype(i32)
    swap = [(0, 1), (1, 0)]
    along_x, along_y = [(i, i ^ 1) for i in range(scenes)], [(i, i ^ 2) for i in range(scenes)]

    request, alive = pl.pallas_call(
        functools.partial(request_kernel, views, slots, groups),
        in_specs=[SMEM],
        out_specs=(SMEM, SMEM),
        out_shape=(shape((groups,), i32), shape((groups * views,), i32)),
        cost_estimate=MUCH,
        compiler_params=params(4),
        name="requests",
    )(partners)
    between = [[(i, i ^ d) for i in range(groups)] for d in range(1, groups)]
    granted = [lax.ppermute(request, "view", pairs) for pairs in between]

    lat = latents[0].reshape(views, strip, width)
    cot = cotangent[0].reshape(views, strip, width)
    lat_other = lax.ppermute(lat, "row", swap)
    cot_other = lax.ppermute(cot, "row", swap)

    outgoing = pl.pallas_call(
        functools.partial(pick_kernel, groups),
        in_specs=[SMEM] * groups + [VMEM],
        out_specs=[VMEM] * (groups - 1),
        out_shape=[shape((strip, width), bf16)] * (groups - 1),
        compiler_params=params(8),
        cost_estimate=MUCH,
        name="pick",
    )(scalars, *granted, lat)
    got_own = [lax.ppermute(part_out, "view", pairs) for part_out, pairs in zip(outgoing, between)]
    head_pairs = part // (2 * HEAD_DIM)
    normed_t, keys, values, upstream, query_stack, grad_stack, scores_own, dprob_own = pl.pallas_call(
        project_kernel,
        in_specs=[SMEM] + [VMEM] * 10,
        out_specs=[VMEM] * 8,
        out_shape=[
            shape((width, tokens), bf16),
            shape((tokens, part), bf16),
            shape((tokens, part), bf16),
            shape((tokens, width), bf16),
            shape((head_pairs, 2 * tokens, 2 * HEAD_DIM), bf16),
            shape((head_pairs, 2 * tokens, 2 * HEAD_DIM), bf16),
            shape((head_pairs, 2 * strip, 2 * tokens), f32),
            shape((head_pairs, 2 * strip, 2 * tokens), f32),
        ],
        scratch_shapes=[pltpu.VMEM((tokens, width), bf16)],
        compiler_params=params(28),
        cost_estimate=LITTLE,
        name="project",
    )(scalars, lat, lat_other, cot, cot_other, norm_gain, kernel, w_query, w_key, w_value, w_out)

    got_own, normed_t = lax.optimization_barrier((got_own, normed_t))
    got_other = [lax.ppermute(got, "row", swap) for got in got_own]

    def call(kernel_body, results, operands, name, first=VMEM, mebibytes=16, cost=LITTLE):
        outputs = pl.pallas_call(
            kernel_body,
            in_specs=[first] + [VMEM] * (len(operands) - 1),
            out_specs=[VMEM] * len(results),
            out_shape=results,
            compiler_params=params(mebibytes),
            cost_estimate=cost,
            name=name,
        )(*operands)
        return list(outputs)

    far_tokens = key_tokens - tokens
    normed_far_t, keys_far, values_far, attention_own, attention_far, mixed_t, dvalue = pl.pallas_call(
        functools.partial(forward_kernel, views, groups),
        in_specs=[SMEM] * 2 + [VMEM] * (2 * groups - 2 + 7),
        out_specs=[VMEM] * 7,
        out_shape=[
            shape((width, far_tokens), bf16),
            shape((far_tokens, part), bf16),
            shape((far_tokens, part), bf16),
            shape((head_pairs, 2 * strip, 2 * tokens), f32),
            shape((head_pairs, far_tokens, 2 * tokens), f32),
            shape((part, tokens), bf16),
            shape((key_tokens, part), bf16),
        ],
        scratch_shapes=[pltpu.VMEM((far_tokens, width), bf16)],
        compiler_params=params(28 + groups // 2),
        cost_estimate=LITTLE,
        name="attention_forward",
    )(
        scalars, alive, *got_own, *got_other, query_stack, grad_stack, scores_own, values, norm_gain, w_key, w_value
    )
    mixed_other = lax.ppermute(mixed_t, "row", swap)
    dquery, dkey = call(
        functools.partial(backward_kernel, views),
        [shape((tokens, part), bf16), shape((key_tokens, part), bf16)],
        (query_stack, grad_stack, dprob_own, keys, keys_far, values_far, attention_own, attention_far),
        "attention_backward",
        mebibytes=28 + groups // 2,
    )

    def after(value, *earlier):
        return lax.optimization_barrier((value, *earlier))[0]

    targets = groups * rows
    q_size = width // 4
    q_rows, o_rows = q_size // targets, inner // (4 * targets)
    q_block = (q_size, part)

    def first_exchange(sends):
        return lax.ppermute(sends[0], "scene", along_x), lax.ppermute(sends[1], "scene", along_y)

    def first_sum(parts, got, name, cost=LITTLE):
        blocks = [part_now.shape[1:] for part_now in parts[:2]]
        results = [shape(block, bf16) for block in blocks] + [shape(block, f32) for block in blocks]
        return call(first_sum_kernel, results, (parts[2], got[0], parts[3], got[1]), name, cost=cost)

    def second_exchange(sums):
        return lax.ppermute(sums[0], "scene", along_y), lax.ppermute(sums[1], "scene", along_x)

    def across_views(packed):
        return lax.all_to_all(packed, ("view", "row"), split_axis=0, concat_axis=0, tiled=True)

    pairs = groups // 2
    tile = (2 * o_rows, width)
    send, keep = call(
        value_out_kernel,
        [shape((2, 2, pairs, *tile), kind) for kind in (bf16, f32)],
        (scalars, normed_t, normed_far_t, after(dvalue, dkey), mixed_t, mixed_other, upstream),
        "grad_value_out",
        SMEM,
        24,
    )
    got = lax.ppermute(send, "view", [(i, i ^ 1) for i in range(groups)])
    results = [shape((2, *q_block), bf16)] * 2 + [shape((2, *q_block), f32)] * 2
    qk_parts = call(
        query_key_kernel, results, (scalars, normed_t, normed_far_t, after(dquery, send), dkey), "grad_query_key", SMEM, 24
    )
    qk_got = first_exchange(qk_parts)
    qk_sums = first_sum(qk_parts, qk_got, "first_sum_query_key")
    qk_got = second_exchange(qk_sums)
    packed = call(
        pack_query_key_kernel,
        [shape((q_size, 2 * part), bf16)],
        (qk_sums[2], qk_got[0], qk_sums[3], qk_got[1]),
        "second_sum_query_key",
    )[0]
    part_shape = (2, pairs, 2 * o_rows, width // 2)
    vo_parts = call(
        view_sum_kernel,
        [shape(part_shape, bf16)] * 2 + [shape(part_shape, f32)] * 2,
        (keep, after(got, packed)),
        "view_sum_value_out",
    )
    vo_got = first_exchange(vo_parts)
    packed = across_views(after(packed, vo_parts[0]).reshape(targets, q_rows, 2 * part))
    grad_query, grad_key = call(
        functools.partial(last_query_key_kernel, rows),
        [shape((q_rows, inner), f32)] * 2,
        (packed,),
        "last_sum_query_key",
    )

    vo_sums = first_sum(vo_parts, vo_got, "first_sum_value_out", MUCH)
    v_got, o_got = second_exchange(vo_sums)
    addends = (vo_sums[3], o_got, vo_sums[2], v_got)
    for bit in reversed(range(1, pairs.bit_length() - 1)):
        send, keep = call(
            functools.partial(tile_halves_kernel, bit),
            [shape((1 << bit, *tile), kind) for kind in (bf16, f32)],
            (scalars, *addends),
            "view_bit_value_out",
            SMEM,
        )
        addends = (keep, lax.ppermute(send, "view", [(i, i ^ (2 << bit)) for i in range(groups)]))
    far_same, far_cross, near_cross, mine = call(
        tile_cores_kernel,
        [shape((o_rows, width), kind) for kind in (bf16, bf16, f32, f32)],
        (scalars, *addends),
        "last_parts_value_out",
        SMEM,
    )
    far_same = lax.ppermute(far_same, "view", [(i, i ^ 2) for i in range(groups)])
    far_cross = lax.ppermute(far_cross, ("view", "row"), [(i, i ^ 5) for i in range(targets)])
    near_cross = lax.ppermute(near_cross, "row", swap)
    grad_value, grad_out = call(
        place_kernel,
        [shape((q_rows, inner), f32), shape((o_rows, width), f32)],
        (scalars, after(mine, grad_key), far_same, near_cross, far_cross),
        "last_sum_value_out",
        SMEM,
    )
    return grad_query, grad_key, grad_value, grad_out


def solution(mesh):
    tokens = P("scene", "view", "row", None, None)
    everywhere = P()
    grads = P(("scene", "view", "row"), None)
    return jax.shard_map(
        shards,
        mesh=mesh,
        in_specs=(
            tokens, everywhere, everywhere, everywhere, everywhere, everywhere, everywhere,
            P("scene", "view", None), P("scene", "view"), tokens,
        ),
        out_specs=(grads, grads, grads, grads),
        check_vma=False,
    )
```

```python
import functools

import jax
import jax.numpy as jnp
from jax import lax
from jax.experimental import pallas as pl
from jax.experimental.pallas import tpu as pltpu
from jax.sharding import PartitionSpec as P

HEAD_DIM = 64
EPSILON = 1e-06
SCALE = HEAD_DIM ** (-0.5)
MASKED = -1e30
MIB = 1024 * 1024
LITTLE = pl.CostEstimate(flops=1, bytes_accessed=1, transcendentals=0)
MUCH = pl.CostEstimate(flops=40_000_000_000, bytes_accessed=1, transcendentals=0)

VMEM = pl.BlockSpec(memory_space=pltpu.VMEM)
SMEM = pl.BlockSpec(memory_space=pltpu.SMEM)


def dot_nn(a, b):
    return lax.dot_general(a, b, (((1,), (0,)), ((), ())), preferred_element_type=jnp.float32)


def dot_nt(a, b):
    return lax.dot_general(a, b, (((1,), (1,)), ((), ())), preferred_element_type=jnp.float32)


def dot_tn(a, b):
    return lax.dot_general(a, b, (((0,), (0,)), ((), ())), preferred_element_type=jnp.float32)


def normalized(tokens, gain):
    x = tokens.astype(jnp.float32)
    mean = jnp.mean(x * x, -1, keepdims=True)
    return (x * lax.rsqrt(mean + EPSILON) * gain).astype(jnp.bfloat16)


def alive_kernel(views, groups, partners, alive):
    for g in range(groups * views):
        alive[g] = 0
    for u in range(views):
        for j in range(partners.shape[2]):
            partner = partners[0, u, j]

            @pl.when(partner >= 0)
            def _():
                alive[lax.div(partner, jnp.int32(views)) * views + u] = 1


def pick_kernel(groups, scalars, *refs):
    tables, lat, outgoing = refs[: groups - 1], refs[groups - 1], refs[groups:]
    views = lat.shape[0]
    for table, out in zip(tables, outgoing):
        wanted = jnp.int32(0)
        for u in range(table.shape[1]):
            for j in range(table.shape[2]):
                partner = table[0, u, j]
                here = (partner >= 0) & (lax.div(partner, jnp.int32(views)) == scalars[1])
                wanted = jnp.where(here, lax.rem(partner, jnp.int32(views)), wanted)
        out[...] = lat[wanted]


def core_half(scalars, size):
    return pl.ds(pl.multiple_of(scalars[0] * size, size), size)


def stacked(x, views):
    tokens, pair = x.shape
    low = (lax.broadcasted_iota(jnp.int32, (1, 1, pair), 2) < pair // 2).astype(x.dtype)
    x = x.reshape(views, tokens // views, pair)
    return jnp.concatenate((x * low, x * (1 - low)), axis=1).reshape(2 * tokens, pair)


def unstacked(x, views):
    rows, pair = x.shape
    low = lax.broadcasted_iota(jnp.int32, (1, 1, pair), 2) < pair // 2
    x = x.reshape(views, 2, rows // (2 * views), pair)
    return jnp.where(low, x[:, 0], x[:, 1]).reshape(rows // 2, pair)


def view_parts(x, views, axis):
    size = x.shape[axis] // views
    return [lax.slice_in_dim(x, u * size, (u + 1) * size, axis=axis) for u in range(views)]


def own_nt(a, b, views):
    pairs = zip(view_parts(a, views, 0), view_parts(b, views, 0))
    return jnp.concatenate([dot_nt(x, y) for x, y in pairs], axis=1)


def own_tn(a, b, views):
    pairs = zip(view_parts(a, views, 1), view_parts(b, views, 0))
    return jnp.concatenate([dot_tn(x, y) for x, y in pairs], axis=0)


def own_nn(a, b, views):
    pairs = zip(view_parts(a, views, 1), view_parts(b, views, 0))
    return jnp.concatenate([dot_nn(x, y) for x, y in pairs], axis=0)


def project_kernel(
    scalars, lat_own, lat_other, cot_own, cot_other, gain, taps, w_query, w_key, w_value, w_out,
    normed_t, keys, values, upstream, query_stack, grad_stack, scores_own, dprob_own, normed,
):
    views, strip, width = lat_own.shape
    scale = gain[...].reshape(1, width)
    row = scalars[0]

    def strip_of(u, half):
        index = 2 * u + (row if half == 0 else 1 - row)
        return pl.ds(pl.multiple_of(index * strip, strip), strip)

    for half, source in enumerate((lat_own, lat_other)):
        for u in range(views):
            normed[strip_of(u, half), :] = normalized(source[u], scale)
    first = row == 0
    chunk = 512
    column = lax.broadcasted_iota(jnp.int32, (strip, 1), 0)
    not_first = (column > 0).astype(jnp.float32)
    not_last = (column < strip - 1).astype(jnp.float32)
    for c in range(0, width, chunk):
        lanes = slice(c, c + chunk)
        tap = taps[:, lanes].astype(jnp.float32)
        top, middle, bottom = tap[0:3], tap[3:6], tap[6:9]
        cross = (jnp.where(first, top, bottom), jnp.where(first, bottom, top))
        for u in range(views):
            strips = [ref[u, :, lanes].astype(jnp.float32) for ref in (cot_own, cot_other)]
            shifted = []
            for x in strips:
                after = pltpu.roll(x, strip - 1, 0) * not_last
                before = pltpu.roll(x, 1, 0) * not_first
                shifted.append((after, x, before))
            for half in range(2):
                total = strips[half]
                for b in range(3):
                    total = total + middle[b : b + 1] * shifted[half][b]
                    total = total + cross[half][b : b + 1] * shifted[1 - half][b]
                upstream[strip_of(u, half), lanes] = total.astype(jnp.bfloat16)
    rows = normed[...]
    normed_t[...] = rows.T
    part = keys.shape[1]
    half = core_half(scalars, part)
    queries = dot_nn(rows, w_query[:, half]).astype(jnp.bfloat16)
    keys[...] = dot_nn(rows, w_key[:, half]).astype(jnp.bfloat16)
    values[...] = dot_nn(rows, w_value[:, half]).astype(jnp.bfloat16)
    out_grad = dot_nt(upstream[...], w_out[half, :]).astype(jnp.bfloat16)
    pair = 2 * HEAD_DIM
    for p in range(part // pair):
        lanes = slice(p * pair, (p + 1) * pair)
        q, g = stacked(queries[:, lanes], views), stacked(out_grad[:, lanes], views)
        query_stack[p], grad_stack[p] = q, g
        scores_own[p] = own_nt(keys[:, lanes], q, views) * SCALE
        dprob_own[p] = own_nt(values[:, lanes], g, views)


def forward_kernel(views, groups, scalars, alive, *refs):
    got_own, got_other, refs = refs[: groups - 1], refs[groups - 1 : 2 * groups - 2], refs[2 * groups - 2 :]
    query_stack, grad_stack, scores_own, values, gain, w_key, w_value, *refs = refs
    normed_far_t, keys_far, values_far, attention_own, attention_far, mixed_t, dvalue, normed_far = refs
    strip = got_own[0].shape[0]
    tokens, part = values.shape
    view_tokens = tokens // views
    here = scalars[1]
    scale_row = gain[...].reshape(1, normed_far.shape[1])
    pair = 2 * HEAD_DIM
    span = 2 * view_tokens
    column_view = lax.broadcasted_iota(jnp.int32, (1, views * span), 1) // span
    slot_alive = []
    for j in range(groups - 1):
        group = lax.bitwise_xor(here, jnp.int32(groups - 1 - j))
        start = 2 * j * strip
        normed_far[start : start + strip, :] = normalized(got_own[j][...], scale_row)
        normed_far[start + strip : start + 2 * strip, :] = normalized(got_other[j][...], scale_row)
        taken = jnp.zeros((1, views * span), jnp.int32)
        for u in range(views):
            taken = jnp.where(column_view == u, alive[group * views + u], taken)
        slot_alive.append(taken > 0)
    fetched = normed_far[...]
    normed_far_t[...] = fetched.T
    half = core_half(scalars, part)
    keys_far[...] = dot_nn(fetched, w_key[:, half]).astype(jnp.bfloat16)
    values_far[...] = dot_nn(fetched, w_value[:, half]).astype(jnp.bfloat16)
    for p in range(part // pair):
        lanes = slice(p * pair, (p + 1) * pair)
        q, g, s_own = query_stack[p], grad_stack[p], scores_own[p]
        s_far = dot_nt(keys_far[:, lanes], q) * SCALE
        s_far = jnp.concatenate(
            [
                jnp.where(slot_alive[j], s_far[j * view_tokens : (j + 1) * view_tokens], MASKED)
                for j in range(groups - 1)
            ],
            axis=0,
        )
        highest = jnp.maximum(jnp.max(s_own, 0, keepdims=True), jnp.max(s_far, 0, keepdims=True))
        e_own = jnp.exp(s_own - highest)
        e_far = jnp.exp(s_far - highest)
        inverse = 1.0 / (jnp.sum(e_own, 0, keepdims=True) + jnp.sum(e_far, 0, keepdims=True))
        a_own, a_far = e_own * inverse, e_far * inverse
        attention_own[p], attention_far[p] = a_own, a_far
        a_own, a_far = a_own.astype(jnp.bfloat16), a_far.astype(jnp.bfloat16)
        mix = own_tn(a_own, values[:, lanes], views) + dot_tn(a_far, values_far[:, lanes])
        mixed_t[lanes, :] = unstacked(mix, views).T.astype(jnp.bfloat16)
        dvalue[:tokens, lanes] = own_nn(a_own, g, views).astype(jnp.bfloat16)
        dvalue[tokens:, lanes] = dot_nn(a_far, g).astype(jnp.bfloat16)


def backward_kernel(
    views, query_stack, grad_stack, dprob_own, keys, keys_far, values_far, attention_own, attention_far, dquery, dkey
):
    tokens, part = keys.shape
    pair = 2 * HEAD_DIM
    for p in range(part // pair):
        lanes = slice(p * pair, (p + 1) * pair)
        q, g, dp_own = query_stack[p], grad_stack[p], dprob_own[p]
        a_own, a_far = attention_own[p], attention_far[p]
        dp_far = dot_nt(values_far[:, lanes], g)
        delta = jnp.sum(a_own * dp_own, 0, keepdims=True) + jnp.sum(a_far * dp_far, 0, keepdims=True)
        ds_own = (a_own * (dp_own - delta) * SCALE).astype(jnp.bfloat16)
        ds_far = (a_far * (dp_far - delta) * SCALE).astype(jnp.bfloat16)
        dq = own_tn(ds_own, keys[:, lanes], views) + dot_tn(ds_far, keys_far[:, lanes])
        dquery[:, lanes] = unstacked(dq, views).astype(jnp.bfloat16)
        dkey[:tokens, lanes] = own_nn(ds_own, q, views).astype(jnp.bfloat16)
        dkey[tokens:, lanes] = dot_nn(ds_far, q).astype(jnp.bfloat16)


def times(lefts, right):
    total, start = 0.0, 0
    for left in lefts:
        total = total + dot_nn(left, right[start : start + left.shape[1], :])
        start += left.shape[1]
    return total


def by_quarters(scalars, lefts, right, send, keep, x_first):
    size = send.shape[1]
    x, y = scalars[3], scalars[4]
    for target, first in ((send, 1), (keep, 0)):
        for second in (1, 0):
            dx, dy = (first, second) if x_first else (second, first)
            block = 2 * lax.bitwise_xor(y, jnp.int32(dy)) + lax.bitwise_xor(x, jnp.int32(dx))
            rows = pl.ds(pl.multiple_of(block * size, size), size)
            target[second] = times([left[rows, :] for left in lefts], right).astype(target.dtype)


def query_key_kernel(scalars, normed_t, normed_far_t, dquery, dkey, q_send, k_send, q_keep, k_keep):
    by_quarters(scalars, (normed_t,), dquery, q_send, q_keep, True)
    by_quarters(scalars, (normed_t, normed_far_t), dkey, k_send, k_keep, False)


def value_out_kernel(scalars, normed_t, normed_far_t, dvalue, mine, theirs, upstream, send, keep):
    row, x, y = scalars[0], scalars[3], scalars[4]
    odd = lax.rem(scalars[1], jnp.int32(2)) == 1
    _, _, pairs, size, width = send.shape
    half, quarter = width // 2, width // 4
    places = [(dy, dx, pair) for dy in range(2) for dx in range(2) for pair in range(pairs)]
    rows = {"send": ([], [], []), "keep": ([], [], [])}
    for dy in range(2):
        to_y = lax.bitwise_xor(y, jnp.int32(dy))
        for dx in range(2):
            to_x = lax.bitwise_xor(x, jnp.int32(dx))
            out_rows = pl.ds(pl.multiple_of(to_x * (half // 4), half // 4), half // 4)
            out_block = jnp.where(row == to_y, mine[out_rows, :], theirs[out_rows, :])
            value_rows = pl.ds(pl.multiple_of((2 * to_y + to_x) * quarter, quarter), quarter)
            blocks = (normed_t[value_rows, :], normed_far_t[value_rows, :], out_block)
            for pair in range(pairs):
                for i, block in enumerate(blocks):
                    count = size if i == 2 else 2 * size
                    first = block[2 * pair * count : (2 * pair + 1) * count]
                    second = block[(2 * pair + 1) * count : (2 * pair + 2) * count]
                    rows["send"][i].append(jnp.where(odd, first, second))
                    rows["keep"][i].append(jnp.where(odd, second, first))
    right = upstream[:, core_half(scalars, half)]
    for target, name in ((send, "send"), (keep, "keep")):
        own, far, out = [jnp.concatenate(parts, axis=0) for parts in rows[name]]
        grad_v = times((own, far), dvalue).astype(target.dtype)
        grad_o = dot_nn(out, right).astype(target.dtype)
        for i, place in enumerate(places):
            target[(*place, slice(None), slice(0, half))] = grad_o[i * size : (i + 1) * size]
            for core in range(2):
                columns = slice(half + core * quarter, half + (core + 1) * quarter)
                part = grad_v[(2 * i + core) * size : (2 * i + core + 1) * size]
                target[(*place, slice(None), columns)] = part


def view_sum_kernel(keep, got, x_send, y_send, x_keep, y_keep):
    half = keep.shape[4] // 2
    for second in range(2):
        for target, first in ((x_send, 1), (x_keep, 0)):
            total = keep[second, first, :, :, half:] + got[second, first, :, :, half:].astype(jnp.float32)
            target[second] = total.astype(target.dtype)
        for target, first in ((y_send, 1), (y_keep, 0)):
            total = keep[first, second, :, :, :half] + got[first, second, :, :, :half].astype(jnp.float32)
            target[second] = total.astype(target.dtype)


def first_sum_kernel(x_keep, x_got, y_keep, y_got, x_later, y_later, x_now, y_now):
    for keep, got, later, now in ((x_keep, x_got, x_later, x_now), (y_keep, y_got, y_later, y_now)):
        later[...] = (keep[1] + got[1].astype(jnp.float32)).astype(jnp.bfloat16)
        now[...] = keep[0] + got[0].astype(jnp.float32)


def pack_query_key_kernel(q_now, q_got, k_now, k_got, packed):
    size = q_now.shape[1]
    packed[:, :size] = (q_now[...] + q_got[...].astype(jnp.float32)).astype(jnp.bfloat16)
    packed[:, size:] = (k_now[...] + k_got[...].astype(jnp.float32)).astype(jnp.bfloat16)


def summed_tile(addends, place):
    place = pl.ds(place, 1)
    total = [now[place] + got[place].astype(jnp.float32) for now, got in zip(addends[::2], addends[1::2])]
    return (jnp.concatenate(total, axis=2) if len(total) == 2 else total[0])[0]


def view_bit(scalars, bit):
    return lax.rem(lax.div(scalars[1], jnp.int32(2 << bit)), jnp.int32(2))


def tile_halves_kernel(bit, scalars, *refs):
    addends, (send, keep) = refs[:-2], refs[-2:]
    count = keep.shape[0]
    mine = view_bit(scalars, bit)
    for target, part in ((send, 1 - mine), (keep, mine)):
        for i in range(count):
            target[i] = summed_tile(addends, part * count + i).astype(target.dtype)


def tile_cores_kernel(scalars, *refs):
    addends, (far_same, far_cross, near_cross, mine) = refs[:-4], refs[-4:]
    size, width = mine.shape
    half, quarter = width // 2, width // 4
    bit = view_bit(scalars, 0)
    for place, same, cross in ((1 - bit, far_same, far_cross), (bit, mine, near_cross)):
        total = summed_tile(addends, place)
        parts = []
        for core in range(2):
            value = total[:, half + core * quarter : half + (core + 1) * quarter]
            out = total[core * size : (core + 1) * size, :half]
            parts.append(jnp.concatenate((out, value[:size], value[size:]), axis=1))
        same[...] = jnp.where(scalars[0] == 0, parts[0], parts[1]).astype(same.dtype)
        cross[...] = jnp.where(scalars[0] == 0, parts[1], parts[0]).astype(cross.dtype)


def place_kernel(scalars, mine, far_same, near_cross, far_cross, value, out):
    size, width = mine.shape
    half, quarter = width // 2, width // 4
    for near, far, core in ((mine, far_same, scalars[0]), (near_cross, far_cross, 1 - scalars[0])):
        total = near[...] + far[...].astype(jnp.float32)
        out[:, pl.ds(pl.multiple_of(core * half, half), half)] = total[:, :half]
        columns = pl.ds(pl.multiple_of(core * quarter, quarter), quarter)
        value[:size, columns] = total[:, half : half + quarter]
        value[size:, columns] = total[:, half + quarter :]


def summed_views(rows, packed):
    for r in range(rows):
        total = packed[r].astype(jnp.float32)
        for i in range(r + rows, packed.shape[0], rows):
            total = total + packed[i].astype(jnp.float32)
        yield r, total


def last_query_key_kernel(rows, packed, query, key):
    size = packed.shape[2] // 2
    for r, total in summed_views(rows, packed):
        columns = slice(r * size, (r + 1) * size)
        query[:, columns] = total[:, :size]
        key[:, columns] = total[:, size:]


def params(mebibytes):
    return pltpu.CompilerParams(vmem_limit_bytes=mebibytes * MIB)


def shape(dims, kind):
    return jax.ShapeDtypeStruct(dims, kind)


def shards(latents, norm_gain, w_query, w_key, w_value, w_out, kernel, partners, counts, cotangent):
    views, strip_rows, columns, width = latents.shape[1:]
    inner = w_query.shape[1]
    groups, rows = lax.axis_size("view"), lax.axis_size("row")
    scenes = lax.axis_size("scene")
    assert (strip_rows, rows, scenes) == (1, 2, 4)
    strip = strip_rows * columns
    part = inner // rows
    tokens = views * 2 * strip
    key_tokens = tokens + (groups - 1) * 2 * strip
    bf16, f32, i32 = jnp.bfloat16, jnp.float32, jnp.int32

    row, view, scene = lax.axis_index("row"), lax.axis_index("view"), lax.axis_index("scene")
    scalars = jnp.stack((row, view, scene, scene % 2, scene // 2)).astype(i32)
    swap = [(0, 1), (1, 0)]
    along_x, along_y = [(i, i ^ 1) for i in range(scenes)], [(i, i ^ 2) for i in range(scenes)]

    alive = pl.pallas_call(
        functools.partial(alive_kernel, views, groups),
        in_specs=[SMEM],
        out_specs=SMEM,
        out_shape=shape((groups * views,), i32),
        cost_estimate=MUCH,
        compiler_params=params(4),
        name="alive",
    )(partners)
    between = [[(i, i ^ d) for i in range(groups)] for d in reversed(range(1, groups))]
    granted = [lax.ppermute(partners, "view", pairs) for pairs in between]

    granted, alive = lax.optimization_barrier((granted, alive))
    lat = latents[0].reshape(views, strip, width)
    cot = cotangent[0].reshape(views, strip, width)
    lat_other = lax.ppermute(lat, "row", swap)
    cot_other = lax.ppermute(cot, "row", swap)

    outgoing = pl.pallas_call(
        functools.partial(pick_kernel, groups),
        in_specs=[SMEM] * groups + [VMEM],
        out_specs=[VMEM] * (groups - 1),
        out_shape=[shape((strip, width), bf16)] * (groups - 1),
        compiler_params=params(8),
        cost_estimate=MUCH,
        name="pick",
    )(scalars, *granted, lat)
    got_own = [lax.ppermute(part_out, "view", pairs) for part_out, pairs in zip(outgoing, between)]
    head_pairs = part // (2 * HEAD_DIM)
    normed_t, keys, values, upstream, query_stack, grad_stack, scores_own, dprob_own = pl.pallas_call(
        project_kernel,
        in_specs=[SMEM] + [VMEM] * 10,
        out_specs=[VMEM] * 8,
        out_shape=[
            shape((width, tokens), bf16),
            shape((tokens, part), bf16),
            shape((tokens, part), bf16),
            shape((tokens, width), bf16),
            shape((head_pairs, 2 * tokens, 2 * HEAD_DIM), bf16),
            shape((head_pairs, 2 * tokens, 2 * HEAD_DIM), bf16),
            shape((head_pairs, 2 * strip, 2 * tokens), f32),
            shape((head_pairs, 2 * strip, 2 * tokens), f32),
        ],
        scratch_shapes=[pltpu.VMEM((tokens, width), bf16)],
        compiler_params=params(28),
        cost_estimate=LITTLE,
        name="project",
    )(scalars, lat, lat_other, cot, cot_other, norm_gain, kernel, w_query, w_key, w_value, w_out)

    got_own, normed_t = lax.optimization_barrier((got_own, normed_t))
    got_other = [lax.ppermute(got, "row", swap) for got in got_own]

    def call(kernel_body, results, operands, name, first=VMEM, mebibytes=16, cost=LITTLE):
        outputs = pl.pallas_call(
            kernel_body,
            in_specs=[first] + [VMEM] * (len(operands) - 1),
            out_specs=[VMEM] * len(results),
            out_shape=results,
            compiler_params=params(mebibytes),
            cost_estimate=cost,
            name=name,
        )(*operands)
        return list(outputs)

    far_tokens = key_tokens - tokens
    normed_far_t, keys_far, values_far, attention_own, attention_far, mixed_t, dvalue = pl.pallas_call(
        functools.partial(forward_kernel, views, groups),
        in_specs=[SMEM] * 2 + [VMEM] * (2 * groups - 2 + 7),
        out_specs=[VMEM] * 7,
        out_shape=[
            shape((width, far_tokens), bf16),
            shape((far_tokens, part), bf16),
            shape((far_tokens, part), bf16),
            shape((head_pairs, 2 * strip, 2 * tokens), f32),
            shape((head_pairs, far_tokens, 2 * tokens), f32),
            shape((part, tokens), bf16),
            shape((key_tokens, part), bf16),
        ],
        scratch_shapes=[pltpu.VMEM((far_tokens, width), bf16)],
        compiler_params=params(28 + groups // 2),
        cost_estimate=LITTLE,
        name="attention_forward",
    )(
        scalars, alive, *got_own, *got_other, query_stack, grad_stack, scores_own, values, norm_gain, w_key, w_value
    )
    mixed_other = lax.ppermute(mixed_t, "row", swap)
    dquery, dkey = call(
        functools.partial(backward_kernel, views),
        [shape((tokens, part), bf16), shape((key_tokens, part), bf16)],
        (query_stack, grad_stack, dprob_own, keys, keys_far, values_far, attention_own, attention_far),
        "attention_backward",
        mebibytes=28 + groups // 2,
    )

    def after(value, *earlier):
        return lax.optimization_barrier((value, *earlier))[0]

    targets = groups * rows
    q_size = width // 4
    q_rows, o_rows = q_size // targets, inner // (4 * targets)
    q_block = (q_size, part)

    def first_exchange(sends):
        return lax.ppermute(sends[0], "scene", along_x), lax.ppermute(sends[1], "scene", along_y)

    def first_sum(parts, got, name, cost=LITTLE):
        blocks = [part_now.shape[1:] for part_now in parts[:2]]
        results = [shape(block, bf16) for block in blocks] + [shape(block, f32) for block in blocks]
        return call(first_sum_kernel, results, (parts[2], got[0], parts[3], got[1]), name, cost=cost)

    def second_exchange(sums):
        return lax.ppermute(sums[0], "scene", along_y), lax.ppermute(sums[1], "scene", along_x)

    def across_views(packed):
        return lax.all_to_all(packed, ("view", "row"), split_axis=0, concat_axis=0, tiled=True)

    pairs = groups // 2
    tile = (2 * o_rows, width)
    send, keep = call(
        value_out_kernel,
        [shape((2, 2, pairs, *tile), kind) for kind in (bf16, f32)],
        (scalars, normed_t, normed_far_t, after(dvalue, dkey), mixed_t, mixed_other, upstream),
        "grad_value_out",
        SMEM,
        24,
    )
    got = lax.ppermute(send, "view", [(i, i ^ 1) for i in range(groups)])
    results = [shape((2, *q_block), bf16)] * 2 + [shape((2, *q_block), f32)] * 2
    qk_parts = call(
        query_key_kernel, results, (scalars, normed_t, normed_far_t, after(dquery, send), dkey), "grad_query_key", SMEM, 24
    )
    qk_got = first_exchange(qk_parts)
    qk_sums = first_sum(qk_parts, qk_got, "first_sum_query_key")
    qk_got = second_exchange(qk_sums)
    packed = call(
        pack_query_key_kernel,
        [shape((q_size, 2 * part), bf16)],
        (qk_sums[2], qk_got[0], qk_sums[3], qk_got[1]),
        "second_sum_query_key",
    )[0]
    part_shape = (2, pairs, 2 * o_rows, width // 2)
    vo_parts = call(
        view_sum_kernel,
        [shape(part_shape, bf16)] * 2 + [shape(part_shape, f32)] * 2,
        (keep, after(got, packed)),
        "view_sum_value_out",
    )
    vo_got = first_exchange(vo_parts)
    packed = across_views(after(packed, vo_parts[0]).reshape(targets, q_rows, 2 * part))
    grad_query, grad_key = call(
        functools.partial(last_query_key_kernel, rows),
        [shape((q_rows, inner), f32)] * 2,
        (packed,),
        "last_sum_query_key",
    )

    vo_sums = first_sum(vo_parts, vo_got, "first_sum_value_out", MUCH)
    v_got, o_got = second_exchange(vo_sums)
    addends = (vo_sums[3], o_got, vo_sums[2], v_got)
    for bit in reversed(range(1, pairs.bit_length() - 1)):
        send, keep = call(
            functools.partial(tile_halves_kernel, bit),
            [shape((1 << bit, *tile), kind) for kind in (bf16, f32)],
            (scalars, *addends),
            "view_bit_value_out",
            SMEM,
        )
        addends = (keep, lax.ppermute(send, "view", [(i, i ^ (2 << bit)) for i in range(groups)]))
    far_same, far_cross, near_cross, mine = call(
        tile_cores_kernel,
        [shape((o_rows, width), kind) for kind in (bf16, bf16, f32, f32)],
        (scalars, *addends),
        "last_parts_value_out",
        SMEM,
    )
    far_same = lax.ppermute(far_same, "view", [(i, i ^ 2) for i in range(groups)])
    far_cross = lax.ppermute(far_cross, ("view", "row"), [(i, i ^ 5) for i in range(targets)])
    near_cross = lax.ppermute(near_cross, "row", swap)
    grad_value, grad_out = call(
        place_kernel,
        [shape((q_rows, inner), f32), shape((o_rows, width), f32)],
        (scalars, after(mine, grad_key), far_same, near_cross, far_cross),
        "last_sum_value_out",
        SMEM,
    )
    return grad_query, grad_key, grad_value, grad_out


def solution(mesh):
    tokens = P("scene", "view", "row", None, None)
    everywhere = P()
    grads = P(("scene", "view", "row"), None)
    return jax.shard_map(
        shards,
        mesh=mesh,
        in_specs=(
            tokens, everywhere, everywhere, everywhere, everywhere, everywhere, everywhere,
            P("scene", "view", None), P("scene", "view"), tokens,
        ),
        out_specs=(grads, grads, grads, grads),
        check_vma=False,
    )
```

```python
import functools

import jax
import jax.numpy as jnp
from jax import lax
from jax.experimental import pallas as pl
from jax.experimental.pallas import tpu as pltpu
from jax.sharding import PartitionSpec as P

HEAD_DIM = 64
EPSILON = 1e-06
SCALE = HEAD_DIM ** (-0.5)
MASKED = -1e30
MIB = 1024 * 1024
LITTLE = pl.CostEstimate(flops=1, bytes_accessed=1, transcendentals=0)
MUCH = pl.CostEstimate(flops=40_000_000_000, bytes_accessed=1, transcendentals=0)

VMEM = pl.BlockSpec(memory_space=pltpu.VMEM)
SMEM = pl.BlockSpec(memory_space=pltpu.SMEM)


def dot_nn(a, b):
    return lax.dot_general(a, b, (((1,), (0,)), ((), ())), preferred_element_type=jnp.float32)


def dot_nt(a, b):
    return lax.dot_general(a, b, (((1,), (1,)), ((), ())), preferred_element_type=jnp.float32)


def dot_tn(a, b):
    return lax.dot_general(a, b, (((0,), (0,)), ((), ())), preferred_element_type=jnp.float32)


def normalized(tokens, gain):
    x = tokens.astype(jnp.float32)
    mean = jnp.mean(x * x, -1, keepdims=True)
    return (x * lax.rsqrt(mean + EPSILON) * gain).astype(jnp.bfloat16)


def alive_kernel(views, groups, partners, alive):
    for g in range(groups * views):
        alive[g] = 0
    for u in range(views):
        for j in range(partners.shape[2]):
            partner = partners[0, u, j]

            @pl.when(partner >= 0)
            def _():
                alive[lax.div(partner, jnp.int32(views)) * views + u] = 1


def pick_kernel(groups, scalars, *refs):
    tables, lat, outgoing = refs[: groups - 1], refs[groups - 1], refs[groups:]
    views = lat.shape[0]
    for table, out in zip(tables, outgoing):
        wanted = jnp.int32(0)
        for u in range(table.shape[1]):
            for j in range(table.shape[2]):
                partner = table[0, u, j]
                here = (partner >= 0) & (lax.div(partner, jnp.int32(views)) == scalars[1])
                wanted = jnp.where(here, lax.rem(partner, jnp.int32(views)), wanted)
        out[...] = lat[wanted]


def core_half(scalars, size):
    return pl.ds(pl.multiple_of(scalars[0] * size, size), size)


def stacked(x, views):
    tokens, pair = x.shape
    low = (lax.broadcasted_iota(jnp.int32, (1, 1, pair), 2) < pair // 2).astype(x.dtype)
    x = x.reshape(views, tokens // views, pair)
    return jnp.concatenate((x * low, x * (1 - low)), axis=1).reshape(2 * tokens, pair)


def unstacked(x, views):
    rows, pair = x.shape
    low = lax.broadcasted_iota(jnp.int32, (1, 1, pair), 2) < pair // 2
    x = x.reshape(views, 2, rows // (2 * views), pair)
    return jnp.where(low, x[:, 0], x[:, 1]).reshape(rows // 2, pair)


def view_parts(x, views, axis):
    size = x.shape[axis] // views
    return [lax.slice_in_dim(x, u * size, (u + 1) * size, axis=axis) for u in range(views)]


def own_nt(a, b, views):
    pairs = zip(view_parts(a, views, 0), view_parts(b, views, 0))
    return jnp.concatenate([dot_nt(x, y) for x, y in pairs], axis=1)


def own_tn(a, b, views):
    pairs = zip(view_parts(a, views, 1), view_parts(b, views, 0))
    return jnp.concatenate([dot_tn(x, y) for x, y in pairs], axis=0)


def own_nn(a, b, views):
    pairs = zip(view_parts(a, views, 1), view_parts(b, views, 0))
    return jnp.concatenate([dot_nn(x, y) for x, y in pairs], axis=0)


def project_kernel(
    scalars, lat_own, lat_other, cot_own, cot_other, gain, taps, w_query, w_key, w_value, w_out,
    normed_t, keys, values, upstream, query_stack, grad_stack, scores_own, dprob_own, normed,
):
    views, strip, width = lat_own.shape
    scale = gain[...].reshape(1, width)
    row = scalars[0]

    def strip_of(u, half):
        index = 2 * u + (row if half == 0 else 1 - row)
        return pl.ds(pl.multiple_of(index * strip, strip), strip)

    for half, source in enumerate((lat_own, lat_other)):
        for u in range(views):
            normed[strip_of(u, half), :] = normalized(source[u], scale)
    first = row == 0
    chunk = 512
    column = lax.broadcasted_iota(jnp.int32, (strip, 1), 0)
    not_first = (column > 0).astype(jnp.float32)
    not_last = (column < strip - 1).astype(jnp.float32)
    for c in range(0, width, chunk):
        lanes = slice(c, c + chunk)
        tap = taps[:, lanes].astype(jnp.float32)
        top, middle, bottom = tap[0:3], tap[3:6], tap[6:9]
        cross = (jnp.where(first, top, bottom), jnp.where(first, bottom, top))
        for u in range(views):
            strips = [ref[u, :, lanes].astype(jnp.float32) for ref in (cot_own, cot_other)]
            shifted = []
            for x in strips:
                after = pltpu.roll(x, strip - 1, 0) * not_last
                before = pltpu.roll(x, 1, 0) * not_first
                shifted.append((after, x, before))
            for half in range(2):
                total = strips[half]
                for b in range(3):
                    total = total + middle[b : b + 1] * shifted[half][b]
                    total = total + cross[half][b : b + 1] * shifted[1 - half][b]
                upstream[strip_of(u, half), lanes] = total.astype(jnp.bfloat16)
    rows = normed[...]
    normed_t[...] = rows.T
    part = keys.shape[1]
    half = core_half(scalars, part)
    queries = dot_nn(rows, w_query[:, half]).astype(jnp.bfloat16)
    keys[...] = dot_nn(rows, w_key[:, half]).astype(jnp.bfloat16)
    values[...] = dot_nn(rows, w_value[:, half]).astype(jnp.bfloat16)
    out_grad = dot_nt(upstream[...], w_out[half, :]).astype(jnp.bfloat16)
    pair = 2 * HEAD_DIM
    for p in range(part // pair):
        lanes = slice(p * pair, (p + 1) * pair)
        q, g = stacked(queries[:, lanes], views), stacked(out_grad[:, lanes], views)
        query_stack[p], grad_stack[p] = q, g
        scores_own[p] = own_nt(keys[:, lanes], q, views) * SCALE
        dprob_own[p] = own_nt(values[:, lanes], g, views)


def forward_kernel(views, groups, scalars, alive, *refs):
    got_own, got_other, refs = refs[: groups - 1], refs[groups - 1 : 2 * groups - 2], refs[2 * groups - 2 :]
    query_stack, grad_stack, scores_own, values, gain, w_key, w_value, *refs = refs
    normed_far_t, keys_far, values_far, attention_own, attention_far, mixed_t, dvalue, normed_far = refs
    strip = got_own[0].shape[0]
    tokens, part = values.shape
    view_tokens = tokens // views
    here = scalars[1]
    scale_row = gain[...].reshape(1, normed_far.shape[1])
    pair = 2 * HEAD_DIM
    span = 2 * view_tokens
    column_view = lax.broadcasted_iota(jnp.int32, (1, views * span), 1) // span
    slot_alive = []
    for j in range(groups - 1):
        group = lax.bitwise_xor(here, jnp.int32(groups - 1 - j))
        start = 2 * j * strip
        normed_far[start : start + strip, :] = normalized(got_own[j][...], scale_row)
        normed_far[start + strip : start + 2 * strip, :] = normalized(got_other[j][...], scale_row)
        taken = jnp.zeros((1, views * span), jnp.int32)
        for u in range(views):
            taken = jnp.where(column_view == u, alive[group * views + u], taken)
        slot_alive.append(taken > 0)
    fetched = normed_far[...]
    normed_far_t[...] = fetched.T
    half = core_half(scalars, part)
    keys_far[...] = dot_nn(fetched, w_key[:, half]).astype(jnp.bfloat16)
    values_far[...] = dot_nn(fetched, w_value[:, half]).astype(jnp.bfloat16)
    for p in range(part // pair):
        lanes = slice(p * pair, (p + 1) * pair)
        q, g, s_own = query_stack[p], grad_stack[p], scores_own[p]
        s_far = dot_nt(keys_far[:, lanes], q) * SCALE
        s_far = jnp.concatenate(
            [
                jnp.where(slot_alive[j], s_far[j * view_tokens : (j + 1) * view_tokens], MASKED)
                for j in range(groups - 1)
            ],
            axis=0,
        )
        highest = jnp.maximum(jnp.max(s_own, 0, keepdims=True), jnp.max(s_far, 0, keepdims=True))
        e_own = jnp.exp(s_own - highest)
        e_far = jnp.exp(s_far - highest)
        inverse = 1.0 / (jnp.sum(e_own, 0, keepdims=True) + jnp.sum(e_far, 0, keepdims=True))
        a_own, a_far = e_own * inverse, e_far * inverse
        attention_own[p], attention_far[p] = a_own, a_far
        a_own, a_far = a_own.astype(jnp.bfloat16), a_far.astype(jnp.bfloat16)
        mix = own_tn(a_own, values[:, lanes], views) + dot_tn(a_far, values_far[:, lanes])
        mixed_t[lanes, :] = unstacked(mix, views).T.astype(jnp.bfloat16)
        dvalue[:tokens, lanes] = own_nn(a_own, g, views).astype(jnp.bfloat16)
        dvalue[tokens:, lanes] = dot_nn(a_far, g).astype(jnp.bfloat16)


def backward_kernel(
    views, query_stack, grad_stack, dprob_own, keys, keys_far, values_far, attention_own, attention_far, dquery, dkey
):
    tokens, part = keys.shape
    pair = 2 * HEAD_DIM
    for p in range(part // pair):
        lanes = slice(p * pair, (p + 1) * pair)
        q, g, dp_own = query_stack[p], grad_stack[p], dprob_own[p]
        a_own, a_far = attention_own[p], attention_far[p]
        dp_far = dot_nt(values_far[:, lanes], g)
        delta = jnp.sum(a_own * dp_own, 0, keepdims=True) + jnp.sum(a_far * dp_far, 0, keepdims=True)
        ds_own = (a_own * (dp_own - delta) * SCALE).astype(jnp.bfloat16)
        ds_far = (a_far * (dp_far - delta) * SCALE).astype(jnp.bfloat16)
        dq = own_tn(ds_own, keys[:, lanes], views) + dot_tn(ds_far, keys_far[:, lanes])
        dquery[:, lanes] = unstacked(dq, views).astype(jnp.bfloat16)
        dkey[:tokens, lanes] = own_nn(ds_own, q, views).astype(jnp.bfloat16)
        dkey[tokens:, lanes] = dot_nn(ds_far, q).astype(jnp.bfloat16)


def times(lefts, right):
    total, start = 0.0, 0
    for left in lefts:
        total = total + dot_nn(left, right[start : start + left.shape[1], :])
        start += left.shape[1]
    return total


def by_quarters(scalars, lefts, right, sends, keep, x_first):
    size = keep.shape[1]
    x, y = scalars[3], scalars[4]
    for targets, first in ((sends, 1), ([keep.at[0], keep.at[1]], 0)):
        for second in (1, 0):
            dx, dy = (first, second) if x_first else (second, first)
            block = 2 * lax.bitwise_xor(y, jnp.int32(dy)) + lax.bitwise_xor(x, jnp.int32(dx))
            rows = pl.ds(pl.multiple_of(block * size, size), size)
            target = targets[second]
            target[...] = times([left[rows, :] for left in lefts], right).astype(target.dtype)


def query_key_kernel(
    scalars, normed_t, normed_far_t, dquery, dkey, q_later, k_later, q_now, k_now, q_keep, k_keep
):
    by_quarters(scalars, (normed_t,), dquery, (q_now, q_later), q_keep, True)
    by_quarters(scalars, (normed_t, normed_far_t), dkey, (k_now, k_later), k_keep, False)


def go_on_kernel(q_keep, q_got, k_keep, k_got, q_later, k_later):
    for keep, got, later in ((q_keep, q_got, q_later), (k_keep, k_got, k_later)):
        later[...] = (keep[1] + got[...].astype(jnp.float32)).astype(jnp.bfloat16)


def value_out_kernel(scalars, normed_t, normed_far_t, dvalue, mine, theirs, upstream, send, keep):
    row, x, y = scalars[0], scalars[3], scalars[4]
    odd = lax.rem(scalars[1], jnp.int32(2)) == 1
    _, _, pairs, size, width = send.shape
    half, quarter = width // 2, width // 4
    places = [(dy, dx, pair) for dy in range(2) for dx in range(2) for pair in range(pairs)]
    rows = {"send": ([], [], []), "keep": ([], [], [])}
    for dy in range(2):
        to_y = lax.bitwise_xor(y, jnp.int32(dy))
        for dx in range(2):
            to_x = lax.bitwise_xor(x, jnp.int32(dx))
            out_rows = pl.ds(pl.multiple_of(to_x * (half // 4), half // 4), half // 4)
            out_block = jnp.where(row == to_y, mine[out_rows, :], theirs[out_rows, :])
            value_rows = pl.ds(pl.multiple_of((2 * to_y + to_x) * quarter, quarter), quarter)
            blocks = (normed_t[value_rows, :], normed_far_t[value_rows, :], out_block)
            for pair in range(pairs):
                for i, block in enumerate(blocks):
                    count = size if i == 2 else 2 * size
                    first = block[2 * pair * count : (2 * pair + 1) * count]
                    second = block[(2 * pair + 1) * count : (2 * pair + 2) * count]
                    rows["send"][i].append(jnp.where(odd, first, second))
                    rows["keep"][i].append(jnp.where(odd, second, first))
    right = upstream[:, core_half(scalars, half)]
    for target, name in ((send, "send"), (keep, "keep")):
        own, far, out = [jnp.concatenate(parts, axis=0) for parts in rows[name]]
        grad_v = times((own, far), dvalue).astype(target.dtype)
        grad_o = dot_nn(out, right).astype(target.dtype)
        for i, place in enumerate(places):
            target[(*place, slice(None), slice(0, half))] = grad_o[i * size : (i + 1) * size]
            for core in range(2):
                columns = slice(half + core * quarter, half + (core + 1) * quarter)
                part = grad_v[(2 * i + core) * size : (2 * i + core + 1) * size]
                target[(*place, slice(None), columns)] = part


def view_sum_kernel(keep, got, x_send, y_send, x_keep, y_keep):
    half = keep.shape[4] // 2
    for second in range(2):
        for target, first in ((x_send, 1), (x_keep, 0)):
            total = keep[second, first, :, :, half:] + got[second, first, :, :, half:].astype(jnp.float32)
            target[second] = total.astype(target.dtype)
        for target, first in ((y_send, 1), (y_keep, 0)):
            total = keep[first, second, :, :, :half] + got[first, second, :, :, :half].astype(jnp.float32)
            target[second] = total.astype(target.dtype)


def first_sum_kernel(x_keep, x_got, y_keep, y_got, x_later, y_later, x_now, y_now):
    for keep, got, later, now in ((x_keep, x_got, x_later, x_now), (y_keep, y_got, y_later, y_now)):
        later[...] = (keep[1] + got[1].astype(jnp.float32)).astype(jnp.bfloat16)
        now[...] = keep[0] + got[0].astype(jnp.float32)


def pack_query_key_kernel(q_keep, q_first, q_second, k_keep, k_first, k_second, packed):
    size = q_first.shape[1]
    for i, (keep, first, second) in enumerate(((q_keep, q_first, q_second), (k_keep, k_first, k_second))):
        total = keep[0] + first[...].astype(jnp.float32) + second[...].astype(jnp.float32)
        packed[:, i * size : (i + 1) * size] = total.astype(jnp.bfloat16)


def summed_tile(addends, place):
    place = pl.ds(place, 1)
    total = [now[place] + got[place].astype(jnp.float32) for now, got in zip(addends[::2], addends[1::2])]
    return (jnp.concatenate(total, axis=2) if len(total) == 2 else total[0])[0]


def view_bit(scalars, bit):
    return lax.rem(lax.div(scalars[1], jnp.int32(2 << bit)), jnp.int32(2))


def tile_halves_kernel(bit, scalars, *refs):
    addends, (send, keep) = refs[:-2], refs[-2:]
    count = keep.shape[0]
    mine = view_bit(scalars, bit)
    for target, part in ((send, 1 - mine), (keep, mine)):
        for i in range(count):
            target[i] = summed_tile(addends, part * count + i).astype(target.dtype)


def tile_cores_kernel(scalars, *refs):
    addends, (far_same, far_cross, near_cross, mine) = refs[:-4], refs[-4:]
    size, width = mine.shape
    half, quarter = width // 2, width // 4
    bit = view_bit(scalars, 0)
    for place, same, cross in ((1 - bit, far_same, far_cross), (bit, mine, near_cross)):
        total = summed_tile(addends, place)
        parts = []
        for core in range(2):
            value = total[:, half + core * quarter : half + (core + 1) * quarter]
            out = total[core * size : (core + 1) * size, :half]
            parts.append(jnp.concatenate((out, value[:size], value[size:]), axis=1))
        same[...] = jnp.where(scalars[0] == 0, parts[0], parts[1]).astype(same.dtype)
        cross[...] = jnp.where(scalars[0] == 0, parts[1], parts[0]).astype(cross.dtype)


def place_kernel(scalars, mine, far_same, near_cross, far_cross, value, out):
    size, width = mine.shape
    half, quarter = width // 2, width // 4
    for near, far, core in ((mine, far_same, scalars[0]), (near_cross, far_cross, 1 - scalars[0])):
        total = near[...] + far[...].astype(jnp.float32)
        out[:, pl.ds(pl.multiple_of(core * half, half), half)] = total[:, :half]
        columns = pl.ds(pl.multiple_of(core * quarter, quarter), quarter)
        value[:size, columns] = total[:, half : half + quarter]
        value[size:, columns] = total[:, half + quarter :]


def summed_views(rows, packed):
    for r in range(rows):
        total = packed[r].astype(jnp.float32)
        for i in range(r + rows, packed.shape[0], rows):
            total = total + packed[i].astype(jnp.float32)
        yield r, total


def last_query_key_kernel(rows, packed, query, key):
    size = packed.shape[2] // 2
    for r, total in summed_views(rows, packed):
        columns = slice(r * size, (r + 1) * size)
        query[:, columns] = total[:, :size]
        key[:, columns] = total[:, size:]


def params(mebibytes):
    return pltpu.CompilerParams(vmem_limit_bytes=mebibytes * MIB)


def shape(dims, kind):
    return jax.ShapeDtypeStruct(dims, kind)


def shards(latents, norm_gain, w_query, w_key, w_value, w_out, kernel, partners, counts, cotangent):
    views, strip_rows, columns, width = latents.shape[1:]
    inner = w_query.shape[1]
    groups, rows = lax.axis_size("view"), lax.axis_size("row")
    scenes = lax.axis_size("scene")
    assert (strip_rows, rows, scenes) == (1, 2, 4)
    strip = strip_rows * columns
    part = inner // rows
    tokens = views * 2 * strip
    key_tokens = tokens + (groups - 1) * 2 * strip
    bf16, f32, i32 = jnp.bfloat16, jnp.float32, jnp.int32

    row, view, scene = lax.axis_index("row"), lax.axis_index("view"), lax.axis_index("scene")
    scalars = jnp.stack((row, view, scene, scene % 2, scene // 2)).astype(i32)
    swap = [(0, 1), (1, 0)]
    along_x, along_y = [(i, i ^ 1) for i in range(scenes)], [(i, i ^ 2) for i in range(scenes)]

    alive = pl.pallas_call(
        functools.partial(alive_kernel, views, groups),
        in_specs=[SMEM],
        out_specs=SMEM,
        out_shape=shape((groups * views,), i32),
        cost_estimate=MUCH,
        compiler_params=params(4),
        name="alive",
    )(partners)
    between = [[(i, i ^ d) for i in range(groups)] for d in reversed(range(1, groups))]
    granted = [lax.ppermute(partners, "view", pairs) for pairs in between]

    granted, alive = lax.optimization_barrier((granted, alive))
    lat = latents[0].reshape(views, strip, width)
    cot = cotangent[0].reshape(views, strip, width)
    lat_other = lax.ppermute(lat, "row", swap)
    cot_other = lax.ppermute(cot, "row", swap)

    outgoing = pl.pallas_call(
        functools.partial(pick_kernel, groups),
        in_specs=[SMEM] * groups + [VMEM],
        out_specs=[VMEM] * (groups - 1),
        out_shape=[shape((strip, width), bf16)] * (groups - 1),
        compiler_params=params(8),
        cost_estimate=MUCH,
        name="pick",
    )(scalars, *granted, lat)
    got_own = [lax.ppermute(part_out, "view", pairs) for part_out, pairs in zip(outgoing, between)]
    head_pairs = part // (2 * HEAD_DIM)
    normed_t, keys, values, upstream, query_stack, grad_stack, scores_own, dprob_own = pl.pallas_call(
        project_kernel,
        in_specs=[SMEM] + [VMEM] * 10,
        out_specs=[VMEM] * 8,
        out_shape=[
            shape((width, tokens), bf16),
            shape((tokens, part), bf16),
            shape((tokens, part), bf16),
            shape((tokens, width), bf16),
            shape((head_pairs, 2 * tokens, 2 * HEAD_DIM), bf16),
            shape((head_pairs, 2 * tokens, 2 * HEAD_DIM), bf16),
            shape((head_pairs, 2 * strip, 2 * tokens), f32),
            shape((head_pairs, 2 * strip, 2 * tokens), f32),
        ],
        scratch_shapes=[pltpu.VMEM((tokens, width), bf16)],
        compiler_params=params(28),
        cost_estimate=LITTLE,
        name="project",
    )(scalars, lat, lat_other, cot, cot_other, norm_gain, kernel, w_query, w_key, w_value, w_out)

    got_own, normed_t = lax.optimization_barrier((got_own, normed_t))
    got_other = [lax.ppermute(got, "row", swap) for got in got_own]

    def call(kernel_body, results, operands, name, first=VMEM, mebibytes=16, cost=LITTLE):
        outputs = pl.pallas_call(
            kernel_body,
            in_specs=[first] + [VMEM] * (len(operands) - 1),
            out_specs=[VMEM] * len(results),
            out_shape=results,
            compiler_params=params(mebibytes),
            cost_estimate=cost,
            name=name,
        )(*operands)
        return list(outputs)

    far_tokens = key_tokens - tokens
    normed_far_t, keys_far, values_far, attention_own, attention_far, mixed_t, dvalue = pl.pallas_call(
        functools.partial(forward_kernel, views, groups),
        in_specs=[SMEM] * 2 + [VMEM] * (2 * groups - 2 + 7),
        out_specs=[VMEM] * 7,
        out_shape=[
            shape((width, far_tokens), bf16),
            shape((far_tokens, part), bf16),
            shape((far_tokens, part), bf16),
            shape((head_pairs, 2 * strip, 2 * tokens), f32),
            shape((head_pairs, far_tokens, 2 * tokens), f32),
            shape((part, tokens), bf16),
            shape((key_tokens, part), bf16),
        ],
        scratch_shapes=[pltpu.VMEM((far_tokens, width), bf16)],
        compiler_params=params(28 + groups // 2),
        cost_estimate=LITTLE,
        name="attention_forward",
    )(
        scalars, alive, *got_own, *got_other, query_stack, grad_stack, scores_own, values, norm_gain, w_key, w_value
    )
    mixed_other = lax.ppermute(mixed_t, "row", swap)
    dquery, dkey = call(
        functools.partial(backward_kernel, views),
        [shape((tokens, part), bf16), shape((key_tokens, part), bf16)],
        (query_stack, grad_stack, dprob_own, keys, keys_far, values_far, attention_own, attention_far),
        "attention_backward",
        mebibytes=28 + groups // 2,
    )

    def after(value, *earlier):
        return lax.optimization_barrier((value, *earlier))[0]

    targets = groups * rows
    q_size = width // 4
    q_rows, o_rows = q_size // targets, inner // (4 * targets)
    q_block = (q_size, part)

    def first_exchange(sends):
        return lax.ppermute(sends[0], "scene", along_x), lax.ppermute(sends[1], "scene", along_y)

    def first_sum(parts, got, name, cost=LITTLE):
        blocks = [part_now.shape[1:] for part_now in parts[:2]]
        results = [shape(block, bf16) for block in blocks] + [shape(block, f32) for block in blocks]
        return call(first_sum_kernel, results, (parts[2], got[0], parts[3], got[1]), name, cost=cost)

    def second_exchange(sums):
        return lax.ppermute(sums[0], "scene", along_y), lax.ppermute(sums[1], "scene", along_x)

    def across_views(packed):
        return lax.all_to_all(packed, ("view", "row"), split_axis=0, concat_axis=0, tiled=True)

    pairs = groups // 2
    tile = (2 * o_rows, width)
    send, keep = call(
        value_out_kernel,
        [shape((2, 2, pairs, *tile), kind) for kind in (bf16, f32)],
        (scalars, normed_t, normed_far_t, after(dvalue, dkey), mixed_t, mixed_other, upstream),
        "grad_value_out",
        SMEM,
        24,
    )
    got = lax.ppermute(send, "view", [(i, i ^ 1) for i in range(groups)])
    q_later, k_later, q_now, k_now, q_keep, k_keep = call(
        query_key_kernel,
        [shape(q_block, bf16)] * 4 + [shape((2, *q_block), f32)] * 2,
        (scalars, normed_t, normed_far_t, after(dquery, send), dkey),
        "grad_query_key",
        SMEM,
        24,
    )
    q_got, k_got = first_exchange((q_later, k_later))
    q_first, k_first = first_exchange((q_now, k_now))
    later = call(
        go_on_kernel, [shape(q_block, bf16)] * 2, (q_keep, q_got, k_keep, k_got), "first_sum_query_key"
    )
    q_second, k_second = second_exchange(later)
    packed = call(
        pack_query_key_kernel,
        [shape((q_size, 2 * part), bf16)],
        (q_keep, q_first, q_second, k_keep, k_first, k_second),
        "second_sum_query_key",
    )[0]
    part_shape = (2, pairs, 2 * o_rows, width // 2)
    vo_parts = call(
        view_sum_kernel,
        [shape(part_shape, bf16)] * 2 + [shape(part_shape, f32)] * 2,
        (keep, after(got, packed)),
        "view_sum_value_out",
        cost=MUCH,
    )
    vo_got = first_exchange(vo_parts)
    packed = across_views(packed.reshape(targets, q_rows, 2 * part))
    grad_query, grad_key = call(
        functools.partial(last_query_key_kernel, rows),
        [shape((q_rows, inner), f32)] * 2,
        (packed,),
        "last_sum_query_key",
    )

    vo_sums = first_sum(vo_parts, vo_got, "first_sum_value_out")
    v_got, o_got = second_exchange(vo_sums)
    addends = (vo_sums[3], o_got, vo_sums[2], v_got)
    for bit in reversed(range(1, pairs.bit_length() - 1)):
        send, keep = call(
            functools.partial(tile_halves_kernel, bit),
            [shape((1 << bit, *tile), kind) for kind in (bf16, f32)],
            (scalars, *addends),
            "view_bit_value_out",
            SMEM,
        )
        addends = (keep, lax.ppermute(send, "view", [(i, i ^ (2 << bit)) for i in range(groups)]))
    far_same, far_cross, near_cross, mine = call(
        tile_cores_kernel,
        [shape((o_rows, width), kind) for kind in (bf16, bf16, f32, f32)],
        (scalars, *addends),
        "last_parts_value_out",
        SMEM,
    )
    far_same = lax.ppermute(far_same, "view", [(i, i ^ 2) for i in range(groups)])
    far_cross = lax.ppermute(far_cross, ("view", "row"), [(i, i ^ 5) for i in range(targets)])
    near_cross = lax.ppermute(near_cross, "row", swap)
    grad_value, grad_out = call(
        place_kernel,
        [shape((q_rows, inner), f32), shape((o_rows, width), f32)],
        (scalars, after(mine, grad_key), far_same, near_cross, far_cross),
        "last_sum_value_out",
        SMEM,
    )
    return grad_query, grad_key, grad_value, grad_out


def solution(mesh):
    tokens = P("scene", "view", "row", None, None)
    everywhere = P()
    grads = P(("scene", "view", "row"), None)
    return jax.shard_map(
        shards,
        mesh=mesh,
        in_specs=(
            tokens, everywhere, everywhere, everywhere, everywhere, everywhere, everywhere,
            P("scene", "view", None), P("scene", "view"), tokens,
        ),
        out_specs=(grads, grads, grads, grads),
        check_vma=False,
    )
```

```python
import functools

import jax
import jax.numpy as jnp
from jax import lax
from jax.experimental import pallas as pl
from jax.experimental.pallas import tpu as pltpu
from jax.sharding import PartitionSpec as P

HEAD_DIM = 64
EPSILON = 1e-06
SCALE = HEAD_DIM ** (-0.5)
MASKED = -1e30
MIB = 1024 * 1024
LITTLE = pl.CostEstimate(flops=1, bytes_accessed=1, transcendentals=0)
MUCH = pl.CostEstimate(flops=40_000_000_000, bytes_accessed=1, transcendentals=0)

VMEM = pl.BlockSpec(memory_space=pltpu.VMEM)
SMEM = pl.BlockSpec(memory_space=pltpu.SMEM)


def dot_nn(a, b):
    return lax.dot_general(a, b, (((1,), (0,)), ((), ())), preferred_element_type=jnp.float32)


def dot_nt(a, b):
    return lax.dot_general(a, b, (((1,), (1,)), ((), ())), preferred_element_type=jnp.float32)


def dot_tn(a, b):
    return lax.dot_general(a, b, (((0,), (0,)), ((), ())), preferred_element_type=jnp.float32)


def normalized(tokens, gain):
    x = tokens.astype(jnp.float32)
    mean = jnp.mean(x * x, -1, keepdims=True)
    return (x * lax.rsqrt(mean + EPSILON) * gain).astype(jnp.bfloat16)


def alive_kernel(views, groups, partners, alive):
    for g in range(groups * views):
        alive[g] = 0
    for u in range(views):
        for j in range(partners.shape[2]):
            partner = partners[0, u, j]

            @pl.when(partner >= 0)
            def _():
                alive[lax.div(partner, jnp.int32(views)) * views + u] = 1


def pick_kernel(groups, scalars, *refs):
    tables, lat, outgoing = refs[: groups - 1], refs[groups - 1], refs[groups:]
    views = lat.shape[0]
    for table, out in zip(tables, outgoing):
        wanted = jnp.int32(0)
        for u in range(table.shape[1]):
            for j in range(table.shape[2]):
                partner = table[0, u, j]
                here = (partner >= 0) & (lax.div(partner, jnp.int32(views)) == scalars[1])
                wanted = jnp.where(here, lax.rem(partner, jnp.int32(views)), wanted)
        out[...] = lat[wanted]


def core_half(scalars, size):
    return pl.ds(pl.multiple_of(scalars[0] * size, size), size)


def stacked(x, views):
    tokens, pair = x.shape
    low = (lax.broadcasted_iota(jnp.int32, (1, 1, pair), 2) < pair // 2).astype(x.dtype)
    x = x.reshape(views, tokens // views, pair)
    return jnp.concatenate((x * low, x * (1 - low)), axis=1).reshape(2 * tokens, pair)


def unstacked(x, views):
    rows, pair = x.shape
    low = lax.broadcasted_iota(jnp.int32, (1, 1, pair), 2) < pair // 2
    x = x.reshape(views, 2, rows // (2 * views), pair)
    return jnp.where(low, x[:, 0], x[:, 1]).reshape(rows // 2, pair)


def view_parts(x, views, axis):
    size = x.shape[axis] // views
    return [lax.slice_in_dim(x, u * size, (u + 1) * size, axis=axis) for u in range(views)]


def own_nt(a, b, views):
    pairs = zip(view_parts(a, views, 0), view_parts(b, views, 0))
    return jnp.concatenate([dot_nt(x, y) for x, y in pairs], axis=1)


def own_tn(a, b, views):
    pairs = zip(view_parts(a, views, 1), view_parts(b, views, 0))
    return jnp.concatenate([dot_tn(x, y) for x, y in pairs], axis=0)


def own_nn(a, b, views):
    pairs = zip(view_parts(a, views, 1), view_parts(b, views, 0))
    return jnp.concatenate([dot_nn(x, y) for x, y in pairs], axis=0)


def project_kernel(
    scalars, lat_own, lat_other, cot_own, cot_other, gain, taps, w_query, w_key, w_value, w_out,
    normed_t, keys, values, upstream, query_stack, grad_stack, scores_own, dprob_own, normed,
):
    views, strip, width = lat_own.shape
    scale = gain[...].reshape(1, width)
    row = scalars[0]

    def strip_of(u, half):
        index = 2 * u + (row if half == 0 else 1 - row)
        return pl.ds(pl.multiple_of(index * strip, strip), strip)

    for half, source in enumerate((lat_own, lat_other)):
        for u in range(views):
            normed[strip_of(u, half), :] = normalized(source[u], scale)
    first = row == 0
    chunk = 512
    column = lax.broadcasted_iota(jnp.int32, (strip, 1), 0)
    not_first = (column > 0).astype(jnp.float32)
    not_last = (column < strip - 1).astype(jnp.float32)
    for c in range(0, width, chunk):
        lanes = slice(c, c + chunk)
        tap = taps[:, lanes].astype(jnp.float32)
        top, middle, bottom = tap[0:3], tap[3:6], tap[6:9]
        cross = (jnp.where(first, top, bottom), jnp.where(first, bottom, top))
        for u in range(views):
            strips = [ref[u, :, lanes].astype(jnp.float32) for ref in (cot_own, cot_other)]
            shifted = []
            for x in strips:
                after = pltpu.roll(x, strip - 1, 0) * not_last
                before = pltpu.roll(x, 1, 0) * not_first
                shifted.append((after, x, before))
            for half in range(2):
                total = strips[half]
                for b in range(3):
                    total = total + middle[b : b + 1] * shifted[half][b]
                    total = total + cross[half][b : b + 1] * shifted[1 - half][b]
                upstream[strip_of(u, half), lanes] = total.astype(jnp.bfloat16)
    rows = normed[...]
    normed_t[...] = rows.T
    part = keys.shape[1]
    half = core_half(scalars, part)
    queries = dot_nn(rows, w_query[:, half]).astype(jnp.bfloat16)
    keys[...] = dot_nn(rows, w_key[:, half]).astype(jnp.bfloat16)
    values[...] = dot_nn(rows, w_value[:, half]).astype(jnp.bfloat16)
    out_grad = dot_nt(upstream[...], w_out[half, :]).astype(jnp.bfloat16)
    pair = 2 * HEAD_DIM
    for p in range(part // pair):
        lanes = slice(p * pair, (p + 1) * pair)
        q, g = stacked(queries[:, lanes], views), stacked(out_grad[:, lanes], views)
        query_stack[p], grad_stack[p] = q, g
        scores_own[p] = own_nt(keys[:, lanes], q, views) * SCALE
        dprob_own[p] = own_nt(values[:, lanes], g, views)


def forward_kernel(views, groups, scalars, alive, *refs):
    got_own, got_other, refs = refs[: groups - 1], refs[groups - 1 : 2 * groups - 2], refs[2 * groups - 2 :]
    query_stack, grad_stack, scores_own, values, gain, w_key, w_value, *refs = refs
    normed_far_t, keys_far, values_far, attention_own, attention_far, mixed_t, dvalue, normed_far = refs
    strip = got_own[0].shape[0]
    tokens, part = values.shape
    view_tokens = tokens // views
    here = scalars[1]
    scale_row = gain[...].reshape(1, normed_far.shape[1])
    pair = 2 * HEAD_DIM
    span = 2 * view_tokens
    column_view = lax.broadcasted_iota(jnp.int32, (1, views * span), 1) // span
    slot_alive = []
    for j in range(groups - 1):
        group = lax.bitwise_xor(here, jnp.int32(groups - 1 - j))
        start = 2 * j * strip
        normed_far[start : start + strip, :] = normalized(got_own[j][...], scale_row)
        normed_far[start + strip : start + 2 * strip, :] = normalized(got_other[j][...], scale_row)
        taken = jnp.zeros((1, views * span), jnp.int32)
        for u in range(views):
            taken = jnp.where(column_view == u, alive[group * views + u], taken)
        slot_alive.append(taken > 0)
    fetched = normed_far[...]
    normed_far_t[...] = fetched.T
    half = core_half(scalars, part)
    keys_far[...] = dot_nn(fetched, w_key[:, half]).astype(jnp.bfloat16)
    values_far[...] = dot_nn(fetched, w_value[:, half]).astype(jnp.bfloat16)
    for p in range(part // pair):
        lanes = slice(p * pair, (p + 1) * pair)
        q, g, s_own = query_stack[p], grad_stack[p], scores_own[p]
        s_far = dot_nt(keys_far[:, lanes], q) * SCALE
        s_far = jnp.concatenate(
            [
                jnp.where(slot_alive[j], s_far[j * view_tokens : (j + 1) * view_tokens], MASKED)
                for j in range(groups - 1)
            ],
            axis=0,
        )
        highest = jnp.maximum(jnp.max(s_own, 0, keepdims=True), jnp.max(s_far, 0, keepdims=True))
        e_own = jnp.exp(s_own - highest)
        e_far = jnp.exp(s_far - highest)
        inverse = 1.0 / (jnp.sum(e_own, 0, keepdims=True) + jnp.sum(e_far, 0, keepdims=True))
        a_own, a_far = e_own * inverse, e_far * inverse
        attention_own[p], attention_far[p] = a_own, a_far
        a_own, a_far = a_own.astype(jnp.bfloat16), a_far.astype(jnp.bfloat16)
        mix = own_tn(a_own, values[:, lanes], views) + dot_tn(a_far, values_far[:, lanes])
        mixed_t[lanes, :] = unstacked(mix, views).T.astype(jnp.bfloat16)
        dvalue[:tokens, lanes] = own_nn(a_own, g, views).astype(jnp.bfloat16)
        dvalue[tokens:, lanes] = dot_nn(a_far, g).astype(jnp.bfloat16)


def backward_kernel(
    views, query_stack, grad_stack, dprob_own, keys, keys_far, values_far, attention_own, attention_far, dquery, dkey
):
    tokens, part = keys.shape
    pair = 2 * HEAD_DIM
    for p in range(part // pair):
        lanes = slice(p * pair, (p + 1) * pair)
        q, g, dp_own = query_stack[p], grad_stack[p], dprob_own[p]
        a_own, a_far = attention_own[p], attention_far[p]
        dp_far = dot_nt(values_far[:, lanes], g)
        delta = jnp.sum(a_own * dp_own, 0, keepdims=True) + jnp.sum(a_far * dp_far, 0, keepdims=True)
        ds_own = (a_own * (dp_own - delta) * SCALE).astype(jnp.bfloat16)
        ds_far = (a_far * (dp_far - delta) * SCALE).astype(jnp.bfloat16)
        dq = own_tn(ds_own, keys[:, lanes], views) + dot_tn(ds_far, keys_far[:, lanes])
        dquery[:, lanes] = unstacked(dq, views).astype(jnp.bfloat16)
        dkey[:tokens, lanes] = own_nn(ds_own, q, views).astype(jnp.bfloat16)
        dkey[tokens:, lanes] = dot_nn(ds_far, q).astype(jnp.bfloat16)


def times(lefts, right):
    total, start = 0.0, 0
    for left in lefts:
        total = total + dot_nn(left, right[start : start + left.shape[1], :])
        start += left.shape[1]
    return total


def by_quarters(scalars, lefts, right, sends, keep, x_first):
    size = keep.shape[1]
    x, y = scalars[3], scalars[4]
    for targets, first in ((sends, 1), ([keep.at[0], keep.at[1]], 0)):
        for second in (1, 0):
            dx, dy = (first, second) if x_first else (second, first)
            block = 2 * lax.bitwise_xor(y, jnp.int32(dy)) + lax.bitwise_xor(x, jnp.int32(dx))
            rows = pl.ds(pl.multiple_of(block * size, size), size)
            target = targets[second]
            target[...] = times([left[rows, :] for left in lefts], right).astype(target.dtype)


def query_key_kernel(
    scalars, normed_t, normed_far_t, dquery, dkey, q_later, k_later, q_now, k_now, q_keep, k_keep
):
    by_quarters(scalars, (normed_t,), dquery, (q_now, q_later), q_keep, True)
    by_quarters(scalars, (normed_t, normed_far_t), dkey, (k_now, k_later), k_keep, False)


def go_on_kernel(q_keep, q_got, k_keep, k_got, q_later, k_later):
    for keep, got, later in ((q_keep, q_got, q_later), (k_keep, k_got, k_later)):
        later[...] = (keep[1] + got[...].astype(jnp.float32)).astype(jnp.bfloat16)


def value_out_kernel(scalars, normed_t, normed_far_t, dvalue, mine, theirs, upstream, send, keep):
    row, x, y = scalars[0], scalars[3], scalars[4]
    odd = lax.rem(scalars[1], jnp.int32(2)) == 1
    _, _, pairs, size, width = send.shape
    half, quarter = width // 2, width // 4
    places = [(dy, dx, pair) for dy in range(2) for dx in range(2) for pair in range(pairs)]
    rows = {"send": ([], [], []), "keep": ([], [], [])}
    for dy in range(2):
        to_y = lax.bitwise_xor(y, jnp.int32(dy))
        for dx in range(2):
            to_x = lax.bitwise_xor(x, jnp.int32(dx))
            out_rows = pl.ds(pl.multiple_of(to_x * (half // 4), half // 4), half // 4)
            out_block = jnp.where(row == to_y, mine[out_rows, :], theirs[out_rows, :])
            value_rows = pl.ds(pl.multiple_of((2 * to_y + to_x) * quarter, quarter), quarter)
            blocks = (normed_t[value_rows, :], normed_far_t[value_rows, :], out_block)
            for pair in range(pairs):
                for i, block in enumerate(blocks):
                    count = size if i == 2 else 2 * size
                    first = block[2 * pair * count : (2 * pair + 1) * count]
                    second = block[(2 * pair + 1) * count : (2 * pair + 2) * count]
                    rows["send"][i].append(jnp.where(odd, first, second))
                    rows["keep"][i].append(jnp.where(odd, second, first))
    right = upstream[:, core_half(scalars, half)]
    for target, name in ((send, "send"), (keep, "keep")):
        own, far, out = [jnp.concatenate(parts, axis=0) for parts in rows[name]]
        grad_v = times((own, far), dvalue).astype(target.dtype)
        grad_o = dot_nn(out, right).astype(target.dtype)
        for i, place in enumerate(places):
            target[(*place, slice(None), slice(0, half))] = grad_o[i * size : (i + 1) * size]
            for core in range(2):
                columns = slice(half + core * quarter, half + (core + 1) * quarter)
                part = grad_v[(2 * i + core) * size : (2 * i + core + 1) * size]
                target[(*place, slice(None), columns)] = part


def view_sum_kernel(keep, got, x_send, y_send, x_keep, y_keep):
    half = keep.shape[4] // 2
    for second in range(2):
        for target, first in ((x_send, 1), (x_keep, 0)):
            total = keep[second, first, :, :, half:] + got[second, first, :, :, half:].astype(jnp.float32)
            target[second] = total.astype(target.dtype)
        for target, first in ((y_send, 1), (y_keep, 0)):
            total = keep[first, second, :, :, :half] + got[first, second, :, :, :half].astype(jnp.float32)
            target[second] = total.astype(target.dtype)


def first_sum_kernel(x_keep, x_got, y_keep, y_got, x_later, y_later, x_now, y_now):
    for keep, got, later, now in ((x_keep, x_got, x_later, x_now), (y_keep, y_got, y_later, y_now)):
        later[...] = (keep[1] + got[1].astype(jnp.float32)).astype(jnp.bfloat16)
        now[...] = keep[0] + got[0].astype(jnp.float32)


def pack_query_key_kernel(q_keep, q_first, q_second, k_keep, k_first, k_second, packed):
    size = q_first.shape[1]
    for i, (keep, first, second) in enumerate(((q_keep, q_first, q_second), (k_keep, k_first, k_second))):
        total = keep[0] + first[...].astype(jnp.float32) + second[...].astype(jnp.float32)
        packed[:, i * size : (i + 1) * size] = total.astype(jnp.bfloat16)


def summed_tile(addends, place):
    place = pl.ds(place, 1)
    total = [now[place] + got[place].astype(jnp.float32) for now, got in zip(addends[::2], addends[1::2])]
    return (jnp.concatenate(total, axis=2) if len(total) == 2 else total[0])[0]


def view_bit(scalars, bit):
    return lax.rem(lax.div(scalars[1], jnp.int32(2 << bit)), jnp.int32(2))


def tile_halves_kernel(bit, scalars, *refs):
    addends, (send, keep) = refs[:-2], refs[-2:]
    count = keep.shape[0]
    mine = view_bit(scalars, bit)
    for target, part in ((send, 1 - mine), (keep, mine)):
        for i in range(count):
            target[i] = summed_tile(addends, part * count + i).astype(target.dtype)


def tile_cores_kernel(scalars, *refs):
    addends, (far_same, far_cross, near_cross, mine) = refs[:-4], refs[-4:]
    size, width = mine.shape
    half, quarter = width // 2, width // 4
    bit = view_bit(scalars, 0)
    for place, same, cross in ((1 - bit, far_same, far_cross), (bit, mine, near_cross)):
        total = summed_tile(addends, place)
        parts = []
        for core in range(2):
            value = total[:, half + core * quarter : half + (core + 1) * quarter]
            out = total[core * size : (core + 1) * size, :half]
            parts.append(jnp.concatenate((out, value[:size], value[size:]), axis=1))
        same[...] = jnp.where(scalars[0] == 0, parts[0], parts[1]).astype(same.dtype)
        cross[...] = jnp.where(scalars[0] == 0, parts[1], parts[0]).astype(cross.dtype)


def place_kernel(scalars, mine, far_same, near_cross, far_cross, value, out):
    size, width = mine.shape
    half, quarter = width // 2, width // 4
    for near, far, core in ((mine, far_same, scalars[0]), (near_cross, far_cross, 1 - scalars[0])):
        total = near[...] + far[...].astype(jnp.float32)
        out[:, pl.ds(pl.multiple_of(core * half, half), half)] = total[:, :half]
        columns = pl.ds(pl.multiple_of(core * quarter, quarter), quarter)
        value[:size, columns] = total[:, half : half + quarter]
        value[size:, columns] = total[:, half + quarter :]


def summed_views(rows, packed):
    for r in range(rows):
        total = packed[r].astype(jnp.float32)
        for i in range(r + rows, packed.shape[0], rows):
            total = total + packed[i].astype(jnp.float32)
        yield r, total


def last_query_key_kernel(rows, packed, query, key):
    size = packed.shape[2] // 2
    for r, total in summed_views(rows, packed):
        columns = slice(r * size, (r + 1) * size)
        query[:, columns] = total[:, :size]
        key[:, columns] = total[:, size:]


def params(mebibytes):
    return pltpu.CompilerParams(vmem_limit_bytes=mebibytes * MIB)


def shape(dims, kind):
    return jax.ShapeDtypeStruct(dims, kind)


def shards(latents, norm_gain, w_query, w_key, w_value, w_out, kernel, partners, counts, cotangent):
    views, strip_rows, columns, width = latents.shape[1:]
    inner = w_query.shape[1]
    groups, rows = lax.axis_size("view"), lax.axis_size("row")
    scenes = lax.axis_size("scene")
    assert (strip_rows, rows, scenes) == (1, 2, 4)
    strip = strip_rows * columns
    part = inner // rows
    tokens = views * 2 * strip
    key_tokens = tokens + (groups - 1) * 2 * strip
    bf16, f32, i32 = jnp.bfloat16, jnp.float32, jnp.int32

    row, view, scene = lax.axis_index("row"), lax.axis_index("view"), lax.axis_index("scene")
    scalars = jnp.stack((row, view, scene, scene % 2, scene // 2)).astype(i32)
    swap = [(0, 1), (1, 0)]
    along_x, along_y = [(i, i ^ 1) for i in range(scenes)], [(i, i ^ 2) for i in range(scenes)]

    alive = pl.pallas_call(
        functools.partial(alive_kernel, views, groups),
        in_specs=[SMEM],
        out_specs=SMEM,
        out_shape=shape((groups * views,), i32),
        cost_estimate=MUCH,
        compiler_params=params(4),
        name="alive",
    )(partners)
    between = [[(i, i ^ d) for i in range(groups)] for d in reversed(range(1, groups))]
    granted = [lax.ppermute(partners, "view", pairs) for pairs in between]

    granted, alive = lax.optimization_barrier((granted, alive))
    lat = latents[0].reshape(views, strip, width)
    cot = cotangent[0].reshape(views, strip, width)
    lat_other = lax.ppermute(lat, "row", swap)
    cot_other = lax.ppermute(cot, "row", swap)

    outgoing = pl.pallas_call(
        functools.partial(pick_kernel, groups),
        in_specs=[SMEM] * groups + [VMEM],
        out_specs=[VMEM] * (groups - 1),
        out_shape=[shape((strip, width), bf16)] * (groups - 1),
        compiler_params=params(8),
        cost_estimate=MUCH,
        name="pick",
    )(scalars, *granted, lat)
    got_own = [lax.ppermute(part_out, "view", pairs) for part_out, pairs in zip(outgoing, between)]
    head_pairs = part // (2 * HEAD_DIM)
    normed_t, keys, values, upstream, query_stack, grad_stack, scores_own, dprob_own = pl.pallas_call(
        project_kernel,
        in_specs=[SMEM] + [VMEM] * 10,
        out_specs=[VMEM] * 8,
        out_shape=[
            shape((width, tokens), bf16),
            shape((tokens, part), bf16),
            shape((tokens, part), bf16),
            shape((tokens, width), bf16),
            shape((head_pairs, 2 * tokens, 2 * HEAD_DIM), bf16),
            shape((head_pairs, 2 * tokens, 2 * HEAD_DIM), bf16),
            shape((head_pairs, 2 * strip, 2 * tokens), f32),
            shape((head_pairs, 2 * strip, 2 * tokens), f32),
        ],
        scratch_shapes=[pltpu.VMEM((tokens, width), bf16)],
        compiler_params=params(28),
        cost_estimate=LITTLE,
        name="project",
    )(scalars, lat, lat_other, cot, cot_other, norm_gain, kernel, w_query, w_key, w_value, w_out)

    got_own, normed_t = lax.optimization_barrier((got_own, normed_t))
    got_other = [lax.ppermute(got, "row", swap) for got in got_own]

    def call(kernel_body, results, operands, name, first=VMEM, mebibytes=16, cost=LITTLE):
        outputs = pl.pallas_call(
            kernel_body,
            in_specs=[first] + [VMEM] * (len(operands) - 1),
            out_specs=[VMEM] * len(results),
            out_shape=results,
            compiler_params=params(mebibytes),
            cost_estimate=cost,
            name=name,
        )(*operands)
        return list(outputs)

    far_tokens = key_tokens - tokens
    normed_far_t, keys_far, values_far, attention_own, attention_far, mixed_t, dvalue = pl.pallas_call(
        functools.partial(forward_kernel, views, groups),
        in_specs=[SMEM] * 2 + [VMEM] * (2 * groups - 2 + 7),
        out_specs=[VMEM] * 7,
        out_shape=[
            shape((width, far_tokens), bf16),
            shape((far_tokens, part), bf16),
            shape((far_tokens, part), bf16),
            shape((head_pairs, 2 * strip, 2 * tokens), f32),
            shape((head_pairs, far_tokens, 2 * tokens), f32),
            shape((part, tokens), bf16),
            shape((key_tokens, part), bf16),
        ],
        scratch_shapes=[pltpu.VMEM((far_tokens, width), bf16)],
        compiler_params=params(28 + groups // 2),
        cost_estimate=LITTLE,
        name="attention_forward",
    )(
        scalars, alive, *got_own, *got_other, query_stack, grad_stack, scores_own, values, norm_gain, w_key, w_value
    )
    mixed_other = lax.ppermute(mixed_t, "row", swap)
    dquery, dkey = call(
        functools.partial(backward_kernel, views),
        [shape((tokens, part), bf16), shape((key_tokens, part), bf16)],
        (query_stack, grad_stack, dprob_own, keys, keys_far, values_far, attention_own, attention_far),
        "attention_backward",
        mebibytes=28 + groups // 2,
    )

    def after(value, *earlier):
        return lax.optimization_barrier((value, *earlier))[0]

    targets = groups * rows
    q_size = width // 4
    q_rows, o_rows = q_size // targets, inner // (4 * targets)
    q_block = (q_size, part)

    def first_exchange(sends):
        return lax.ppermute(sends[0], "scene", along_x), lax.ppermute(sends[1], "scene", along_y)

    def first_sum(parts, got, name, cost=LITTLE):
        blocks = [part_now.shape[1:] for part_now in parts[:2]]
        results = [shape(block, bf16) for block in blocks] + [shape(block, f32) for block in blocks]
        return call(first_sum_kernel, results, (parts[2], got[0], parts[3], got[1]), name, cost=cost)

    def second_exchange(sums):
        return lax.ppermute(sums[0], "scene", along_y), lax.ppermute(sums[1], "scene", along_x)

    def across_views(packed):
        return lax.all_to_all(packed, ("view", "row"), split_axis=0, concat_axis=0, tiled=True)

    pairs = groups // 2
    tile = (2 * o_rows, width)
    send, keep = call(
        value_out_kernel,
        [shape((2, 2, pairs, *tile), kind) for kind in (bf16, f32)],
        (scalars, normed_t, normed_far_t, after(dvalue, dkey), mixed_t, mixed_other, upstream),
        "grad_value_out",
        SMEM,
        24,
    )
    got = lax.ppermute(send, "view", [(i, i ^ 1) for i in range(groups)])
    q_later, k_later, q_now, k_now, q_keep, k_keep = call(
        query_key_kernel,
        [shape(q_block, bf16)] * 4 + [shape((2, *q_block), f32)] * 2,
        (scalars, normed_t, normed_far_t, after(dquery, send), dkey),
        "grad_query_key",
        SMEM,
        24,
    )
    q_got, k_got = first_exchange((q_later, k_later))
    q_first, k_first = first_exchange((q_now, k_now))
    later = call(
        go_on_kernel, [shape(q_block, bf16)] * 2, (q_keep, q_got, k_keep, k_got), "first_sum_query_key"
    )
    q_second, k_second = second_exchange(later)
    packed = call(
        pack_query_key_kernel,
        [shape((q_size, 2 * part), bf16)],
        (q_keep, q_first, q_second, k_keep, k_first, k_second),
        "second_sum_query_key",
    )[0]
    part_shape = (2, pairs, 2 * o_rows, width // 2)
    vo_parts = call(
        view_sum_kernel,
        [shape(part_shape, bf16)] * 2 + [shape(part_shape, f32)] * 2,
        (keep, after(got, packed)),
        "view_sum_value_out",
    )
    vo_got = first_exchange(vo_parts)
    packed = across_views(after(packed, vo_parts[0]).reshape(targets, q_rows, 2 * part))
    grad_query, grad_key = call(
        functools.partial(last_query_key_kernel, rows),
        [shape((q_rows, inner), f32)] * 2,
        (packed,),
        "last_sum_query_key",
    )

    vo_sums = first_sum(vo_parts, vo_got, "first_sum_value_out", MUCH)
    v_got, o_got = second_exchange(vo_sums)
    addends = (vo_sums[3], o_got, vo_sums[2], v_got)
    for bit in reversed(range(1, pairs.bit_length() - 1)):
        send, keep = call(
            functools.partial(tile_halves_kernel, bit),
            [shape((1 << bit, *tile), kind) for kind in (bf16, f32)],
            (scalars, *addends),
            "view_bit_value_out",
            SMEM,
        )
        addends = (keep, lax.ppermute(send, "view", [(i, i ^ (2 << bit)) for i in range(groups)]))
    far_same, far_cross, near_cross, mine = call(
        tile_cores_kernel,
        [shape((o_rows, width), kind) for kind in (bf16, bf16, f32, f32)],
        (scalars, *addends),
        "last_parts_value_out",
        SMEM,
    )
    far_same = lax.ppermute(far_same, "view", [(i, i ^ 2) for i in range(groups)])
    far_cross = lax.ppermute(far_cross, ("view", "row"), [(i, i ^ 5) for i in range(targets)])
    near_cross = lax.ppermute(near_cross, "row", swap)
    grad_value, grad_out = call(
        place_kernel,
        [shape((q_rows, inner), f32), shape((o_rows, width), f32)],
        (scalars, after(mine, grad_key), far_same, near_cross, far_cross),
        "last_sum_value_out",
        SMEM,
    )
    return grad_query, grad_key, grad_value, grad_out


def solution(mesh):
    tokens = P("scene", "view", "row", None, None)
    everywhere = P()
    grads = P(("scene", "view", "row"), None)
    return jax.shard_map(
        shards,
        mesh=mesh,
        in_specs=(
            tokens, everywhere, everywhere, everywhere, everywhere, everywhere, everywhere,
            P("scene", "view", None), P("scene", "view"), tokens,
        ),
        out_specs=(grads, grads, grads, grads),
        check_vma=False,
    )
```

```python
import functools

import jax
import jax.numpy as jnp
from jax import lax
from jax.experimental import pallas as pl
from jax.experimental.pallas import tpu as pltpu
from jax.sharding import PartitionSpec as P

HEAD_DIM = 64
EPSILON = 1e-06
SCALE = HEAD_DIM ** (-0.5)
MASKED = -1e30
PAIR = 2 * HEAD_DIM
MIB = 1024 * 1024
LITTLE = pl.CostEstimate(flops=1, bytes_accessed=1, transcendentals=0)
MUCH = pl.CostEstimate(flops=40_000_000_000, bytes_accessed=1, transcendentals=0)

VMEM = pl.BlockSpec(memory_space=pltpu.VMEM)
SMEM = pl.BlockSpec(memory_space=pltpu.SMEM)


def dot_nn(a, b):
    return lax.dot_general(a, b, (((1,), (0,)), ((), ())), preferred_element_type=jnp.float32)


def dot_nt(a, b):
    return lax.dot_general(a, b, (((1,), (1,)), ((), ())), preferred_element_type=jnp.float32)


def dot_tn(a, b):
    return lax.dot_general(a, b, (((0,), (0,)), ((), ())), preferred_element_type=jnp.float32)


def normalized(tokens, gain):
    x = tokens.astype(jnp.float32)
    mean = jnp.mean(x * x, -1, keepdims=True)
    return (x * lax.rsqrt(mean + EPSILON) * gain).astype(jnp.bfloat16)


def alive_kernel(views, groups, partners, alive):
    for g in range(groups * views):
        alive[g] = 0
    for u in range(views):
        for j in range(partners.shape[2]):
            partner = partners[0, u, j]

            @pl.when(partner >= 0)
            def _():
                alive[lax.div(partner, jnp.int32(views)) * views + u] = 1


def pick_kernel(groups, scalars, *refs):
    tables, lat, outgoing = refs[: groups - 1], refs[groups - 1], refs[groups:]
    views = lat.shape[0]
    for table, out in zip(tables, outgoing):
        wanted = jnp.int32(0)
        for u in range(table.shape[1]):
            for j in range(table.shape[2]):
                partner = table[0, u, j]
                here = (partner >= 0) & (lax.div(partner, jnp.int32(views)) == scalars[1])
                wanted = jnp.where(here, lax.rem(partner, jnp.int32(views)), wanted)
        out[...] = lat[wanted]


def core_half(scalars, size):
    return pl.ds(pl.multiple_of(scalars[0] * size, size), size)


def stacked(x, views):
    tokens, pair = x.shape
    low = (lax.broadcasted_iota(jnp.int32, (1, 1, pair), 2) < pair // 2).astype(x.dtype)
    x = x.reshape(views, tokens // views, pair)
    return jnp.concatenate((x * low, x * (1 - low)), axis=1).reshape(2 * tokens, pair)


def unstacked(x, views):
    rows, pair = x.shape
    low = lax.broadcasted_iota(jnp.int32, (1, 1, pair), 2) < pair // 2
    x = x.reshape(views, 2, rows // (2 * views), pair)
    return jnp.where(low, x[:, 0], x[:, 1]).reshape(rows // 2, pair)


def view_parts(x, views, axis):
    size = x.shape[axis] // views
    return [lax.slice_in_dim(x, u * size, (u + 1) * size, axis=axis) for u in range(views)]


def own_nt(a, b, views):
    pairs = zip(view_parts(a, views, 0), view_parts(b, views, 0))
    return jnp.concatenate([dot_nt(x, y) for x, y in pairs], axis=1)


def own_tn(a, b, views):
    pairs = zip(view_parts(a, views, 1), view_parts(b, views, 0))
    return jnp.concatenate([dot_tn(x, y) for x, y in pairs], axis=0)


def own_nn(a, b, views):
    pairs = zip(view_parts(a, views, 1), view_parts(b, views, 0))
    return jnp.concatenate([dot_nn(x, y) for x, y in pairs], axis=0)


def project_kernel(
    scalars, lat_own, lat_other, cot_own, cot_other, gain, taps, w_query, w_key, w_value, w_out,
    normed_t, keys, values, upstream, query_stack, grad_stack, scores_own, dprob_own, normed,
):
    views, strip, width = lat_own.shape
    scale = gain[...].reshape(1, width)
    row = scalars[0]

    def strip_of(u, half):
        index = 2 * u + (row if half == 0 else 1 - row)
        return pl.ds(pl.multiple_of(index * strip, strip), strip)

    for half, source in enumerate((lat_own, lat_other)):
        for u in range(views):
            normed[strip_of(u, half), :] = normalized(source[u], scale)
    first = row == 0
    chunk = 512
    column = lax.broadcasted_iota(jnp.int32, (strip, 1), 0)
    not_first = (column > 0).astype(jnp.float32)
    not_last = (column < strip - 1).astype(jnp.float32)
    for c in range(0, width, chunk):
        lanes = slice(c, c + chunk)
        tap = taps[:, lanes].astype(jnp.float32)
        top, middle, bottom = tap[0:3], tap[3:6], tap[6:9]
        cross = (jnp.where(first, top, bottom), jnp.where(first, bottom, top))
        for u in range(views):
            strips = [ref[u, :, lanes].astype(jnp.float32) for ref in (cot_own, cot_other)]
            shifted = []
            for x in strips:
                after = pltpu.roll(x, strip - 1, 0) * not_last
                before = pltpu.roll(x, 1, 0) * not_first
                shifted.append((after, x, before))
            for half in range(2):
                total = strips[half]
                for b in range(3):
                    total = total + middle[b : b + 1] * shifted[half][b]
                    total = total + cross[half][b : b + 1] * shifted[1 - half][b]
                upstream[strip_of(u, half), lanes] = total.astype(jnp.bfloat16)
    rows = normed[...]
    normed_t[...] = rows.T
    part = keys.shape[1]
    half = core_half(scalars, part)
    queries = dot_nn(rows, w_query[:, half]).astype(jnp.bfloat16)
    keys[...] = dot_nn(rows, w_key[:, half]).astype(jnp.bfloat16)
    values[...] = dot_nn(rows, w_value[:, half]).astype(jnp.bfloat16)
    out_grad = dot_nt(upstream[...], w_out[half, :]).astype(jnp.bfloat16)
    pair = 2 * HEAD_DIM
    for p in range(part // pair):
        lanes = slice(p * pair, (p + 1) * pair)
        q, g = stacked(queries[:, lanes], views), stacked(out_grad[:, lanes], views)
        query_stack[p], grad_stack[p] = q, g
        scores_own[p] = own_nt(keys[:, lanes], q, views) * SCALE
        dprob_own[p] = own_nt(values[:, lanes], g, views)


def forward_kernel(views, groups, scalars, alive, *refs):
    got_own, got_other, refs = refs[: groups - 1], refs[groups - 1 : 2 * groups - 2], refs[2 * groups - 2 :]
    query_stack, grad_stack, scores_own, values, gain, w_key, w_value, *refs = refs
    normed_far_t, keys_far, values_far, attention_own, attention_far, mixed_t, dvalue, normed_far = refs
    strip = got_own[0].shape[0]
    tokens, part = values.shape
    view_tokens = tokens // views
    here = scalars[1]
    scale_row = gain[...].reshape(1, normed_far.shape[1])
    pair = 2 * HEAD_DIM
    span = 2 * view_tokens
    column_view = lax.broadcasted_iota(jnp.int32, (1, views * span), 1) // span
    slot_alive = []
    for j in range(groups - 1):
        group = lax.bitwise_xor(here, jnp.int32(groups - 1 - j))
        start = 2 * j * strip
        normed_far[start : start + strip, :] = normalized(got_own[j][...], scale_row)
        normed_far[start + strip : start + 2 * strip, :] = normalized(got_other[j][...], scale_row)
        taken = jnp.zeros((1, views * span), jnp.int32)
        for u in range(views):
            taken = jnp.where(column_view == u, alive[group * views + u], taken)
        slot_alive.append(taken > 0)
    fetched = normed_far[...]
    normed_far_t[...] = fetched.T
    half = core_half(scalars, part)
    keys_far[...] = dot_nn(fetched, w_key[:, half]).astype(jnp.bfloat16)
    values_far[...] = dot_nn(fetched, w_value[:, half]).astype(jnp.bfloat16)
    for p in range(part // pair):
        lanes = slice(p * pair, (p + 1) * pair)
        q, g, s_own = query_stack[p], grad_stack[p], scores_own[p]
        s_far = dot_nt(keys_far[:, lanes], q) * SCALE
        s_far = jnp.concatenate(
            [
                jnp.where(slot_alive[j], s_far[j * view_tokens : (j + 1) * view_tokens], MASKED)
                for j in range(groups - 1)
            ],
            axis=0,
        )
        highest = jnp.maximum(jnp.max(s_own, 0, keepdims=True), jnp.max(s_far, 0, keepdims=True))
        e_own = jnp.exp(s_own - highest)
        e_far = jnp.exp(s_far - highest)
        inverse = 1.0 / (jnp.sum(e_own, 0, keepdims=True) + jnp.sum(e_far, 0, keepdims=True))
        a_own, a_far = e_own * inverse, e_far * inverse
        attention_own[p], attention_far[p] = a_own, a_far
        a_own, a_far = a_own.astype(jnp.bfloat16), a_far.astype(jnp.bfloat16)
        mix = own_tn(a_own, values[:, lanes], views) + dot_tn(a_far, values_far[:, lanes])
        mixed_t[lanes, :] = unstacked(mix, views).T.astype(jnp.bfloat16)
        dvalue[:tokens, lanes] = own_nn(a_own, g, views).astype(jnp.bfloat16)
        dvalue[tokens:, lanes] = dot_nn(a_far, g).astype(jnp.bfloat16)


def backward_kernel(
    views, query_stack, grad_stack, dprob_own, keys, keys_far, values_far, attention_own, attention_far, dquery, dkey
):
    tokens, part = keys.shape
    pair = 2 * HEAD_DIM
    for p in range(part // pair):
        lanes = slice(p * pair, (p + 1) * pair)
        q, g, dp_own = query_stack[p], grad_stack[p], dprob_own[p]
        a_own, a_far = attention_own[p], attention_far[p]
        dp_far = dot_nt(values_far[:, lanes], g)
        delta = jnp.sum(a_own * dp_own, 0, keepdims=True) + jnp.sum(a_far * dp_far, 0, keepdims=True)
        ds_own = (a_own * (dp_own - delta) * SCALE).astype(jnp.bfloat16)
        ds_far = (a_far * (dp_far - delta) * SCALE).astype(jnp.bfloat16)
        dq = own_tn(ds_own, keys[:, lanes], views) + dot_tn(ds_far, keys_far[:, lanes])
        dquery[:, lanes] = unstacked(dq, views).astype(jnp.bfloat16)
        dkey[:tokens, lanes] = own_nn(ds_own, q, views).astype(jnp.bfloat16)
        dkey[tokens:, lanes] = dot_nn(ds_far, q).astype(jnp.bfloat16)


def times(lefts, right):
    total, start = 0.0, 0
    for left in lefts:
        total = total + dot_nn(left, right[start : start + left.shape[1], :])
        start += left.shape[1]
    return total


def by_quarters(scalars, lefts, right, sends, keep, x_first):
    size = keep.shape[1]
    x, y = scalars[3], scalars[4]
    for targets, first in ((sends, 1), ([keep.at[0], keep.at[1]], 0)):
        for second in (1, 0):
            dx, dy = (first, second) if x_first else (second, first)
            block = 2 * lax.bitwise_xor(y, jnp.int32(dy)) + lax.bitwise_xor(x, jnp.int32(dx))
            rows = pl.ds(pl.multiple_of(block * size, size), size)
            target = targets[second]
            target[...] = times([left[rows, :] for left in lefts], right).astype(target.dtype)


def query_key_kernel(
    scalars, normed_t, normed_far_t, dquery, dkey, dvalue, q_later, k_later, q_now, k_now, q_keep, k_keep
):
    by_quarters(scalars, (normed_t,), dquery[...], (q_now, q_later), q_keep, True)
    right = jnp.concatenate((dkey[...], dvalue[:, :PAIR]), axis=1)
    by_quarters(scalars, (normed_t, normed_far_t), right, (k_now, k_later), k_keep, False)


def go_on_kernel(q_keep, q_got, k_keep, k_got, q_later, k_later):
    for keep, got, later in ((q_keep, q_got, q_later), (k_keep, k_got, k_later)):
        later[...] = (keep[1] + got[...].astype(jnp.float32)).astype(jnp.bfloat16)


def value_out_kernel(scalars, normed_t, normed_far_t, dvalue, mine, theirs, upstream, send, keep):
    row, x, y = scalars[0], scalars[3], scalars[4]
    odd = lax.rem(scalars[1], jnp.int32(2)) == 1
    _, _, pairs, size, _ = send.shape
    half, quarter = upstream.shape[1] // 2, normed_t.shape[0] // 4
    value_right = dvalue[:, PAIR:]
    lanes = value_right.shape[1]
    places = [(dy, dx, pair) for dy in range(2) for dx in range(2) for pair in range(pairs)]
    rows = {"send": ([], [], []), "keep": ([], [], [])}
    for dy in range(2):
        to_y = lax.bitwise_xor(y, jnp.int32(dy))
        for dx in range(2):
            to_x = lax.bitwise_xor(x, jnp.int32(dx))
            out_rows = pl.ds(pl.multiple_of(to_x * (half // 4), half // 4), half // 4)
            out_block = jnp.where(row == to_y, mine[out_rows, :], theirs[out_rows, :])
            value_rows = pl.ds(pl.multiple_of((2 * to_y + to_x) * quarter, quarter), quarter)
            blocks = (normed_t[value_rows, :], normed_far_t[value_rows, :], out_block)
            for pair in range(pairs):
                for i, block in enumerate(blocks):
                    count = size if i == 2 else 2 * size
                    first = block[2 * pair * count : (2 * pair + 1) * count]
                    second = block[(2 * pair + 1) * count : (2 * pair + 2) * count]
                    rows["send"][i].append(jnp.where(odd, first, second))
                    rows["keep"][i].append(jnp.where(odd, second, first))
    right = upstream[:, core_half(scalars, half)]
    for target, name in ((send, "send"), (keep, "keep")):
        own, far, out = [jnp.concatenate(parts, axis=0) for parts in rows[name]]
        grad_v = times((own, far), value_right).astype(target.dtype)
        grad_o = dot_nn(out, right).astype(target.dtype)
        for i, place in enumerate(places):
            target[(*place, slice(None), slice(0, half))] = grad_o[i * size : (i + 1) * size]
            for core in range(2):
                columns = slice(half + core * lanes, half + (core + 1) * lanes)
                part = grad_v[(2 * i + core) * size : (2 * i + core + 1) * size]
                target[(*place, slice(None), columns)] = part


def view_sum_kernel(keep, got, x_send, y_send, x_keep, y_keep):
    half = y_send.shape[3]
    for second in range(2):
        for target, first in ((x_send, 1), (x_keep, 0)):
            total = keep[second, first, :, :, half:] + got[second, first, :, :, half:].astype(jnp.float32)
            target[second] = total.astype(target.dtype)
        for target, first in ((y_send, 1), (y_keep, 0)):
            total = keep[first, second, :, :, :half] + got[first, second, :, :, :half].astype(jnp.float32)
            target[second] = total.astype(target.dtype)


def first_sum_kernel(x_keep, x_got, y_keep, y_got, x_later, y_later, x_now, y_now):
    for keep, got, later, now in ((x_keep, x_got, x_later, x_now), (y_keep, y_got, y_later, y_now)):
        later[...] = (keep[1] + got[1].astype(jnp.float32)).astype(jnp.bfloat16)
        now[...] = keep[0] + got[0].astype(jnp.float32)


def query_key_tiles_kernel(scalars, q_keep, q_first, q_second, k_keep, k_first, k_second, send, keep):
    odd = lax.rem(scalars[1], jnp.int32(2)) == 1
    total = [
        kept[0] + first[...].astype(jnp.float32) + second[...].astype(jnp.float32)
        for kept, first, second in ((q_keep, q_first, q_second), (k_keep, k_first, k_second))
    ]
    total = jnp.concatenate(total, axis=1)
    pairs, size, _ = send.shape
    for pair in range(pairs):
        first = total[2 * pair * size : (2 * pair + 1) * size]
        second = total[(2 * pair + 1) * size : (2 * pair + 2) * size]
        send[pair] = jnp.where(odd, first, second).astype(send.dtype)
        keep[pair] = jnp.where(odd, second, first)


def summed_tile(addends, place):
    place = pl.ds(place, 1)
    total = [now[place] + got[place].astype(jnp.float32) for now, got in zip(addends[::2], addends[1::2])]
    return (jnp.concatenate(total, axis=2) if len(total) == 2 else total[0])[0]


def view_bit(scalars, bit):
    return lax.rem(lax.div(scalars[1], jnp.int32(2 << bit)), jnp.int32(2))


def tile_halves_kernel(bit, scalars, *refs):
    addends, (send, keep) = refs[:-2], refs[-2:]
    count = keep.shape[0]
    mine = view_bit(scalars, bit)
    for target, part in ((send, 1 - mine), (keep, mine)):
        for i in range(count):
            target[i] = summed_tile(addends, part * count + i).astype(target.dtype)


def query_key_cores(tile, half):
    size = tile.shape[0] // 2
    return tile[:size], tile[size:]


def value_out_cores(tile, half):
    size, lanes = tile.shape[0] // 2, (tile.shape[1] - half) // 2
    parts = []
    for core in range(2):
        value = tile[:, half + core * lanes : half + (core + 1) * lanes]
        out = tile[core * size : (core + 1) * size, :half]
        parts.append(jnp.concatenate((out, value[:size], value[size:]), axis=1))
    return parts


def tile_cores_kernel(split, half, scalars, *refs):
    addends, (far_same, far_cross, near_cross, mine) = refs[:-4], refs[-4:]
    bit = view_bit(scalars, 0)
    for place, same, cross in ((1 - bit, far_same, far_cross), (bit, mine, near_cross)):
        parts = split(summed_tile(addends, place), half)
        same[...] = jnp.where(scalars[0] == 0, parts[0], parts[1]).astype(same.dtype)
        cross[...] = jnp.where(scalars[0] == 0, parts[1], parts[0]).astype(cross.dtype)


def last_sums(scalars, mine, far_same, near_cross, far_cross):
    for near, far, core in ((mine, far_same, scalars[0]), (near_cross, far_cross, 1 - scalars[0])):
        yield near[...] + far[...].astype(jnp.float32), core


def place_query_key_kernel(scalars, mine, far_same, near_cross, far_cross, query, key, value):
    size = query.shape[1] // 2
    for total, core in last_sums(scalars, mine, far_same, near_cross, far_cross):
        columns = pl.ds(pl.multiple_of(core * size, size), size)
        query[:, columns] = total[:, :size]
        key[:, columns] = total[:, size : 2 * size]
        value[:, pl.ds(pl.multiple_of(core * PAIR, PAIR), PAIR)] = total[:, 2 * size :]


def place_value_out_kernel(scalars, mine, far_same, near_cross, far_cross, first_pairs, value, out):
    size, width = mine.shape
    half, part = out.shape[1] // 2, value.shape[1] // 2
    lanes = part - PAIR
    for core in range(2):
        value[:, core * part : core * part + PAIR] = first_pairs[:, core * PAIR : (core + 1) * PAIR]
    for total, core in last_sums(scalars, mine, far_same, near_cross, far_cross):
        out[:, pl.ds(pl.multiple_of(core * half, half), half)] = total[:, :half]
        columns = pl.ds(pl.multiple_of(core * part + PAIR, PAIR), lanes)
        value[:size, columns] = total[:, half : half + lanes]
        value[size:, columns] = total[:, half + lanes :]


def params(mebibytes):
    return pltpu.CompilerParams(vmem_limit_bytes=mebibytes * MIB)


def shape(dims, kind):
    return jax.ShapeDtypeStruct(dims, kind)


def shards(latents, norm_gain, w_query, w_key, w_value, w_out, kernel, partners, counts, cotangent):
    views, strip_rows, columns, width = latents.shape[1:]
    inner = w_query.shape[1]
    groups, rows = lax.axis_size("view"), lax.axis_size("row")
    scenes = lax.axis_size("scene")
    assert (strip_rows, rows, scenes) == (1, 2, 4)
    strip = strip_rows * columns
    part = inner // rows
    tokens = views * 2 * strip
    key_tokens = tokens + (groups - 1) * 2 * strip
    bf16, f32, i32 = jnp.bfloat16, jnp.float32, jnp.int32

    row, view, scene = lax.axis_index("row"), lax.axis_index("view"), lax.axis_index("scene")
    scalars = jnp.stack((row, view, scene, scene % 2, scene // 2)).astype(i32)
    swap = [(0, 1), (1, 0)]
    along_x, along_y = [(i, i ^ 1) for i in range(scenes)], [(i, i ^ 2) for i in range(scenes)]

    alive = pl.pallas_call(
        functools.partial(alive_kernel, views, groups),
        in_specs=[SMEM],
        out_specs=SMEM,
        out_shape=shape((groups * views,), i32),
        cost_estimate=MUCH,
        compiler_params=params(4),
        name="alive",
    )(partners)
    between = [[(i, i ^ d) for i in range(groups)] for d in reversed(range(1, groups))]
    granted = [lax.ppermute(partners, "view", pairs) for pairs in between]

    granted, alive = lax.optimization_barrier((granted, alive))
    lat = latents[0].reshape(views, strip, width)
    cot = cotangent[0].reshape(views, strip, width)
    lat_other = lax.ppermute(lat, "row", swap)
    cot_other = lax.ppermute(cot, "row", swap)

    outgoing = pl.pallas_call(
        functools.partial(pick_kernel, groups),
        in_specs=[SMEM] * groups + [VMEM],
        out_specs=[VMEM] * (groups - 1),
        out_shape=[shape((strip, width), bf16)] * (groups - 1),
        compiler_params=params(8),
        cost_estimate=MUCH,
        name="pick",
    )(scalars, *granted, lat)
    got_own = [lax.ppermute(part_out, "view", pairs) for part_out, pairs in zip(outgoing, between)]
    head_pairs = part // (2 * HEAD_DIM)
    normed_t, keys, values, upstream, query_stack, grad_stack, scores_own, dprob_own = pl.pallas_call(
        project_kernel,
        in_specs=[SMEM] + [VMEM] * 10,
        out_specs=[VMEM] * 8,
        out_shape=[
            shape((width, tokens), bf16),
            shape((tokens, part), bf16),
            shape((tokens, part), bf16),
            shape((tokens, width), bf16),
            shape((head_pairs, 2 * tokens, 2 * HEAD_DIM), bf16),
            shape((head_pairs, 2 * tokens, 2 * HEAD_DIM), bf16),
            shape((head_pairs, 2 * strip, 2 * tokens), f32),
            shape((head_pairs, 2 * strip, 2 * tokens), f32),
        ],
        scratch_shapes=[pltpu.VMEM((tokens, width), bf16)],
        compiler_params=params(28),
        cost_estimate=LITTLE,
        name="project",
    )(scalars, lat, lat_other, cot, cot_other, norm_gain, kernel, w_query, w_key, w_value, w_out)

    got_own, normed_t = lax.optimization_barrier((got_own, normed_t))
    got_other = [lax.ppermute(got, "row", swap) for got in got_own]

    def call(kernel_body, results, operands, name, first=VMEM, mebibytes=16, cost=LITTLE):
        outputs = pl.pallas_call(
            kernel_body,
            in_specs=[first] + [VMEM] * (len(operands) - 1),
            out_specs=[VMEM] * len(results),
            out_shape=results,
            compiler_params=params(mebibytes),
            cost_estimate=cost,
            name=name,
        )(*operands)
        return list(outputs)

    far_tokens = key_tokens - tokens
    normed_far_t, keys_far, values_far, attention_own, attention_far, mixed_t, dvalue = pl.pallas_call(
        functools.partial(forward_kernel, views, groups),
        in_specs=[SMEM] * 2 + [VMEM] * (2 * groups - 2 + 7),
        out_specs=[VMEM] * 7,
        out_shape=[
            shape((width, far_tokens), bf16),
            shape((far_tokens, part), bf16),
            shape((far_tokens, part), bf16),
            shape((head_pairs, 2 * strip, 2 * tokens), f32),
            shape((head_pairs, far_tokens, 2 * tokens), f32),
            shape((part, tokens), bf16),
            shape((key_tokens, part), bf16),
        ],
        scratch_shapes=[pltpu.VMEM((far_tokens, width), bf16)],
        compiler_params=params(28 + groups // 2),
        cost_estimate=LITTLE,
        name="attention_forward",
    )(
        scalars, alive, *got_own, *got_other, query_stack, grad_stack, scores_own, values, norm_gain, w_key, w_value
    )
    mixed_other = lax.ppermute(mixed_t, "row", swap)
    dquery, dkey = call(
        functools.partial(backward_kernel, views),
        [shape((tokens, part), bf16), shape((key_tokens, part), bf16)],
        (query_stack, grad_stack, dprob_own, keys, keys_far, values_far, attention_own, attention_far),
        "attention_backward",
        mebibytes=28 + groups // 2,
    )

    def after(value, *earlier):
        return lax.optimization_barrier((value, *earlier))[0]

    targets = groups * rows
    q_size = width // 4
    q_rows, o_rows = q_size // targets, inner // (4 * targets)
    q_block = (q_size, part)

    def first_exchange(sends):
        return lax.ppermute(sends[0], "scene", along_x), lax.ppermute(sends[1], "scene", along_y)

    def first_sum(parts, got, name, cost=LITTLE):
        blocks = [part_now.shape[1:] for part_now in parts[:2]]
        results = [shape(block, bf16) for block in blocks] + [shape(block, f32) for block in blocks]
        return call(first_sum_kernel, results, (parts[2], got[0], parts[3], got[1]), name, cost=cost)

    def second_exchange(sums):
        return lax.ppermute(sums[0], "scene", along_y), lax.ppermute(sums[1], "scene", along_x)

    pairs = groups // 2
    neighbours = [(i, i ^ 1) for i in range(groups)]
    split_rows = {"query_key": q_rows, "value_out": o_rows}

    def last_parts(addends, split, name):
        tile = (addends[0].shape[1], sum(now.shape[2] for now in addends[::2]))
        for bit in reversed(range(1, pairs.bit_length() - 1)):
            send, keep = call(
                functools.partial(tile_halves_kernel, bit),
                [shape((1 << bit, *tile), kind) for kind in (bf16, f32)],
                (scalars, *addends),
                "view_bit_" + name,
                SMEM,
            )
            addends = (keep, lax.ppermute(send, "view", [(i, i ^ (2 << bit)) for i in range(groups)]))
        lanes = tile[0] * tile[1] // (2 * split_rows[name])
        columns = width // 2
        far_same, far_cross, near_cross, mine = call(
            functools.partial(tile_cores_kernel, split, columns),
            [shape((split_rows[name], lanes), kind) for kind in (bf16, bf16, f32, f32)],
            (scalars, *addends),
            "last_parts_" + name,
            SMEM,
        )
        far_same = lax.ppermute(far_same, "view", [(i, i ^ 2) for i in range(groups)])
        far_cross = lax.ppermute(far_cross, ("view", "row"), [(i, i ^ 5) for i in range(targets)])
        near_cross = lax.ppermute(near_cross, "row", swap)
        return mine, far_same, near_cross, far_cross

    rest = part - PAIR
    tile = (2 * o_rows, width // 2 + 2 * rest)
    send, keep = call(
        value_out_kernel,
        [shape((2, 2, pairs, *tile), kind) for kind in (bf16, f32)],
        (scalars, normed_t, normed_far_t, after(dvalue, dkey), mixed_t, mixed_other, upstream),
        "grad_value_out",
        SMEM,
        24,
    )
    got = lax.ppermute(send, "view", neighbours)
    k_block = (q_size, part + PAIR)
    q_later, k_later, q_now, k_now, q_keep, k_keep = call(
        query_key_kernel,
        [shape(block, bf16) for block in (q_block, k_block, q_block, k_block)]
        + [shape((2, *block), f32) for block in (q_block, k_block)],
        (scalars, normed_t, normed_far_t, after(dquery, send), dkey, dvalue),
        "grad_query_key",
        SMEM,
        24,
    )
    q_got, k_got = first_exchange((q_later, k_later))
    q_first, k_first = first_exchange((q_now, k_now))
    later = call(
        go_on_kernel, [shape(q_block, bf16), shape(k_block, bf16)], (q_keep, q_got, k_keep, k_got), "first_sum_query_key"
    )
    q_second, k_second = second_exchange(later)
    x_shape, y_shape = (2, pairs, 2 * o_rows, 2 * rest), (2, pairs, 2 * o_rows, width // 2)
    vo_parts = call(
        view_sum_kernel,
        [shape(x_shape, bf16), shape(y_shape, bf16), shape(x_shape, f32), shape(y_shape, f32)],
        (keep, after(got, later[0], q_first, k_first)),
        "view_sum_value_out",
    )
    vo_got = first_exchange(vo_parts)
    qk_tile = (2 * q_rows, 2 * part + PAIR)
    qk_send, qk_keep = call(
        query_key_tiles_kernel,
        [shape((pairs, *qk_tile), kind) for kind in (bf16, f32)],
        (scalars, after(q_keep, vo_parts[0]), q_first, q_second, k_keep, k_first, k_second),
        "second_sum_query_key",
        SMEM,
    )
    qk_addends = (qk_keep, lax.ppermute(qk_send, "view", neighbours))
    vo_parts[2] = after(vo_parts[2], qk_send)
    vo_sums = first_sum(vo_parts, vo_got, "first_sum_value_out")
    v_got, o_got = second_exchange(vo_sums)
    addends = (vo_sums[3], o_got, vo_sums[2], v_got)
    qk_last = last_parts((after(qk_addends[0], vo_sums[0]), qk_addends[1]), query_key_cores, "query_key")
    vo_last = last_parts((after(addends[0], qk_last[0]), *addends[1:]), value_out_cores, "value_out")
    grad_query, grad_key, first_pairs = call(
        place_query_key_kernel,
        [shape((q_rows, inner), f32)] * 2 + [shape((q_rows, rows * PAIR), f32)],
        (scalars, *qk_last),
        "last_sum_query_key",
        SMEM,
    )
    grad_value, grad_out = call(
        place_value_out_kernel,
        [shape((q_rows, inner), f32), shape((o_rows, width), f32)],
        (scalars, *vo_last, first_pairs),
        "last_sum_value_out",
        SMEM,
    )
    return grad_query, grad_key, grad_value, grad_out


def solution(mesh):
    tokens = P("scene", "view", "row", None, None)
    everywhere = P()
    grads = P(("scene", "view", "row"), None)
    return jax.shard_map(
        shards,
        mesh=mesh,
        in_specs=(
            tokens, everywhere, everywhere, everywhere, everywhere, everywhere, everywhere,
            P("scene", "view", None), P("scene", "view"), tokens,
        ),
        out_specs=(grads, grads, grads, grads),
        check_vma=False,
    )
```

```python
import functools

import jax
import jax.numpy as jnp
from jax import lax
from jax.experimental import pallas as pl
from jax.experimental.pallas import tpu as pltpu
from jax.sharding import PartitionSpec as P

HEAD_DIM = 64
EPSILON = 1e-06
SCALE = HEAD_DIM ** (-0.5)
MASKED = -1e30
MIB = 1024 * 1024
LITTLE = pl.CostEstimate(flops=1, bytes_accessed=1, transcendentals=0)
MUCH = pl.CostEstimate(flops=40_000_000_000, bytes_accessed=1, transcendentals=0)

VMEM = pl.BlockSpec(memory_space=pltpu.VMEM)
SMEM = pl.BlockSpec(memory_space=pltpu.SMEM)


def dot_nn(a, b):
    return lax.dot_general(a, b, (((1,), (0,)), ((), ())), preferred_element_type=jnp.float32)


def dot_nt(a, b):
    return lax.dot_general(a, b, (((1,), (1,)), ((), ())), preferred_element_type=jnp.float32)


def dot_tn(a, b):
    return lax.dot_general(a, b, (((0,), (0,)), ((), ())), preferred_element_type=jnp.float32)


def normalized(tokens, gain):
    x = tokens.astype(jnp.float32)
    mean = jnp.mean(x * x, -1, keepdims=True)
    return (x * lax.rsqrt(mean + EPSILON) * gain).astype(jnp.bfloat16)


def alive_kernel(views, groups, partners, alive):
    for g in range(groups * views):
        alive[g] = 0
    for u in range(views):
        for j in range(partners.shape[2]):
            partner = partners[0, u, j]

            @pl.when(partner >= 0)
            def _():
                alive[lax.div(partner, jnp.int32(views)) * views + u] = 1


def pick_kernel(groups, scalars, *refs):
    tables, lat, outgoing = refs[: groups - 1], refs[groups - 1], refs[groups:]
    views = lat.shape[0]
    for table, out in zip(tables, outgoing):
        wanted = jnp.int32(0)
        for u in range(table.shape[1]):
            for j in range(table.shape[2]):
                partner = table[0, u, j]
                here = (partner >= 0) & (lax.div(partner, jnp.int32(views)) == scalars[1])
                wanted = jnp.where(here, lax.rem(partner, jnp.int32(views)), wanted)
        out[...] = lat[wanted]


def core_half(scalars, size):
    return pl.ds(pl.multiple_of(scalars[0] * size, size), size)


def stacked(x, views):
    tokens, pair = x.shape
    low = (lax.broadcasted_iota(jnp.int32, (1, 1, pair), 2) < pair // 2).astype(x.dtype)
    x = x.reshape(views, tokens // views, pair)
    return jnp.concatenate((x * low, x * (1 - low)), axis=1).reshape(2 * tokens, pair)


def unstacked(x, views):
    rows, pair = x.shape
    low = lax.broadcasted_iota(jnp.int32, (1, 1, pair), 2) < pair // 2
    x = x.reshape(views, 2, rows // (2 * views), pair)
    return jnp.where(low, x[:, 0], x[:, 1]).reshape(rows // 2, pair)


def view_parts(x, views, axis):
    size = x.shape[axis] // views
    return [lax.slice_in_dim(x, u * size, (u + 1) * size, axis=axis) for u in range(views)]


def own_nt(a, b, views):
    pairs = zip(view_parts(a, views, 0), view_parts(b, views, 0))
    return jnp.concatenate([dot_nt(x, y) for x, y in pairs], axis=1)


def own_tn(a, b, views):
    pairs = zip(view_parts(a, views, 1), view_parts(b, views, 0))
    return jnp.concatenate([dot_tn(x, y) for x, y in pairs], axis=0)


def own_nn(a, b, views):
    pairs = zip(view_parts(a, views, 1), view_parts(b, views, 0))
    return jnp.concatenate([dot_nn(x, y) for x, y in pairs], axis=0)


def project_kernel(
    scalars, lat_own, lat_other, cot_own, cot_other, gain, taps, w_query, w_key, w_value, w_out,
    normed_t, keys, values, upstream, query_stack, grad_stack, scores_own, dprob_own, normed,
):
    views, strip, width = lat_own.shape
    scale = gain[...].reshape(1, width)
    row = scalars[0]

    def strip_of(u, half):
        index = 2 * u + (row if half == 0 else 1 - row)
        return pl.ds(pl.multiple_of(index * strip, strip), strip)

    for half, source in enumerate((lat_own, lat_other)):
        for u in range(views):
            normed[strip_of(u, half), :] = normalized(source[u], scale)
    first = row == 0
    chunk = 512
    column = lax.broadcasted_iota(jnp.int32, (strip, 1), 0)
    not_first = (column > 0).astype(jnp.float32)
    not_last = (column < strip - 1).astype(jnp.float32)
    for c in range(0, width, chunk):
        lanes = slice(c, c + chunk)
        tap = taps[:, lanes].astype(jnp.float32)
        top, middle, bottom = tap[0:3], tap[3:6], tap[6:9]
        cross = (jnp.where(first, top, bottom), jnp.where(first, bottom, top))
        for u in range(views):
            strips = [ref[u, :, lanes].astype(jnp.float32) for ref in (cot_own, cot_other)]
            shifted = []
            for x in strips:
                after = pltpu.roll(x, strip - 1, 0) * not_last
                before = pltpu.roll(x, 1, 0) * not_first
                shifted.append((after, x, before))
            for half in range(2):
                total = strips[half]
                for b in range(3):
                    total = total + middle[b : b + 1] * shifted[half][b]
                    total = total + cross[half][b : b + 1] * shifted[1 - half][b]
                upstream[strip_of(u, half), lanes] = total.astype(jnp.bfloat16)
    rows = normed[...]
    normed_t[...] = rows.T
    part = keys.shape[1]
    half = core_half(scalars, part)
    queries = dot_nn(rows, w_query[:, half]).astype(jnp.bfloat16)
    keys[...] = dot_nn(rows, w_key[:, half]).astype(jnp.bfloat16)
    values[...] = dot_nn(rows, w_value[:, half]).astype(jnp.bfloat16)
    out_grad = dot_nt(upstream[...], w_out[half, :]).astype(jnp.bfloat16)
    pair = 2 * HEAD_DIM
    for p in range(part // pair):
        lanes = slice(p * pair, (p + 1) * pair)
        q, g = stacked(queries[:, lanes], views), stacked(out_grad[:, lanes], views)
        query_stack[p], grad_stack[p] = q, g
        scores_own[p] = own_nt(keys[:, lanes], q, views) * SCALE
        dprob_own[p] = own_nt(values[:, lanes], g, views)


def forward_kernel(views, groups, scalars, alive, *refs):
    got_own, got_other, refs = refs[: groups - 1], refs[groups - 1 : 2 * groups - 2], refs[2 * groups - 2 :]
    query_stack, grad_stack, scores_own, values, gain, w_key, w_value, *refs = refs
    normed_far_t, keys_far, values_far, attention_own, attention_far, mixed_t, dvalue, normed_far = refs
    strip = got_own[0].shape[0]
    tokens, part = values.shape
    view_tokens = tokens // views
    here = scalars[1]
    scale_row = gain[...].reshape(1, normed_far.shape[1])
    pair = 2 * HEAD_DIM
    span = 2 * view_tokens
    column_view = lax.broadcasted_iota(jnp.int32, (1, views * span), 1) // span
    slot_alive = []
    for j in range(groups - 1):
        group = lax.bitwise_xor(here, jnp.int32(groups - 1 - j))
        start = 2 * j * strip
        normed_far[start : start + strip, :] = normalized(got_own[j][...], scale_row)
        normed_far[start + strip : start + 2 * strip, :] = normalized(got_other[j][...], scale_row)
        taken = jnp.zeros((1, views * span), jnp.int32)
        for u in range(views):
            taken = jnp.where(column_view == u, alive[group * views + u], taken)
        slot_alive.append(taken > 0)
    fetched = normed_far[...]
    normed_far_t[...] = fetched.T
    half = core_half(scalars, part)
    keys_far[...] = dot_nn(fetched, w_key[:, half]).astype(jnp.bfloat16)
    values_far[...] = dot_nn(fetched, w_value[:, half]).astype(jnp.bfloat16)
    for p in range(part // pair):
        lanes = slice(p * pair, (p + 1) * pair)
        q, g, s_own = query_stack[p], grad_stack[p], scores_own[p]
        s_far = dot_nt(keys_far[:, lanes], q) * SCALE
        s_far = jnp.concatenate(
            [
                jnp.where(slot_alive[j], s_far[j * view_tokens : (j + 1) * view_tokens], MASKED)
                for j in range(groups - 1)
            ],
            axis=0,
        )
        highest = jnp.maximum(jnp.max(s_own, 0, keepdims=True), jnp.max(s_far, 0, keepdims=True))
        e_own = jnp.exp(s_own - highest)
        e_far = jnp.exp(s_far - highest)
        inverse = 1.0 / (jnp.sum(e_own, 0, keepdims=True) + jnp.sum(e_far, 0, keepdims=True))
        a_own, a_far = e_own * inverse, e_far * inverse
        attention_own[p], attention_far[p] = a_own, a_far
        a_own, a_far = a_own.astype(jnp.bfloat16), a_far.astype(jnp.bfloat16)
        mix = own_tn(a_own, values[:, lanes], views) + dot_tn(a_far, values_far[:, lanes])
        mixed_t[lanes, :] = unstacked(mix, views).T.astype(jnp.bfloat16)
        dvalue[:tokens, lanes] = own_nn(a_own, g, views).astype(jnp.bfloat16)
        dvalue[tokens:, lanes] = dot_nn(a_far, g).astype(jnp.bfloat16)


def backward_kernel(
    views, query_stack, grad_stack, dprob_own, keys, keys_far, values_far, attention_own, attention_far, dquery, dkey
):
    tokens, part = keys.shape
    pair = 2 * HEAD_DIM
    for p in range(part // pair):
        lanes = slice(p * pair, (p + 1) * pair)
        q, g, dp_own = query_stack[p], grad_stack[p], dprob_own[p]
        a_own, a_far = attention_own[p], attention_far[p]
        dp_far = dot_nt(values_far[:, lanes], g)
        delta = jnp.sum(a_own * dp_own, 0, keepdims=True) + jnp.sum(a_far * dp_far, 0, keepdims=True)
        ds_own = (a_own * (dp_own - delta) * SCALE).astype(jnp.bfloat16)
        ds_far = (a_far * (dp_far - delta) * SCALE).astype(jnp.bfloat16)
        dq = own_tn(ds_own, keys[:, lanes], views) + dot_tn(ds_far, keys_far[:, lanes])
        dquery[:, lanes] = unstacked(dq, views).astype(jnp.bfloat16)
        dkey[:tokens, lanes] = own_nn(ds_own, q, views).astype(jnp.bfloat16)
        dkey[tokens:, lanes] = dot_nn(ds_far, q).astype(jnp.bfloat16)


def times(lefts, right):
    total, start = 0.0, 0
    for left in lefts:
        total = total + dot_nn(left, right[start : start + left.shape[1], :])
        start += left.shape[1]
    return total


def by_quarters(scalars, lefts, right, sends, keep, x_first):
    size = keep.shape[1]
    x, y = scalars[3], scalars[4]
    for targets, first in ((sends, 1), ([keep.at[0], keep.at[1]], 0)):
        for second in (1, 0):
            dx, dy = (first, second) if x_first else (second, first)
            block = 2 * lax.bitwise_xor(y, jnp.int32(dy)) + lax.bitwise_xor(x, jnp.int32(dx))
            rows = pl.ds(pl.multiple_of(block * size, size), size)
            target = targets[second]
            target[...] = times([left[rows, :] for left in lefts], right).astype(target.dtype)


def query_key_kernel(
    scalars, normed_t, normed_far_t, dquery, dkey, q_later, k_later, q_now, k_now, q_keep, k_keep
):
    by_quarters(scalars, (normed_t,), dquery[...], (q_now, q_later), q_keep, True)
    by_quarters(scalars, (normed_t, normed_far_t), dkey[...], (k_now, k_later), k_keep, False)


def go_on_kernel(q_keep, q_got, k_keep, k_got, q_later, k_later):
    for keep, got, later in ((q_keep, q_got, q_later), (k_keep, k_got, k_later)):
        later[...] = (keep[1] + got[...].astype(jnp.float32)).astype(jnp.bfloat16)


def value_out_kernel(scalars, normed_t, normed_far_t, dvalue, mine, theirs, upstream, send, keep):
    row, x, y = scalars[0], scalars[3], scalars[4]
    odd = lax.rem(scalars[1], jnp.int32(2)) == 1
    _, _, pairs, size, _ = send.shape
    half, quarter = upstream.shape[1] // 2, normed_t.shape[0] // 4
    value_right = dvalue[...]
    lanes = value_right.shape[1]
    places = [(dy, dx, pair) for dy in range(2) for dx in range(2) for pair in range(pairs)]
    rows = {"send": ([], [], []), "keep": ([], [], [])}
    for dy in range(2):
        to_y = lax.bitwise_xor(y, jnp.int32(dy))
        for dx in range(2):
            to_x = lax.bitwise_xor(x, jnp.int32(dx))
            out_rows = pl.ds(pl.multiple_of(to_x * (half // 4), half // 4), half // 4)
            out_block = jnp.where(row == to_y, mine[out_rows, :], theirs[out_rows, :])
            value_rows = pl.ds(pl.multiple_of((2 * to_y + to_x) * quarter, quarter), quarter)
            blocks = (normed_t[value_rows, :], normed_far_t[value_rows, :], out_block)
            for pair in range(pairs):
                for i, block in enumerate(blocks):
                    count = size if i == 2 else 2 * size
                    first = block[2 * pair * count : (2 * pair + 1) * count]
                    second = block[(2 * pair + 1) * count : (2 * pair + 2) * count]
                    rows["send"][i].append(jnp.where(odd, first, second))
                    rows["keep"][i].append(jnp.where(odd, second, first))
    right = upstream[:, core_half(scalars, half)]
    for target, name in ((send, "send"), (keep, "keep")):
        own, far, out = [jnp.concatenate(parts, axis=0) for parts in rows[name]]
        grad_v = times((own, far), value_right).astype(target.dtype)
        grad_o = dot_nn(out, right).astype(target.dtype)
        for i, place in enumerate(places):
            target[(*place, slice(None), slice(0, half))] = grad_o[i * size : (i + 1) * size]
            for core in range(2):
                columns = slice(half + core * lanes, half + (core + 1) * lanes)
                part = grad_v[(2 * i + core) * size : (2 * i + core + 1) * size]
                target[(*place, slice(None), columns)] = part


def view_sum_kernel(keep, got, x_send, y_send, x_keep, y_keep):
    half = y_send.shape[3]
    for second in range(2):
        for target, first in ((x_send, 1), (x_keep, 0)):
            total = keep[second, first, :, :, half:] + got[second, first, :, :, half:].astype(jnp.float32)
            target[second] = total.astype(target.dtype)
        for target, first in ((y_send, 1), (y_keep, 0)):
            total = keep[first, second, :, :, :half] + got[first, second, :, :, :half].astype(jnp.float32)
            target[second] = total.astype(target.dtype)


def first_sum_kernel(x_keep, x_got, y_keep, y_got, x_later, y_later, x_now, y_now):
    for keep, got, later, now in ((x_keep, x_got, x_later, x_now), (y_keep, y_got, y_later, y_now)):
        later[...] = (keep[1] + got[1].astype(jnp.float32)).astype(jnp.bfloat16)
        now[...] = keep[0] + got[0].astype(jnp.float32)


def query_key_tiles_kernel(scalars, q_keep, q_first, q_second, k_keep, k_first, k_second, send, keep):
    odd = lax.rem(scalars[1], jnp.int32(2)) == 1
    total = [
        kept[0] + first[...].astype(jnp.float32) + second[...].astype(jnp.float32)
        for kept, first, second in ((q_keep, q_first, q_second), (k_keep, k_first, k_second))
    ]
    total = jnp.concatenate(total, axis=1)
    pairs, size, _ = send.shape
    for pair in range(pairs):
        first = total[2 * pair * size : (2 * pair + 1) * size]
        second = total[(2 * pair + 1) * size : (2 * pair + 2) * size]
        send[pair] = jnp.where(odd, first, second).astype(send.dtype)
        keep[pair] = jnp.where(odd, second, first)


def summed_tile(addends, place):
    place = pl.ds(place, 1)
    total = [now[place] + got[place].astype(jnp.float32) for now, got in zip(addends[::2], addends[1::2])]
    return (jnp.concatenate(total, axis=2) if len(total) == 2 else total[0])[0]


def view_bit(scalars, bit):
    return lax.rem(lax.div(scalars[1], jnp.int32(2 << bit)), jnp.int32(2))


def tile_halves_kernel(bit, scalars, *refs):
    addends, (send, keep) = refs[:-2], refs[-2:]
    count = keep.shape[0]
    mine = view_bit(scalars, bit)
    for target, part in ((send, 1 - mine), (keep, mine)):
        for i in range(count):
            target[i] = summed_tile(addends, part * count + i).astype(target.dtype)


def query_key_cores(tile, half):
    size = tile.shape[0] // 2
    return tile[:size], tile[size:]


def value_out_cores(tile, half):
    size, lanes = tile.shape[0] // 2, (tile.shape[1] - half) // 2
    parts = []
    for core in range(2):
        value = tile[:, half + core * lanes : half + (core + 1) * lanes]
        out = tile[core * size : (core + 1) * size, :half]
        parts.append(jnp.concatenate((out, value[:size], value[size:]), axis=1))
    return parts


def tile_cores_kernel(split, half, scalars, *refs):
    addends, (far_same, far_cross, near_cross, mine) = refs[:-4], refs[-4:]
    bit = view_bit(scalars, 0)
    for place, same, cross in ((1 - bit, far_same, far_cross), (bit, mine, near_cross)):
        parts = split(summed_tile(addends, place), half)
        same[...] = jnp.where(scalars[0] == 0, parts[0], parts[1]).astype(same.dtype)
        cross[...] = jnp.where(scalars[0] == 0, parts[1], parts[0]).astype(cross.dtype)


def last_sums(scalars, mine, far_same, near_cross, far_cross):
    for near, far, core in ((mine, far_same, scalars[0]), (near_cross, far_cross, 1 - scalars[0])):
        yield near[...] + far[...].astype(jnp.float32), core


def place_query_key_kernel(scalars, mine, far_same, near_cross, far_cross, query, key):
    size = query.shape[1] // 2
    for total, core in last_sums(scalars, mine, far_same, near_cross, far_cross):
        columns = pl.ds(pl.multiple_of(core * size, size), size)
        query[:, columns] = total[:, :size]
        key[:, columns] = total[:, size:]


def place_value_out_kernel(scalars, mine, far_same, near_cross, far_cross, value, out):
    size, width = mine.shape
    half, part = out.shape[1] // 2, value.shape[1] // 2
    for total, core in last_sums(scalars, mine, far_same, near_cross, far_cross):
        out[:, pl.ds(pl.multiple_of(core * half, half), half)] = total[:, :half]
        columns = pl.ds(pl.multiple_of(core * part, part), part)
        value[:size, columns] = total[:, half : half + part]
        value[size:, columns] = total[:, half + part :]


def params(mebibytes):
    return pltpu.CompilerParams(vmem_limit_bytes=mebibytes * MIB)


def shape(dims, kind):
    return jax.ShapeDtypeStruct(dims, kind)


def shards(latents, norm_gain, w_query, w_key, w_value, w_out, kernel, partners, counts, cotangent):
    views, strip_rows, columns, width = latents.shape[1:]
    inner = w_query.shape[1]
    groups, rows = lax.axis_size("view"), lax.axis_size("row")
    scenes = lax.axis_size("scene")
    assert (strip_rows, rows, scenes) == (1, 2, 4)
    strip = strip_rows * columns
    part = inner // rows
    tokens = views * 2 * strip
    key_tokens = tokens + (groups - 1) * 2 * strip
    bf16, f32, i32 = jnp.bfloat16, jnp.float32, jnp.int32

    row, view, scene = lax.axis_index("row"), lax.axis_index("view"), lax.axis_index("scene")
    scalars = jnp.stack((row, view, scene, scene % 2, scene // 2)).astype(i32)
    swap = [(0, 1), (1, 0)]
    along_x, along_y = [(i, i ^ 1) for i in range(scenes)], [(i, i ^ 2) for i in range(scenes)]

    alive = pl.pallas_call(
        functools.partial(alive_kernel, views, groups),
        in_specs=[SMEM],
        out_specs=SMEM,
        out_shape=shape((groups * views,), i32),
        cost_estimate=MUCH,
        compiler_params=params(4),
        name="alive",
    )(partners)
    between = [[(i, i ^ d) for i in range(groups)] for d in reversed(range(1, groups))]
    granted = [lax.ppermute(partners, "view", pairs) for pairs in between]

    granted, alive = lax.optimization_barrier((granted, alive))
    lat = latents[0].reshape(views, strip, width)
    cot = cotangent[0].reshape(views, strip, width)
    lat_other = lax.ppermute(lat, "row", swap)
    cot_other = lax.ppermute(cot, "row", swap)

    outgoing = pl.pallas_call(
        functools.partial(pick_kernel, groups),
        in_specs=[SMEM] * groups + [VMEM],
        out_specs=[VMEM] * (groups - 1),
        out_shape=[shape((strip, width), bf16)] * (groups - 1),
        compiler_params=params(8),
        cost_estimate=MUCH,
        name="pick",
    )(scalars, *granted, lat)
    got_own = [lax.ppermute(part_out, "view", pairs) for part_out, pairs in zip(outgoing, between)]
    head_pairs = part // (2 * HEAD_DIM)
    normed_t, keys, values, upstream, query_stack, grad_stack, scores_own, dprob_own = pl.pallas_call(
        project_kernel,
        in_specs=[SMEM] + [VMEM] * 10,
        out_specs=[VMEM] * 8,
        out_shape=[
            shape((width, tokens), bf16),
            shape((tokens, part), bf16),
            shape((tokens, part), bf16),
            shape((tokens, width), bf16),
            shape((head_pairs, 2 * tokens, 2 * HEAD_DIM), bf16),
            shape((head_pairs, 2 * tokens, 2 * HEAD_DIM), bf16),
            shape((head_pairs, 2 * strip, 2 * tokens), f32),
            shape((head_pairs, 2 * strip, 2 * tokens), f32),
        ],
        scratch_shapes=[pltpu.VMEM((tokens, width), bf16)],
        compiler_params=params(28),
        cost_estimate=LITTLE,
        name="project",
    )(scalars, lat, lat_other, cot, cot_other, norm_gain, kernel, w_query, w_key, w_value, w_out)

    got_own, normed_t = lax.optimization_barrier((got_own, normed_t))
    got_other = [lax.ppermute(got, "row", swap) for got in got_own]

    def call(kernel_body, results, operands, name, first=VMEM, mebibytes=16, cost=LITTLE):
        outputs = pl.pallas_call(
            kernel_body,
            in_specs=[first] + [VMEM] * (len(operands) - 1),
            out_specs=[VMEM] * len(results),
            out_shape=results,
            compiler_params=params(mebibytes),
            cost_estimate=cost,
            name=name,
        )(*operands)
        return list(outputs)

    far_tokens = key_tokens - tokens
    normed_far_t, keys_far, values_far, attention_own, attention_far, mixed_t, dvalue = pl.pallas_call(
        functools.partial(forward_kernel, views, groups),
        in_specs=[SMEM] * 2 + [VMEM] * (2 * groups - 2 + 7),
        out_specs=[VMEM] * 7,
        out_shape=[
            shape((width, far_tokens), bf16),
            shape((far_tokens, part), bf16),
            shape((far_tokens, part), bf16),
            shape((head_pairs, 2 * strip, 2 * tokens), f32),
            shape((head_pairs, far_tokens, 2 * tokens), f32),
            shape((part, tokens), bf16),
            shape((key_tokens, part), bf16),
        ],
        scratch_shapes=[pltpu.VMEM((far_tokens, width), bf16)],
        compiler_params=params(28 + groups // 2),
        cost_estimate=LITTLE,
        name="attention_forward",
    )(
        scalars, alive, *got_own, *got_other, query_stack, grad_stack, scores_own, values, norm_gain, w_key, w_value
    )
    mixed_other = lax.ppermute(mixed_t, "row", swap)
    dquery, dkey = call(
        functools.partial(backward_kernel, views),
        [shape((tokens, part), bf16), shape((key_tokens, part), bf16)],
        (query_stack, grad_stack, dprob_own, keys, keys_far, values_far, attention_own, attention_far),
        "attention_backward",
        mebibytes=28 + groups // 2,
    )

    def after(value, *earlier):
        return lax.optimization_barrier((value, *earlier))[0]

    targets = groups * rows
    q_size = width // 4
    q_rows, o_rows = q_size // targets, inner // (4 * targets)
    q_block = (q_size, part)

    def first_exchange(sends):
        return lax.ppermute(sends[0], "scene", along_x), lax.ppermute(sends[1], "scene", along_y)

    def first_sum(parts, got, name, cost=LITTLE):
        blocks = [part_now.shape[1:] for part_now in parts[:2]]
        results = [shape(block, bf16) for block in blocks] + [shape(block, f32) for block in blocks]
        return call(first_sum_kernel, results, (parts[2], got[0], parts[3], got[1]), name, cost=cost)

    def second_exchange(sums):
        return lax.ppermute(sums[0], "scene", along_y), lax.ppermute(sums[1], "scene", along_x)

    pairs = groups // 2
    neighbours = [(i, i ^ 1) for i in range(groups)]
    split_rows = {"query_key": q_rows, "value_out": o_rows}

    def last_parts(addends, split, name):
        tile = (addends[0].shape[1], sum(now.shape[2] for now in addends[::2]))
        for bit in reversed(range(1, pairs.bit_length() - 1)):
            send, keep = call(
                functools.partial(tile_halves_kernel, bit),
                [shape((1 << bit, *tile), kind) for kind in (bf16, f32)],
                (scalars, *addends),
                "view_bit_" + name,
                SMEM,
            )
            addends = (keep, lax.ppermute(send, "view", [(i, i ^ (2 << bit)) for i in range(groups)]))
        lanes = tile[0] * tile[1] // (2 * split_rows[name])
        columns = width // 2
        far_same, far_cross, near_cross, mine = call(
            functools.partial(tile_cores_kernel, split, columns),
            [shape((split_rows[name], lanes), kind) for kind in (bf16, bf16, f32, f32)],
            (scalars, *addends),
            "last_parts_" + name,
            SMEM,
        )
        far_same = lax.ppermute(far_same, "view", [(i, i ^ 2) for i in range(groups)])
        far_cross = lax.ppermute(far_cross, ("view", "row"), [(i, i ^ 5) for i in range(targets)])
        near_cross = lax.ppermute(near_cross, "row", swap)
        return mine, far_same, near_cross, far_cross

    tile = (2 * o_rows, width // 2 + 2 * part)
    send, keep = call(
        value_out_kernel,
        [shape((2, 2, pairs, *tile), kind) for kind in (bf16, f32)],
        (scalars, normed_t, normed_far_t, after(dvalue, dkey), mixed_t, mixed_other, upstream),
        "grad_value_out",
        SMEM,
        24,
    )
    got = lax.ppermute(send, "view", neighbours)
    q_later, k_later, q_now, k_now, q_keep, k_keep = call(
        query_key_kernel,
        [shape(block, bf16) for block in (q_block, q_block, q_block, q_block)]
        + [shape((2, *block), f32) for block in (q_block, q_block)],
        (scalars, normed_t, normed_far_t, after(dquery, send), dkey),
        "grad_query_key",
        SMEM,
        24,
    )
    q_got, k_got = first_exchange((q_later, k_later))
    q_first, k_first = first_exchange((q_now, k_now))
    later = call(
        go_on_kernel, [shape(q_block, bf16), shape(q_block, bf16)], (q_keep, q_got, k_keep, k_got), "first_sum_query_key"
    )
    q_second, k_second = second_exchange(later)
    qk_tile = (2 * q_rows, 2 * part)
    qk_send, qk_keep = call(
        query_key_tiles_kernel,
        [shape((pairs, *qk_tile), kind) for kind in (bf16, f32)],
        (scalars, q_keep, q_first, q_second, k_keep, k_first, k_second),
        "second_sum_query_key",
        SMEM,
    )
    qk_addends = (qk_keep, lax.ppermute(qk_send, "view", neighbours))
    x_shape, y_shape = (2, pairs, 2 * o_rows, 2 * part), (2, pairs, 2 * o_rows, width // 2)
    vo_parts = call(
        view_sum_kernel,
        [shape(x_shape, bf16), shape(y_shape, bf16), shape(x_shape, f32), shape(y_shape, f32)],
        (keep, after(got, qk_send)),
        "view_sum_value_out",
    )
    vo_got = first_exchange(vo_parts)
    qk_last = last_parts(qk_addends, query_key_cores, "query_key")
    vo_parts[2] = after(vo_parts[2], qk_last[0])
    vo_sums = first_sum(vo_parts, vo_got, "first_sum_value_out")
    v_got, o_got = second_exchange(vo_sums)
    addends = (vo_sums[3], o_got, vo_sums[2], v_got)
    vo_last = last_parts((after(addends[0], qk_last[1], qk_last[3]), *addends[1:]), value_out_cores, "value_out")
    grad_query, grad_key = call(
        place_query_key_kernel,
        [shape((q_rows, inner), f32)] * 2,
        (scalars, *qk_last),
        "last_sum_query_key",
        SMEM,
    )
    grad_value, grad_out = call(
        place_value_out_kernel,
        [shape((q_rows, inner), f32), shape((o_rows, width), f32)],
        (scalars, after(vo_last[0], grad_query), *vo_last[1:]),
        "last_sum_value_out",
        SMEM,
    )
    return grad_query, grad_key, grad_value, grad_out


def solution(mesh):
    tokens = P("scene", "view", "row", None, None)
    everywhere = P()
    grads = P(("scene", "view", "row"), None)
    return jax.shard_map(
        shards,
        mesh=mesh,
        in_specs=(
            tokens, everywhere, everywhere, everywhere, everywhere, everywhere, everywhere,
            P("scene", "view", None), P("scene", "view"), tokens,
        ),
        out_specs=(grads, grads, grads, grads),
        check_vma=False,
    )
```

```python
import functools

import jax
import jax.numpy as jnp
from jax import lax
from jax.experimental import pallas as pl
from jax.experimental.pallas import tpu as pltpu
from jax.sharding import PartitionSpec as P

HEAD_DIM = 64
EPSILON = 1e-06
SCALE = HEAD_DIM ** (-0.5)
MASKED = -1e30
MIB = 1024 * 1024
LITTLE = pl.CostEstimate(flops=1, bytes_accessed=1, transcendentals=0)
MUCH = pl.CostEstimate(flops=40_000_000_000, bytes_accessed=1, transcendentals=0)

VMEM = pl.BlockSpec(memory_space=pltpu.VMEM)
SMEM = pl.BlockSpec(memory_space=pltpu.SMEM)


def dot_nn(a, b):
    return lax.dot_general(a, b, (((1,), (0,)), ((), ())), preferred_element_type=jnp.float32)


def dot_nt(a, b):
    return lax.dot_general(a, b, (((1,), (1,)), ((), ())), preferred_element_type=jnp.float32)


def dot_tn(a, b):
    return lax.dot_general(a, b, (((0,), (0,)), ((), ())), preferred_element_type=jnp.float32)


def normalized(tokens, gain):
    x = tokens.astype(jnp.float32)
    mean = jnp.mean(x * x, -1, keepdims=True)
    return (x * lax.rsqrt(mean + EPSILON) * gain).astype(jnp.bfloat16)


def alive_kernel(views, groups, partners, alive):
    for g in range(groups * views):
        alive[g] = 0
    for u in range(views):
        for j in range(partners.shape[2]):
            partner = partners[0, u, j]

            @pl.when(partner >= 0)
            def _():
                alive[lax.div(partner, jnp.int32(views)) * views + u] = 1


def pick_kernel(groups, scalars, *refs):
    tables, lat, outgoing = refs[: groups - 1], refs[groups - 1], refs[groups:]
    views = lat.shape[0]
    for table, out in zip(tables, outgoing):
        wanted = jnp.int32(0)
        for u in range(table.shape[1]):
            for j in range(table.shape[2]):
                partner = table[0, u, j]
                here = (partner >= 0) & (lax.div(partner, jnp.int32(views)) == scalars[1])
                wanted = jnp.where(here, lax.rem(partner, jnp.int32(views)), wanted)
        out[...] = lat[wanted]


def core_half(scalars, size):
    return pl.ds(pl.multiple_of(scalars[0] * size, size), size)


def stacked(x, views):
    tokens, pair = x.shape
    low = (lax.broadcasted_iota(jnp.int32, (1, 1, pair), 2) < pair // 2).astype(x.dtype)
    x = x.reshape(views, tokens // views, pair)
    return jnp.concatenate((x * low, x * (1 - low)), axis=1).reshape(2 * tokens, pair)


def unstacked(x, views):
    rows, pair = x.shape
    low = lax.broadcasted_iota(jnp.int32, (1, 1, pair), 2) < pair // 2
    x = x.reshape(views, 2, rows // (2 * views), pair)
    return jnp.where(low, x[:, 0], x[:, 1]).reshape(rows // 2, pair)


def view_parts(x, views, axis):
    size = x.shape[axis] // views
    return [lax.slice_in_dim(x, u * size, (u + 1) * size, axis=axis) for u in range(views)]


def own_nt(a, b, views):
    pairs = zip(view_parts(a, views, 0), view_parts(b, views, 0))
    return jnp.concatenate([dot_nt(x, y) for x, y in pairs], axis=1)


def own_tn(a, b, views):
    pairs = zip(view_parts(a, views, 1), view_parts(b, views, 0))
    return jnp.concatenate([dot_tn(x, y) for x, y in pairs], axis=0)


def own_nn(a, b, views):
    pairs = zip(view_parts(a, views, 1), view_parts(b, views, 0))
    return jnp.concatenate([dot_nn(x, y) for x, y in pairs], axis=0)


def project_kernel(
    scalars, lat_own, lat_other, cot_own, cot_other, gain, taps, w_query, w_key, w_value, w_out,
    normed_t, keys, values, upstream, query_stack, grad_stack, scores_own, dprob_own, normed,
):
    views, strip, width = lat_own.shape
    scale = gain[...].reshape(1, width)
    row = scalars[0]

    def strip_of(u, half):
        index = 2 * u + (row if half == 0 else 1 - row)
        return pl.ds(pl.multiple_of(index * strip, strip), strip)

    for half, source in enumerate((lat_own, lat_other)):
        for u in range(views):
            normed[strip_of(u, half), :] = normalized(source[u], scale)
    first = row == 0
    chunk = 512
    column = lax.broadcasted_iota(jnp.int32, (strip, 1), 0)
    not_first = (column > 0).astype(jnp.float32)
    not_last = (column < strip - 1).astype(jnp.float32)
    for c in range(0, width, chunk):
        lanes = slice(c, c + chunk)
        tap = taps[:, lanes].astype(jnp.float32)
        top, middle, bottom = tap[0:3], tap[3:6], tap[6:9]
        cross = (jnp.where(first, top, bottom), jnp.where(first, bottom, top))
        for u in range(views):
            strips = [ref[u, :, lanes].astype(jnp.float32) for ref in (cot_own, cot_other)]
            shifted = []
            for x in strips:
                after = pltpu.roll(x, strip - 1, 0) * not_last
                before = pltpu.roll(x, 1, 0) * not_first
                shifted.append((after, x, before))
            for half in range(2):
                total = strips[half]
                for b in range(3):
                    total = total + middle[b : b + 1] * shifted[half][b]
                    total = total + cross[half][b : b + 1] * shifted[1 - half][b]
                upstream[strip_of(u, half), lanes] = total.astype(jnp.bfloat16)
    rows = normed[...]
    normed_t[...] = rows.T
    part = keys.shape[1]
    half = core_half(scalars, part)
    queries = dot_nn(rows, w_query[:, half]).astype(jnp.bfloat16)
    keys[...] = dot_nn(rows, w_key[:, half]).astype(jnp.bfloat16)
    values[...] = dot_nn(rows, w_value[:, half]).astype(jnp.bfloat16)
    out_grad = dot_nt(upstream[...], w_out[half, :]).astype(jnp.bfloat16)
    pair = 2 * HEAD_DIM
    for p in range(part // pair):
        lanes = slice(p * pair, (p + 1) * pair)
        q, g = stacked(queries[:, lanes], views), stacked(out_grad[:, lanes], views)
        query_stack[p], grad_stack[p] = q, g
        scores_own[p] = own_nt(keys[:, lanes], q, views) * SCALE
        dprob_own[p] = own_nt(values[:, lanes], g, views)


def forward_kernel(views, groups, scalars, alive, *refs):
    got_own, got_other, refs = refs[: groups - 1], refs[groups - 1 : 2 * groups - 2], refs[2 * groups - 2 :]
    query_stack, grad_stack, scores_own, values, gain, w_key, w_value, *refs = refs
    normed_far_t, keys_far, values_far, attention_own, attention_far, mixed_t, dvalue, normed_far = refs
    strip = got_own[0].shape[0]
    tokens, part = values.shape
    view_tokens = tokens // views
    here = scalars[1]
    scale_row = gain[...].reshape(1, normed_far.shape[1])
    pair = 2 * HEAD_DIM
    span = 2 * view_tokens
    column_view = lax.broadcasted_iota(jnp.int32, (1, views * span), 1) // span
    slot_alive = []
    for j in range(groups - 1):
        group = lax.bitwise_xor(here, jnp.int32(groups - 1 - j))
        start = 2 * j * strip
        normed_far[start : start + strip, :] = normalized(got_own[j][...], scale_row)
        normed_far[start + strip : start + 2 * strip, :] = normalized(got_other[j][...], scale_row)
        taken = jnp.zeros((1, views * span), jnp.int32)
        for u in range(views):
            taken = jnp.where(column_view == u, alive[group * views + u], taken)
        slot_alive.append(taken > 0)
    fetched = normed_far[...]
    normed_far_t[...] = fetched.T
    half = core_half(scalars, part)
    keys_far[...] = dot_nn(fetched, w_key[:, half]).astype(jnp.bfloat16)
    values_far[...] = dot_nn(fetched, w_value[:, half]).astype(jnp.bfloat16)
    for p in range(part // pair):
        lanes = slice(p * pair, (p + 1) * pair)
        q, g, s_own = query_stack[p], grad_stack[p], scores_own[p]
        s_far = dot_nt(keys_far[:, lanes], q) * SCALE
        s_far = jnp.concatenate(
            [
                jnp.where(slot_alive[j], s_far[j * view_tokens : (j + 1) * view_tokens], MASKED)
                for j in range(groups - 1)
            ],
            axis=0,
        )
        highest = jnp.maximum(jnp.max(s_own, 0, keepdims=True), jnp.max(s_far, 0, keepdims=True))
        e_own = jnp.exp(s_own - highest)
        e_far = jnp.exp(s_far - highest)
        inverse = 1.0 / (jnp.sum(e_own, 0, keepdims=True) + jnp.sum(e_far, 0, keepdims=True))
        a_own, a_far = e_own * inverse, e_far * inverse
        attention_own[p], attention_far[p] = a_own, a_far
        a_own, a_far = a_own.astype(jnp.bfloat16), a_far.astype(jnp.bfloat16)
        mix = own_tn(a_own, values[:, lanes], views) + dot_tn(a_far, values_far[:, lanes])
        mixed_t[lanes, :] = unstacked(mix, views).T.astype(jnp.bfloat16)
        dvalue[:tokens, lanes] = own_nn(a_own, g, views).astype(jnp.bfloat16)
        dvalue[tokens:, lanes] = dot_nn(a_far, g).astype(jnp.bfloat16)


def backward_kernel(
    views, query_stack, grad_stack, dprob_own, keys, keys_far, values_far, attention_own, attention_far, dquery, dkey
):
    tokens, part = keys.shape
    pair = 2 * HEAD_DIM
    for p in range(part // pair):
        lanes = slice(p * pair, (p + 1) * pair)
        q, g, dp_own = query_stack[p], grad_stack[p], dprob_own[p]
        a_own, a_far = attention_own[p], attention_far[p]
        dp_far = dot_nt(values_far[:, lanes], g)
        delta = jnp.sum(a_own * dp_own, 0, keepdims=True) + jnp.sum(a_far * dp_far, 0, keepdims=True)
        ds_own = (a_own * (dp_own - delta) * SCALE).astype(jnp.bfloat16)
        ds_far = (a_far * (dp_far - delta) * SCALE).astype(jnp.bfloat16)
        dq = own_tn(ds_own, keys[:, lanes], views) + dot_tn(ds_far, keys_far[:, lanes])
        dquery[:, lanes] = unstacked(dq, views).astype(jnp.bfloat16)
        dkey[:tokens, lanes] = own_nn(ds_own, q, views).astype(jnp.bfloat16)
        dkey[tokens:, lanes] = dot_nn(ds_far, q).astype(jnp.bfloat16)


def times(lefts, right):
    total, start = 0.0, 0
    for left in lefts:
        total = total + dot_nn(left, right[start : start + left.shape[1], :])
        start += left.shape[1]
    return total


def by_quarters(scalars, lefts, right, sends, keep, x_first):
    size = keep.shape[1]
    x, y = scalars[3], scalars[4]
    for targets, first in ((sends, 1), ([keep.at[0], keep.at[1]], 0)):
        for second in (1, 0):
            dx, dy = (first, second) if x_first else (second, first)
            block = 2 * lax.bitwise_xor(y, jnp.int32(dy)) + lax.bitwise_xor(x, jnp.int32(dx))
            rows = pl.ds(pl.multiple_of(block * size, size), size)
            target = targets[second]
            target[...] = times([left[rows, :] for left in lefts], right).astype(target.dtype)


def query_key_kernel(
    scalars, normed_t, normed_far_t, dquery, dkey, q_later, k_later, q_now, k_now, q_keep, k_keep
):
    by_quarters(scalars, (normed_t,), dquery[...], (q_now, q_later), q_keep, True)
    by_quarters(scalars, (normed_t, normed_far_t), dkey[...], (k_now, k_later), k_keep, False)


def go_on_kernel(q_keep, q_got, k_keep, k_got, q_later, k_later):
    for keep, got, later in ((q_keep, q_got, q_later), (k_keep, k_got, k_later)):
        later[...] = (keep[1] + got[...].astype(jnp.float32)).astype(jnp.bfloat16)


def value_out_kernel(scalars, normed_t, normed_far_t, dvalue, mine, theirs, upstream, send, keep):
    row, x, y = scalars[0], scalars[3], scalars[4]
    odd = lax.rem(scalars[1], jnp.int32(2)) == 1
    _, _, pairs, size, _ = send.shape
    half, quarter = upstream.shape[1] // 2, normed_t.shape[0] // 4
    value_right = dvalue[...]
    lanes = value_right.shape[1]
    places = [(dy, dx, pair) for dy in range(2) for dx in range(2) for pair in range(pairs)]
    rows = {"send": ([], [], []), "keep": ([], [], [])}
    for dy in range(2):
        to_y = lax.bitwise_xor(y, jnp.int32(dy))
        for dx in range(2):
            to_x = lax.bitwise_xor(x, jnp.int32(dx))
            out_rows = pl.ds(pl.multiple_of(to_x * (half // 4), half // 4), half // 4)
            out_block = jnp.where(row == to_y, mine[out_rows, :], theirs[out_rows, :])
            value_rows = pl.ds(pl.multiple_of((2 * to_y + to_x) * quarter, quarter), quarter)
            blocks = (normed_t[value_rows, :], normed_far_t[value_rows, :], out_block)
            for pair in range(pairs):
                for i, block in enumerate(blocks):
                    count = size if i == 2 else 2 * size
                    first = block[2 * pair * count : (2 * pair + 1) * count]
                    second = block[(2 * pair + 1) * count : (2 * pair + 2) * count]
                    rows["send"][i].append(jnp.where(odd, first, second))
                    rows["keep"][i].append(jnp.where(odd, second, first))
    right = upstream[:, core_half(scalars, half)]
    for target, name in ((send, "send"), (keep, "keep")):
        own, far, out = [jnp.concatenate(parts, axis=0) for parts in rows[name]]
        grad_v = times((own, far), value_right).astype(target.dtype)
        grad_o = dot_nn(out, right).astype(target.dtype)
        for i, place in enumerate(places):
            target[(*place, slice(None), slice(0, half))] = grad_o[i * size : (i + 1) * size]
            for core in range(2):
                columns = slice(half + core * lanes, half + (core + 1) * lanes)
                part = grad_v[(2 * i + core) * size : (2 * i + core + 1) * size]
                target[(*place, slice(None), columns)] = part


def view_sum_kernel(keep, got, x_send, y_send, x_keep, y_keep):
    half = y_send.shape[3]
    for second in range(2):
        for target, first in ((x_send, 1), (x_keep, 0)):
            total = keep[second, first, :, :, half:] + got[second, first, :, :, half:].astype(jnp.float32)
            target[second] = total.astype(target.dtype)
        for target, first in ((y_send, 1), (y_keep, 0)):
            total = keep[first, second, :, :, :half] + got[first, second, :, :, :half].astype(jnp.float32)
            target[second] = total.astype(target.dtype)


def first_sum_kernel(x_keep, x_got, y_keep, y_got, x_later, y_later, x_now, y_now):
    for keep, got, later, now in ((x_keep, x_got, x_later, x_now), (y_keep, y_got, y_later, y_now)):
        later[...] = (keep[1] + got[1].astype(jnp.float32)).astype(jnp.bfloat16)
        now[...] = keep[0] + got[0].astype(jnp.float32)


def query_key_tiles_kernel(scalars, q_keep, q_first, q_second, k_keep, k_first, k_second, send, keep):
    odd = lax.rem(scalars[1], jnp.int32(2)) == 1
    total = [
        kept[0] + first[...].astype(jnp.float32) + second[...].astype(jnp.float32)
        for kept, first, second in ((q_keep, q_first, q_second), (k_keep, k_first, k_second))
    ]
    total = jnp.concatenate(total, axis=1)
    pairs, size, _ = send.shape
    for pair in range(pairs):
        first = total[2 * pair * size : (2 * pair + 1) * size]
        second = total[(2 * pair + 1) * size : (2 * pair + 2) * size]
        send[pair] = jnp.where(odd, first, second).astype(send.dtype)
        keep[pair] = jnp.where(odd, second, first)


def summed_tile(addends, place):
    place = pl.ds(place, 1)
    total = [now[place] + got[place].astype(jnp.float32) for now, got in zip(addends[::2], addends[1::2])]
    return (jnp.concatenate(total, axis=2) if len(total) == 2 else total[0])[0]


def view_bit(scalars, bit):
    return lax.rem(lax.div(scalars[1], jnp.int32(2 << bit)), jnp.int32(2))


def tile_halves_kernel(bit, scalars, *refs):
    addends, (send, keep) = refs[:-2], refs[-2:]
    count = keep.shape[0]
    mine = view_bit(scalars, bit)
    for target, part in ((send, 1 - mine), (keep, mine)):
        for i in range(count):
            target[i] = summed_tile(addends, part * count + i).astype(target.dtype)


def query_key_cores(tile, half):
    size = tile.shape[0] // 2
    return tile[:size], tile[size:]


def value_out_cores(tile, half):
    size, lanes = tile.shape[0] // 2, (tile.shape[1] - half) // 2
    parts = []
    for core in range(2):
        value = tile[:, half + core * lanes : half + (core + 1) * lanes]
        out = tile[core * size : (core + 1) * size, :half]
        parts.append(jnp.concatenate((out, value[:size], value[size:]), axis=1))
    return parts


def tile_cores_kernel(split, half, scalars, *refs):
    addends, (far_same, far_cross, near_cross, mine) = refs[:-4], refs[-4:]
    bit = view_bit(scalars, 0)
    for place, same, cross in ((1 - bit, far_same, far_cross), (bit, mine, near_cross)):
        parts = split(summed_tile(addends, place), half)
        same[...] = jnp.where(scalars[0] == 0, parts[0], parts[1]).astype(same.dtype)
        cross[...] = jnp.where(scalars[0] == 0, parts[1], parts[0]).astype(cross.dtype)


def last_sums(scalars, mine, far_same, near_cross, far_cross):
    for near, far, core in ((mine, far_same, scalars[0]), (near_cross, far_cross, 1 - scalars[0])):
        yield near[...] + far[...].astype(jnp.float32), core


def place_query_key_kernel(scalars, mine, far_same, near_cross, far_cross, query, key):
    size = query.shape[1] // 2
    for total, core in last_sums(scalars, mine, far_same, near_cross, far_cross):
        columns = pl.ds(pl.multiple_of(core * size, size), size)
        query[:, columns] = total[:, :size]
        key[:, columns] = total[:, size:]


def place_value_out_kernel(scalars, mine, far_same, near_cross, far_cross, value, out):
    size, width = mine.shape
    half, part = out.shape[1] // 2, value.shape[1] // 2
    for total, core in last_sums(scalars, mine, far_same, near_cross, far_cross):
        out[:, pl.ds(pl.multiple_of(core * half, half), half)] = total[:, :half]
        columns = pl.ds(pl.multiple_of(core * part, part), part)
        value[:size, columns] = total[:, half : half + part]
        value[size:, columns] = total[:, half + part :]


def params(mebibytes):
    return pltpu.CompilerParams(vmem_limit_bytes=mebibytes * MIB)


def shape(dims, kind):
    return jax.ShapeDtypeStruct(dims, kind)


def shards(latents, norm_gain, w_query, w_key, w_value, w_out, kernel, partners, counts, cotangent):
    views, strip_rows, columns, width = latents.shape[1:]
    inner = w_query.shape[1]
    groups, rows = lax.axis_size("view"), lax.axis_size("row")
    scenes = lax.axis_size("scene")
    assert (strip_rows, rows, scenes) == (1, 2, 4)
    strip = strip_rows * columns
    part = inner // rows
    tokens = views * 2 * strip
    key_tokens = tokens + (groups - 1) * 2 * strip
    bf16, f32, i32 = jnp.bfloat16, jnp.float32, jnp.int32

    row, view, scene = lax.axis_index("row"), lax.axis_index("view"), lax.axis_index("scene")
    scalars = jnp.stack((row, view, scene, scene % 2, scene // 2)).astype(i32)
    swap = [(0, 1), (1, 0)]
    along_x, along_y = [(i, i ^ 1) for i in range(scenes)], [(i, i ^ 2) for i in range(scenes)]

    alive = pl.pallas_call(
        functools.partial(alive_kernel, views, groups),
        in_specs=[SMEM],
        out_specs=SMEM,
        out_shape=shape((groups * views,), i32),
        cost_estimate=MUCH,
        compiler_params=params(4),
        name="alive",
    )(partners)
    between = [[(i, i ^ d) for i in range(groups)] for d in reversed(range(1, groups))]
    granted = [lax.ppermute(partners, "view", pairs) for pairs in between]

    granted, alive = lax.optimization_barrier((granted, alive))
    lat = latents[0].reshape(views, strip, width)
    cot = cotangent[0].reshape(views, strip, width)
    lat_other = lax.ppermute(lat, "row", swap)
    cot_other = lax.ppermute(cot, "row", swap)

    outgoing = pl.pallas_call(
        functools.partial(pick_kernel, groups),
        in_specs=[SMEM] * groups + [VMEM],
        out_specs=[VMEM] * (groups - 1),
        out_shape=[shape((strip, width), bf16)] * (groups - 1),
        compiler_params=params(8),
        cost_estimate=MUCH,
        name="pick",
    )(scalars, *granted, lat)
    got_own = [lax.ppermute(part_out, "view", pairs) for part_out, pairs in zip(outgoing, between)]
    head_pairs = part // (2 * HEAD_DIM)
    normed_t, keys, values, upstream, query_stack, grad_stack, scores_own, dprob_own = pl.pallas_call(
        project_kernel,
        in_specs=[SMEM] + [VMEM] * 10,
        out_specs=[VMEM] * 8,
        out_shape=[
            shape((width, tokens), bf16),
            shape((tokens, part), bf16),
            shape((tokens, part), bf16),
            shape((tokens, width), bf16),
            shape((head_pairs, 2 * tokens, 2 * HEAD_DIM), bf16),
            shape((head_pairs, 2 * tokens, 2 * HEAD_DIM), bf16),
            shape((head_pairs, 2 * strip, 2 * tokens), f32),
            shape((head_pairs, 2 * strip, 2 * tokens), f32),
        ],
        scratch_shapes=[pltpu.VMEM((tokens, width), bf16)],
        compiler_params=params(28),
        cost_estimate=LITTLE,
        name="project",
    )(scalars, lat, lat_other, cot, cot_other, norm_gain, kernel, w_query, w_key, w_value, w_out)

    got_own, normed_t = lax.optimization_barrier((got_own, normed_t))
    got_other = [lax.ppermute(got, "row", swap) for got in got_own]

    def call(kernel_body, results, operands, name, first=VMEM, mebibytes=16, cost=LITTLE):
        outputs = pl.pallas_call(
            kernel_body,
            in_specs=[first] + [VMEM] * (len(operands) - 1),
            out_specs=[VMEM] * len(results),
            out_shape=results,
            compiler_params=params(mebibytes),
            cost_estimate=cost,
            name=name,
        )(*operands)
        return list(outputs)

    far_tokens = key_tokens - tokens
    normed_far_t, keys_far, values_far, attention_own, attention_far, mixed_t, dvalue = pl.pallas_call(
        functools.partial(forward_kernel, views, groups),
        in_specs=[SMEM] * 2 + [VMEM] * (2 * groups - 2 + 7),
        out_specs=[VMEM] * 7,
        out_shape=[
            shape((width, far_tokens), bf16),
            shape((far_tokens, part), bf16),
            shape((far_tokens, part), bf16),
            shape((head_pairs, 2 * strip, 2 * tokens), f32),
            shape((head_pairs, far_tokens, 2 * tokens), f32),
            shape((part, tokens), bf16),
            shape((key_tokens, part), bf16),
        ],
        scratch_shapes=[pltpu.VMEM((far_tokens, width), bf16)],
        compiler_params=params(28 + groups // 2),
        cost_estimate=LITTLE,
        name="attention_forward",
    )(
        scalars, alive, *got_own, *got_other, query_stack, grad_stack, scores_own, values, norm_gain, w_key, w_value
    )
    mixed_other = lax.ppermute(mixed_t, "row", swap)
    dquery, dkey = call(
        functools.partial(backward_kernel, views),
        [shape((tokens, part), bf16), shape((key_tokens, part), bf16)],
        (query_stack, grad_stack, dprob_own, keys, keys_far, values_far, attention_own, attention_far),
        "attention_backward",
        mebibytes=28 + groups // 2,
    )

    def after(value, *earlier):
        return lax.optimization_barrier((value, *earlier))[0]

    targets = groups * rows
    q_size = width // 4
    q_rows, o_rows = q_size // targets, inner // (4 * targets)
    q_block = (q_size, part)

    def first_exchange(sends):
        return lax.ppermute(sends[0], "scene", along_x), lax.ppermute(sends[1], "scene", along_y)

    def first_sum(parts, got, name, cost=LITTLE):
        blocks = [part_now.shape[1:] for part_now in parts[:2]]
        results = [shape(block, bf16) for block in blocks] + [shape(block, f32) for block in blocks]
        return call(first_sum_kernel, results, (parts[2], got[0], parts[3], got[1]), name, cost=cost)

    def second_exchange(sums):
        return lax.ppermute(sums[0], "scene", along_y), lax.ppermute(sums[1], "scene", along_x)

    pairs = groups // 2
    neighbours = [(i, i ^ 1) for i in range(groups)]
    split_rows = {"query_key": q_rows, "value_out": o_rows}

    def last_parts(addends, split, name):
        tile = (addends[0].shape[1], sum(now.shape[2] for now in addends[::2]))
        for bit in reversed(range(1, pairs.bit_length() - 1)):
            send, keep = call(
                functools.partial(tile_halves_kernel, bit),
                [shape((1 << bit, *tile), kind) for kind in (bf16, f32)],
                (scalars, *addends),
                "view_bit_" + name,
                SMEM,
            )
            addends = (keep, lax.ppermute(send, "view", [(i, i ^ (2 << bit)) for i in range(groups)]))
        lanes = tile[0] * tile[1] // (2 * split_rows[name])
        columns = width // 2
        far_same, far_cross, near_cross, mine = call(
            functools.partial(tile_cores_kernel, split, columns),
            [shape((split_rows[name], lanes), kind) for kind in (bf16, bf16, f32, f32)],
            (scalars, *addends),
            "last_parts_" + name,
            SMEM,
        )
        far_same = lax.ppermute(far_same, "view", [(i, i ^ 2) for i in range(groups)])
        far_cross = lax.ppermute(far_cross, ("view", "row"), [(i, i ^ 5) for i in range(targets)])
        near_cross = lax.ppermute(near_cross, "row", swap)
        return mine, far_same, near_cross, far_cross

    tile = (2 * o_rows, width // 2 + 2 * part)
    send, keep = call(
        value_out_kernel,
        [shape((2, 2, pairs, *tile), kind) for kind in (bf16, f32)],
        (scalars, normed_t, normed_far_t, after(dvalue, dkey), mixed_t, mixed_other, upstream),
        "grad_value_out",
        SMEM,
        24,
    )
    got = lax.ppermute(send, "view", neighbours)
    q_later, k_later, q_now, k_now, q_keep, k_keep = call(
        query_key_kernel,
        [shape(block, bf16) for block in (q_block, q_block, q_block, q_block)]
        + [shape((2, *block), f32) for block in (q_block, q_block)],
        (scalars, normed_t, normed_far_t, after(dquery, send), dkey),
        "grad_query_key",
        SMEM,
        24,
    )
    q_got, k_got = first_exchange((q_later, k_later))
    q_first, k_first = first_exchange((q_now, k_now))
    later = call(
        go_on_kernel, [shape(q_block, bf16), shape(q_block, bf16)], (q_keep, q_got, k_keep, k_got), "first_sum_query_key"
    )
    q_second, k_second = second_exchange(later)
    qk_tile = (2 * q_rows, 2 * part)
    qk_send, qk_keep = call(
        query_key_tiles_kernel,
        [shape((pairs, *qk_tile), kind) for kind in (bf16, f32)],
        (scalars, q_keep, q_first, q_second, k_keep, k_first, k_second),
        "second_sum_query_key",
        SMEM,
    )
    qk_addends = (qk_keep, lax.ppermute(qk_send, "view", neighbours))
    x_shape, y_shape = (2, pairs, 2 * o_rows, 2 * part), (2, pairs, 2 * o_rows, width // 2)
    vo_parts = call(
        view_sum_kernel,
        [shape(x_shape, bf16), shape(y_shape, bf16), shape(x_shape, f32), shape(y_shape, f32)],
        (keep, after(got, qk_send)),
        "view_sum_value_out",
    )
    vo_got = first_exchange(vo_parts)
    qk_last = last_parts(qk_addends, query_key_cores, "query_key")
    vo_parts[2] = after(vo_parts[2], qk_last[0])
    vo_sums = first_sum(vo_parts, vo_got, "first_sum_value_out")
    v_got, o_got = second_exchange(vo_sums)
    addends = (vo_sums[3], o_got, vo_sums[2], v_got)
    grad_query, grad_key = call(
        place_query_key_kernel,
        [shape((q_rows, inner), f32)] * 2,
        (scalars, *qk_last),
        "last_sum_query_key",
        SMEM,
        cost=MUCH,
    )
    vo_last = last_parts((after(addends[0], grad_query), *addends[1:]), value_out_cores, "value_out")
    grad_value, grad_out = call(
        place_value_out_kernel,
        [shape((q_rows, inner), f32), shape((o_rows, width), f32)],
        (scalars, *vo_last),
        "last_sum_value_out",
        SMEM,
    )
    return grad_query, grad_key, grad_value, grad_out


def solution(mesh):
    tokens = P("scene", "view", "row", None, None)
    everywhere = P()
    grads = P(("scene", "view", "row"), None)
    return jax.shard_map(
        shards,
        mesh=mesh,
        in_specs=(
            tokens, everywhere, everywhere, everywhere, everywhere, everywhere, everywhere,
            P("scene", "view", None), P("scene", "view"), tokens,
        ),
        out_specs=(grads, grads, grads, grads),
        check_vma=False,
    )
```

```python
import functools

import jax
import jax.numpy as jnp
from jax import lax
from jax.experimental import pallas as pl
from jax.experimental.pallas import tpu as pltpu
from jax.sharding import PartitionSpec as P

HEAD_DIM = 64
EPSILON = 1e-06
SCALE = HEAD_DIM ** (-0.5)
MASKED = -1e30
MIB = 1024 * 1024
LITTLE = pl.CostEstimate(flops=1, bytes_accessed=1, transcendentals=0)
MUCH = pl.CostEstimate(flops=40_000_000_000, bytes_accessed=1, transcendentals=0)

VMEM = pl.BlockSpec(memory_space=pltpu.VMEM)
SMEM = pl.BlockSpec(memory_space=pltpu.SMEM)


def dot_nn(a, b):
    return lax.dot_general(a, b, (((1,), (0,)), ((), ())), preferred_element_type=jnp.float32)


def dot_nt(a, b):
    return lax.dot_general(a, b, (((1,), (1,)), ((), ())), preferred_element_type=jnp.float32)


def dot_tn(a, b):
    return lax.dot_general(a, b, (((0,), (0,)), ((), ())), preferred_element_type=jnp.float32)


def normalized(tokens, gain):
    x = tokens.astype(jnp.float32)
    mean = jnp.mean(x * x, -1, keepdims=True)
    return (x * lax.rsqrt(mean + EPSILON) * gain).astype(jnp.bfloat16)


def alive_kernel(views, groups, partners, alive):
    for g in range(groups * views):
        alive[g] = 0
    for u in range(views):
        for j in range(partners.shape[2]):
            partner = partners[0, u, j]

            @pl.when(partner >= 0)
            def _():
                alive[lax.div(partner, jnp.int32(views)) * views + u] = 1


def pick_kernel(groups, scalars, *refs):
    tables, lat, outgoing = refs[: groups - 1], refs[groups - 1], refs[groups:]
    views = lat.shape[0]
    for table, out in zip(tables, outgoing):
        wanted = jnp.int32(0)
        for u in range(table.shape[1]):
            for j in range(table.shape[2]):
                partner = table[0, u, j]
                here = (partner >= 0) & (lax.div(partner, jnp.int32(views)) == scalars[1])
                wanted = jnp.where(here, lax.rem(partner, jnp.int32(views)), wanted)
        out[...] = lat[wanted]


def core_half(scalars, size):
    return pl.ds(pl.multiple_of(scalars[0] * size, size), size)


def stacked(x, views):
    tokens, pair = x.shape
    low = (lax.broadcasted_iota(jnp.int32, (1, 1, pair), 2) < pair // 2).astype(x.dtype)
    x = x.reshape(views, tokens // views, pair)
    return jnp.concatenate((x * low, x * (1 - low)), axis=1).reshape(2 * tokens, pair)


def unstacked(x, views):
    rows, pair = x.shape
    low = lax.broadcasted_iota(jnp.int32, (1, 1, pair), 2) < pair // 2
    x = x.reshape(views, 2, rows // (2 * views), pair)
    return jnp.where(low, x[:, 0], x[:, 1]).reshape(rows // 2, pair)


def view_parts(x, views, axis):
    size = x.shape[axis] // views
    return [lax.slice_in_dim(x, u * size, (u + 1) * size, axis=axis) for u in range(views)]


def own_nt(a, b, views):
    pairs = zip(view_parts(a, views, 0), view_parts(b, views, 0))
    return jnp.concatenate([dot_nt(x, y) for x, y in pairs], axis=1)


def own_tn(a, b, views):
    pairs = zip(view_parts(a, views, 1), view_parts(b, views, 0))
    return jnp.concatenate([dot_tn(x, y) for x, y in pairs], axis=0)


def own_nn(a, b, views):
    pairs = zip(view_parts(a, views, 1), view_parts(b, views, 0))
    return jnp.concatenate([dot_nn(x, y) for x, y in pairs], axis=0)


def project_kernel(
    scalars, lat_own, lat_other, cot_own, cot_other, gain, taps, w_query, w_key, w_value, w_out,
    normed_t, keys, values, upstream, query_stack, grad_stack, scores_own, dprob_own, normed,
):
    views, strip, width = lat_own.shape
    scale = gain[...].reshape(1, width)
    row = scalars[0]

    def strip_of(u, half):
        index = 2 * u + (row if half == 0 else 1 - row)
        return pl.ds(pl.multiple_of(index * strip, strip), strip)

    for half, source in enumerate((lat_own, lat_other)):
        for u in range(views):
            normed[strip_of(u, half), :] = normalized(source[u], scale)
    first = row == 0
    chunk = 512
    column = lax.broadcasted_iota(jnp.int32, (strip, 1), 0)
    not_first = (column > 0).astype(jnp.float32)
    not_last = (column < strip - 1).astype(jnp.float32)
    for c in range(0, width, chunk):
        lanes = slice(c, c + chunk)
        tap = taps[:, lanes].astype(jnp.float32)
        top, middle, bottom = tap[0:3], tap[3:6], tap[6:9]
        cross = (jnp.where(first, top, bottom), jnp.where(first, bottom, top))
        for u in range(views):
            strips = [ref[u, :, lanes].astype(jnp.float32) for ref in (cot_own, cot_other)]
            shifted = []
            for x in strips:
                after = pltpu.roll(x, strip - 1, 0) * not_last
                before = pltpu.roll(x, 1, 0) * not_first
                shifted.append((after, x, before))
            for half in range(2):
                total = strips[half]
                for b in range(3):
                    total = total + middle[b : b + 1] * shifted[half][b]
                    total = total + cross[half][b : b + 1] * shifted[1 - half][b]
                upstream[strip_of(u, half), lanes] = total.astype(jnp.bfloat16)
    rows = normed[...]
    normed_t[...] = rows.T
    part = keys.shape[1]
    half = core_half(scalars, part)
    queries = dot_nn(rows, w_query[:, half]).astype(jnp.bfloat16)
    keys[...] = dot_nn(rows, w_key[:, half]).astype(jnp.bfloat16)
    values[...] = dot_nn(rows, w_value[:, half]).astype(jnp.bfloat16)
    out_grad = dot_nt(upstream[...], w_out[half, :]).astype(jnp.bfloat16)
    pair = 2 * HEAD_DIM
    for p in range(part // pair):
        lanes = slice(p * pair, (p + 1) * pair)
        q, g = stacked(queries[:, lanes], views), stacked(out_grad[:, lanes], views)
        query_stack[p], grad_stack[p] = q, g
        scores_own[p] = own_nt(keys[:, lanes], q, views) * SCALE
        dprob_own[p] = own_nt(values[:, lanes], g, views)


def forward_kernel(views, groups, scalars, alive, *refs):
    got_own, got_other, refs = refs[: groups - 1], refs[groups - 1 : 2 * groups - 2], refs[2 * groups - 2 :]
    query_stack, grad_stack, scores_own, values, gain, w_key, w_value, *refs = refs
    normed_far_t, keys_far, values_far, attention_own, attention_far, mixed_t, dvalue, normed_far = refs
    strip = got_own[0].shape[0]
    tokens, part = values.shape
    view_tokens = tokens // views
    here = scalars[1]
    scale_row = gain[...].reshape(1, normed_far.shape[1])
    pair = 2 * HEAD_DIM
    span = 2 * view_tokens
    column_view = lax.broadcasted_iota(jnp.int32, (1, views * span), 1) // span
    slot_alive = []
    for j in range(groups - 1):
        group = lax.bitwise_xor(here, jnp.int32(groups - 1 - j))
        start = 2 * j * strip
        normed_far[start : start + strip, :] = normalized(got_own[j][...], scale_row)
        normed_far[start + strip : start + 2 * strip, :] = normalized(got_other[j][...], scale_row)
        taken = jnp.zeros((1, views * span), jnp.int32)
        for u in range(views):
            taken = jnp.where(column_view == u, alive[group * views + u], taken)
        slot_alive.append(taken > 0)
    fetched = normed_far[...]
    normed_far_t[...] = fetched.T
    half = core_half(scalars, part)
    keys_far[...] = dot_nn(fetched, w_key[:, half]).astype(jnp.bfloat16)
    values_far[...] = dot_nn(fetched, w_value[:, half]).astype(jnp.bfloat16)
    for p in range(part // pair):
        lanes = slice(p * pair, (p + 1) * pair)
        q, g, s_own = query_stack[p], grad_stack[p], scores_own[p]
        s_far = dot_nt(keys_far[:, lanes], q) * SCALE
        s_far = jnp.concatenate(
            [
                jnp.where(slot_alive[j], s_far[j * view_tokens : (j + 1) * view_tokens], MASKED)
                for j in range(groups - 1)
            ],
            axis=0,
        )
        highest = jnp.maximum(jnp.max(s_own, 0, keepdims=True), jnp.max(s_far, 0, keepdims=True))
        e_own = jnp.exp(s_own - highest)
        e_far = jnp.exp(s_far - highest)
        inverse = 1.0 / (jnp.sum(e_own, 0, keepdims=True) + jnp.sum(e_far, 0, keepdims=True))
        a_own, a_far = e_own * inverse, e_far * inverse
        attention_own[p], attention_far[p] = a_own, a_far
        a_own, a_far = a_own.astype(jnp.bfloat16), a_far.astype(jnp.bfloat16)
        mix = own_tn(a_own, values[:, lanes], views) + dot_tn(a_far, values_far[:, lanes])
        mixed_t[lanes, :] = unstacked(mix, views).T.astype(jnp.bfloat16)
        dvalue[:tokens, lanes] = own_nn(a_own, g, views).astype(jnp.bfloat16)
        dvalue[tokens:, lanes] = dot_nn(a_far, g).astype(jnp.bfloat16)


def backward_kernel(
    views, query_stack, grad_stack, dprob_own, keys, keys_far, values_far, attention_own, attention_far, dquery, dkey
):
    tokens, part = keys.shape
    pair = 2 * HEAD_DIM
    for p in range(part // pair):
        lanes = slice(p * pair, (p + 1) * pair)
        q, g, dp_own = query_stack[p], grad_stack[p], dprob_own[p]
        a_own, a_far = attention_own[p], attention_far[p]
        dp_far = dot_nt(values_far[:, lanes], g)
        delta = jnp.sum(a_own * dp_own, 0, keepdims=True) + jnp.sum(a_far * dp_far, 0, keepdims=True)
        ds_own = (a_own * (dp_own - delta) * SCALE).astype(jnp.bfloat16)
        ds_far = (a_far * (dp_far - delta) * SCALE).astype(jnp.bfloat16)
        dq = own_tn(ds_own, keys[:, lanes], views) + dot_tn(ds_far, keys_far[:, lanes])
        dquery[:, lanes] = unstacked(dq, views).astype(jnp.bfloat16)
        dkey[:tokens, lanes] = own_nn(ds_own, q, views).astype(jnp.bfloat16)
        dkey[tokens:, lanes] = dot_nn(ds_far, q).astype(jnp.bfloat16)


def times(lefts, right):
    total, start = 0.0, 0
    for left in lefts:
        total = total + dot_nn(left, right[start : start + left.shape[1], :])
        start += left.shape[1]
    return total


def by_quarters(scalars, lefts, right, sends, keep, x_first):
    size = keep.shape[1]
    x, y = scalars[3], scalars[4]
    for targets, first in ((sends, 1), ([keep.at[0], keep.at[1]], 0)):
        for second in (1, 0):
            dx, dy = (first, second) if x_first else (second, first)
            block = 2 * lax.bitwise_xor(y, jnp.int32(dy)) + lax.bitwise_xor(x, jnp.int32(dx))
            rows = pl.ds(pl.multiple_of(block * size, size), size)
            target = targets[second]
            target[...] = times([left[rows, :] for left in lefts], right).astype(target.dtype)


def query_key_kernel(
    scalars, normed_t, normed_far_t, dquery, dkey, q_later, k_later, q_now, k_now, q_keep, k_keep
):
    by_quarters(scalars, (normed_t,), dquery[...], (q_now, q_later), q_keep, True)
    by_quarters(scalars, (normed_t, normed_far_t), dkey[...], (k_now, k_later), k_keep, False)


def go_on_kernel(q_keep, q_got, k_keep, k_got, q_later, k_later):
    for keep, got, later in ((q_keep, q_got, q_later), (k_keep, k_got, k_later)):
        later[...] = (keep[1] + got[...].astype(jnp.float32)).astype(jnp.bfloat16)


def value_out_kernel(scalars, normed_t, normed_far_t, dvalue, mine, theirs, upstream, send, keep):
    row, x, y = scalars[0], scalars[3], scalars[4]
    odd = lax.rem(scalars[1], jnp.int32(2)) == 1
    _, _, pairs, size, _ = send.shape
    half, quarter = upstream.shape[1] // 2, normed_t.shape[0] // 4
    value_right = dvalue[...]
    lanes = value_right.shape[1]
    places = [(dy, dx, pair) for dy in range(2) for dx in range(2) for pair in range(pairs)]
    rows = {"send": ([], [], []), "keep": ([], [], [])}
    for dy in range(2):
        to_y = lax.bitwise_xor(y, jnp.int32(dy))
        for dx in range(2):
            to_x = lax.bitwise_xor(x, jnp.int32(dx))
            out_rows = pl.ds(pl.multiple_of(to_x * (half // 4), half // 4), half // 4)
            out_block = jnp.where(row == to_y, mine[out_rows, :], theirs[out_rows, :])
            value_rows = pl.ds(pl.multiple_of((2 * to_y + to_x) * quarter, quarter), quarter)
            blocks = (normed_t[value_rows, :], normed_far_t[value_rows, :], out_block)
            for pair in range(pairs):
                for i, block in enumerate(blocks):
                    count = size if i == 2 else 2 * size
                    first = block[2 * pair * count : (2 * pair + 1) * count]
                    second = block[(2 * pair + 1) * count : (2 * pair + 2) * count]
                    rows["send"][i].append(jnp.where(odd, first, second))
                    rows["keep"][i].append(jnp.where(odd, second, first))
    right = upstream[:, core_half(scalars, half)]
    for target, name in ((send, "send"), (keep, "keep")):
        own, far, out = [jnp.concatenate(parts, axis=0) for parts in rows[name]]
        grad_v = times((own, far), value_right).astype(target.dtype)
        grad_o = dot_nn(out, right).astype(target.dtype)
        for i, place in enumerate(places):
            target[(*place, slice(None), slice(0, half))] = grad_o[i * size : (i + 1) * size]
            for core in range(2):
                columns = slice(half + core * lanes, half + (core + 1) * lanes)
                part = grad_v[(2 * i + core) * size : (2 * i + core + 1) * size]
                target[(*place, slice(None), columns)] = part


def view_sum_kernel(keep, got, x_send, y_send, x_keep, y_keep):
    half = y_send.shape[3]
    for second in range(2):
        for target, first in ((x_send, 1), (x_keep, 0)):
            total = keep[second, first, :, :, half:] + got[second, first, :, :, half:].astype(jnp.float32)
            target[second] = total.astype(target.dtype)
        for target, first in ((y_send, 1), (y_keep, 0)):
            total = keep[first, second, :, :, :half] + got[first, second, :, :, :half].astype(jnp.float32)
            target[second] = total.astype(target.dtype)


def first_sum_kernel(x_keep, x_got, y_keep, y_got, x_later, y_later, x_now, y_now):
    for keep, got, later, now in ((x_keep, x_got, x_later, x_now), (y_keep, y_got, y_later, y_now)):
        later[...] = (keep[1] + got[1].astype(jnp.float32)).astype(jnp.bfloat16)
        now[...] = keep[0] + got[0].astype(jnp.float32)


def query_key_tiles_kernel(scalars, q_keep, q_first, q_second, k_keep, k_first, k_second, send, keep):
    odd = lax.rem(scalars[1], jnp.int32(2)) == 1
    total = [
        kept[0] + first[...].astype(jnp.float32) + second[...].astype(jnp.float32)
        for kept, first, second in ((q_keep, q_first, q_second), (k_keep, k_first, k_second))
    ]
    total = jnp.concatenate(total, axis=1)
    pairs, size, _ = send.shape
    for pair in range(pairs):
        first = total[2 * pair * size : (2 * pair + 1) * size]
        second = total[(2 * pair + 1) * size : (2 * pair + 2) * size]
        send[pair] = jnp.where(odd, first, second).astype(send.dtype)
        keep[pair] = jnp.where(odd, second, first)


def summed_tile(addends, place):
    place = pl.ds(place, 1)
    total = [now[place] + got[place].astype(jnp.float32) for now, got in zip(addends[::2], addends[1::2])]
    return (jnp.concatenate(total, axis=2) if len(total) == 2 else total[0])[0]


def view_bit(scalars, bit):
    return lax.rem(lax.div(scalars[1], jnp.int32(2 << bit)), jnp.int32(2))


def tile_halves_kernel(bit, scalars, *refs):
    addends, (send, keep) = refs[:-2], refs[-2:]
    count = keep.shape[0]
    mine = view_bit(scalars, bit)
    for target, part in ((send, 1 - mine), (keep, mine)):
        for i in range(count):
            target[i] = summed_tile(addends, part * count + i).astype(target.dtype)


def query_key_cores(tile, half):
    size = tile.shape[0] // 2
    return tile[:size], tile[size:]


def value_out_cores(tile, half):
    size, lanes = tile.shape[0] // 2, (tile.shape[1] - half) // 2
    parts = []
    for core in range(2):
        value = tile[:, half + core * lanes : half + (core + 1) * lanes]
        out = tile[core * size : (core + 1) * size, :half]
        parts.append(jnp.concatenate((out, value[:size], value[size:]), axis=1))
    return parts


def tile_cores_kernel(split, half, scalars, *refs):
    addends, (far_same, far_cross, near_cross, mine) = refs[:-4], refs[-4:]
    bit = view_bit(scalars, 0)
    for place, same, cross in ((1 - bit, far_same, far_cross), (bit, mine, near_cross)):
        parts = split(summed_tile(addends, place), half)
        same[...] = jnp.where(scalars[0] == 0, parts[0], parts[1]).astype(same.dtype)
        cross[...] = jnp.where(scalars[0] == 0, parts[1], parts[0]).astype(cross.dtype)


def last_sums(scalars, mine, far_same, near_cross, far_cross):
    for near, far, core in ((mine, far_same, scalars[0]), (near_cross, far_cross, 1 - scalars[0])):
        yield near[...] + far[...].astype(jnp.float32), core


def add_kernel(mine, far_same, near_cross, far_cross, same, cross):
    same[...] = mine[...] + far_same[...].astype(jnp.float32)
    cross[...] = near_cross[...] + far_cross[...].astype(jnp.float32)


def place_query_key_kernel(scalars, same, cross, query, key):
    size = query.shape[1] // 2
    for total, core in ((same, scalars[0]), (cross, 1 - scalars[0])):
        columns = pl.ds(pl.multiple_of(core * size, size), size)
        query[:, columns] = total[:, :size]
        key[:, columns] = total[:, size:]


def place_value_out_kernel(scalars, mine, far_same, near_cross, far_cross, value, out):
    size, width = mine.shape
    half, part = out.shape[1] // 2, value.shape[1] // 2
    for total, core in last_sums(scalars, mine, far_same, near_cross, far_cross):
        out[:, pl.ds(pl.multiple_of(core * half, half), half)] = total[:, :half]
        columns = pl.ds(pl.multiple_of(core * part, part), part)
        value[:size, columns] = total[:, half : half + part]
        value[size:, columns] = total[:, half + part :]


def params(mebibytes):
    return pltpu.CompilerParams(vmem_limit_bytes=mebibytes * MIB)


def shape(dims, kind):
    return jax.ShapeDtypeStruct(dims, kind)


def shards(latents, norm_gain, w_query, w_key, w_value, w_out, kernel, partners, counts, cotangent):
    views, strip_rows, columns, width = latents.shape[1:]
    inner = w_query.shape[1]
    groups, rows = lax.axis_size("view"), lax.axis_size("row")
    scenes = lax.axis_size("scene")
    assert (strip_rows, rows, scenes) == (1, 2, 4)
    strip = strip_rows * columns
    part = inner // rows
    tokens = views * 2 * strip
    key_tokens = tokens + (groups - 1) * 2 * strip
    bf16, f32, i32 = jnp.bfloat16, jnp.float32, jnp.int32

    row, view, scene = lax.axis_index("row"), lax.axis_index("view"), lax.axis_index("scene")
    scalars = jnp.stack((row, view, scene, scene % 2, scene // 2)).astype(i32)
    swap = [(0, 1), (1, 0)]
    along_x, along_y = [(i, i ^ 1) for i in range(scenes)], [(i, i ^ 2) for i in range(scenes)]

    alive = pl.pallas_call(
        functools.partial(alive_kernel, views, groups),
        in_specs=[SMEM],
        out_specs=SMEM,
        out_shape=shape((groups * views,), i32),
        cost_estimate=MUCH,
        compiler_params=params(4),
        name="alive",
    )(partners)
    between = [[(i, i ^ d) for i in range(groups)] for d in reversed(range(1, groups))]
    granted = [lax.ppermute(partners, "view", pairs) for pairs in between]

    granted, alive = lax.optimization_barrier((granted, alive))
    lat = latents[0].reshape(views, strip, width)
    cot = cotangent[0].reshape(views, strip, width)
    lat_other = lax.ppermute(lat, "row", swap)
    cot_other = lax.ppermute(cot, "row", swap)

    outgoing = pl.pallas_call(
        functools.partial(pick_kernel, groups),
        in_specs=[SMEM] * groups + [VMEM],
        out_specs=[VMEM] * (groups - 1),
        out_shape=[shape((strip, width), bf16)] * (groups - 1),
        compiler_params=params(8),
        cost_estimate=MUCH,
        name="pick",
    )(scalars, *granted, lat)
    got_own = [lax.ppermute(part_out, "view", pairs) for part_out, pairs in zip(outgoing, between)]
    head_pairs = part // (2 * HEAD_DIM)
    normed_t, keys, values, upstream, query_stack, grad_stack, scores_own, dprob_own = pl.pallas_call(
        project_kernel,
        in_specs=[SMEM] + [VMEM] * 10,
        out_specs=[VMEM] * 8,
        out_shape=[
            shape((width, tokens), bf16),
            shape((tokens, part), bf16),
            shape((tokens, part), bf16),
            shape((tokens, width), bf16),
            shape((head_pairs, 2 * tokens, 2 * HEAD_DIM), bf16),
            shape((head_pairs, 2 * tokens, 2 * HEAD_DIM), bf16),
            shape((head_pairs, 2 * strip, 2 * tokens), f32),
            shape((head_pairs, 2 * strip, 2 * tokens), f32),
        ],
        scratch_shapes=[pltpu.VMEM((tokens, width), bf16)],
        compiler_params=params(28),
        cost_estimate=LITTLE,
        name="project",
    )(scalars, lat, lat_other, cot, cot_other, norm_gain, kernel, w_query, w_key, w_value, w_out)

    got_own, normed_t = lax.optimization_barrier((got_own, normed_t))
    got_other = [lax.ppermute(got, "row", swap) for got in got_own]

    def call(kernel_body, results, operands, name, first=VMEM, mebibytes=16, cost=LITTLE):
        outputs = pl.pallas_call(
            kernel_body,
            in_specs=[first] + [VMEM] * (len(operands) - 1),
            out_specs=[VMEM] * len(results),
            out_shape=results,
            compiler_params=params(mebibytes),
            cost_estimate=cost,
            name=name,
        )(*operands)
        return list(outputs)

    far_tokens = key_tokens - tokens
    normed_far_t, keys_far, values_far, attention_own, attention_far, mixed_t, dvalue = pl.pallas_call(
        functools.partial(forward_kernel, views, groups),
        in_specs=[SMEM] * 2 + [VMEM] * (2 * groups - 2 + 7),
        out_specs=[VMEM] * 7,
        out_shape=[
            shape((width, far_tokens), bf16),
            shape((far_tokens, part), bf16),
            shape((far_tokens, part), bf16),
            shape((head_pairs, 2 * strip, 2 * tokens), f32),
            shape((head_pairs, far_tokens, 2 * tokens), f32),
            shape((part, tokens), bf16),
            shape((key_tokens, part), bf16),
        ],
        scratch_shapes=[pltpu.VMEM((far_tokens, width), bf16)],
        compiler_params=params(28 + groups // 2),
        cost_estimate=LITTLE,
        name="attention_forward",
    )(
        scalars, alive, *got_own, *got_other, query_stack, grad_stack, scores_own, values, norm_gain, w_key, w_value
    )
    mixed_other = lax.ppermute(mixed_t, "row", swap)
    dquery, dkey = call(
        functools.partial(backward_kernel, views),
        [shape((tokens, part), bf16), shape((key_tokens, part), bf16)],
        (query_stack, grad_stack, dprob_own, keys, keys_far, values_far, attention_own, attention_far),
        "attention_backward",
        mebibytes=28 + groups // 2,
    )

    def after(value, *earlier):
        return lax.optimization_barrier((value, *earlier))[0]

    targets = groups * rows
    q_size = width // 4
    q_rows, o_rows = q_size // targets, inner // (4 * targets)
    q_block = (q_size, part)

    def first_exchange(sends):
        return lax.ppermute(sends[0], "scene", along_x), lax.ppermute(sends[1], "scene", along_y)

    def first_sum(parts, got, name, cost=LITTLE):
        blocks = [part_now.shape[1:] for part_now in parts[:2]]
        results = [shape(block, bf16) for block in blocks] + [shape(block, f32) for block in blocks]
        return call(first_sum_kernel, results, (parts[2], got[0], parts[3], got[1]), name, cost=cost)

    def second_exchange(sums):
        return lax.ppermute(sums[0], "scene", along_y), lax.ppermute(sums[1], "scene", along_x)

    pairs = groups // 2
    neighbours = [(i, i ^ 1) for i in range(groups)]
    split_rows = {"query_key": q_rows, "value_out": o_rows}

    def last_parts(addends, split, name):
        tile = (addends[0].shape[1], sum(now.shape[2] for now in addends[::2]))
        for bit in reversed(range(1, pairs.bit_length() - 1)):
            send, keep = call(
                functools.partial(tile_halves_kernel, bit),
                [shape((1 << bit, *tile), kind) for kind in (bf16, f32)],
                (scalars, *addends),
                "view_bit_" + name,
                SMEM,
            )
            addends = (keep, lax.ppermute(send, "view", [(i, i ^ (2 << bit)) for i in range(groups)]))
        lanes = tile[0] * tile[1] // (2 * split_rows[name])
        columns = width // 2
        far_same, far_cross, near_cross, mine = call(
            functools.partial(tile_cores_kernel, split, columns),
            [shape((split_rows[name], lanes), kind) for kind in (bf16, bf16, f32, f32)],
            (scalars, *addends),
            "last_parts_" + name,
            SMEM,
        )
        far_same = lax.ppermute(far_same, "view", [(i, i ^ 2) for i in range(groups)])
        far_cross = lax.ppermute(far_cross, ("view", "row"), [(i, i ^ 5) for i in range(targets)])
        near_cross = lax.ppermute(near_cross, "row", swap)
        return mine, far_same, near_cross, far_cross

    tile = (2 * o_rows, width // 2 + 2 * part)
    send, keep = call(
        value_out_kernel,
        [shape((2, 2, pairs, *tile), kind) for kind in (bf16, f32)],
        (scalars, normed_t, normed_far_t, after(dvalue, dkey), mixed_t, mixed_other, upstream),
        "grad_value_out",
        SMEM,
        24,
    )
    got = lax.ppermute(send, "view", neighbours)
    q_later, k_later, q_now, k_now, q_keep, k_keep = call(
        query_key_kernel,
        [shape(block, bf16) for block in (q_block, q_block, q_block, q_block)]
        + [shape((2, *block), f32) for block in (q_block, q_block)],
        (scalars, normed_t, normed_far_t, after(dquery, send), dkey),
        "grad_query_key",
        SMEM,
        24,
    )
    q_got, k_got = first_exchange((q_later, k_later))
    q_first, k_first = first_exchange((q_now, k_now))
    later = call(
        go_on_kernel, [shape(q_block, bf16), shape(q_block, bf16)], (q_keep, q_got, k_keep, k_got), "first_sum_query_key"
    )
    q_second, k_second = second_exchange(later)
    qk_tile = (2 * q_rows, 2 * part)
    qk_send, qk_keep = call(
        query_key_tiles_kernel,
        [shape((pairs, *qk_tile), kind) for kind in (bf16, f32)],
        (scalars, q_keep, q_first, q_second, k_keep, k_first, k_second),
        "second_sum_query_key",
        SMEM,
    )
    qk_addends = (qk_keep, lax.ppermute(qk_send, "view", neighbours))
    x_shape, y_shape = (2, pairs, 2 * o_rows, 2 * part), (2, pairs, 2 * o_rows, width // 2)
    vo_parts = call(
        view_sum_kernel,
        [shape(x_shape, bf16), shape(y_shape, bf16), shape(x_shape, f32), shape(y_shape, f32)],
        (keep, after(got, qk_send)),
        "view_sum_value_out",
    )
    vo_got = first_exchange(vo_parts)
    qk_last = last_parts(qk_addends, query_key_cores, "query_key")
    vo_parts[2] = after(vo_parts[2], qk_last[0])
    vo_sums = first_sum(vo_parts, vo_got, "first_sum_value_out")
    v_got, o_got = second_exchange(vo_sums)
    addends = (vo_sums[3], o_got, vo_sums[2], v_got)
    qk_total = call(
        add_kernel, [shape((q_rows, 2 * part), f32)] * 2, qk_last, "last_sum_query_key", cost=MUCH
    )
    vo_last = last_parts((after(addends[0], qk_total[0]), *addends[1:]), value_out_cores, "value_out")
    grad_query, grad_key = call(
        place_query_key_kernel,
        [shape((q_rows, inner), f32)] * 2,
        (scalars, *qk_total),
        "place_query_key",
        SMEM,
    )
    grad_value, grad_out = call(
        place_value_out_kernel,
        [shape((q_rows, inner), f32), shape((o_rows, width), f32)],
        (scalars, after(vo_last[0], grad_query), *vo_last[1:]),
        "last_sum_value_out",
        SMEM,
    )
    return grad_query, grad_key, grad_value, grad_out


def solution(mesh):
    tokens = P("scene", "view", "row", None, None)
    everywhere = P()
    grads = P(("scene", "view", "row"), None)
    return jax.shard_map(
        shards,
        mesh=mesh,
        in_specs=(
            tokens, everywhere, everywhere, everywhere, everywhere, everywhere, everywhere,
            P("scene", "view", None), P("scene", "view"), tokens,
        ),
        out_specs=(grads, grads, grads, grads),
        check_vma=False,
    )
```

```python
import functools

import jax
import jax.numpy as jnp
from jax import lax
from jax.experimental import pallas as pl
from jax.experimental.pallas import tpu as pltpu
from jax.sharding import PartitionSpec as P

HEAD_DIM = 64
EPSILON = 1e-06
SCALE = HEAD_DIM ** (-0.5)
MASKED = -1e30
MIB = 1024 * 1024
LITTLE = pl.CostEstimate(flops=1, bytes_accessed=1, transcendentals=0)
MUCH = pl.CostEstimate(flops=40_000_000_000, bytes_accessed=1, transcendentals=0)

VMEM = pl.BlockSpec(memory_space=pltpu.VMEM)
SMEM = pl.BlockSpec(memory_space=pltpu.SMEM)


def dot_nn(a, b):
    return lax.dot_general(a, b, (((1,), (0,)), ((), ())), preferred_element_type=jnp.float32)


def dot_nt(a, b):
    return lax.dot_general(a, b, (((1,), (1,)), ((), ())), preferred_element_type=jnp.float32)


def dot_tn(a, b):
    return lax.dot_general(a, b, (((0,), (0,)), ((), ())), preferred_element_type=jnp.float32)


def normalized(tokens, gain):
    x = tokens.astype(jnp.float32)
    mean = jnp.mean(x * x, -1, keepdims=True)
    return (x * lax.rsqrt(mean + EPSILON) * gain).astype(jnp.bfloat16)


def alive_kernel(views, groups, partners, alive):
    for g in range(groups * views):
        alive[g] = 0
    for u in range(views):
        for j in range(partners.shape[2]):
            partner = partners[0, u, j]

            @pl.when(partner >= 0)
            def _():
                alive[lax.div(partner, jnp.int32(views)) * views + u] = 1


def pick_kernel(groups, scalars, *refs):
    tables, lat, outgoing = refs[: groups - 1], refs[groups - 1], refs[groups:]
    views = lat.shape[0]
    for table, out in zip(tables, outgoing):
        wanted = jnp.int32(0)
        for u in range(table.shape[1]):
            for j in range(table.shape[2]):
                partner = table[0, u, j]
                here = (partner >= 0) & (lax.div(partner, jnp.int32(views)) == scalars[1])
                wanted = jnp.where(here, lax.rem(partner, jnp.int32(views)), wanted)
        out[...] = lat[wanted]


def core_half(scalars, size):
    return pl.ds(pl.multiple_of(scalars[0] * size, size), size)


def stacked(x, views):
    tokens, pair = x.shape
    low = (lax.broadcasted_iota(jnp.int32, (1, 1, pair), 2) < pair // 2).astype(x.dtype)
    x = x.reshape(views, tokens // views, pair)
    return jnp.concatenate((x * low, x * (1 - low)), axis=1).reshape(2 * tokens, pair)


def unstacked(x, views):
    rows, pair = x.shape
    low = lax.broadcasted_iota(jnp.int32, (1, 1, pair), 2) < pair // 2
    x = x.reshape(views, 2, rows // (2 * views), pair)
    return jnp.where(low, x[:, 0], x[:, 1]).reshape(rows // 2, pair)


def view_parts(x, views, axis):
    size = x.shape[axis] // views
    return [lax.slice_in_dim(x, u * size, (u + 1) * size, axis=axis) for u in range(views)]


def own_nt(a, b, views):
    pairs = zip(view_parts(a, views, 0), view_parts(b, views, 0))
    return jnp.concatenate([dot_nt(x, y) for x, y in pairs], axis=1)


def own_tn(a, b, views):
    pairs = zip(view_parts(a, views, 1), view_parts(b, views, 0))
    return jnp.concatenate([dot_tn(x, y) for x, y in pairs], axis=0)


def own_nn(a, b, views):
    pairs = zip(view_parts(a, views, 1), view_parts(b, views, 0))
    return jnp.concatenate([dot_nn(x, y) for x, y in pairs], axis=0)


def project_kernel(
    scalars, lat_own, lat_other, cot_own, cot_other, gain, taps, w_query, w_key, w_value, w_out,
    normed_t, keys, values, upstream, query_stack, grad_stack, scores_own, dprob_own, normed,
):
    views, strip, width = lat_own.shape
    scale = gain[...].reshape(1, width)
    row = scalars[0]

    def strip_of(u, half):
        index = 2 * u + (row if half == 0 else 1 - row)
        return pl.ds(pl.multiple_of(index * strip, strip), strip)

    for half, source in enumerate((lat_own, lat_other)):
        for u in range(views):
            normed[strip_of(u, half), :] = normalized(source[u], scale)
    first = row == 0
    chunk = 512
    column = lax.broadcasted_iota(jnp.int32, (strip, 1), 0)
    not_first = (column > 0).astype(jnp.float32)
    not_last = (column < strip - 1).astype(jnp.float32)
    for c in range(0, width, chunk):
        lanes = slice(c, c + chunk)
        tap = taps[:, lanes].astype(jnp.float32)
        top, middle, bottom = tap[0:3], tap[3:6], tap[6:9]
        cross = (jnp.where(first, top, bottom), jnp.where(first, bottom, top))
        for u in range(views):
            strips = [ref[u, :, lanes].astype(jnp.float32) for ref in (cot_own, cot_other)]
            shifted = []
            for x in strips:
                after = pltpu.roll(x, strip - 1, 0) * not_last
                before = pltpu.roll(x, 1, 0) * not_first
                shifted.append((after, x, before))
            for half in range(2):
                total = strips[half]
                for b in range(3):
                    total = total + middle[b : b + 1] * shifted[half][b]
                    total = total + cross[half][b : b + 1] * shifted[1 - half][b]
                upstream[strip_of(u, half), lanes] = total.astype(jnp.bfloat16)
    rows = normed[...]
    normed_t[...] = rows.T
    part = keys.shape[1]
    half = core_half(scalars, part)
    queries = dot_nn(rows, w_query[:, half]).astype(jnp.bfloat16)
    keys[...] = dot_nn(rows, w_key[:, half]).astype(jnp.bfloat16)
    values[...] = dot_nn(rows, w_value[:, half]).astype(jnp.bfloat16)
    out_grad = dot_nt(upstream[...], w_out[half, :]).astype(jnp.bfloat16)
    pair = 2 * HEAD_DIM
    for p in range(part // pair):
        lanes = slice(p * pair, (p + 1) * pair)
        q, g = stacked(queries[:, lanes], views), stacked(out_grad[:, lanes], views)
        query_stack[p], grad_stack[p] = q, g
        scores_own[p] = own_nt(keys[:, lanes], q, views) * SCALE
        dprob_own[p] = own_nt(values[:, lanes], g, views)


def forward_kernel(views, groups, scalars, alive, *refs):
    got_own, got_other, refs = refs[: groups - 1], refs[groups - 1 : 2 * groups - 2], refs[2 * groups - 2 :]
    query_stack, grad_stack, scores_own, values, gain, w_key, w_value, *refs = refs
    normed_far_t, keys_far, values_far, attention_own, attention_far, mixed_t, dvalue, normed_far = refs
    strip = got_own[0].shape[0]
    tokens, part = values.shape
    view_tokens = tokens // views
    here = scalars[1]
    scale_row = gain[...].reshape(1, normed_far.shape[1])
    pair = 2 * HEAD_DIM
    span = 2 * view_tokens
    column_view = lax.broadcasted_iota(jnp.int32, (1, views * span), 1) // span
    slot_alive = []
    for j in range(groups - 1):
        group = lax.bitwise_xor(here, jnp.int32(groups - 1 - j))
        start = 2 * j * strip
        normed_far[start : start + strip, :] = normalized(got_own[j][...], scale_row)
        normed_far[start + strip : start + 2 * strip, :] = normalized(got_other[j][...], scale_row)
        taken = jnp.zeros((1, views * span), jnp.int32)
        for u in range(views):
            taken = jnp.where(column_view == u, alive[group * views + u], taken)
        slot_alive.append(taken > 0)
    fetched = normed_far[...]
    normed_far_t[...] = fetched.T
    half = core_half(scalars, part)
    keys_far[...] = dot_nn(fetched, w_key[:, half]).astype(jnp.bfloat16)
    values_far[...] = dot_nn(fetched, w_value[:, half]).astype(jnp.bfloat16)
    for p in range(part // pair):
        lanes = slice(p * pair, (p + 1) * pair)
        q, g, s_own = query_stack[p], grad_stack[p], scores_own[p]
        s_far = dot_nt(keys_far[:, lanes], q) * SCALE
        s_far = jnp.concatenate(
            [
                jnp.where(slot_alive[j], s_far[j * view_tokens : (j + 1) * view_tokens], MASKED)
                for j in range(groups - 1)
            ],
            axis=0,
        )
        highest = jnp.maximum(jnp.max(s_own, 0, keepdims=True), jnp.max(s_far, 0, keepdims=True))
        e_own = jnp.exp(s_own - highest)
        e_far = jnp.exp(s_far - highest)
        inverse = 1.0 / (jnp.sum(e_own, 0, keepdims=True) + jnp.sum(e_far, 0, keepdims=True))
        a_own, a_far = e_own * inverse, e_far * inverse
        attention_own[p], attention_far[p] = a_own, a_far
        a_own, a_far = a_own.astype(jnp.bfloat16), a_far.astype(jnp.bfloat16)
        mix = own_tn(a_own, values[:, lanes], views) + dot_tn(a_far, values_far[:, lanes])
        mixed_t[lanes, :] = unstacked(mix, views).T.astype(jnp.bfloat16)
        dvalue[:tokens, lanes] = own_nn(a_own, g, views).astype(jnp.bfloat16)
        dvalue[tokens:, lanes] = dot_nn(a_far, g).astype(jnp.bfloat16)


def backward_kernel(
    views, query_stack, grad_stack, dprob_own, keys, keys_far, values_far, attention_own, attention_far, dquery, dkey
):
    tokens, part = keys.shape
    pair = 2 * HEAD_DIM
    for p in range(part // pair):
        lanes = slice(p * pair, (p + 1) * pair)
        q, g, dp_own = query_stack[p], grad_stack[p], dprob_own[p]
        a_own, a_far = attention_own[p], attention_far[p]
        dp_far = dot_nt(values_far[:, lanes], g)
        delta = jnp.sum(a_own * dp_own, 0, keepdims=True) + jnp.sum(a_far * dp_far, 0, keepdims=True)
        ds_own = (a_own * (dp_own - delta) * SCALE).astype(jnp.bfloat16)
        ds_far = (a_far * (dp_far - delta) * SCALE).astype(jnp.bfloat16)
        dq = own_tn(ds_own, keys[:, lanes], views) + dot_tn(ds_far, keys_far[:, lanes])
        dquery[:, lanes] = unstacked(dq, views).astype(jnp.bfloat16)
        dkey[:tokens, lanes] = own_nn(ds_own, q, views).astype(jnp.bfloat16)
        dkey[tokens:, lanes] = dot_nn(ds_far, q).astype(jnp.bfloat16)


def times(lefts, right):
    total, start = 0.0, 0
    for left in lefts:
        total = total + dot_nn(left, right[start : start + left.shape[1], :])
        start += left.shape[1]
    return total


def by_quarters(scalars, lefts, right, sends, keep, x_first):
    size = keep.shape[1]
    x, y = scalars[3], scalars[4]
    for targets, first in ((sends, 1), ([keep.at[0], keep.at[1]], 0)):
        for second in (1, 0):
            dx, dy = (first, second) if x_first else (second, first)
            block = 2 * lax.bitwise_xor(y, jnp.int32(dy)) + lax.bitwise_xor(x, jnp.int32(dx))
            rows = pl.ds(pl.multiple_of(block * size, size), size)
            target = targets[second]
            target[...] = times([left[rows, :] for left in lefts], right).astype(target.dtype)


def query_key_kernel(
    scalars, normed_t, normed_far_t, dquery, dkey, q_later, k_later, q_now, k_now, q_keep, k_keep
):
    by_quarters(scalars, (normed_t,), dquery[...], (q_now, q_later), q_keep, True)
    by_quarters(scalars, (normed_t, normed_far_t), dkey[...], (k_now, k_later), k_keep, False)


def go_on_kernel(q_keep, q_got, k_keep, k_got, q_later, k_later):
    for keep, got, later in ((q_keep, q_got, q_later), (k_keep, k_got, k_later)):
        later[...] = (keep[1] + got[...].astype(jnp.float32)).astype(jnp.bfloat16)


def value_out_kernel(sent, scalars, normed_t, normed_far_t, dvalue, mine, theirs, upstream, target):
    row, x, y = scalars[0], scalars[3], scalars[4]
    take_second = lax.rem(scalars[1], jnp.int32(2)) == (0 if sent else 1)
    _, _, pairs, size, _ = target.shape
    half, quarter = upstream.shape[1] // 2, normed_t.shape[0] // 4
    value_right = dvalue[...]
    lanes = value_right.shape[1]
    places = [(dy, dx, pair) for dy in range(2) for dx in range(2) for pair in range(pairs)]
    rows = ([], [], [])
    for dy in range(2):
        to_y = lax.bitwise_xor(y, jnp.int32(dy))
        for dx in range(2):
            to_x = lax.bitwise_xor(x, jnp.int32(dx))
            out_rows = pl.ds(pl.multiple_of(to_x * (half // 4), half // 4), half // 4)
            out_block = jnp.where(row == to_y, mine[out_rows, :], theirs[out_rows, :])
            value_rows = pl.ds(pl.multiple_of((2 * to_y + to_x) * quarter, quarter), quarter)
            blocks = (normed_t[value_rows, :], normed_far_t[value_rows, :], out_block)
            for pair in range(pairs):
                for i, block in enumerate(blocks):
                    count = size if i == 2 else 2 * size
                    first = block[2 * pair * count : (2 * pair + 1) * count]
                    second = block[(2 * pair + 1) * count : (2 * pair + 2) * count]
                    rows[i].append(jnp.where(take_second, second, first))
    right = upstream[:, core_half(scalars, half)]
    own, far, out = [jnp.concatenate(parts, axis=0) for parts in rows]
    grad_v = times((own, far), value_right).astype(target.dtype)
    grad_o = dot_nn(out, right).astype(target.dtype)
    for i, place in enumerate(places):
        target[(*place, slice(None), slice(0, half))] = grad_o[i * size : (i + 1) * size]
        for core in range(2):
            columns = slice(half + core * lanes, half + (core + 1) * lanes)
            part = grad_v[(2 * i + core) * size : (2 * i + core + 1) * size]
            target[(*place, slice(None), columns)] = part


def view_sum_kernel(keep, got, x_send, y_send, x_keep, y_keep):
    half = y_send.shape[3]
    for second in range(2):
        for target, first in ((x_send, 1), (x_keep, 0)):
            total = keep[second, first, :, :, half:] + got[second, first, :, :, half:].astype(jnp.float32)
            target[second] = total.astype(target.dtype)
        for target, first in ((y_send, 1), (y_keep, 0)):
            total = keep[first, second, :, :, :half] + got[first, second, :, :, :half].astype(jnp.float32)
            target[second] = total.astype(target.dtype)


def first_sum_kernel(x_keep, x_got, y_keep, y_got, x_later, y_later, x_now, y_now):
    for keep, got, later, now in ((x_keep, x_got, x_later, x_now), (y_keep, y_got, y_later, y_now)):
        later[...] = (keep[1] + got[1].astype(jnp.float32)).astype(jnp.bfloat16)
        now[...] = keep[0] + got[0].astype(jnp.float32)


def query_key_tiles_kernel(scalars, q_keep, q_first, q_second, k_keep, k_first, k_second, send, keep):
    odd = lax.rem(scalars[1], jnp.int32(2)) == 1
    total = [
        kept[0] + first[...].astype(jnp.float32) + second[...].astype(jnp.float32)
        for kept, first, second in ((q_keep, q_first, q_second), (k_keep, k_first, k_second))
    ]
    total = jnp.concatenate(total, axis=1)
    pairs, size, _ = send.shape
    for pair in range(pairs):
        first = total[2 * pair * size : (2 * pair + 1) * size]
        second = total[(2 * pair + 1) * size : (2 * pair + 2) * size]
        send[pair] = jnp.where(odd, first, second).astype(send.dtype)
        keep[pair] = jnp.where(odd, second, first)


def summed_tile(addends, place):
    place = pl.ds(place, 1)
    total = [now[place] + got[place].astype(jnp.float32) for now, got in zip(addends[::2], addends[1::2])]
    return (jnp.concatenate(total, axis=2) if len(total) == 2 else total[0])[0]


def view_bit(scalars, bit):
    return lax.rem(lax.div(scalars[1], jnp.int32(2 << bit)), jnp.int32(2))


def tile_halves_kernel(bit, scalars, *refs):
    addends, (send, keep) = refs[:-2], refs[-2:]
    count = keep.shape[0]
    mine = view_bit(scalars, bit)
    for target, part in ((send, 1 - mine), (keep, mine)):
        for i in range(count):
            target[i] = summed_tile(addends, part * count + i).astype(target.dtype)


def query_key_cores(tile, half):
    size = tile.shape[0] // 2
    return tile[:size], tile[size:]


def value_out_cores(tile, half):
    size, lanes = tile.shape[0] // 2, (tile.shape[1] - half) // 2
    parts = []
    for core in range(2):
        value = tile[:, half + core * lanes : half + (core + 1) * lanes]
        out = tile[core * size : (core + 1) * size, :half]
        parts.append(jnp.concatenate((out, value[:size], value[size:]), axis=1))
    return parts


def tile_cores_kernel(split, half, scalars, *refs):
    addends, (far_same, far_cross, near_cross, mine) = refs[:-4], refs[-4:]
    bit = view_bit(scalars, 0)
    for place, same, cross in ((1 - bit, far_same, far_cross), (bit, mine, near_cross)):
        parts = split(summed_tile(addends, place), half)
        same[...] = jnp.where(scalars[0] == 0, parts[0], parts[1]).astype(same.dtype)
        cross[...] = jnp.where(scalars[0] == 0, parts[1], parts[0]).astype(cross.dtype)


def last_sums(scalars, mine, far_same, near_cross, far_cross):
    for near, far, core in ((mine, far_same, scalars[0]), (near_cross, far_cross, 1 - scalars[0])):
        yield near[...] + far[...].astype(jnp.float32), core


def add_kernel(mine, far_same, near_cross, far_cross, same, cross):
    same[...] = mine[...] + far_same[...].astype(jnp.float32)
    cross[...] = near_cross[...] + far_cross[...].astype(jnp.float32)


def place_query_key_kernel(scalars, same, cross, query, key):
    size = query.shape[1] // 2
    for total, core in ((same, scalars[0]), (cross, 1 - scalars[0])):
        columns = pl.ds(pl.multiple_of(core * size, size), size)
        query[:, columns] = total[:, :size]
        key[:, columns] = total[:, size:]


def place_value_out_kernel(scalars, mine, far_same, near_cross, far_cross, value, out):
    size, width = mine.shape
    half, part = out.shape[1] // 2, value.shape[1] // 2
    for total, core in last_sums(scalars, mine, far_same, near_cross, far_cross):
        out[:, pl.ds(pl.multiple_of(core * half, half), half)] = total[:, :half]
        columns = pl.ds(pl.multiple_of(core * part, part), part)
        value[:size, columns] = total[:, half : half + part]
        value[size:, columns] = total[:, half + part :]


def params(mebibytes):
    return pltpu.CompilerParams(vmem_limit_bytes=mebibytes * MIB)


def shape(dims, kind):
    return jax.ShapeDtypeStruct(dims, kind)


def shards(latents, norm_gain, w_query, w_key, w_value, w_out, kernel, partners, counts, cotangent):
    views, strip_rows, columns, width = latents.shape[1:]
    inner = w_query.shape[1]
    groups, rows = lax.axis_size("view"), lax.axis_size("row")
    scenes = lax.axis_size("scene")
    assert (strip_rows, rows, scenes) == (1, 2, 4)
    strip = strip_rows * columns
    part = inner // rows
    tokens = views * 2 * strip
    key_tokens = tokens + (groups - 1) * 2 * strip
    bf16, f32, i32 = jnp.bfloat16, jnp.float32, jnp.int32

    row, view, scene = lax.axis_index("row"), lax.axis_index("view"), lax.axis_index("scene")
    scalars = jnp.stack((row, view, scene, scene % 2, scene // 2)).astype(i32)
    swap = [(0, 1), (1, 0)]
    along_x, along_y = [(i, i ^ 1) for i in range(scenes)], [(i, i ^ 2) for i in range(scenes)]

    alive = pl.pallas_call(
        functools.partial(alive_kernel, views, groups),
        in_specs=[SMEM],
        out_specs=SMEM,
        out_shape=shape((groups * views,), i32),
        cost_estimate=MUCH,
        compiler_params=params(4),
        name="alive",
    )(partners)
    between = [[(i, i ^ d) for i in range(groups)] for d in reversed(range(1, groups))]
    granted = [lax.ppermute(partners, "view", pairs) for pairs in between]

    granted, alive = lax.optimization_barrier((granted, alive))
    lat = latents[0].reshape(views, strip, width)
    cot = cotangent[0].reshape(views, strip, width)
    lat_other = lax.ppermute(lat, "row", swap)
    cot_other = lax.ppermute(cot, "row", swap)

    outgoing = pl.pallas_call(
        functools.partial(pick_kernel, groups),
        in_specs=[SMEM] * groups + [VMEM],
        out_specs=[VMEM] * (groups - 1),
        out_shape=[shape((strip, width), bf16)] * (groups - 1),
        compiler_params=params(8),
        cost_estimate=MUCH,
        name="pick",
    )(scalars, *granted, lat)
    got_own = [lax.ppermute(part_out, "view", pairs) for part_out, pairs in zip(outgoing, between)]
    head_pairs = part // (2 * HEAD_DIM)
    normed_t, keys, values, upstream, query_stack, grad_stack, scores_own, dprob_own = pl.pallas_call(
        project_kernel,
        in_specs=[SMEM] + [VMEM] * 10,
        out_specs=[VMEM] * 8,
        out_shape=[
            shape((width, tokens), bf16),
            shape((tokens, part), bf16),
            shape((tokens, part), bf16),
            shape((tokens, width), bf16),
            shape((head_pairs, 2 * tokens, 2 * HEAD_DIM), bf16),
            shape((head_pairs, 2 * tokens, 2 * HEAD_DIM), bf16),
            shape((head_pairs, 2 * strip, 2 * tokens), f32),
            shape((head_pairs, 2 * strip, 2 * tokens), f32),
        ],
        scratch_shapes=[pltpu.VMEM((tokens, width), bf16)],
        compiler_params=params(28),
        cost_estimate=LITTLE,
        name="project",
    )(scalars, lat, lat_other, cot, cot_other, norm_gain, kernel, w_query, w_key, w_value, w_out)

    got_own, normed_t = lax.optimization_barrier((got_own, normed_t))
    got_other = [lax.ppermute(got, "row", swap) for got in got_own]

    def call(kernel_body, results, operands, name, first=VMEM, mebibytes=16, cost=LITTLE):
        outputs = pl.pallas_call(
            kernel_body,
            in_specs=[first] + [VMEM] * (len(operands) - 1),
            out_specs=[VMEM] * len(results),
            out_shape=results,
            compiler_params=params(mebibytes),
            cost_estimate=cost,
            name=name,
        )(*operands)
        return list(outputs)

    far_tokens = key_tokens - tokens
    normed_far_t, keys_far, values_far, attention_own, attention_far, mixed_t, dvalue = pl.pallas_call(
        functools.partial(forward_kernel, views, groups),
        in_specs=[SMEM] * 2 + [VMEM] * (2 * groups - 2 + 7),
        out_specs=[VMEM] * 7,
        out_shape=[
            shape((width, far_tokens), bf16),
            shape((far_tokens, part), bf16),
            shape((far_tokens, part), bf16),
            shape((head_pairs, 2 * strip, 2 * tokens), f32),
            shape((head_pairs, far_tokens, 2 * tokens), f32),
            shape((part, tokens), bf16),
            shape((key_tokens, part), bf16),
        ],
        scratch_shapes=[pltpu.VMEM((far_tokens, width), bf16)],
        compiler_params=params(28 + groups // 2),
        cost_estimate=LITTLE,
        name="attention_forward",
    )(
        scalars, alive, *got_own, *got_other, query_stack, grad_stack, scores_own, values, norm_gain, w_key, w_value
    )
    mixed_other = lax.ppermute(mixed_t, "row", swap)
    dquery, dkey = call(
        functools.partial(backward_kernel, views),
        [shape((tokens, part), bf16), shape((key_tokens, part), bf16)],
        (query_stack, grad_stack, dprob_own, keys, keys_far, values_far, attention_own, attention_far),
        "attention_backward",
        mebibytes=28 + groups // 2,
    )

    def after(value, *earlier):
        return lax.optimization_barrier((value, *earlier))[0]

    targets = groups * rows
    q_size = width // 4
    q_rows, o_rows = q_size // targets, inner // (4 * targets)
    q_block = (q_size, part)

    def first_exchange(sends):
        return lax.ppermute(sends[0], "scene", along_x), lax.ppermute(sends[1], "scene", along_y)

    def first_sum(parts, got, name, cost=LITTLE):
        blocks = [part_now.shape[1:] for part_now in parts[:2]]
        results = [shape(block, bf16) for block in blocks] + [shape(block, f32) for block in blocks]
        return call(first_sum_kernel, results, (parts[2], got[0], parts[3], got[1]), name, cost=cost)

    def second_exchange(sums):
        return lax.ppermute(sums[0], "scene", along_y), lax.ppermute(sums[1], "scene", along_x)

    pairs = groups // 2
    neighbours = [(i, i ^ 1) for i in range(groups)]
    split_rows = {"query_key": q_rows, "value_out": o_rows}

    def last_parts(addends, split, name):
        tile = (addends[0].shape[1], sum(now.shape[2] for now in addends[::2]))
        for bit in reversed(range(1, pairs.bit_length() - 1)):
            send, keep = call(
                functools.partial(tile_halves_kernel, bit),
                [shape((1 << bit, *tile), kind) for kind in (bf16, f32)],
                (scalars, *addends),
                "view_bit_" + name,
                SMEM,
            )
            addends = (keep, lax.ppermute(send, "view", [(i, i ^ (2 << bit)) for i in range(groups)]))
        lanes = tile[0] * tile[1] // (2 * split_rows[name])
        columns = width // 2
        far_same, far_cross, near_cross, mine = call(
            functools.partial(tile_cores_kernel, split, columns),
            [shape((split_rows[name], lanes), kind) for kind in (bf16, bf16, f32, f32)],
            (scalars, *addends),
            "last_parts_" + name,
            SMEM,
        )
        far_same = lax.ppermute(far_same, "view", [(i, i ^ 2) for i in range(groups)])
        far_cross = lax.ppermute(far_cross, ("view", "row"), [(i, i ^ 5) for i in range(targets)])
        near_cross = lax.ppermute(near_cross, "row", swap)
        return mine, far_same, near_cross, far_cross

    tile = (2 * o_rows, width // 2 + 2 * part)
    operands = (scalars, normed_t, normed_far_t, after(dvalue, dkey), mixed_t, mixed_other, upstream)
    send, keep = (
        call(
            functools.partial(value_out_kernel, sent),
            [shape((2, 2, pairs, *tile), kind)],
            operands,
            name,
            SMEM,
            24,
        )[0]
        for sent, kind, name in ((True, bf16, "grad_value_out_sent"), (False, f32, "grad_value_out_kept"))
    )
    got = lax.ppermute(send, "view", neighbours)
    q_later, k_later, q_now, k_now, q_keep, k_keep = call(
        query_key_kernel,
        [shape(block, bf16) for block in (q_block, q_block, q_block, q_block)]
        + [shape((2, *block), f32) for block in (q_block, q_block)],
        (scalars, normed_t, normed_far_t, after(dquery, send), dkey),
        "grad_query_key",
        SMEM,
        24,
    )
    q_got, k_got = first_exchange((q_later, k_later))
    q_first, k_first = first_exchange((q_now, k_now))
    later = call(
        go_on_kernel, [shape(q_block, bf16), shape(q_block, bf16)], (after(q_keep, keep), q_got, k_keep, k_got), "first_sum_query_key"
    )
    q_second, k_second = second_exchange(later)
    qk_tile = (2 * q_rows, 2 * part)
    qk_send, qk_keep = call(
        query_key_tiles_kernel,
        [shape((pairs, *qk_tile), kind) for kind in (bf16, f32)],
        (scalars, q_keep, q_first, q_second, k_keep, k_first, k_second),
        "second_sum_query_key",
        SMEM,
    )
    qk_addends = (qk_keep, lax.ppermute(qk_send, "view", neighbours))
    x_shape, y_shape = (2, pairs, 2 * o_rows, 2 * part), (2, pairs, 2 * o_rows, width // 2)
    vo_parts = call(
        view_sum_kernel,
        [shape(x_shape, bf16), shape(y_shape, bf16), shape(x_shape, f32), shape(y_shape, f32)],
        (keep, after(got, qk_send)),
        "view_sum_value_out",
    )
    vo_got = first_exchange(vo_parts)
    qk_last = last_parts(qk_addends, query_key_cores, "query_key")
    vo_parts[2] = after(vo_parts[2], qk_last[0])
    vo_sums = first_sum(vo_parts, vo_got, "first_sum_value_out")
    v_got, o_got = second_exchange(vo_sums)
    addends = (vo_sums[3], o_got, vo_sums[2], v_got)
    qk_total = call(
        add_kernel, [shape((q_rows, 2 * part), f32)] * 2, qk_last, "last_sum_query_key", cost=MUCH
    )
    vo_last = last_parts((after(addends[0], qk_total[0]), *addends[1:]), value_out_cores, "value_out")
    grad_query, grad_key = call(
        place_query_key_kernel,
        [shape((q_rows, inner), f32)] * 2,
        (scalars, *qk_total),
        "place_query_key",
        SMEM,
    )
    grad_value, grad_out = call(
        place_value_out_kernel,
        [shape((q_rows, inner), f32), shape((o_rows, width), f32)],
        (scalars, after(vo_last[0], grad_query), *vo_last[1:]),
        "last_sum_value_out",
        SMEM,
    )
    return grad_query, grad_key, grad_value, grad_out


def solution(mesh):
    tokens = P("scene", "view", "row", None, None)
    everywhere = P()
    grads = P(("scene", "view", "row"), None)
    return jax.shard_map(
        shards,
        mesh=mesh,
        in_specs=(
            tokens, everywhere, everywhere, everywhere, everywhere, everywhere, everywhere,
            P("scene", "view", None), P("scene", "view"), tokens,
        ),
        out_specs=(grads, grads, grads, grads),
        check_vma=False,
    )
```

```python
import functools

import jax
import jax.numpy as jnp
from jax import lax
from jax.experimental import pallas as pl
from jax.experimental.pallas import tpu as pltpu
from jax.sharding import PartitionSpec as P

HEAD_DIM = 64
EPSILON = 1e-06
SCALE = HEAD_DIM ** (-0.5)
MASKED = -1e30
MIB = 1024 * 1024
LITTLE = pl.CostEstimate(flops=1, bytes_accessed=1, transcendentals=0)
MUCH = pl.CostEstimate(flops=40_000_000_000, bytes_accessed=1, transcendentals=0)

VMEM = pl.BlockSpec(memory_space=pltpu.VMEM)
SMEM = pl.BlockSpec(memory_space=pltpu.SMEM)


def dot_nn(a, b):
    return lax.dot_general(a, b, (((1,), (0,)), ((), ())), preferred_element_type=jnp.float32)


def dot_nt(a, b):
    return lax.dot_general(a, b, (((1,), (1,)), ((), ())), preferred_element_type=jnp.float32)


def dot_tn(a, b):
    return lax.dot_general(a, b, (((0,), (0,)), ((), ())), preferred_element_type=jnp.float32)


def normalized(tokens, gain):
    x = tokens.astype(jnp.float32)
    mean = jnp.mean(x * x, -1, keepdims=True)
    return (x * lax.rsqrt(mean + EPSILON) * gain).astype(jnp.bfloat16)


def alive_kernel(views, groups, partners, alive):
    for g in range(groups * views):
        alive[g] = 0
    for u in range(views):
        for j in range(partners.shape[2]):
            partner = partners[0, u, j]

            @pl.when(partner >= 0)
            def _():
                alive[lax.div(partner, jnp.int32(views)) * views + u] = 1


def pick_kernel(groups, scalars, *refs):
    tables, lat, outgoing = refs[: groups - 1], refs[groups - 1], refs[groups:]
    views = lat.shape[0]
    for table, out in zip(tables, outgoing):
        wanted = jnp.int32(0)
        for u in range(table.shape[1]):
            for j in range(table.shape[2]):
                partner = table[0, u, j]
                here = (partner >= 0) & (lax.div(partner, jnp.int32(views)) == scalars[1])
                wanted = jnp.where(here, lax.rem(partner, jnp.int32(views)), wanted)
        out[...] = lat[wanted]


def core_half(scalars, size):
    return pl.ds(pl.multiple_of(scalars[0] * size, size), size)


def stacked(x, views):
    tokens, pair = x.shape
    low = (lax.broadcasted_iota(jnp.int32, (1, 1, pair), 2) < pair // 2).astype(x.dtype)
    x = x.reshape(views, tokens // views, pair)
    return jnp.concatenate((x * low, x * (1 - low)), axis=1).reshape(2 * tokens, pair)


def unstacked(x, views):
    rows, pair = x.shape
    low = lax.broadcasted_iota(jnp.int32, (1, 1, pair), 2) < pair // 2
    x = x.reshape(views, 2, rows // (2 * views), pair)
    return jnp.where(low, x[:, 0], x[:, 1]).reshape(rows // 2, pair)


def view_parts(x, views, axis):
    size = x.shape[axis] // views
    return [lax.slice_in_dim(x, u * size, (u + 1) * size, axis=axis) for u in range(views)]


def own_nt(a, b, views):
    pairs = zip(view_parts(a, views, 0), view_parts(b, views, 0))
    return jnp.concatenate([dot_nt(x, y) for x, y in pairs], axis=1)


def own_tn(a, b, views):
    pairs = zip(view_parts(a, views, 1), view_parts(b, views, 0))
    return jnp.concatenate([dot_tn(x, y) for x, y in pairs], axis=0)


def own_nn(a, b, views):
    pairs = zip(view_parts(a, views, 1), view_parts(b, views, 0))
    return jnp.concatenate([dot_nn(x, y) for x, y in pairs], axis=0)


def project_kernel(
    scalars, lat_own, lat_other, cot_own, cot_other, gain, taps, w_query, w_key, w_value, w_out,
    normed_t, keys, values, upstream, query_stack, grad_stack, scores_own, dprob_own, normed,
):
    views, strip, width = lat_own.shape
    scale = gain[...].reshape(1, width)
    row = scalars[0]

    def strip_of(u, half):
        index = 2 * u + (row if half == 0 else 1 - row)
        return pl.ds(pl.multiple_of(index * strip, strip), strip)

    for half, source in enumerate((lat_own, lat_other)):
        for u in range(views):
            normed[strip_of(u, half), :] = normalized(source[u], scale)
    first = row == 0
    chunk = 512
    column = lax.broadcasted_iota(jnp.int32, (strip, 1), 0)
    not_first = (column > 0).astype(jnp.float32)
    not_last = (column < strip - 1).astype(jnp.float32)
    for c in range(0, width, chunk):
        lanes = slice(c, c + chunk)
        tap = taps[:, lanes].astype(jnp.float32)
        top, middle, bottom = tap[0:3], tap[3:6], tap[6:9]
        cross = (jnp.where(first, top, bottom), jnp.where(first, bottom, top))
        for u in range(views):
            strips = [ref[u, :, lanes].astype(jnp.float32) for ref in (cot_own, cot_other)]
            shifted = []
            for x in strips:
                after = pltpu.roll(x, strip - 1, 0) * not_last
                before = pltpu.roll(x, 1, 0) * not_first
                shifted.append((after, x, before))
            for half in range(2):
                total = strips[half]
                for b in range(3):
                    total = total + middle[b : b + 1] * shifted[half][b]
                    total = total + cross[half][b : b + 1] * shifted[1 - half][b]
                upstream[strip_of(u, half), lanes] = total.astype(jnp.bfloat16)
    rows = normed[...]
    normed_t[...] = rows.T
    part = keys.shape[1]
    half = core_half(scalars, part)
    queries = dot_nn(rows, w_query[:, half]).astype(jnp.bfloat16)
    keys[...] = dot_nn(rows, w_key[:, half]).astype(jnp.bfloat16)
    values[...] = dot_nn(rows, w_value[:, half]).astype(jnp.bfloat16)
    out_grad = dot_nt(upstream[...], w_out[half, :]).astype(jnp.bfloat16)
    pair = 2 * HEAD_DIM
    for p in range(part // pair):
        lanes = slice(p * pair, (p + 1) * pair)
        q, g = stacked(queries[:, lanes], views), stacked(out_grad[:, lanes], views)
        query_stack[p], grad_stack[p] = q, g
        scores_own[p] = own_nt(keys[:, lanes], q, views) * SCALE
        dprob_own[p] = own_nt(values[:, lanes], g, views)


def forward_kernel(views, groups, scalars, alive, *refs):
    got_own, got_other, refs = refs[: groups - 1], refs[groups - 1 : 2 * groups - 2], refs[2 * groups - 2 :]
    query_stack, grad_stack, scores_own, values, gain, w_key, w_value, *refs = refs
    normed_far_t, keys_far, values_far, attention_own, attention_far, mixed_t, dvalue, normed_far = refs
    strip = got_own[0].shape[0]
    tokens, part = values.shape
    view_tokens = tokens // views
    here = scalars[1]
    scale_row = gain[...].reshape(1, normed_far.shape[1])
    pair = 2 * HEAD_DIM
    span = 2 * view_tokens
    column_view = lax.broadcasted_iota(jnp.int32, (1, views * span), 1) // span
    slot_alive = []
    for j in range(groups - 1):
        group = lax.bitwise_xor(here, jnp.int32(groups - 1 - j))
        start = 2 * j * strip
        normed_far[start : start + strip, :] = normalized(got_own[j][...], scale_row)
        normed_far[start + strip : start + 2 * strip, :] = normalized(got_other[j][...], scale_row)
        taken = jnp.zeros((1, views * span), jnp.int32)
        for u in range(views):
            taken = jnp.where(column_view == u, alive[group * views + u], taken)
        slot_alive.append(taken > 0)
    fetched = normed_far[...]
    normed_far_t[...] = fetched.T
    half = core_half(scalars, part)
    keys_far[...] = dot_nn(fetched, w_key[:, half]).astype(jnp.bfloat16)
    values_far[...] = dot_nn(fetched, w_value[:, half]).astype(jnp.bfloat16)
    for p in range(part // pair):
        lanes = slice(p * pair, (p + 1) * pair)
        q, g, s_own = query_stack[p], grad_stack[p], scores_own[p]
        s_far = dot_nt(keys_far[:, lanes], q) * SCALE
        s_far = jnp.concatenate(
            [
                jnp.where(slot_alive[j], s_far[j * view_tokens : (j + 1) * view_tokens], MASKED)
                for j in range(groups - 1)
            ],
            axis=0,
        )
        highest = jnp.maximum(jnp.max(s_own, 0, keepdims=True), jnp.max(s_far, 0, keepdims=True))
        e_own = jnp.exp(s_own - highest)
        e_far = jnp.exp(s_far - highest)
        inverse = 1.0 / (jnp.sum(e_own, 0, keepdims=True) + jnp.sum(e_far, 0, keepdims=True))
        a_own, a_far = e_own * inverse, e_far * inverse
        attention_own[p], attention_far[p] = a_own, a_far
        a_own, a_far = a_own.astype(jnp.bfloat16), a_far.astype(jnp.bfloat16)
        mix = own_tn(a_own, values[:, lanes], views) + dot_tn(a_far, values_far[:, lanes])
        mixed_t[lanes, :] = unstacked(mix, views).T.astype(jnp.bfloat16)
        dvalue[:tokens, lanes] = own_nn(a_own, g, views).astype(jnp.bfloat16)
        dvalue[tokens:, lanes] = dot_nn(a_far, g).astype(jnp.bfloat16)


def backward_kernel(
    views, query_stack, grad_stack, dprob_own, keys, keys_far, values_far, attention_own, attention_far, dquery, dkey
):
    tokens, part = keys.shape
    pair = 2 * HEAD_DIM
    for p in range(part // pair):
        lanes = slice(p * pair, (p + 1) * pair)
        q, g, dp_own = query_stack[p], grad_stack[p], dprob_own[p]
        a_own, a_far = attention_own[p], attention_far[p]
        dp_far = dot_nt(values_far[:, lanes], g)
        delta = jnp.sum(a_own * dp_own, 0, keepdims=True) + jnp.sum(a_far * dp_far, 0, keepdims=True)
        ds_own = (a_own * (dp_own - delta) * SCALE).astype(jnp.bfloat16)
        ds_far = (a_far * (dp_far - delta) * SCALE).astype(jnp.bfloat16)
        dq = own_tn(ds_own, keys[:, lanes], views) + dot_tn(ds_far, keys_far[:, lanes])
        dquery[:, lanes] = unstacked(dq, views).astype(jnp.bfloat16)
        dkey[:tokens, lanes] = own_nn(ds_own, q, views).astype(jnp.bfloat16)
        dkey[tokens:, lanes] = dot_nn(ds_far, q).astype(jnp.bfloat16)


def times(lefts, right):
    total, start = 0.0, 0
    for left in lefts:
        total = total + dot_nn(left, right[start : start + left.shape[1], :])
        start += left.shape[1]
    return total


def by_quarters(scalars, lefts, right, sends, keep, x_first):
    size = keep.shape[1]
    x, y = scalars[3], scalars[4]
    for targets, first in ((sends, 1), ([keep.at[0], keep.at[1]], 0)):
        for second in (1, 0):
            dx, dy = (first, second) if x_first else (second, first)
            block = 2 * lax.bitwise_xor(y, jnp.int32(dy)) + lax.bitwise_xor(x, jnp.int32(dx))
            rows = pl.ds(pl.multiple_of(block * size, size), size)
            target = targets[second]
            target[...] = times([left[rows, :] for left in lefts], right).astype(target.dtype)


def query_key_kernel(
    scalars, normed_t, normed_far_t, dquery, dkey, q_later, k_later, q_now, k_now, q_keep, k_keep
):
    by_quarters(scalars, (normed_t,), dquery[...], (q_now, q_later), q_keep, True)
    by_quarters(scalars, (normed_t, normed_far_t), dkey[...], (k_now, k_later), k_keep, False)


def go_on_kernel(q_keep, q_got, k_keep, k_got, q_later, k_later):
    for keep, got, later in ((q_keep, q_got, q_later), (k_keep, k_got, k_later)):
        later[...] = (keep[1] + got[...].astype(jnp.float32)).astype(jnp.bfloat16)


def value_out_kernel(sent, scalars, normed_t, normed_far_t, dvalue, mine, theirs, upstream, *targets):
    row, x, y = scalars[0], scalars[3], scalars[4]
    take_second = lax.rem(scalars[1], jnp.int32(2)) == (0 if sent else 1)
    stay, go_on = targets if sent else (targets[0].at[0], targets[0].at[1])
    _, pairs, size, _ = stay.shape
    half, quarter = upstream.shape[1] // 2, normed_t.shape[0] // 4
    value_right = dvalue[...]
    lanes = value_right.shape[1]
    places = [(dy, dx, pair) for dy in range(2) for dx in range(2) for pair in range(pairs)]
    rows = ([], [], [])
    for dy in range(2):
        to_y = lax.bitwise_xor(y, jnp.int32(dy))
        for dx in range(2):
            to_x = lax.bitwise_xor(x, jnp.int32(dx))
            out_rows = pl.ds(pl.multiple_of(to_x * (half // 4), half // 4), half // 4)
            out_block = jnp.where(row == to_y, mine[out_rows, :], theirs[out_rows, :])
            value_rows = pl.ds(pl.multiple_of((2 * to_y + to_x) * quarter, quarter), quarter)
            blocks = (normed_t[value_rows, :], normed_far_t[value_rows, :], out_block)
            for pair in range(pairs):
                for i, block in enumerate(blocks):
                    count = size if i == 2 else 2 * size
                    first = block[2 * pair * count : (2 * pair + 1) * count]
                    second = block[(2 * pair + 1) * count : (2 * pair + 2) * count]
                    rows[i].append(jnp.where(take_second, second, first))
    right = upstream[:, core_half(scalars, half)]
    own, far, out = [jnp.concatenate(parts, axis=0) for parts in rows]
    grad_v = times((own, far), value_right).astype(stay.dtype)
    grad_o = dot_nn(out, right).astype(stay.dtype)
    for i, (dy, dx, pair) in enumerate(places):
        (stay, go_on)[dy][dx, pair, :, :half] = grad_o[i * size : (i + 1) * size]
        for core in range(2):
            columns = slice(half + core * lanes, half + (core + 1) * lanes)
            part = grad_v[(2 * i + core) * size : (2 * i + core + 1) * size]
            (stay, go_on)[dx][dy, pair, :, columns] = part


def view_sum_kernel(block, keep, got, x_part, y_part):
    half = y_part.shape[3]
    for i in range(2):
        total = keep[block, i] + got[i].astype(jnp.float32)
        x_part[i] = total[:, :, half:].astype(x_part.dtype)
        y_part[i] = total[:, :, :half].astype(y_part.dtype)


def first_sum_kernel(x_keep, x_got, y_keep, y_got, x_later, y_later, x_now, y_now):
    for keep, got, later, now in ((x_keep, x_got, x_later, x_now), (y_keep, y_got, y_later, y_now)):
        later[...] = (keep[1] + got[1].astype(jnp.float32)).astype(jnp.bfloat16)
        now[...] = keep[0] + got[0].astype(jnp.float32)


def query_key_tiles_kernel(scalars, q_keep, q_first, q_second, k_keep, k_first, k_second, send, keep):
    odd = lax.rem(scalars[1], jnp.int32(2)) == 1
    total = [
        kept[0] + first[...].astype(jnp.float32) + second[...].astype(jnp.float32)
        for kept, first, second in ((q_keep, q_first, q_second), (k_keep, k_first, k_second))
    ]
    total = jnp.concatenate(total, axis=1)
    pairs, size, _ = send.shape
    for pair in range(pairs):
        first = total[2 * pair * size : (2 * pair + 1) * size]
        second = total[(2 * pair + 1) * size : (2 * pair + 2) * size]
        send[pair] = jnp.where(odd, first, second).astype(send.dtype)
        keep[pair] = jnp.where(odd, second, first)


def summed_tile(addends, place):
    place = pl.ds(place, 1)
    total = [now[place] + got[place].astype(jnp.float32) for now, got in zip(addends[::2], addends[1::2])]
    return (jnp.concatenate(total, axis=2) if len(total) == 2 else total[0])[0]


def view_bit(scalars, bit):
    return lax.rem(lax.div(scalars[1], jnp.int32(2 << bit)), jnp.int32(2))


def tile_halves_kernel(bit, scalars, *refs):
    addends, (send, keep) = refs[:-2], refs[-2:]
    count = keep.shape[0]
    mine = view_bit(scalars, bit)
    for target, part in ((send, 1 - mine), (keep, mine)):
        for i in range(count):
            target[i] = summed_tile(addends, part * count + i).astype(target.dtype)


def query_key_cores(tile, half):
    size = tile.shape[0] // 2
    return tile[:size], tile[size:]


def value_out_cores(tile, half):
    size, lanes = tile.shape[0] // 2, (tile.shape[1] - half) // 2
    parts = []
    for core in range(2):
        value = tile[:, half + core * lanes : half + (core + 1) * lanes]
        out = tile[core * size : (core + 1) * size, :half]
        parts.append(jnp.concatenate((out, value[:size], value[size:]), axis=1))
    return parts


def tile_cores_kernel(split, half, scalars, *refs):
    addends, (far_same, far_cross, near_cross, mine) = refs[:-4], refs[-4:]
    bit = view_bit(scalars, 0)
    for place, same, cross in ((1 - bit, far_same, far_cross), (bit, mine, near_cross)):
        parts = split(summed_tile(addends, place), half)
        same[...] = jnp.where(scalars[0] == 0, parts[0], parts[1]).astype(same.dtype)
        cross[...] = jnp.where(scalars[0] == 0, parts[1], parts[0]).astype(cross.dtype)


def last_sums(scalars, mine, far_same, near_cross, far_cross):
    for near, far, core in ((mine, far_same, scalars[0]), (near_cross, far_cross, 1 - scalars[0])):
        yield near[...] + far[...].astype(jnp.float32), core


def add_kernel(mine, far_same, near_cross, far_cross, same, cross):
    same[...] = mine[...] + far_same[...].astype(jnp.float32)
    cross[...] = near_cross[...] + far_cross[...].astype(jnp.float32)


def place_query_key_kernel(scalars, same, cross, query, key):
    size = query.shape[1] // 2
    for total, core in ((same, scalars[0]), (cross, 1 - scalars[0])):
        columns = pl.ds(pl.multiple_of(core * size, size), size)
        query[:, columns] = total[:, :size]
        key[:, columns] = total[:, size:]


def place_value_out_kernel(scalars, mine, far_same, near_cross, far_cross, value, out):
    size, width = mine.shape
    half, part = out.shape[1] // 2, value.shape[1] // 2
    for total, core in last_sums(scalars, mine, far_same, near_cross, far_cross):
        out[:, pl.ds(pl.multiple_of(core * half, half), half)] = total[:, :half]
        columns = pl.ds(pl.multiple_of(core * part, part), part)
        value[:size, columns] = total[:, half : half + part]
        value[size:, columns] = total[:, half + part :]


def params(mebibytes):
    return pltpu.CompilerParams(vmem_limit_bytes=mebibytes * MIB)


def shape(dims, kind):
    return jax.ShapeDtypeStruct(dims, kind)


def shards(latents, norm_gain, w_query, w_key, w_value, w_out, kernel, partners, counts, cotangent):
    views, strip_rows, columns, width = latents.shape[1:]
    inner = w_query.shape[1]
    groups, rows = lax.axis_size("view"), lax.axis_size("row")
    scenes = lax.axis_size("scene")
    assert (strip_rows, rows, scenes) == (1, 2, 4)
    strip = strip_rows * columns
    part = inner // rows
    tokens = views * 2 * strip
    key_tokens = tokens + (groups - 1) * 2 * strip
    bf16, f32, i32 = jnp.bfloat16, jnp.float32, jnp.int32

    row, view, scene = lax.axis_index("row"), lax.axis_index("view"), lax.axis_index("scene")
    scalars = jnp.stack((row, view, scene, scene % 2, scene // 2)).astype(i32)
    swap = [(0, 1), (1, 0)]
    along_x, along_y = [(i, i ^ 1) for i in range(scenes)], [(i, i ^ 2) for i in range(scenes)]

    alive = pl.pallas_call(
        functools.partial(alive_kernel, views, groups),
        in_specs=[SMEM],
        out_specs=SMEM,
        out_shape=shape((groups * views,), i32),
        cost_estimate=MUCH,
        compiler_params=params(4),
        name="alive",
    )(partners)
    between = [[(i, i ^ d) for i in range(groups)] for d in reversed(range(1, groups))]
    granted = [lax.ppermute(partners, "view", pairs) for pairs in between]

    granted, alive = lax.optimization_barrier((granted, alive))
    lat = latents[0].reshape(views, strip, width)
    cot = cotangent[0].reshape(views, strip, width)
    lat_other = lax.ppermute(lat, "row", swap)
    cot_other = lax.ppermute(cot, "row", swap)

    outgoing = pl.pallas_call(
        functools.partial(pick_kernel, groups),
        in_specs=[SMEM] * groups + [VMEM],
        out_specs=[VMEM] * (groups - 1),
        out_shape=[shape((strip, width), bf16)] * (groups - 1),
        compiler_params=params(8),
        cost_estimate=MUCH,
        name="pick",
    )(scalars, *granted, lat)
    got_own = [lax.ppermute(part_out, "view", pairs) for part_out, pairs in zip(outgoing, between)]
    head_pairs = part // (2 * HEAD_DIM)
    normed_t, keys, values, upstream, query_stack, grad_stack, scores_own, dprob_own = pl.pallas_call(
        project_kernel,
        in_specs=[SMEM] + [VMEM] * 10,
        out_specs=[VMEM] * 8,
        out_shape=[
            shape((width, tokens), bf16),
            shape((tokens, part), bf16),
            shape((tokens, part), bf16),
            shape((tokens, width), bf16),
            shape((head_pairs, 2 * tokens, 2 * HEAD_DIM), bf16),
            shape((head_pairs, 2 * tokens, 2 * HEAD_DIM), bf16),
            shape((head_pairs, 2 * strip, 2 * tokens), f32),
            shape((head_pairs, 2 * strip, 2 * tokens), f32),
        ],
        scratch_shapes=[pltpu.VMEM((tokens, width), bf16)],
        compiler_params=params(28),
        cost_estimate=LITTLE,
        name="project",
    )(scalars, lat, lat_other, cot, cot_other, norm_gain, kernel, w_query, w_key, w_value, w_out)

    got_own, normed_t = lax.optimization_barrier((got_own, normed_t))
    got_other = [lax.ppermute(got, "row", swap) for got in got_own]

    def call(kernel_body, results, operands, name, first=VMEM, mebibytes=16, cost=LITTLE):
        outputs = pl.pallas_call(
            kernel_body,
            in_specs=[first] + [VMEM] * (len(operands) - 1),
            out_specs=[VMEM] * len(results),
            out_shape=results,
            compiler_params=params(mebibytes),
            cost_estimate=cost,
            name=name,
        )(*operands)
        return list(outputs)

    far_tokens = key_tokens - tokens
    normed_far_t, keys_far, values_far, attention_own, attention_far, mixed_t, dvalue = pl.pallas_call(
        functools.partial(forward_kernel, views, groups),
        in_specs=[SMEM] * 2 + [VMEM] * (2 * groups - 2 + 7),
        out_specs=[VMEM] * 7,
        out_shape=[
            shape((width, far_tokens), bf16),
            shape((far_tokens, part), bf16),
            shape((far_tokens, part), bf16),
            shape((head_pairs, 2 * strip, 2 * tokens), f32),
            shape((head_pairs, far_tokens, 2 * tokens), f32),
            shape((part, tokens), bf16),
            shape((key_tokens, part), bf16),
        ],
        scratch_shapes=[pltpu.VMEM((far_tokens, width), bf16)],
        compiler_params=params(28 + groups // 2),
        cost_estimate=LITTLE,
        name="attention_forward",
    )(
        scalars, alive, *got_own, *got_other, query_stack, grad_stack, scores_own, values, norm_gain, w_key, w_value
    )
    mixed_other = lax.ppermute(mixed_t, "row", swap)
    dquery, dkey = call(
        functools.partial(backward_kernel, views),
        [shape((tokens, part), bf16), shape((key_tokens, part), bf16)],
        (query_stack, grad_stack, dprob_own, keys, keys_far, values_far, attention_own, attention_far),
        "attention_backward",
        mebibytes=28 + groups // 2,
    )

    def after(value, *earlier):
        return lax.optimization_barrier((value, *earlier))[0]

    targets = groups * rows
    q_size = width // 4
    q_rows, o_rows = q_size // targets, inner // (4 * targets)
    q_block = (q_size, part)

    def first_exchange(sends):
        return lax.ppermute(sends[0], "scene", along_x), lax.ppermute(sends[1], "scene", along_y)

    def first_sum(parts, got, name, cost=LITTLE):
        blocks = [part_now.shape[1:] for part_now in parts[:2]]
        results = [shape(block, bf16) for block in blocks] + [shape(block, f32) for block in blocks]
        return call(first_sum_kernel, results, (parts[2], got[0], parts[3], got[1]), name, cost=cost)

    def second_exchange(sums):
        return lax.ppermute(sums[0], "scene", along_y), lax.ppermute(sums[1], "scene", along_x)

    pairs = groups // 2
    neighbours = [(i, i ^ 1) for i in range(groups)]
    split_rows = {"query_key": q_rows, "value_out": o_rows}

    def last_parts(addends, split, name):
        tile = (addends[0].shape[1], sum(now.shape[2] for now in addends[::2]))
        for bit in reversed(range(1, pairs.bit_length() - 1)):
            send, keep = call(
                functools.partial(tile_halves_kernel, bit),
                [shape((1 << bit, *tile), kind) for kind in (bf16, f32)],
                (scalars, *addends),
                "view_bit_" + name,
                SMEM,
            )
            addends = (keep, lax.ppermute(send, "view", [(i, i ^ (2 << bit)) for i in range(groups)]))
        lanes = tile[0] * tile[1] // (2 * split_rows[name])
        columns = width // 2
        far_same, far_cross, near_cross, mine = call(
            functools.partial(tile_cores_kernel, split, columns),
            [shape((split_rows[name], lanes), kind) for kind in (bf16, bf16, f32, f32)],
            (scalars, *addends),
            "last_parts_" + name,
            SMEM,
        )
        far_same = lax.ppermute(far_same, "view", [(i, i ^ 2) for i in range(groups)])
        far_cross = lax.ppermute(far_cross, ("view", "row"), [(i, i ^ 5) for i in range(targets)])
        near_cross = lax.ppermute(near_cross, "row", swap)
        return mine, far_same, near_cross, far_cross

    tile = (2 * o_rows, width // 2 + 2 * part)
    operands = (scalars, normed_t, normed_far_t, after(dvalue, dkey), mixed_t, mixed_other, upstream)
    tiles = (2, pairs, *tile)
    stay, send = call(
        functools.partial(value_out_kernel, True), [shape(tiles, bf16)] * 2, operands, "grad_value_out_sent", SMEM, 24
    )
    got = lax.ppermute(send, "view", neighbours)
    got_stay = lax.ppermute(after(stay, got), "view", neighbours)
    keep = call(
        functools.partial(value_out_kernel, False), [shape((2, *tiles), f32)], operands, "grad_value_out_kept", SMEM, 24
    )[0]
    q_later, k_later, q_now, k_now, q_keep, k_keep = call(
        query_key_kernel,
        [shape(block, bf16) for block in (q_block, q_block, q_block, q_block)]
        + [shape((2, *block), f32) for block in (q_block, q_block)],
        (scalars, normed_t, normed_far_t, after(dquery, send), dkey),
        "grad_query_key",
        SMEM,
        24,
    )
    q_got, k_got = first_exchange((q_later, k_later))
    q_first, k_first = first_exchange((q_now, k_now))
    later = call(
        go_on_kernel, [shape(q_block, bf16), shape(q_block, bf16)], (after(q_keep, keep), q_got, k_keep, k_got), "first_sum_query_key"
    )
    q_second, k_second = second_exchange(later)
    vo_shapes = ((2, pairs, 2 * o_rows, 2 * part), (2, pairs, 2 * o_rows, width // 2))

    def view_sum(block, arrived, kind, name):
        results = [shape(dims, kind) for dims in vo_shapes]
        return call(functools.partial(view_sum_kernel, block), results, (keep, arrived), name)

    vo_parts = view_sum(1, after(got, q_first, k_first), bf16, "view_sum_sent")
    vo_got = first_exchange(vo_parts)
    qk_tile = (2 * q_rows, 2 * part)
    qk_send, qk_keep = call(
        query_key_tiles_kernel,
        [shape((pairs, *qk_tile), kind) for kind in (bf16, f32)],
        (scalars, q_keep, q_first, q_second, k_keep, k_first, k_second),
        "second_sum_query_key",
        SMEM,
    )
    qk_addends = (qk_keep, lax.ppermute(qk_send, "view", neighbours))
    vo_parts = vo_parts + view_sum(0, after(got_stay, qk_send), f32, "view_sum_kept")
    vo_sums = first_sum(vo_parts, vo_got, "first_sum_value_out")
    v_got, o_got = second_exchange(vo_sums)
    addends = (vo_sums[3], o_got, vo_sums[2], v_got)
    qk_last = last_parts((after(qk_addends[0], vo_sums[0]), qk_addends[1]), query_key_cores, "query_key")
    qk_total = call(
        add_kernel, [shape((q_rows, 2 * part), f32)] * 2, qk_last, "last_sum_query_key"
    )
    vo_last = last_parts((after(addends[0], qk_last[0]), *addends[1:]), value_out_cores, "value_out")
    grad_query, grad_key = call(
        place_query_key_kernel,
        [shape((q_rows, inner), f32)] * 2,
        (scalars, *qk_total),
        "place_query_key",
        SMEM,
    )
    grad_value, grad_out = call(
        place_value_out_kernel,
        [shape((q_rows, inner), f32), shape((o_rows, width), f32)],
        (scalars, after(vo_last[0], grad_query), *vo_last[1:]),
        "last_sum_value_out",
        SMEM,
    )
    return grad_query, grad_key, grad_value, grad_out


def solution(mesh):
    tokens = P("scene", "view", "row", None, None)
    everywhere = P()
    grads = P(("scene", "view", "row"), None)
    return jax.shard_map(
        shards,
        mesh=mesh,
        in_specs=(
            tokens, everywhere, everywhere, everywhere, everywhere, everywhere, everywhere,
            P("scene", "view", None), P("scene", "view"), tokens,
        ),
        out_specs=(grads, grads, grads, grads),
        check_vma=False,
    )
```

```python
import functools

import jax
import jax.numpy as jnp
from jax import lax
from jax.experimental import pallas as pl
from jax.experimental.pallas import tpu as pltpu
from jax.sharding import PartitionSpec as P

HEAD_DIM = 64
EPSILON = 1e-06
SCALE = HEAD_DIM ** (-0.5)
MASKED = -1e30
MIB = 1024 * 1024
LITTLE = pl.CostEstimate(flops=1, bytes_accessed=1, transcendentals=0)
MUCH = pl.CostEstimate(flops=40_000_000_000, bytes_accessed=1, transcendentals=0)

VMEM = pl.BlockSpec(memory_space=pltpu.VMEM)
SMEM = pl.BlockSpec(memory_space=pltpu.SMEM)


def dot_nn(a, b):
    return lax.dot_general(a, b, (((1,), (0,)), ((), ())), preferred_element_type=jnp.float32)


def dot_nt(a, b):
    return lax.dot_general(a, b, (((1,), (1,)), ((), ())), preferred_element_type=jnp.float32)


def dot_tn(a, b):
    return lax.dot_general(a, b, (((0,), (0,)), ((), ())), preferred_element_type=jnp.float32)


def normalized(tokens, gain):
    x = tokens.astype(jnp.float32)
    mean = jnp.mean(x * x, -1, keepdims=True)
    return (x * lax.rsqrt(mean + EPSILON) * gain).astype(jnp.bfloat16)


def alive_kernel(views, groups, partners, alive):
    for g in range(groups * views):
        alive[g] = 0
    for u in range(views):
        for j in range(partners.shape[2]):
            partner = partners[0, u, j]

            @pl.when(partner >= 0)
            def _():
                alive[lax.div(partner, jnp.int32(views)) * views + u] = 1


def pick_kernel(groups, scalars, *refs):
    tables, lat, outgoing = refs[: groups - 1], refs[groups - 1], refs[groups:]
    views = lat.shape[0]
    for table, out in zip(tables, outgoing):
        wanted = jnp.int32(0)
        for u in range(table.shape[1]):
            for j in range(table.shape[2]):
                partner = table[0, u, j]
                here = (partner >= 0) & (lax.div(partner, jnp.int32(views)) == scalars[1])
                wanted = jnp.where(here, lax.rem(partner, jnp.int32(views)), wanted)
        out[...] = lat[wanted]


def core_half(scalars, size):
    return pl.ds(pl.multiple_of(scalars[0] * size, size), size)


def stacked(x, views):
    tokens, pair = x.shape
    low = (lax.broadcasted_iota(jnp.int32, (1, 1, pair), 2) < pair // 2).astype(x.dtype)
    x = x.reshape(views, tokens // views, pair)
    return jnp.concatenate((x * low, x * (1 - low)), axis=1).reshape(2 * tokens, pair)


def unstacked(x, views):
    rows, pair = x.shape
    low = lax.broadcasted_iota(jnp.int32, (1, 1, pair), 2) < pair // 2
    x = x.reshape(views, 2, rows // (2 * views), pair)
    return jnp.where(low, x[:, 0], x[:, 1]).reshape(rows // 2, pair)


def view_parts(x, views, axis):
    size = x.shape[axis] // views
    return [lax.slice_in_dim(x, u * size, (u + 1) * size, axis=axis) for u in range(views)]


def own_nt(a, b, views):
    pairs = zip(view_parts(a, views, 0), view_parts(b, views, 0))
    return jnp.concatenate([dot_nt(x, y) for x, y in pairs], axis=1)


def own_tn(a, b, views):
    pairs = zip(view_parts(a, views, 1), view_parts(b, views, 0))
    return jnp.concatenate([dot_tn(x, y) for x, y in pairs], axis=0)


def own_nn(a, b, views):
    pairs = zip(view_parts(a, views, 1), view_parts(b, views, 0))
    return jnp.concatenate([dot_nn(x, y) for x, y in pairs], axis=0)


def project_kernel(
    scalars, lat_own, lat_other, cot_own, cot_other, gain, taps, w_query, w_key, w_value, w_out,
    normed_t, keys, values, upstream, query_stack, grad_stack, scores_own, dprob_own, normed,
):
    views, strip, width = lat_own.shape
    scale = gain[...].reshape(1, width)
    row = scalars[0]

    def strip_of(u, half):
        index = 2 * u + (row if half == 0 else 1 - row)
        return pl.ds(pl.multiple_of(index * strip, strip), strip)

    for half, source in enumerate((lat_own, lat_other)):
        for u in range(views):
            normed[strip_of(u, half), :] = normalized(source[u], scale)
    first = row == 0
    chunk = 512
    column = lax.broadcasted_iota(jnp.int32, (strip, 1), 0)
    not_first = (column > 0).astype(jnp.float32)
    not_last = (column < strip - 1).astype(jnp.float32)
    for c in range(0, width, chunk):
        lanes = slice(c, c + chunk)
        tap = taps[:, lanes].astype(jnp.float32)
        top, middle, bottom = tap[0:3], tap[3:6], tap[6:9]
        cross = (jnp.where(first, top, bottom), jnp.where(first, bottom, top))
        for u in range(views):
            strips = [ref[u, :, lanes].astype(jnp.float32) for ref in (cot_own, cot_other)]
            shifted = []
            for x in strips:
                after = pltpu.roll(x, strip - 1, 0) * not_last
                before = pltpu.roll(x, 1, 0) * not_first
                shifted.append((after, x, before))
            for half in range(2):
                total = strips[half]
                for b in range(3):
                    total = total + middle[b : b + 1] * shifted[half][b]
                    total = total + cross[half][b : b + 1] * shifted[1 - half][b]
                upstream[strip_of(u, half), lanes] = total.astype(jnp.bfloat16)
    rows = normed[...]
    normed_t[...] = rows.T
    part = keys.shape[1]
    half = core_half(scalars, part)
    queries = dot_nn(rows, w_query[:, half]).astype(jnp.bfloat16)
    keys[...] = dot_nn(rows, w_key[:, half]).astype(jnp.bfloat16)
    values[...] = dot_nn(rows, w_value[:, half]).astype(jnp.bfloat16)
    out_grad = dot_nt(upstream[...], w_out[half, :]).astype(jnp.bfloat16)
    pair = 2 * HEAD_DIM
    for p in range(part // pair):
        lanes = slice(p * pair, (p + 1) * pair)
        q, g = stacked(queries[:, lanes], views), stacked(out_grad[:, lanes], views)
        query_stack[p], grad_stack[p] = q, g
        scores_own[p] = own_nt(keys[:, lanes], q, views) * SCALE
        dprob_own[p] = own_nt(values[:, lanes], g, views)


def forward_kernel(views, groups, scalars, alive, *refs):
    got_own, got_other, refs = refs[: groups - 1], refs[groups - 1 : 2 * groups - 2], refs[2 * groups - 2 :]
    query_stack, grad_stack, scores_own, values, gain, w_key, w_value, *refs = refs
    normed_far_t, keys_far, values_far, attention_own, attention_far, mixed_t, dvalue, normed_far = refs
    strip = got_own[0].shape[0]
    tokens, part = values.shape
    view_tokens = tokens // views
    here = scalars[1]
    scale_row = gain[...].reshape(1, normed_far.shape[1])
    pair = 2 * HEAD_DIM
    span = 2 * view_tokens
    column_view = lax.broadcasted_iota(jnp.int32, (1, views * span), 1) // span
    slot_alive = []
    for j in range(groups - 1):
        group = lax.bitwise_xor(here, jnp.int32(groups - 1 - j))
        start = 2 * j * strip
        normed_far[start : start + strip, :] = normalized(got_own[j][...], scale_row)
        normed_far[start + strip : start + 2 * strip, :] = normalized(got_other[j][...], scale_row)
        taken = jnp.zeros((1, views * span), jnp.int32)
        for u in range(views):
            taken = jnp.where(column_view == u, alive[group * views + u], taken)
        slot_alive.append(taken > 0)
    fetched = normed_far[...]
    normed_far_t[...] = fetched.T
    half = core_half(scalars, part)
    keys_far[...] = dot_nn(fetched, w_key[:, half]).astype(jnp.bfloat16)
    values_far[...] = dot_nn(fetched, w_value[:, half]).astype(jnp.bfloat16)
    for p in range(part // pair):
        lanes = slice(p * pair, (p + 1) * pair)
        q, g, s_own = query_stack[p], grad_stack[p], scores_own[p]
        s_far = dot_nt(keys_far[:, lanes], q) * SCALE
        s_far = jnp.concatenate(
            [
                jnp.where(slot_alive[j], s_far[j * view_tokens : (j + 1) * view_tokens], MASKED)
                for j in range(groups - 1)
            ],
            axis=0,
        )
        highest = jnp.maximum(jnp.max(s_own, 0, keepdims=True), jnp.max(s_far, 0, keepdims=True))
        e_own = jnp.exp(s_own - highest)
        e_far = jnp.exp(s_far - highest)
        inverse = 1.0 / (jnp.sum(e_own, 0, keepdims=True) + jnp.sum(e_far, 0, keepdims=True))
        a_own, a_far = e_own * inverse, e_far * inverse
        attention_own[p], attention_far[p] = a_own, a_far
        a_own, a_far = a_own.astype(jnp.bfloat16), a_far.astype(jnp.bfloat16)
        mix = own_tn(a_own, values[:, lanes], views) + dot_tn(a_far, values_far[:, lanes])
        mixed_t[lanes, :] = unstacked(mix, views).T.astype(jnp.bfloat16)
        dvalue[:tokens, lanes] = own_nn(a_own, g, views).astype(jnp.bfloat16)
        dvalue[tokens:, lanes] = dot_nn(a_far, g).astype(jnp.bfloat16)


def backward_kernel(
    views, query_stack, grad_stack, dprob_own, keys, keys_far, values_far, attention_own, attention_far, dquery, dkey
):
    tokens, part = keys.shape
    pair = 2 * HEAD_DIM
    for p in range(part // pair):
        lanes = slice(p * pair, (p + 1) * pair)
        q, g, dp_own = query_stack[p], grad_stack[p], dprob_own[p]
        a_own, a_far = attention_own[p], attention_far[p]
        dp_far = dot_nt(values_far[:, lanes], g)
        delta = jnp.sum(a_own * dp_own, 0, keepdims=True) + jnp.sum(a_far * dp_far, 0, keepdims=True)
        ds_own = (a_own * (dp_own - delta) * SCALE).astype(jnp.bfloat16)
        ds_far = (a_far * (dp_far - delta) * SCALE).astype(jnp.bfloat16)
        dq = own_tn(ds_own, keys[:, lanes], views) + dot_tn(ds_far, keys_far[:, lanes])
        dquery[:, lanes] = unstacked(dq, views).astype(jnp.bfloat16)
        dkey[:tokens, lanes] = own_nn(ds_own, q, views).astype(jnp.bfloat16)
        dkey[tokens:, lanes] = dot_nn(ds_far, q).astype(jnp.bfloat16)


def times(lefts, right):
    total, start = 0.0, 0
    for left in lefts:
        total = total + dot_nn(left, right[start : start + left.shape[1], :])
        start += left.shape[1]
    return total


def by_quarters(scalars, lefts, right, sends, keep, x_first):
    size = keep.shape[1]
    x, y = scalars[3], scalars[4]
    for targets, first in ((sends, 1), ([keep.at[0], keep.at[1]], 0)):
        for second in (1, 0):
            dx, dy = (first, second) if x_first else (second, first)
            block = 2 * lax.bitwise_xor(y, jnp.int32(dy)) + lax.bitwise_xor(x, jnp.int32(dx))
            rows = pl.ds(pl.multiple_of(block * size, size), size)
            target = targets[second]
            target[...] = times([left[rows, :] for left in lefts], right).astype(target.dtype)


def query_key_kernel(
    scalars, normed_t, normed_far_t, dquery, dkey, q_later, k_later, q_now, k_now, q_keep, k_keep
):
    by_quarters(scalars, (normed_t,), dquery[...], (q_now, q_later), q_keep, True)
    by_quarters(scalars, (normed_t, normed_far_t), dkey[...], (k_now, k_later), k_keep, False)


def go_on_kernel(q_keep, q_got, k_keep, k_got, q_later, k_later):
    for keep, got, later in ((q_keep, q_got, q_later), (k_keep, k_got, k_later)):
        later[...] = (keep[1] + got[...].astype(jnp.float32)).astype(jnp.bfloat16)


def value_out_kernel(sent, scalars, normed_t, normed_far_t, dvalue, mine, theirs, upstream, *targets):
    row, x, y = scalars[0], scalars[3], scalars[4]
    take_second = lax.rem(scalars[1], jnp.int32(2)) == (0 if sent else 1)
    stay, go_on = targets if sent else (targets[0].at[0], targets[0].at[1])
    _, pairs, size, _ = stay.shape
    half, quarter = upstream.shape[1] // 2, normed_t.shape[0] // 4
    value_right = dvalue[...]
    lanes = value_right.shape[1]
    places = [(dy, dx, pair) for dy in range(2) for dx in range(2) for pair in range(pairs)]
    rows = ([], [], [])
    for dy in range(2):
        to_y = lax.bitwise_xor(y, jnp.int32(dy))
        for dx in range(2):
            to_x = lax.bitwise_xor(x, jnp.int32(dx))
            out_rows = pl.ds(pl.multiple_of(to_x * (half // 4), half // 4), half // 4)
            out_block = jnp.where(row == to_y, mine[out_rows, :], theirs[out_rows, :])
            value_rows = pl.ds(pl.multiple_of((2 * to_y + to_x) * quarter, quarter), quarter)
            blocks = (normed_t[value_rows, :], normed_far_t[value_rows, :], out_block)
            for pair in range(pairs):
                for i, block in enumerate(blocks):
                    count = size if i == 2 else 2 * size
                    first = block[2 * pair * count : (2 * pair + 1) * count]
                    second = block[(2 * pair + 1) * count : (2 * pair + 2) * count]
                    rows[i].append(jnp.where(take_second, second, first))
    right = upstream[:, core_half(scalars, half)]
    own, far, out = [jnp.concatenate(parts, axis=0) for parts in rows]
    grad_v = times((own, far), value_right).astype(stay.dtype)
    grad_o = dot_nn(out, right).astype(stay.dtype)
    for i, (dy, dx, pair) in enumerate(places):
        (stay, go_on)[dy][dx, pair, :, :half] = grad_o[i * size : (i + 1) * size]
        for core in range(2):
            columns = slice(half + core * lanes, half + (core + 1) * lanes)
            part = grad_v[(2 * i + core) * size : (2 * i + core + 1) * size]
            (stay, go_on)[dx][dy, pair, :, columns] = part


def view_sum_kernel(block, keep, got, x_part, y_part):
    half = y_part.shape[3]
    for i in range(2):
        total = keep[block, i] + got[i].astype(jnp.float32)
        x_part[i] = total[:, :, half:].astype(x_part.dtype)
        y_part[i] = total[:, :, :half].astype(y_part.dtype)


def first_sum_kernel(x_keep, x_got, y_keep, y_got, x_later, y_later, x_now, y_now):
    for keep, got, later, now in ((x_keep, x_got, x_later, x_now), (y_keep, y_got, y_later, y_now)):
        later[...] = (keep[1] + got[1].astype(jnp.float32)).astype(jnp.bfloat16)
        now[...] = keep[0] + got[0].astype(jnp.float32)


def query_key_tiles_kernel(scalars, q_keep, q_first, q_second, k_keep, k_first, k_second, send, keep):
    odd = lax.rem(scalars[1], jnp.int32(2)) == 1
    total = [
        kept[0] + first[...].astype(jnp.float32) + second[...].astype(jnp.float32)
        for kept, first, second in ((q_keep, q_first, q_second), (k_keep, k_first, k_second))
    ]
    total = jnp.concatenate(total, axis=1)
    pairs, size, _ = send.shape
    for pair in range(pairs):
        first = total[2 * pair * size : (2 * pair + 1) * size]
        second = total[(2 * pair + 1) * size : (2 * pair + 2) * size]
        send[pair] = jnp.where(odd, first, second).astype(send.dtype)
        keep[pair] = jnp.where(odd, second, first)


def summed_tile(addends, place):
    place = pl.ds(place, 1)
    total = [now[place] + got[place].astype(jnp.float32) for now, got in zip(addends[::2], addends[1::2])]
    return (jnp.concatenate(total, axis=2) if len(total) == 2 else total[0])[0]


def view_bit(scalars, bit):
    return lax.rem(lax.div(scalars[1], jnp.int32(2 << bit)), jnp.int32(2))


def tile_halves_kernel(bit, scalars, *refs):
    addends, (send, keep) = refs[:-2], refs[-2:]
    count = keep.shape[0]
    mine = view_bit(scalars, bit)
    for target, part in ((send, 1 - mine), (keep, mine)):
        for i in range(count):
            target[i] = summed_tile(addends, part * count + i).astype(target.dtype)


def query_key_cores(tile, half):
    size = tile.shape[0] // 2
    return tile[:size], tile[size:]


def value_out_cores(tile, half):
    size, lanes = tile.shape[0] // 2, (tile.shape[1] - half) // 2
    parts = []
    for core in range(2):
        value = tile[:, half + core * lanes : half + (core + 1) * lanes]
        out = tile[core * size : (core + 1) * size, :half]
        parts.append(jnp.concatenate((out, value[:size], value[size:]), axis=1))
    return parts


def tile_cores_kernel(split, half, scalars, *refs):
    addends, (far_same, far_cross, near_cross, mine) = refs[:-4], refs[-4:]
    bit = view_bit(scalars, 0)
    for place, same, cross in ((1 - bit, far_same, far_cross), (bit, mine, near_cross)):
        parts = split(summed_tile(addends, place), half)
        same[...] = jnp.where(scalars[0] == 0, parts[0], parts[1]).astype(same.dtype)
        cross[...] = jnp.where(scalars[0] == 0, parts[1], parts[0]).astype(cross.dtype)


def last_sums(scalars, mine, far_same, near_cross, far_cross):
    for near, far, core in ((mine, far_same, scalars[0]), (near_cross, far_cross, 1 - scalars[0])):
        yield near[...] + far[...].astype(jnp.float32), core


def add_kernel(mine, far_same, near_cross, far_cross, same, cross):
    same[...] = mine[...] + far_same[...].astype(jnp.float32)
    cross[...] = near_cross[...] + far_cross[...].astype(jnp.float32)


def place_query_key_kernel(scalars, same, cross, query, key):
    size = query.shape[1] // 2
    for total, core in ((same, scalars[0]), (cross, 1 - scalars[0])):
        columns = pl.ds(pl.multiple_of(core * size, size), size)
        query[:, columns] = total[:, :size]
        key[:, columns] = total[:, size:]


def place_value_out_kernel(scalars, mine, far_same, near_cross, far_cross, value, out):
    size, width = mine.shape
    half, part = out.shape[1] // 2, value.shape[1] // 2
    for total, core in last_sums(scalars, mine, far_same, near_cross, far_cross):
        out[:, pl.ds(pl.multiple_of(core * half, half), half)] = total[:, :half]
        columns = pl.ds(pl.multiple_of(core * part, part), part)
        value[:size, columns] = total[:, half : half + part]
        value[size:, columns] = total[:, half + part :]


def params(mebibytes):
    return pltpu.CompilerParams(vmem_limit_bytes=mebibytes * MIB)


def shape(dims, kind):
    return jax.ShapeDtypeStruct(dims, kind)


def shards(latents, norm_gain, w_query, w_key, w_value, w_out, kernel, partners, counts, cotangent):
    views, strip_rows, columns, width = latents.shape[1:]
    inner = w_query.shape[1]
    groups, rows = lax.axis_size("view"), lax.axis_size("row")
    scenes = lax.axis_size("scene")
    assert (strip_rows, rows, scenes) == (1, 2, 4)
    strip = strip_rows * columns
    part = inner // rows
    tokens = views * 2 * strip
    key_tokens = tokens + (groups - 1) * 2 * strip
    bf16, f32, i32 = jnp.bfloat16, jnp.float32, jnp.int32

    row, view, scene = lax.axis_index("row"), lax.axis_index("view"), lax.axis_index("scene")
    scalars = jnp.stack((row, view, scene, scene % 2, scene // 2)).astype(i32)
    swap = [(0, 1), (1, 0)]
    along_x, along_y = [(i, i ^ 1) for i in range(scenes)], [(i, i ^ 2) for i in range(scenes)]

    alive = pl.pallas_call(
        functools.partial(alive_kernel, views, groups),
        in_specs=[SMEM],
        out_specs=SMEM,
        out_shape=shape((groups * views,), i32),
        cost_estimate=MUCH,
        compiler_params=params(4),
        name="alive",
    )(partners)
    between = [[(i, i ^ d) for i in range(groups)] for d in reversed(range(1, groups))]
    granted = [lax.ppermute(partners, "view", pairs) for pairs in between]

    granted, alive = lax.optimization_barrier((granted, alive))
    lat = latents[0].reshape(views, strip, width)
    cot = cotangent[0].reshape(views, strip, width)
    lat_other = lax.ppermute(lat, "row", swap)
    cot_other = lax.ppermute(cot, "row", swap)

    outgoing = pl.pallas_call(
        functools.partial(pick_kernel, groups),
        in_specs=[SMEM] * groups + [VMEM],
        out_specs=[VMEM] * (groups - 1),
        out_shape=[shape((strip, width), bf16)] * (groups - 1),
        compiler_params=params(8),
        cost_estimate=MUCH,
        name="pick",
    )(scalars, *granted, lat)
    got_own = [lax.ppermute(part_out, "view", pairs) for part_out, pairs in zip(outgoing, between)]
    head_pairs = part // (2 * HEAD_DIM)
    normed_t, keys, values, upstream, query_stack, grad_stack, scores_own, dprob_own = pl.pallas_call(
        project_kernel,
        in_specs=[SMEM] + [VMEM] * 10,
        out_specs=[VMEM] * 8,
        out_shape=[
            shape((width, tokens), bf16),
            shape((tokens, part), bf16),
            shape((tokens, part), bf16),
            shape((tokens, width), bf16),
            shape((head_pairs, 2 * tokens, 2 * HEAD_DIM), bf16),
            shape((head_pairs, 2 * tokens, 2 * HEAD_DIM), bf16),
            shape((head_pairs, 2 * strip, 2 * tokens), f32),
            shape((head_pairs, 2 * strip, 2 * tokens), f32),
        ],
        scratch_shapes=[pltpu.VMEM((tokens, width), bf16)],
        compiler_params=params(28),
        cost_estimate=LITTLE,
        name="project",
    )(scalars, lat, lat_other, cot, cot_other, norm_gain, kernel, w_query, w_key, w_value, w_out)

    got_own, normed_t = lax.optimization_barrier((got_own, normed_t))
    got_other = [lax.ppermute(got, "row", swap) for got in got_own]

    def call(kernel_body, results, operands, name, first=VMEM, mebibytes=16, cost=LITTLE):
        outputs = pl.pallas_call(
            kernel_body,
            in_specs=[first] + [VMEM] * (len(operands) - 1),
            out_specs=[VMEM] * len(results),
            out_shape=results,
            compiler_params=params(mebibytes),
            cost_estimate=cost,
            name=name,
        )(*operands)
        return list(outputs)

    far_tokens = key_tokens - tokens
    normed_far_t, keys_far, values_far, attention_own, attention_far, mixed_t, dvalue = pl.pallas_call(
        functools.partial(forward_kernel, views, groups),
        in_specs=[SMEM] * 2 + [VMEM] * (2 * groups - 2 + 7),
        out_specs=[VMEM] * 7,
        out_shape=[
            shape((width, far_tokens), bf16),
            shape((far_tokens, part), bf16),
            shape((far_tokens, part), bf16),
            shape((head_pairs, 2 * strip, 2 * tokens), f32),
            shape((head_pairs, far_tokens, 2 * tokens), f32),
            shape((part, tokens), bf16),
            shape((key_tokens, part), bf16),
        ],
        scratch_shapes=[pltpu.VMEM((far_tokens, width), bf16)],
        compiler_params=params(28 + groups // 2),
        cost_estimate=LITTLE,
        name="attention_forward",
    )(
        scalars, alive, *got_own, *got_other, query_stack, grad_stack, scores_own, values, norm_gain, w_key, w_value
    )
    mixed_other = lax.ppermute(mixed_t, "row", swap)
    dquery, dkey = call(
        functools.partial(backward_kernel, views),
        [shape((tokens, part), bf16), shape((key_tokens, part), bf16)],
        (query_stack, grad_stack, dprob_own, keys, keys_far, values_far, attention_own, attention_far),
        "attention_backward",
        mebibytes=28 + groups // 2,
    )

    def after(value, *earlier):
        return lax.optimization_barrier((value, *earlier))[0]

    targets = groups * rows
    q_size = width // 4
    q_rows, o_rows = q_size // targets, inner // (4 * targets)
    q_block = (q_size, part)

    def first_exchange(sends):
        return lax.ppermute(sends[0], "scene", along_x), lax.ppermute(sends[1], "scene", along_y)

    def first_sum(parts, got, name, cost=LITTLE):
        blocks = [part_now.shape[1:] for part_now in parts[:2]]
        results = [shape(block, bf16) for block in blocks] + [shape(block, f32) for block in blocks]
        return call(first_sum_kernel, results, (parts[2], got[0], parts[3], got[1]), name, cost=cost)

    def second_exchange(sums):
        return lax.ppermute(sums[0], "scene", along_y), lax.ppermute(sums[1], "scene", along_x)

    pairs = groups // 2
    neighbours = [(i, i ^ 1) for i in range(groups)]
    split_rows = {"query_key": q_rows, "value_out": o_rows}

    def last_parts(addends, split, name):
        tile = (addends[0].shape[1], sum(now.shape[2] for now in addends[::2]))
        for bit in reversed(range(1, pairs.bit_length() - 1)):
            send, keep = call(
                functools.partial(tile_halves_kernel, bit),
                [shape((1 << bit, *tile), kind) for kind in (bf16, f32)],
                (scalars, *addends),
                "view_bit_" + name,
                SMEM,
            )
            addends = (keep, lax.ppermute(send, "view", [(i, i ^ (2 << bit)) for i in range(groups)]))
        lanes = tile[0] * tile[1] // (2 * split_rows[name])
        columns = width // 2
        far_same, far_cross, near_cross, mine = call(
            functools.partial(tile_cores_kernel, split, columns),
            [shape((split_rows[name], lanes), kind) for kind in (bf16, bf16, f32, f32)],
            (scalars, *addends),
            "last_parts_" + name,
            SMEM,
        )
        far_same = lax.ppermute(far_same, "view", [(i, i ^ 2) for i in range(groups)])
        far_cross = lax.ppermute(far_cross, ("view", "row"), [(i, i ^ 5) for i in range(targets)])
        near_cross = lax.ppermute(near_cross, "row", swap)
        return mine, far_same, near_cross, far_cross

    tile = (2 * o_rows, width // 2 + 2 * part)
    operands = (scalars, normed_t, normed_far_t, after(dvalue, dkey), mixed_t, mixed_other, upstream)
    tiles = (2, pairs, *tile)
    stay, send = call(
        functools.partial(value_out_kernel, True), [shape(tiles, bf16)] * 2, operands, "grad_value_out_sent", SMEM, 24
    )
    got = lax.ppermute(send, "view", neighbours)
    keep = call(
        functools.partial(value_out_kernel, False), [shape((2, *tiles), f32)], operands, "grad_value_out_kept", SMEM, 24
    )[0]
    q_later, k_later, q_now, k_now, q_keep, k_keep = call(
        query_key_kernel,
        [shape(block, bf16) for block in (q_block, q_block, q_block, q_block)]
        + [shape((2, *block), f32) for block in (q_block, q_block)],
        (scalars, normed_t, normed_far_t, after(dquery, send), dkey),
        "grad_query_key",
        SMEM,
        24,
    )
    q_got, k_got = first_exchange((q_later, k_later))
    q_first, k_first = first_exchange((q_now, k_now))
    later = call(
        go_on_kernel, [shape(q_block, bf16), shape(q_block, bf16)], (after(q_keep, keep), q_got, k_keep, k_got), "first_sum_query_key"
    )
    q_second, k_second = second_exchange(later)
    got_stay = lax.ppermute(after(stay, got, later[0]), "view", neighbours)
    vo_shapes = ((2, pairs, 2 * o_rows, 2 * part), (2, pairs, 2 * o_rows, width // 2))

    def view_sum(block, arrived, kind, name):
        results = [shape(dims, kind) for dims in vo_shapes]
        return call(functools.partial(view_sum_kernel, block), results, (keep, arrived), name)

    vo_parts = view_sum(1, after(got, q_first, k_first), bf16, "view_sum_sent")
    vo_got = first_exchange(vo_parts)
    qk_tile = (2 * q_rows, 2 * part)
    qk_send, qk_keep = call(
        query_key_tiles_kernel,
        [shape((pairs, *qk_tile), kind) for kind in (bf16, f32)],
        (scalars, q_keep, q_first, q_second, k_keep, k_first, k_second),
        "second_sum_query_key",
        SMEM,
    )
    qk_addends = (qk_keep, lax.ppermute(qk_send, "view", neighbours))
    vo_parts = vo_parts + view_sum(0, after(got_stay, qk_send), f32, "view_sum_kept")
    vo_sums = first_sum(vo_parts, vo_got, "first_sum_value_out")
    v_got, o_got = second_exchange(vo_sums)
    addends = (vo_sums[3], o_got, vo_sums[2], v_got)
    qk_last = last_parts((after(qk_addends[0], vo_sums[0]), qk_addends[1]), query_key_cores, "query_key")
    qk_total = call(
        add_kernel, [shape((q_rows, 2 * part), f32)] * 2, qk_last, "last_sum_query_key"
    )
    vo_last = last_parts((after(addends[0], qk_last[0]), *addends[1:]), value_out_cores, "value_out")
    grad_query, grad_key = call(
        place_query_key_kernel,
        [shape((q_rows, inner), f32)] * 2,
        (scalars, *qk_total),
        "place_query_key",
        SMEM,
    )
    grad_value, grad_out = call(
        place_value_out_kernel,
        [shape((q_rows, inner), f32), shape((o_rows, width), f32)],
        (scalars, after(vo_last[0], grad_query), *vo_last[1:]),
        "last_sum_value_out",
        SMEM,
    )
    return grad_query, grad_key, grad_value, grad_out


def solution(mesh):
    tokens = P("scene", "view", "row", None, None)
    everywhere = P()
    grads = P(("scene", "view", "row"), None)
    return jax.shard_map(
        shards,
        mesh=mesh,
        in_specs=(
            tokens, everywhere, everywhere, everywhere, everywhere, everywhere, everywhere,
            P("scene", "view", None), P("scene", "view"), tokens,
        ),
        out_specs=(grads, grads, grads, grads),
        check_vma=False,
    )
```

```python
import functools

import jax
import jax.numpy as jnp
from jax import lax
from jax.experimental import pallas as pl
from jax.experimental.pallas import tpu as pltpu
from jax.sharding import PartitionSpec as P

HEAD_DIM = 64
EPSILON = 1e-06
SCALE = HEAD_DIM ** (-0.5)
MASKED = -1e30
MIB = 1024 * 1024
LITTLE = pl.CostEstimate(flops=1, bytes_accessed=1, transcendentals=0)
MUCH = pl.CostEstimate(flops=40_000_000_000, bytes_accessed=1, transcendentals=0)

VMEM = pl.BlockSpec(memory_space=pltpu.VMEM)
SMEM = pl.BlockSpec(memory_space=pltpu.SMEM)


def dot_nn(a, b):
    return lax.dot_general(a, b, (((1,), (0,)), ((), ())), preferred_element_type=jnp.float32)


def dot_nt(a, b):
    return lax.dot_general(a, b, (((1,), (1,)), ((), ())), preferred_element_type=jnp.float32)


def dot_tn(a, b):
    return lax.dot_general(a, b, (((0,), (0,)), ((), ())), preferred_element_type=jnp.float32)


def normalized(tokens, gain):
    x = tokens.astype(jnp.float32)
    mean = jnp.mean(x * x, -1, keepdims=True)
    return (x * lax.rsqrt(mean + EPSILON) * gain).astype(jnp.bfloat16)


def alive_kernel(views, groups, partners, alive):
    for g in range(groups * views):
        alive[g] = 0
    for u in range(views):
        for j in range(partners.shape[2]):
            partner = partners[0, u, j]

            @pl.when(partner >= 0)
            def _():
                alive[lax.div(partner, jnp.int32(views)) * views + u] = 1


def pick_kernel(groups, scalars, *refs):
    tables, lat, outgoing = refs[: groups - 1], refs[groups - 1], refs[groups:]
    views = lat.shape[0]
    for table, out in zip(tables, outgoing):
        wanted = jnp.int32(0)
        for u in range(table.shape[1]):
            for j in range(table.shape[2]):
                partner = table[0, u, j]
                here = (partner >= 0) & (lax.div(partner, jnp.int32(views)) == scalars[1])
                wanted = jnp.where(here, lax.rem(partner, jnp.int32(views)), wanted)
        out[...] = lat[wanted]


def core_half(scalars, size):
    return pl.ds(pl.multiple_of(scalars[0] * size, size), size)


def stacked(x, views):
    tokens, pair = x.shape
    low = (lax.broadcasted_iota(jnp.int32, (1, 1, pair), 2) < pair // 2).astype(x.dtype)
    x = x.reshape(views, tokens // views, pair)
    return jnp.concatenate((x * low, x * (1 - low)), axis=1).reshape(2 * tokens, pair)


def unstacked(x, views):
    rows, pair = x.shape
    low = lax.broadcasted_iota(jnp.int32, (1, 1, pair), 2) < pair // 2
    x = x.reshape(views, 2, rows // (2 * views), pair)
    return jnp.where(low, x[:, 0], x[:, 1]).reshape(rows // 2, pair)


def view_parts(x, views, axis):
    size = x.shape[axis] // views
    return [lax.slice_in_dim(x, u * size, (u + 1) * size, axis=axis) for u in range(views)]


def own_nt(a, b, views):
    pairs = zip(view_parts(a, views, 0), view_parts(b, views, 0))
    return jnp.concatenate([dot_nt(x, y) for x, y in pairs], axis=1)


def own_tn(a, b, views):
    pairs = zip(view_parts(a, views, 1), view_parts(b, views, 0))
    return jnp.concatenate([dot_tn(x, y) for x, y in pairs], axis=0)


def own_nn(a, b, views):
    pairs = zip(view_parts(a, views, 1), view_parts(b, views, 0))
    return jnp.concatenate([dot_nn(x, y) for x, y in pairs], axis=0)


def project_kernel(
    scalars, lat_own, lat_other, cot_own, cot_other, gain, taps, w_query, w_key, w_value, w_out,
    normed_t, keys, values, upstream, query_stack, grad_stack, scores_own, dprob_own, normed,
):
    views, strip, width = lat_own.shape
    scale = gain[...].reshape(1, width)
    row = scalars[0]

    def strip_of(u, half):
        index = 2 * u + (row if half == 0 else 1 - row)
        return pl.ds(pl.multiple_of(index * strip, strip), strip)

    for half, source in enumerate((lat_own, lat_other)):
        for u in range(views):
            normed[strip_of(u, half), :] = normalized(source[u], scale)
    first = row == 0
    chunk = 512
    column = lax.broadcasted_iota(jnp.int32, (strip, 1), 0)
    not_first = (column > 0).astype(jnp.float32)
    not_last = (column < strip - 1).astype(jnp.float32)
    for c in range(0, width, chunk):
        lanes = slice(c, c + chunk)
        tap = taps[:, lanes].astype(jnp.float32)
        top, middle, bottom = tap[0:3], tap[3:6], tap[6:9]
        cross = (jnp.where(first, top, bottom), jnp.where(first, bottom, top))
        for u in range(views):
            strips = [ref[u, :, lanes].astype(jnp.float32) for ref in (cot_own, cot_other)]
            shifted = []
            for x in strips:
                after = pltpu.roll(x, strip - 1, 0) * not_last
                before = pltpu.roll(x, 1, 0) * not_first
                shifted.append((after, x, before))
            for half in range(2):
                total = strips[half]
                for b in range(3):
                    total = total + middle[b : b + 1] * shifted[half][b]
                    total = total + cross[half][b : b + 1] * shifted[1 - half][b]
                upstream[strip_of(u, half), lanes] = total.astype(jnp.bfloat16)
    rows = normed[...]
    normed_t[...] = rows.T
    part = keys.shape[1]
    half = core_half(scalars, part)
    queries = dot_nn(rows, w_query[:, half]).astype(jnp.bfloat16)
    keys[...] = dot_nn(rows, w_key[:, half]).astype(jnp.bfloat16)
    values[...] = dot_nn(rows, w_value[:, half]).astype(jnp.bfloat16)
    out_grad = dot_nt(upstream[...], w_out[half, :]).astype(jnp.bfloat16)
    pair = 2 * HEAD_DIM
    for p in range(part // pair):
        lanes = slice(p * pair, (p + 1) * pair)
        q, g = stacked(queries[:, lanes], views), stacked(out_grad[:, lanes], views)
        query_stack[p], grad_stack[p] = q, g
        scores_own[p] = own_nt(keys[:, lanes], q, views) * SCALE
        dprob_own[p] = own_nt(values[:, lanes], g, views)


def forward_kernel(views, groups, scalars, alive, *refs):
    got_own, got_other, refs = refs[: groups - 1], refs[groups - 1 : 2 * groups - 2], refs[2 * groups - 2 :]
    query_stack, grad_stack, scores_own, values, gain, w_key, w_value, *refs = refs
    normed_far_t, keys_far, values_far, attention_own, attention_far, mixed_t, dvalue, normed_far = refs
    strip = got_own[0].shape[0]
    tokens, part = values.shape
    view_tokens = tokens // views
    here = scalars[1]
    scale_row = gain[...].reshape(1, normed_far.shape[1])
    pair = 2 * HEAD_DIM
    span = 2 * view_tokens
    column_view = lax.broadcasted_iota(jnp.int32, (1, views * span), 1) // span
    slot_alive = []
    for j in range(groups - 1):
        group = lax.bitwise_xor(here, jnp.int32(groups - 1 - j))
        start = 2 * j * strip
        normed_far[start : start + strip, :] = normalized(got_own[j][...], scale_row)
        normed_far[start + strip : start + 2 * strip, :] = normalized(got_other[j][...], scale_row)
        taken = jnp.zeros((1, views * span), jnp.int32)
        for u in range(views):
            taken = jnp.where(column_view == u, alive[group * views + u], taken)
        slot_alive.append(taken > 0)
    fetched = normed_far[...]
    normed_far_t[...] = fetched.T
    half = core_half(scalars, part)
    keys_far[...] = dot_nn(fetched, w_key[:, half]).astype(jnp.bfloat16)
    values_far[...] = dot_nn(fetched, w_value[:, half]).astype(jnp.bfloat16)
    for p in range(part // pair):
        lanes = slice(p * pair, (p + 1) * pair)
        q, g, s_own = query_stack[p], grad_stack[p], scores_own[p]
        s_far = dot_nt(keys_far[:, lanes], q) * SCALE
        s_far = jnp.concatenate(
            [
                jnp.where(slot_alive[j], s_far[j * view_tokens : (j + 1) * view_tokens], MASKED)
                for j in range(groups - 1)
            ],
            axis=0,
        )
        highest = jnp.maximum(jnp.max(s_own, 0, keepdims=True), jnp.max(s_far, 0, keepdims=True))
        e_own = jnp.exp(s_own - highest)
        e_far = jnp.exp(s_far - highest)
        inverse = 1.0 / (jnp.sum(e_own, 0, keepdims=True) + jnp.sum(e_far, 0, keepdims=True))
        a_own, a_far = e_own * inverse, e_far * inverse
        attention_own[p], attention_far[p] = a_own, a_far
        a_own, a_far = a_own.astype(jnp.bfloat16), a_far.astype(jnp.bfloat16)
        mix = own_tn(a_own, values[:, lanes], views) + dot_tn(a_far, values_far[:, lanes])
        mixed_t[lanes, :] = unstacked(mix, views).T.astype(jnp.bfloat16)
        dvalue[:tokens, lanes] = own_nn(a_own, g, views).astype(jnp.bfloat16)
        dvalue[tokens:, lanes] = dot_nn(a_far, g).astype(jnp.bfloat16)


def backward_kernel(
    views, query_stack, grad_stack, dprob_own, keys, keys_far, values_far, attention_own, attention_far, dquery, dkey
):
    tokens, part = keys.shape
    pair = 2 * HEAD_DIM
    for p in range(part // pair):
        lanes = slice(p * pair, (p + 1) * pair)
        q, g, dp_own = query_stack[p], grad_stack[p], dprob_own[p]
        a_own, a_far = attention_own[p], attention_far[p]
        dp_far = dot_nt(values_far[:, lanes], g)
        delta = jnp.sum(a_own * dp_own, 0, keepdims=True) + jnp.sum(a_far * dp_far, 0, keepdims=True)
        ds_own = (a_own * (dp_own - delta) * SCALE).astype(jnp.bfloat16)
        ds_far = (a_far * (dp_far - delta) * SCALE).astype(jnp.bfloat16)
        dq = own_tn(ds_own, keys[:, lanes], views) + dot_tn(ds_far, keys_far[:, lanes])
        dquery[:, lanes] = unstacked(dq, views).astype(jnp.bfloat16)
        dkey[:tokens, lanes] = own_nn(ds_own, q, views).astype(jnp.bfloat16)
        dkey[tokens:, lanes] = dot_nn(ds_far, q).astype(jnp.bfloat16)


def times(lefts, right):
    total, start = 0.0, 0
    for left in lefts:
        total = total + dot_nn(left, right[start : start + left.shape[1], :])
        start += left.shape[1]
    return total


def by_quarters(scalars, lefts, right, sends, keep, x_first):
    size = keep.shape[1]
    x, y = scalars[3], scalars[4]
    for targets, first in ((sends, 1), ([keep.at[0], keep.at[1]], 0)):
        for second in (1, 0):
            dx, dy = (first, second) if x_first else (second, first)
            block = 2 * lax.bitwise_xor(y, jnp.int32(dy)) + lax.bitwise_xor(x, jnp.int32(dx))
            rows = pl.ds(pl.multiple_of(block * size, size), size)
            target = targets[second]
            target[...] = times([left[rows, :] for left in lefts], right).astype(target.dtype)


def query_key_kernel(
    scalars, normed_t, normed_far_t, dquery, dkey, q_later, k_later, q_now, k_now, q_keep, k_keep
):
    by_quarters(scalars, (normed_t,), dquery[...], (q_now, q_later), q_keep, True)
    by_quarters(scalars, (normed_t, normed_far_t), dkey[...], (k_now, k_later), k_keep, False)


def go_on_kernel(q_keep, q_got, k_keep, k_got, q_later, k_later):
    for keep, got, later in ((q_keep, q_got, q_later), (k_keep, k_got, k_later)):
        later[...] = (keep[1] + got[...].astype(jnp.float32)).astype(jnp.bfloat16)


def value_out_kernel(sent, scalars, normed_t, normed_far_t, dvalue, mine, theirs, upstream, *targets):
    row, x, y = scalars[0], scalars[3], scalars[4]
    take_second = lax.rem(scalars[1], jnp.int32(2)) == (0 if sent else 1)
    stay, go_on = targets if sent else (targets[0].at[0], targets[0].at[1])
    _, pairs, size, _ = stay.shape
    half, quarter = upstream.shape[1] // 2, normed_t.shape[0] // 4
    value_right = dvalue[...]
    lanes = value_right.shape[1]
    places = [(dy, dx, pair) for dy in range(2) for dx in range(2) for pair in range(pairs)]
    rows = ([], [], [])
    for dy in range(2):
        to_y = lax.bitwise_xor(y, jnp.int32(dy))
        for dx in range(2):
            to_x = lax.bitwise_xor(x, jnp.int32(dx))
            out_rows = pl.ds(pl.multiple_of(to_x * (half // 4), half // 4), half // 4)
            out_block = jnp.where(row == to_y, mine[out_rows, :], theirs[out_rows, :])
            value_rows = pl.ds(pl.multiple_of((2 * to_y + to_x) * quarter, quarter), quarter)
            blocks = (normed_t[value_rows, :], normed_far_t[value_rows, :], out_block)
            for pair in range(pairs):
                for i, block in enumerate(blocks):
                    count = size if i == 2 else 2 * size
                    first = block[2 * pair * count : (2 * pair + 1) * count]
                    second = block[(2 * pair + 1) * count : (2 * pair + 2) * count]
                    rows[i].append(jnp.where(take_second, second, first))
    right = upstream[:, core_half(scalars, half)]
    own, far, out = [jnp.concatenate(parts, axis=0) for parts in rows]
    grad_v = times((own, far), value_right).astype(stay.dtype)
    grad_o = dot_nn(out, right).astype(stay.dtype)
    for i, (dy, dx, pair) in enumerate(places):
        (stay, go_on)[dy][dx, pair, :, :half] = grad_o[i * size : (i + 1) * size]
        for core in range(2):
            columns = slice(half + core * lanes, half + (core + 1) * lanes)
            part = grad_v[(2 * i + core) * size : (2 * i + core + 1) * size]
            (stay, go_on)[dx][dy, pair, :, columns] = part


def view_sum_kernel(block, keep, got, x_part, y_part):
    half = y_part.shape[3]
    for i in range(2):
        total = keep[block, i] + got[i].astype(jnp.float32)
        x_part[i] = total[:, :, half:].astype(x_part.dtype)
        y_part[i] = total[:, :, :half].astype(y_part.dtype)


def first_sum_kernel(x_keep, x_got, y_keep, y_got, x_later, y_later, x_now, y_now):
    for keep, got, later, now in ((x_keep, x_got, x_later, x_now), (y_keep, y_got, y_later, y_now)):
        later[...] = (keep[1] + got[1].astype(jnp.float32)).astype(jnp.bfloat16)
        now[...] = keep[0] + got[0].astype(jnp.float32)


def query_key_tiles_kernel(scalars, q_keep, q_first, q_second, k_keep, k_first, k_second, send, keep):
    odd = lax.rem(scalars[1], jnp.int32(2)) == 1
    total = [
        kept[0] + first[...].astype(jnp.float32) + second[...].astype(jnp.float32)
        for kept, first, second in ((q_keep, q_first, q_second), (k_keep, k_first, k_second))
    ]
    total = jnp.concatenate(total, axis=1)
    pairs, size, _ = send.shape
    for pair in range(pairs):
        first = total[2 * pair * size : (2 * pair + 1) * size]
        second = total[(2 * pair + 1) * size : (2 * pair + 2) * size]
        send[pair] = jnp.where(odd, first, second).astype(send.dtype)
        keep[pair] = jnp.where(odd, second, first)


def summed_tile(addends, place):
    place = pl.ds(place, 1)
    total = [now[place] + got[place].astype(jnp.float32) for now, got in zip(addends[::2], addends[1::2])]
    return (jnp.concatenate(total, axis=2) if len(total) == 2 else total[0])[0]


def view_bit(scalars, bit):
    return lax.rem(lax.div(scalars[1], jnp.int32(2 << bit)), jnp.int32(2))


def tile_halves_kernel(bit, scalars, *refs):
    addends, (send, keep) = refs[:-2], refs[-2:]
    count = keep.shape[0]
    mine = view_bit(scalars, bit)
    for target, part in ((send, 1 - mine), (keep, mine)):
        for i in range(count):
            target[i] = summed_tile(addends, part * count + i).astype(target.dtype)


def query_key_cores(tile, half):
    size = tile.shape[0] // 2
    return tile[:size], tile[size:]


def value_out_cores(tile, half):
    size, lanes = tile.shape[0] // 2, (tile.shape[1] - half) // 2
    parts = []
    for core in range(2):
        value = tile[:, half + core * lanes : half + (core + 1) * lanes]
        out = tile[core * size : (core + 1) * size, :half]
        parts.append(jnp.concatenate((out, value[:size], value[size:]), axis=1))
    return parts


def tile_cores_kernel(split, half, scalars, *refs):
    addends, (far_same, far_cross, near_cross, mine) = refs[:-4], refs[-4:]
    bit = view_bit(scalars, 0)
    for place, same, cross in ((1 - bit, far_same, far_cross), (bit, mine, near_cross)):
        parts = split(summed_tile(addends, place), half)
        same[...] = jnp.where(scalars[0] == 0, parts[0], parts[1]).astype(same.dtype)
        cross[...] = jnp.where(scalars[0] == 0, parts[1], parts[0]).astype(cross.dtype)


def last_sums(scalars, mine, far_same, near_cross, far_cross):
    for near, far, core in ((mine, far_same, scalars[0]), (near_cross, far_cross, 1 - scalars[0])):
        yield near[...] + far[...].astype(jnp.float32), core


def add_kernel(mine, far_same, near_cross, far_cross, same, cross):
    same[...] = mine[...] + far_same[...].astype(jnp.float32)
    cross[...] = near_cross[...] + far_cross[...].astype(jnp.float32)


def place_query_key_kernel(scalars, same, cross, query, key):
    size = query.shape[1] // 2
    for total, core in ((same, scalars[0]), (cross, 1 - scalars[0])):
        columns = pl.ds(pl.multiple_of(core * size, size), size)
        query[:, columns] = total[:, :size]
        key[:, columns] = total[:, size:]


def place_value_out_kernel(scalars, mine, far_same, near_cross, far_cross, value, out):
    size, width = mine.shape
    half, part = out.shape[1] // 2, value.shape[1] // 2
    for total, core in last_sums(scalars, mine, far_same, near_cross, far_cross):
        out[:, pl.ds(pl.multiple_of(core * half, half), half)] = total[:, :half]
        columns = pl.ds(pl.multiple_of(core * part, part), part)
        value[:size, columns] = total[:, half : half + part]
        value[size:, columns] = total[:, half + part :]


def params(mebibytes):
    return pltpu.CompilerParams(vmem_limit_bytes=mebibytes * MIB)


def shape(dims, kind):
    return jax.ShapeDtypeStruct(dims, kind)


def shards(latents, norm_gain, w_query, w_key, w_value, w_out, kernel, partners, counts, cotangent):
    views, strip_rows, columns, width = latents.shape[1:]
    inner = w_query.shape[1]
    groups, rows = lax.axis_size("view"), lax.axis_size("row")
    scenes = lax.axis_size("scene")
    assert (strip_rows, rows, scenes) == (1, 2, 4)
    strip = strip_rows * columns
    part = inner // rows
    tokens = views * 2 * strip
    key_tokens = tokens + (groups - 1) * 2 * strip
    bf16, f32, i32 = jnp.bfloat16, jnp.float32, jnp.int32

    row, view, scene = lax.axis_index("row"), lax.axis_index("view"), lax.axis_index("scene")
    scalars = jnp.stack((row, view, scene, scene % 2, scene // 2)).astype(i32)
    swap = [(0, 1), (1, 0)]
    along_x, along_y = [(i, i ^ 1) for i in range(scenes)], [(i, i ^ 2) for i in range(scenes)]

    alive = pl.pallas_call(
        functools.partial(alive_kernel, views, groups),
        in_specs=[SMEM],
        out_specs=SMEM,
        out_shape=shape((groups * views,), i32),
        cost_estimate=MUCH,
        compiler_params=params(4),
        name="alive",
    )(partners)
    between = [[(i, i ^ d) for i in range(groups)] for d in reversed(range(1, groups))]
    granted = [lax.ppermute(partners, "view", pairs) for pairs in between]

    granted, alive = lax.optimization_barrier((granted, alive))
    lat = latents[0].reshape(views, strip, width)
    cot = cotangent[0].reshape(views, strip, width)
    lat_other = lax.ppermute(lat, "row", swap)
    cot_other = lax.ppermute(cot, "row", swap)

    outgoing = pl.pallas_call(
        functools.partial(pick_kernel, groups),
        in_specs=[SMEM] * groups + [VMEM],
        out_specs=[VMEM] * (groups - 1),
        out_shape=[shape((strip, width), bf16)] * (groups - 1),
        compiler_params=params(8),
        cost_estimate=MUCH,
        name="pick",
    )(scalars, *granted, lat)
    got_own = [lax.ppermute(part_out, "view", pairs) for part_out, pairs in zip(outgoing, between)]
    head_pairs = part // (2 * HEAD_DIM)
    normed_t, keys, values, upstream, query_stack, grad_stack, scores_own, dprob_own = pl.pallas_call(
        project_kernel,
        in_specs=[SMEM] + [VMEM] * 10,
        out_specs=[VMEM] * 8,
        out_shape=[
            shape((width, tokens), bf16),
            shape((tokens, part), bf16),
            shape((tokens, part), bf16),
            shape((tokens, width), bf16),
            shape((head_pairs, 2 * tokens, 2 * HEAD_DIM), bf16),
            shape((head_pairs, 2 * tokens, 2 * HEAD_DIM), bf16),
            shape((head_pairs, 2 * strip, 2 * tokens), f32),
            shape((head_pairs, 2 * strip, 2 * tokens), f32),
        ],
        scratch_shapes=[pltpu.VMEM((tokens, width), bf16)],
        compiler_params=params(28),
        cost_estimate=LITTLE,
        name="project",
    )(scalars, lat, lat_other, cot, cot_other, norm_gain, kernel, w_query, w_key, w_value, w_out)

    got_own, normed_t = lax.optimization_barrier((got_own, normed_t))
    got_other = [lax.ppermute(got, "row", swap) for got in got_own]

    def call(kernel_body, results, operands, name, first=VMEM, mebibytes=16, cost=LITTLE):
        outputs = pl.pallas_call(
            kernel_body,
            in_specs=[first] + [VMEM] * (len(operands) - 1),
            out_specs=[VMEM] * len(results),
            out_shape=results,
            compiler_params=params(mebibytes),
            cost_estimate=cost,
            name=name,
        )(*operands)
        return list(outputs)

    far_tokens = key_tokens - tokens
    normed_far_t, keys_far, values_far, attention_own, attention_far, mixed_t, dvalue = pl.pallas_call(
        functools.partial(forward_kernel, views, groups),
        in_specs=[SMEM] * 2 + [VMEM] * (2 * groups - 2 + 7),
        out_specs=[VMEM] * 7,
        out_shape=[
            shape((width, far_tokens), bf16),
            shape((far_tokens, part), bf16),
            shape((far_tokens, part), bf16),
            shape((head_pairs, 2 * strip, 2 * tokens), f32),
            shape((head_pairs, far_tokens, 2 * tokens), f32),
            shape((part, tokens), bf16),
            shape((key_tokens, part), bf16),
        ],
        scratch_shapes=[pltpu.VMEM((far_tokens, width), bf16)],
        compiler_params=params(28 + groups // 2),
        cost_estimate=LITTLE,
        name="attention_forward",
    )(
        scalars, alive, *got_own, *got_other, query_stack, grad_stack, scores_own, values, norm_gain, w_key, w_value
    )
    mixed_other = lax.ppermute(mixed_t, "row", swap)
    dquery, dkey = call(
        functools.partial(backward_kernel, views),
        [shape((tokens, part), bf16), shape((key_tokens, part), bf16)],
        (query_stack, grad_stack, dprob_own, keys, keys_far, values_far, attention_own, attention_far),
        "attention_backward",
        mebibytes=28 + groups // 2,
    )

    def after(value, *earlier):
        return lax.optimization_barrier((value, *earlier))[0]

    targets = groups * rows
    q_size = width // 4
    q_rows, o_rows = q_size // targets, inner // (4 * targets)
    q_block = (q_size, part)

    def first_exchange(sends):
        return lax.ppermute(sends[0], "scene", along_x), lax.ppermute(sends[1], "scene", along_y)

    def first_sum(parts, got, name, cost=LITTLE):
        blocks = [part_now.shape[1:] for part_now in parts[:2]]
        results = [shape(block, bf16) for block in blocks] + [shape(block, f32) for block in blocks]
        return call(first_sum_kernel, results, (parts[2], got[0], parts[3], got[1]), name, cost=cost)

    def second_exchange(sums):
        return lax.ppermute(sums[0], "scene", along_y), lax.ppermute(sums[1], "scene", along_x)

    pairs = groups // 2
    neighbours = [(i, i ^ 1) for i in range(groups)]
    split_rows = {"query_key": q_rows, "value_out": o_rows}

    def last_parts(addends, split, name):
        tile = (addends[0].shape[1], sum(now.shape[2] for now in addends[::2]))
        for bit in reversed(range(1, pairs.bit_length() - 1)):
            send, keep = call(
                functools.partial(tile_halves_kernel, bit),
                [shape((1 << bit, *tile), kind) for kind in (bf16, f32)],
                (scalars, *addends),
                "view_bit_" + name,
                SMEM,
            )
            addends = (keep, lax.ppermute(send, "view", [(i, i ^ (2 << bit)) for i in range(groups)]))
        lanes = tile[0] * tile[1] // (2 * split_rows[name])
        columns = width // 2
        far_same, far_cross, near_cross, mine = call(
            functools.partial(tile_cores_kernel, split, columns),
            [shape((split_rows[name], lanes), kind) for kind in (bf16, bf16, f32, f32)],
            (scalars, *addends),
            "last_parts_" + name,
            SMEM,
        )
        far_same = lax.ppermute(far_same, "view", [(i, i ^ 2) for i in range(groups)])
        far_cross = lax.ppermute(far_cross, ("view", "row"), [(i, i ^ 5) for i in range(targets)])
        near_cross = lax.ppermute(near_cross, "row", swap)
        return mine, far_same, near_cross, far_cross

    tile = (2 * o_rows, width // 2 + 2 * part)
    operands = (scalars, normed_t, normed_far_t, after(dvalue, dkey), mixed_t, mixed_other, upstream)
    tiles = (2, pairs, *tile)
    stay, send = call(
        functools.partial(value_out_kernel, True), [shape(tiles, bf16)] * 2, operands, "grad_value_out_sent", SMEM, 24
    )
    got = lax.ppermute(send, "view", neighbours)
    keep = call(
        functools.partial(value_out_kernel, False), [shape((2, *tiles), f32)], operands, "grad_value_out_kept", SMEM, 24
    )[0]
    q_later, k_later, q_now, k_now, q_keep, k_keep = call(
        query_key_kernel,
        [shape(block, bf16) for block in (q_block, q_block, q_block, q_block)]
        + [shape((2, *block), f32) for block in (q_block, q_block)],
        (scalars, normed_t, normed_far_t, after(dquery, send), dkey),
        "grad_query_key",
        SMEM,
        24,
    )
    q_got, k_got = first_exchange((q_later, k_later))
    q_first, k_first = first_exchange((q_now, k_now))
    later = call(
        go_on_kernel, [shape(q_block, bf16), shape(q_block, bf16)], (after(q_keep, keep), q_got, k_keep, k_got), "first_sum_query_key"
    )
    q_second, k_second = second_exchange(later)
    got_stay = lax.ppermute(after(stay, got, later[0]), "view", neighbours)
    vo_shapes = ((2, pairs, 2 * o_rows, 2 * part), (2, pairs, 2 * o_rows, width // 2))

    def view_sum(block, arrived, kind, name):
        results = [shape(dims, kind) for dims in vo_shapes]
        return call(functools.partial(view_sum_kernel, block), results, (keep, arrived), name)

    vo_parts = view_sum(1, after(got, q_first, k_first), bf16, "view_sum_sent")
    vo_got = first_exchange(vo_parts)
    qk_tile = (2 * q_rows, 2 * part)
    qk_send, qk_keep = call(
        query_key_tiles_kernel,
        [shape((pairs, *qk_tile), kind) for kind in (bf16, f32)],
        (scalars, q_keep, q_first, q_second, k_keep, k_first, k_second),
        "second_sum_query_key",
        SMEM,
    )
    qk_addends = (qk_keep, lax.ppermute(qk_send, "view", neighbours))
    vo_parts = vo_parts + view_sum(0, after(got_stay, qk_send), f32, "view_sum_kept")
    vo_sums = first_sum(vo_parts, vo_got, "first_sum_value_out")
    v_got, o_got = second_exchange(vo_sums)
    addends = (vo_sums[3], o_got, vo_sums[2], v_got)
    qk_last = last_parts((after(qk_addends[0], vo_sums[0]), qk_addends[1]), query_key_cores, "query_key")
    qk_total = call(
        add_kernel, [shape((q_rows, 2 * part), f32)] * 2, qk_last, "last_sum_query_key"
    )
    vo_last = last_parts(addends, value_out_cores, "value_out")
    grad_query, grad_key = call(
        place_query_key_kernel,
        [shape((q_rows, inner), f32)] * 2,
        (scalars, *qk_total),
        "place_query_key",
        SMEM,
    )
    grad_value, grad_out = call(
        place_value_out_kernel,
        [shape((q_rows, inner), f32), shape((o_rows, width), f32)],
        (scalars, after(vo_last[0], grad_query), *vo_last[1:]),
        "last_sum_value_out",
        SMEM,
    )
    return grad_query, grad_key, grad_value, grad_out


def solution(mesh):
    tokens = P("scene", "view", "row", None, None)
    everywhere = P()
    grads = P(("scene", "view", "row"), None)
    return jax.shard_map(
        shards,
        mesh=mesh,
        in_specs=(
            tokens, everywhere, everywhere, everywhere, everywhere, everywhere, everywhere,
            P("scene", "view", None), P("scene", "view"), tokens,
        ),
        out_specs=(grads, grads, grads, grads),
        check_vma=False,
    )
```
